32 devices in a mesh: dp: 8 (over z, x), tensor: 4 (over y, core).
Axes of the slice: x: 2, y: 2, z: 4, core: 2. Of those that a mesh axis runs over, the one named last changes fastest.
Arguments:
- images: bfloat16 [8, 729, 1152], P('dp'), may hold values from -6 to 6
- qkv_weight: bfloat16 [2, 3, 1152, 1152], P(None, None, None, 'tensor'), may hold values from -0.1875 to 0.1875
- qv_bias: float32 [2, 2, 1152], P(None, None, 'tensor'), may hold values from -0.6 to 0.6
- out_weight: bfloat16 [2, 1152, 1152], P(None, 'tensor'), may hold values from -1 to 1
- out_bias: float32 [2, 1152], replicated, may hold values from -1.8 to 1.8
- up_weight: bfloat16 [2, 1152, 4304], P(None, None, 'tensor'), may hold values from -0.1875 to 0.1875
- up_bias: float32 [2, 4304], P(None, 'tensor'), may hold values from -3 to 3
- down_weight: bfloat16 [2, 4304, 1152], P(None, 'tensor'), may hold values from -0.09375 to 0.09375
- down_bias: float32 [2, 1152], replicated, may hold values from -1.8 to 1.8
- norm_gain: float32 [2, 2, 1152], replicated, may hold values from 0.5 to 1.5
- norm_shift: float32 [2, 2, 1152], replicated, may hold values from -1.8 to 1.8
- cotangent: bfloat16 [8, 729, 1152], P('dp'), may hold values from -6 to 6
Outputs:
- encoded: bfloat16 [8, 729, 1152], P('dp')
- image_grad: bfloat16 [8, 729, 1152], P('dp')
- qkv_weight_grad: float32 [2, 3, 1152, 1152], P(None, None, None, 'tensor')
- qv_bias_grad: float32 [2, 2, 1152], P(None, None, 'tensor')
- out_weight_grad: float32 [2, 1152, 1152], P(None, 'tensor')
- out_bias_grad: float32 [2, 1152], replicated
- up_weight_grad: float32 [2, 1152, 4304], P(None, None, 'tensor')
- up_bias_grad: float32 [2, 4304], P(None, 'tensor')
- down_weight_grad: float32 [2, 4304, 1152], P(None, 'tensor')
- down_bias_grad: float32 [2, 1152], replicated
- norm_gain_grad: float32 [2, 2, 1152], replicated
- norm_shift_grad: float32 [2, 2, 1152], replicated
The draws below stay inside these ranges and needn't reach their ends.
All inputs are finite; a program needn't handle non-finite values.
Results may differ from the reference program's by a relative error of at most 0.017.
Values sent between devices are 32-bit elements; how exact they have to be, the bound alone decides.
A program may use at most 256 MiB of HBM per device.

```python
import jax
import jax.numpy as jnp
from jax import lax

D = 1152
HEADS = 16
HEAD = 72
FF = 4304
SEQ = 729
LAYERS = 2
IMAGES = 8


def levels(own_key, dims, split, smallest, high):
    level = 1.0
    for axis_at, shards_of in split:
        steps = jax.random.uniform(jax.random.fold_in(jax.random.fold_in(own_key, 6), axis_at), (shards_of,), jnp.float32, smallest / len(split), high / len(split))
        level = level * jnp.repeat(jnp.exp(steps), dims[axis_at] // shards_of).reshape((-1,) + (1,) * (len(dims) - 1 - axis_at))
    return level


def bell_draw(stream_key, shape, deviation, limit, cuts=(), dtype=jnp.bfloat16):
    loudness = levels(stream_key, shape, cuts, -0.22, 0.18) if cuts else 1.0
    values = jax.random.normal(stream_key, shape, jnp.float32) * deviation * loudness
    return jnp.minimum(jnp.maximum(values, -limit), limit).astype(dtype)


def setup_inputs(seed: int = 0) -> dict:
    streams_of = jax.random.split(jax.random.key(seed), 13)
    return {
        "images": bell_draw(streams_of[0], (IMAGES, SEQ, D), 1.0, 6.0, ((0, 8),)),
        "qkv_weight": bell_draw(streams_of[1], (LAYERS, 3, D, D), D ** -0.5, 0.1875, ((3, 4),)),
        "qv_bias": bell_draw(streams_of[2], (LAYERS, 2, D), 0.1, 0.6, ((2, 4),), jnp.float32),
        "out_weight": bell_draw(streams_of[3], (LAYERS, D, D), (D // 32) ** -0.5, 1.0, ((1, 4),)),
        "out_bias": bell_draw(streams_of[4], (LAYERS, D), 0.3, 1.8, (), jnp.float32),
        "up_weight": bell_draw(streams_of[5], (LAYERS, D, FF), D ** -0.5, 0.1875, ((2, 4),)),
        "up_bias": bell_draw(streams_of[6], (LAYERS, FF), 0.5, 3.0, ((1, 4),), jnp.float32),
        "down_weight": bell_draw(streams_of[7], (LAYERS, FF, D), FF ** -0.5, 0.09375, ((1, 4),)),
        "down_bias": bell_draw(streams_of[8], (LAYERS, D), 0.3, 1.8, (), jnp.float32),
        "norm_gain": jnp.clip(1.0 + 0.1 * jax.random.normal(streams_of[9], (LAYERS, 2, D), jnp.float32), 0.5, 1.5),
        "norm_shift": bell_draw(streams_of[10], (LAYERS, 2, D), 0.3, 1.8, (), jnp.float32),
        "cotangent": bell_draw(streams_of[11], (IMAGES, SEQ, D), 1.0, 6.0, ((0, 8),)),
    }


EPSILON = 1e-06

@jax.custom_vjp
def low(v):
    return lax.optimization_barrier(v.astype(jnp.bfloat16)).astype(jnp.float32)

@jax.custom_vjp
def low_back(v):
    return v

def low_keep(v):
    return (low(v), None)

def low_pass(kept, grad):
    return (grad,)

def back_keep(v):
    return (v, None)

def back_low(kept, grad):
    return (low(grad),)
low.defvjp(low_keep, low_pass)
low_back.defvjp(back_keep, back_low)

def project(left, right):
    return jnp.einsum('...i,ij->...j', left, right, precision=lax.Precision.HIGHEST, preferred_element_type=jnp.float32)

def normalize(state, gain, shift):
    centred = state - lax.optimization_barrier(jnp.mean(state, axis=-1, keepdims=True))
    spread = lax.optimization_barrier(jnp.mean(centred * centred, axis=-1, keepdims=True))
    return centred * lax.rsqrt(spread + EPSILON) * gain + shift

def attend(group):
    queries, keys, values = group
    raw = jnp.einsum('qhe,khe->hqk', queries, keys, precision=lax.Precision.HIGHEST)
    scores = low_back(raw) * HEAD ** (-0.5)
    weights = low(jax.nn.softmax(scores, axis=-1))
    return jnp.einsum('hqk,khe->qhe', weights, values, precision=lax.Precision.HIGHEST)

def encoder(state, params):
    qkv_weight, qv_bias, out_weight, out_bias, up_weight, up_bias, down_weight, down_bias, norm_gain, norm_shift = params
    count = state.shape[0]
    shape = (count, SEQ, HEADS, HEAD)
    for layer in range(LAYERS):
        normed = low(normalize(state, norm_gain[layer, 0], norm_shift[layer, 0]))
        queries = low(low_back(project(normed, qkv_weight[layer, 0])) + qv_bias[layer, 0])
        keys = low(low_back(project(normed, qkv_weight[layer, 1])))
        values = low(low_back(project(normed, qkv_weight[layer, 2])) + qv_bias[layer, 1])
        mixed = lax.map(jax.checkpoint(attend), (queries.reshape(shape), keys.reshape(shape), values.reshape(shape)))
        mixed = low_back(low(mixed.reshape(count, SEQ, D)))
        state = state + low_back(project(mixed, out_weight[layer])) + out_bias[layer]
        normed_two = low(normalize(state, norm_gain[layer, 1], norm_shift[layer, 1]))
        hidden = low_back(project(normed_two, up_weight[layer])) + up_bias[layer]
        active = low(jax.nn.gelu(hidden, approximate=True))
        state = state + low_back(project(active, down_weight[layer])) + down_bias[layer]
    return state

def reference(images, qkv_weight, qv_bias, out_weight, out_bias, up_weight, up_bias, down_weight, down_bias, norm_gain, norm_shift, cotangent):
    params = (qkv_weight.astype(jnp.float32), qv_bias.astype(jnp.float32), out_weight.astype(jnp.float32), out_bias.astype(jnp.float32), up_weight.astype(jnp.float32), up_bias.astype(jnp.float32), down_weight.astype(jnp.float32), down_bias.astype(jnp.float32), norm_gain.astype(jnp.float32), norm_shift.astype(jnp.float32))
    start = images.astype(jnp.float32)
    encoded, pullback = jax.vjp(encoder, start, params)
    grad_images, grads = pullback(cotangent.astype(jnp.float32))
    return (encoded.astype(jnp.bfloat16), grad_images.astype(jnp.bfloat16), grads[0], grads[1], grads[2], grads[3], grads[4], grads[5], grads[6], grads[7], grads[8], grads[9])
```

```python
import functools

import jax
import jax.numpy as jnp
from jax import lax
from jax.experimental import pallas as pl
from jax.experimental.pallas import tpu as pltpu
from jax.sharding import PartitionSpec as P

MESH = pl.DeviceIdType.MESH
SLOTS = 16


def grad_sum_kernel(
    unit, steps, grads, totals,
    x_in, inner_in, mid_in, whole_in, half_in, side_in,
    own_a, total_a, own_b, total_b,
    x_sem, inner_sem, mid_sem, out_pair_sem, out_x_sem, whole_sem, half_sem, side_sem,
    back_mid_sem, back_pair_sem, relay_sem, load_a_sem, load_b_sem, store_a_sem, store_b_sem,
):
    dp = lax.axis_index("dp")
    tensor = lax.axis_index("tensor")
    z = dp // 2
    x = dp % 2
    is_mid = (z == 1) | (z == 2)
    is_end = jnp.logical_not(is_mid)
    x_peer = (dp + 1 - 2 * x, tensor)
    pair_peer = (dp + 2 - 4 * (z % 2), tensor)
    mid_z = jnp.where(is_mid, 3 - z, z)
    mid_peer = (mid_z * 2 + x, tensor)
    side = jnp.where(z == 2, 1, 0)
    barrier = pltpu.get_barrier_semaphore()
    pl.semaphore_signal(barrier, inc=1, device_id=x_peer, device_id_type=MESH)
    pl.semaphore_signal(barrier, inc=1, device_id=pair_peer, device_id_type=MESH)

    @pl.when(is_mid)
    def _():
        pl.semaphore_signal(barrier, inc=1, device_id=mid_peer, device_id_type=MESH)
        pl.semaphore_wait(barrier, 3)

    @pl.when(is_end)
    def _():
        pl.semaphore_wait(barrier, 2)

    def row(chunk, part):
        return pl.ds(pl.multiple_of(chunk * (4 * unit) + part * unit, 8), unit)

    def rows_b(chunk):
        return pl.ds(pl.multiple_of(chunk * (4 * unit) + 2 * unit, 8), 2 * unit)

    def remote(src, dst, sem, slot, peer):
        return pltpu.make_async_remote_copy(
            src_ref=src, dst_ref=dst, send_sem=sem.at[0, slot], recv_sem=sem.at[1, slot],
            device_id=peer, device_id_type=MESH,
        )

    def a_x(c, s):
        return remote(grads.at[row(c, 1 - x)], x_in.at[s], x_sem, s, x_peer)

    def a_load(c, s):
        return pltpu.make_async_copy(grads.at[row(c, x)], own_a.at[s], load_a_sem.at[s])

    def a_inner(c, s):
        return remote(own_a.at[s], inner_in.at[s], inner_sem, s, pair_peer)

    def a_mid(c, s):
        return remote(own_a.at[s], mid_in.at[s], mid_sem, s, mid_peer)

    def a_out_pair(c, s):
        return remote(total_a.at[s], totals.at[row(c, x)], out_pair_sem, s, pair_peer)

    def a_out_x(c, s):
        return remote(total_a.at[s], totals.at[row(c, x)], out_x_sem, s, x_peer)

    def a_store(c, s):
        return pltpu.make_async_copy(total_a.at[s], totals.at[row(c, x)], store_a_sem.at[s])

    def a_relay(c, s):
        return remote(totals.at[row(c, x)], totals.at[row(c, x)], out_x_sem, s, x_peer)

    def a_back(c, s):
        return remote(totals.at[row(c, x)], totals.at[row(c, 1 - x)], out_x_sem, s, x_peer)

    def b_whole(c, s):
        return remote(grads.at[rows_b(c)], whole_in.at[s], whole_sem, s, pair_peer)

    def b_load(c, s):
        return pltpu.make_async_copy(grads.at[rows_b(c)], own_b.at[s], load_b_sem.at[s])

    def b_half(c, s):
        return remote(own_b.at[s, pl.ds((1 - side) * unit, unit)], half_in.at[s], half_sem, s, mid_peer)

    def b_side(c, s):
        return remote(own_b.at[s, pl.ds(side * unit, unit)], side_in.at[s], side_sem, s, x_peer)

    def b_store(c, s):
        return pltpu.make_async_copy(total_b.at[s], totals.at[row(c, 2 + side)], store_b_sem.at[s])

    def b_back_mid(c, s):
        return remote(total_b.at[s], totals.at[row(c, 2 + side)], back_mid_sem, s, mid_peer)

    def b_back_pair(c, s):
        return remote(total_b.at[s], totals.at[row(c, 2 + side)], back_pair_sem, s, pair_peer)

    def b_relay(c, s):
        return remote(
            totals.at[row(c, 3 - side)], totals.at[row(c, 3 - side)], relay_sem, s, pair_peer
        )

    def stage(step, offset, guard, body):
        chunk = step - offset
        ok = (chunk >= 0) & (chunk < steps)
        if guard is not None:
            ok = ok & guard

        @pl.when(ok)
        def _():
            body(chunk, lax.rem(chunk, SLOTS))

    def start_all(c, s):
        a_x(c, s).start()
        a_load(c, s).start()

    def start_end(c, s):
        b_whole(c, s).start()

    def start_mid(c, s):
        b_load(c, s).start()

    def a1_end(c, s):
        a_load(c, s).wait()
        a_x(c, s).wait_recv()
        own_a[s] = own_a[s] + x_in[s]
        a_inner(c, s).start()

    def a1_mid(c, s):
        a_load(c, s).wait()
        a_x(c, s).wait_recv()
        own_a[s] = own_a[s] + x_in[s]

    def a2_mid(c, s):
        a_inner(c, s).wait_recv()
        own_a[s] = own_a[s] + inner_in[s]
        a_mid(c, s).start()

    def a3_mid(c, s):
        a_mid(c, s).wait_recv()
        total_a[s] = own_a[s] + mid_in[s]
        a_out_pair(c, s).start()
        a_out_x(c, s).start()
        a_store(c, s).start()

    def a3_end(c, s):
        a_out_pair(c, s).wait_recv()
        a_relay(c, s).start()

    def b1_mid(c, s):
        b_load(c, s).wait()
        b_whole(c, s).wait_recv()
        own_b[s] = own_b[s] + whole_in[s]
        b_half(c, s).start()

    def b2_mid(c, s):
        b_half(c, s).wait_recv()
        mine = pl.ds(pl.multiple_of(side * unit, 8), unit)
        own_b[s, mine] = own_b[s, mine] + half_in[s]
        b_side(c, s).start()

    def b3_mid(c, s):
        b_side(c, s).wait_recv()
        mine = pl.ds(pl.multiple_of(side * unit, 8), unit)
        total_b[s] = own_b[s, mine] + side_in[s]
        b_back_mid(c, s).start()
        b_back_pair(c, s).start()
        b_store(c, s).start()

    def b4_mid(c, s):
        b_back_mid(c, s).wait_recv()
        b_relay(c, s).start()

    def b5_end(c, s):
        b_back_pair(c, s).wait_recv()
        b_relay(c, s).wait_recv()

    def back_all(c, s):
        a_back(c, s).wait_recv()

    def done_end(c, s):
        a_inner(c, s).wait_send()
        b_whole(c, s).wait_send()

    def done_mid(c, s):
        a_mid(c, s).wait_send()
        a_out_pair(c, s).wait_send()
        a_store(c, s).wait()
        b_half(c, s).wait_send()
        b_side(c, s).wait_send()
        b_back_mid(c, s).wait_send()
        b_back_pair(c, s).wait_send()
        b_store(c, s).wait()
        b_relay(c, s).wait_send()

    def done_all(c, s):
        a_x(c, s).wait_send()
        a_out_x(c, s).wait_send()

    def body(step, carry):
        stage(step, 0, None, start_all)
        stage(step, 0, is_end, start_end)
        stage(step, 0, is_mid, start_mid)
        stage(step, 8, is_mid, b4_mid)
        stage(step, 6, is_mid, a3_mid)
        stage(step, 6, is_mid, b3_mid)
        stage(step, 8, is_end, a3_end)
        stage(step, 4, is_mid, a2_mid)
        stage(step, 4, is_mid, b2_mid)
        stage(step, 2, is_mid, a1_mid)
        stage(step, 2, is_end, a1_end)
        stage(step, 2, is_mid, b1_mid)
        stage(step, 10, None, back_all)
        stage(step, 10, is_end, b5_end)
        stage(step, 11, is_end, done_end)
        stage(step, 11, is_mid, done_mid)
        stage(step, 11, None, done_all)
        return carry

    lax.fori_loop(0, steps + 12, body, 0)


def grad_sum(grads, unit, collective_id):
    rows, width = grads.shape
    steps = rows // (4 * unit)
    one = (SLOTS, unit, width)
    two = (SLOTS, 2 * unit, width)
    return pl.pallas_call(
        functools.partial(grad_sum_kernel, unit, steps),
        out_shape=jax.ShapeDtypeStruct(grads.shape, jnp.float32),
        in_specs=[pl.BlockSpec(memory_space=pl.ANY)],
        out_specs=pl.BlockSpec(memory_space=pl.ANY),
        scratch_shapes=[pltpu.VMEM(s, jnp.float32) for s in (one, one, one, two, one, one, one, one, two, one)]
        + [pltpu.SemaphoreType.DMA((2, SLOTS))] * 11
        + [pltpu.SemaphoreType.DMA((SLOTS,))] * 4,
        compiler_params=pltpu.CompilerParams(
            collective_id=collective_id, has_side_effects=True, vmem_limit_bytes=56 << 20
        ),
    )(grads)


CHUNKS = (24, 48, 48, 48, 48, 48, 48, 32, 24)


def tensor_sum_kernel(
    sizes, part, total, core_in, acc, y_in, core_send, core_recv, y_send, y_recv, back_send, back_recv
):
    dp = lax.axis_index("dp")
    tensor = lax.axis_index("tensor")
    core = tensor % 2
    core_peer = (dp, tensor + 1 - 2 * core)
    y_peer = (dp, lax.rem(tensor + 2, 4))
    half = sum(sizes)
    barrier = pltpu.get_barrier_semaphore()
    for peer in (core_peer, y_peer):
        pl.semaphore_signal(barrier, inc=1, device_id=peer, device_id_type=MESH)
    pl.semaphore_wait(barrier, 2)
    starts = [sum(sizes[:i]) for i in range(len(sizes))]

    def mine(i):
        return pl.ds(pl.multiple_of(core * half + starts[i], 8), sizes[i])

    def other(i):
        return pl.ds(pl.multiple_of((1 - core) * half + starts[i], 8), sizes[i])

    def here(i):
        return pl.ds(starts[i], sizes[i])

    def remote(src, dst, send, recv, i, peer):
        return pltpu.make_async_remote_copy(
            src_ref=src, dst_ref=dst, send_sem=send.at[i], recv_sem=recv.at[i],
            device_id=peer, device_id_type=MESH,
        )

    first = [
        remote(part.at[other(i)], core_in.at[here(i)], core_send, core_recv, i, core_peer)
        for i in range(len(sizes))
    ]
    second = [
        remote(acc.at[here(i)], y_in.at[here(i)], y_send, y_recv, i, y_peer) for i in range(len(sizes))
    ]
    third = [
        remote(total.at[mine(i)], total.at[mine(i)], back_send, back_recv, i, core_peer)
        for i in range(len(sizes))
    ]
    for copy in first:
        copy.start()
    for i in range(len(sizes)):
        first[i].wait_recv()
        acc[here(i)] = part[mine(i)] + core_in[here(i)]
        second[i].start()
    for i in range(len(sizes)):
        second[i].wait_recv()
        total[mine(i)] = acc[here(i)] + y_in[here(i)]
        third[i].start()
    for i in range(len(sizes)):
        first[i].wait_send()
        second[i].wait_send()
        third[i].wait_send()
        pltpu.make_async_remote_copy(
            src_ref=total.at[other(i)], dst_ref=total.at[other(i)],
            send_sem=back_send.at[i], recv_sem=back_recv.at[i],
            device_id=core_peer, device_id_type=MESH,
        ).wait_recv()


def tensor_sum(part, collective_id):
    rows, width = part.shape
    sizes = CHUNKS
    half = (rows // 2, width)
    count = len(sizes)
    return pl.pallas_call(
        functools.partial(tensor_sum_kernel, sizes),
        out_shape=jax.ShapeDtypeStruct(part.shape, jnp.float32),
        in_specs=[pl.BlockSpec(memory_space=pltpu.VMEM)],
        out_specs=pl.BlockSpec(memory_space=pltpu.VMEM),
        scratch_shapes=[pltpu.VMEM(half, jnp.float32)] * 3
        + [pltpu.SemaphoreType.DMA((count,))] * 6,
        compiler_params=pltpu.CompilerParams(
            collective_id=collective_id, has_side_effects=True, vmem_limit_bytes=40 << 20
        ),
    )(part)


UNIT = 8
TAIL_ROWS = 16

HEAD = 72


EPSILON = 1e-06


def standardize(state):
    centred = state - jnp.mean(state, axis=-1, keepdims=True)
    inverse = lax.rsqrt(jnp.mean(centred * centred, axis=-1, keepdims=True) + EPSILON)
    return (centred * inverse, inverse)


def norm_backward(grad_normed, unit, inverse, gain):
    grad_unit = grad_normed * gain
    inner = (
        grad_unit
        - jnp.mean(grad_unit, axis=-1, keepdims=True)
        - unit * jnp.mean(grad_unit * unit, axis=-1, keepdims=True)
    )
    return (inverse * inner, jnp.sum(grad_normed * unit, axis=0), jnp.sum(grad_normed, axis=0))


def attend_forward(queries, keys, values, scale):
    scores = jnp.einsum("qhe,khe->hqk", queries, keys, preferred_element_type=jnp.float32) * scale
    peak = jnp.max(scores, axis=-1, keepdims=True)
    expo = jnp.exp(scores - peak)
    total = jnp.sum(expo, axis=-1, keepdims=True)
    weights = (expo / total).astype(jnp.bfloat16)
    mixed = jnp.einsum("hqk,khe->qhe", weights, values, preferred_element_type=jnp.float32)
    return (mixed.astype(jnp.bfloat16), peak + jnp.log(total))


def attend_backward(queries, keys, values, logsum, grad_mixed, scale):
    scores = jnp.einsum("qhe,khe->hqk", queries, keys, preferred_element_type=jnp.float32) * scale
    probs = jnp.exp(scores - logsum)
    weights = probs.astype(jnp.bfloat16)
    grad_weights = jnp.einsum(
        "qhe,khe->hqk", grad_mixed, values, preferred_element_type=jnp.float32
    )
    grad_values = jnp.einsum(
        "hqk,qhe->khe", weights, grad_mixed, preferred_element_type=jnp.float32
    )
    center = jnp.sum(probs * grad_weights, axis=-1, keepdims=True)
    grad_raw = (probs * (grad_weights - center) * scale).astype(jnp.bfloat16)
    grad_queries = jnp.einsum("hqk,khe->qhe", grad_raw, keys, preferred_element_type=jnp.float32)
    grad_keys = jnp.einsum("hqk,qhe->khe", grad_raw, queries, preferred_element_type=jnp.float32)
    return (grad_queries, grad_keys, grad_values)


def gelu_tanh(hidden):
    return jax.nn.gelu(hidden, approximate=True)


def fit(array, width):
    return jnp.pad(array, ((0, 0), (0, width - array.shape[1])))


def pad_rows(array):
    return jnp.pad(array, ((0, -array.shape[0] % 8), (0, 0)))


def local(
    dp_size,
    images,
    qkv_weight,
    qv_bias,
    out_weight,
    out_bias,
    up_weight,
    up_bias,
    down_weight,
    down_bias,
    norm_gain,
    norm_shift,
    cotangent,
):
    count, length, width = images.shape
    depth = qkv_weight.shape[0]
    local_width = qkv_weight.shape[3]
    heads_here = local_width // HEAD
    scale = HEAD ** (-0.5)
    rows = count * length
    padded = -(-rows // 16) * 16
    state = jnp.pad(images.reshape(rows, width), ((0, padded - rows), (0, 0))).astype(jnp.float32)
    stored = []
    for layer in range(depth):
        unit_one, inverse_one = standardize(state)
        normed = (unit_one * norm_gain[layer, 0] + norm_shift[layer, 0]).astype(jnp.bfloat16)
        queries = (
            jnp.dot(normed, qkv_weight[layer, 0], preferred_element_type=jnp.float32)
            + qv_bias[layer, 0]
        ).astype(jnp.bfloat16)
        keys = jnp.dot(normed, qkv_weight[layer, 1], preferred_element_type=jnp.float32).astype(
            jnp.bfloat16
        )
        values = (
            jnp.dot(normed, qkv_weight[layer, 2], preferred_element_type=jnp.float32)
            + qv_bias[layer, 1]
        ).astype(jnp.bfloat16)
        shaped = (
            queries[:rows].reshape(count, length, heads_here, HEAD),
            keys[:rows].reshape(count, length, heads_here, HEAD),
            values[:rows].reshape(count, length, heads_here, HEAD),
        )
        mixed, logsum = lax.map(
            lambda group: attend_forward(group[0], group[1], group[2], scale), shaped
        )
        mixed = jnp.pad(mixed.reshape(rows, local_width), ((0, padded - rows), (0, 0)))
        partial_out = jnp.dot(mixed, out_weight[layer], preferred_element_type=jnp.float32)
        middle = state + tensor_sum(partial_out, 0) + out_bias[layer]
        unit_two, inverse_two = standardize(middle)
        normed_two = (unit_two * norm_gain[layer, 1] + norm_shift[layer, 1]).astype(jnp.bfloat16)
        hidden = (
            jnp.dot(normed_two, up_weight[layer], preferred_element_type=jnp.float32)
            + up_bias[layer]
        )
        active = gelu_tanh(hidden).astype(jnp.bfloat16)
        partial_down = jnp.dot(active, down_weight[layer], preferred_element_type=jnp.float32)
        stored.append(
            (
                unit_one,
                inverse_one,
                normed,
                shaped,
                logsum,
                mixed,
                unit_two,
                inverse_two,
                normed_two,
                hidden,
                active,
            )
        )
        state = middle + tensor_sum(partial_down, 0) + down_bias[layer]
    encoded = state[:rows].astype(jnp.bfloat16).reshape(count, length, width)
    grad_state = jnp.pad(cotangent.reshape(rows, width), ((0, padded - rows), (0, 0))).astype(jnp.float32)
    layer_grads = []
    for layer in reversed(range(depth)):
        (
            unit_one,
            inverse_one,
            normed,
            shaped,
            logsum,
            mixed,
            unit_two,
            inverse_two,
            normed_two,
            hidden,
            active,
        ) = stored[layer]
        down_bias_grad = jnp.sum(grad_state, axis=0)
        grad_down = grad_state.astype(jnp.bfloat16)
        down_weight_grad = jnp.einsum(
            "rf,rd->fd", active, grad_down, preferred_element_type=jnp.float32
        )
        grad_active = jnp.einsum(
            "rd,fd->rf", grad_down, down_weight[layer], preferred_element_type=jnp.float32
        )
        slope_pullback = jax.vjp(gelu_tanh, hidden)[1]
        grad_hidden = slope_pullback(grad_active)[0]
        up_bias_grad = jnp.sum(grad_hidden, axis=0)
        hidden_low = grad_hidden.astype(jnp.bfloat16)
        up_weight_grad = jnp.einsum(
            "rd,rf->fd", normed_two, hidden_low, preferred_element_type=jnp.float32
        )
        partial_two = jnp.einsum(
            "rf,df->rd", hidden_low, up_weight[layer], preferred_element_type=jnp.float32
        )
        grad_normed_two = tensor_sum(partial_two, 0)
        grad_norm_two, gain_two_grad, shift_two_grad = norm_backward(
            grad_normed_two, unit_two, inverse_two, norm_gain[layer, 1]
        )
        grad_middle = grad_state + grad_norm_two
        out_bias_grad = jnp.sum(grad_middle, axis=0)
        grad_proj = grad_middle.astype(jnp.bfloat16)
        out_weight_grad = jnp.einsum(
            "rh,rd->hd", mixed, grad_proj, preferred_element_type=jnp.float32
        )
        grad_mixed = jnp.einsum(
            "rd,hd->rh", grad_proj, out_weight[layer], preferred_element_type=jnp.float32
        ).astype(jnp.bfloat16)
        grad_mixed = grad_mixed[:rows].reshape(count, length, heads_here, HEAD)
        grad_parts = lax.map(
            lambda group: attend_backward(group[0], group[1], group[2], group[3], group[4], scale),
            (shaped[0], shaped[1], shaped[2], logsum, grad_mixed),
        )
        grad_queries = jnp.pad(grad_parts[0].reshape(rows, local_width), ((0, padded - rows), (0, 0)))
        grad_keys = jnp.pad(grad_parts[1].reshape(rows, local_width), ((0, padded - rows), (0, 0)))
        grad_values = jnp.pad(grad_parts[2].reshape(rows, local_width), ((0, padded - rows), (0, 0)))
        qv_bias_grad = jnp.stack([jnp.sum(grad_queries, axis=0), jnp.sum(grad_values, axis=0)])
        lowered = (
            grad_queries.astype(jnp.bfloat16),
            grad_keys.astype(jnp.bfloat16),
            grad_values.astype(jnp.bfloat16),
        )
        qkv_weight_grad = [
            jnp.einsum("rd,rh->hd", normed, member, preferred_element_type=jnp.float32)
            for member in lowered
        ]
        partial_one = jnp.einsum(
            "rh,dh->rd", lowered[0], qkv_weight[layer, 0], preferred_element_type=jnp.float32
        )
        partial_one = partial_one + jnp.einsum(
            "rh,dh->rd", lowered[1], qkv_weight[layer, 1], preferred_element_type=jnp.float32
        )
        partial_one = partial_one + jnp.einsum(
            "rh,dh->rd", lowered[2], qkv_weight[layer, 2], preferred_element_type=jnp.float32
        )
        grad_normed = tensor_sum(partial_one, 0)
        grad_norm_one, gain_one_grad, shift_one_grad = norm_backward(
            grad_normed, unit_one, inverse_one, norm_gain[layer, 0]
        )
        grad_state = grad_middle + grad_norm_one
        gain_grad = jnp.stack([gain_one_grad, gain_two_grad])
        shift_grad = jnp.stack([shift_one_grad, shift_two_grad])
        pieces = [up_weight_grad, down_weight_grad] + qkv_weight_grad + [out_weight_grad]
        small = jnp.concatenate(
            [
                fit(qv_bias_grad, width),
                fit(out_bias_grad[None], width),
                fit(up_bias_grad[None], width),
                down_bias_grad[None],
                gain_grad,
                shift_grad,
            ]
        )
        layer_grads.insert(0, [pad_rows(piece) for piece in pieces] + [jnp.pad(small, ((0, TAIL_ROWS - 9), (0, 0)))])
    image_grad = grad_state[:rows].astype(jnp.bfloat16).reshape(count, length, width)
    flat = jnp.concatenate([piece for entry in layer_grads for piece in entry])
    if dp_size == 8:
        flat = grad_sum(flat, UNIT, 1)
    else:
        flat = lax.psum(flat, "dp")
    hidden_units = up_weight.shape[2]
    per_layer = flat.reshape(depth, flat.shape[0] // depth, width)
    stop = -(-hidden_units // 8) * 8
    up_grad = jnp.swapaxes(per_layer[:, :hidden_units], 1, 2)
    down_grad = per_layer[:, stop : stop + hidden_units]
    qkv_grad = per_layer[:, 2 * stop : 2 * stop + 3 * local_width]
    qkv_grad = jnp.swapaxes(qkv_grad.reshape(depth, 3, local_width, width), 2, 3)
    out_grad = per_layer[:, 2 * stop + 3 * local_width : 2 * stop + 4 * local_width]
    small = per_layer[:, 2 * stop + 4 * local_width :]
    return (
        encoded,
        image_grad,
        qkv_grad,
        small[:, 0:2, :local_width],
        out_grad,
        small[:, 2],
        up_grad,
        small[:, 3, :hidden_units],
        down_grad,
        small[:, 4],
        small[:, 5:7],
        small[:, 7:9],
    )


def solution(mesh):
    in_specs = (
        P("dp", None, None),
        P(None, None, None, "tensor"),
        P(None, None, "tensor"),
        P(None, "tensor", None),
        P(),
        P(None, None, "tensor"),
        P(None, "tensor"),
        P(None, "tensor", None),
        P(),
        P(),
        P(),
        P("dp", None, None),
    )
    out_specs = (
        P("dp", None, None),
        P("dp", None, None),
        P(None, None, None, "tensor"),
        P(None, None, "tensor"),
        P(None, "tensor", None),
        P(),
        P(None, None, "tensor"),
        P(None, "tensor"),
        P(None, "tensor", None),
        P(),
        P(),
        P(),
    )
    return jax.shard_map(
        functools.partial(local, mesh.shape["dp"]), mesh=mesh, in_specs=in_specs, out_specs=out_specs, check_vma=False)
```

```python
import functools

import jax
import jax.numpy as jnp
from jax import lax
from jax.experimental import pallas as pl
from jax.experimental.pallas import tpu as pltpu
from jax.sharding import PartitionSpec as P

MESH = pl.DeviceIdType.MESH
SLOTS = 16


def grad_sum_ticks(dp_sum, unit, steps, grads, totals, buffers, sems):
    (x_in, inner_in, mid_in, whole_in, half_in, side_in, own_a, total_a, own_b, total_b) = buffers
    (
        x_sem, inner_sem, mid_sem, out_pair_sem, out_x_sem, whole_sem, half_sem, side_sem,
        back_mid_sem, back_pair_sem, relay_sem, load_a_sem, load_b_sem, store_a_sem, store_b_sem,
    ) = sems
    dp = lax.axis_index("dp")
    tensor = lax.axis_index("tensor")
    z = dp // 2
    x = dp % 2
    is_mid = (z == 1) | (z == 2)
    is_end = jnp.logical_not(is_mid)
    x_peer = (dp + 1 - 2 * x, tensor)
    pair_peer = (dp + 2 - 4 * (z % 2), tensor)
    mid_z = jnp.where(is_mid, 3 - z, z)
    mid_peer = (mid_z * 2 + x, tensor)
    side = jnp.where(z == 2, 1, 0)

    def greet(others):
        barrier = pltpu.get_barrier_semaphore()
        for peer in others:
            pl.semaphore_signal(barrier, inc=1, device_id=peer, device_id_type=MESH)
        if not dp_sum:
            pl.semaphore_wait(barrier, len(others))
            return
        for peer in (x_peer, pair_peer):
            pl.semaphore_signal(barrier, inc=1, device_id=peer, device_id_type=MESH)

        @pl.when(is_mid)
        def _():
            pl.semaphore_signal(barrier, inc=1, device_id=mid_peer, device_id_type=MESH)
            pl.semaphore_wait(barrier, 3 + len(others))

        @pl.when(is_end)
        def _():
            pl.semaphore_wait(barrier, 2 + len(others))

    def row(chunk, part):
        return pl.ds(pl.multiple_of(chunk * (4 * unit) + part * unit, 8), unit)

    def rows_b(chunk):
        return pl.ds(pl.multiple_of(chunk * (4 * unit) + 2 * unit, 8), 2 * unit)

    def remote(src, dst, sem, slot, peer):
        return pltpu.make_async_remote_copy(
            src_ref=src, dst_ref=dst, send_sem=sem.at[0, slot], recv_sem=sem.at[1, slot],
            device_id=peer, device_id_type=MESH,
        )

    def a_x(c, s):
        return remote(grads.at[row(c, 1 - x)], x_in.at[s], x_sem, s, x_peer)

    def a_load(c, s):
        return pltpu.make_async_copy(grads.at[row(c, x)], own_a.at[s], load_a_sem.at[s])

    def a_inner(c, s):
        return remote(own_a.at[s], inner_in.at[s], inner_sem, s, pair_peer)

    def a_mid(c, s):
        return remote(own_a.at[s], mid_in.at[s], mid_sem, s, mid_peer)

    def a_out_pair(c, s):
        return remote(total_a.at[s], totals.at[row(c, x)], out_pair_sem, s, pair_peer)

    def a_out_x(c, s):
        return remote(total_a.at[s], totals.at[row(c, x)], out_x_sem, s, x_peer)

    def a_store(c, s):
        return pltpu.make_async_copy(total_a.at[s], totals.at[row(c, x)], store_a_sem.at[s])

    def a_relay(c, s):
        return remote(totals.at[row(c, x)], totals.at[row(c, x)], out_x_sem, s, x_peer)

    def a_back(c, s):
        return remote(totals.at[row(c, x)], totals.at[row(c, 1 - x)], out_x_sem, s, x_peer)

    def b_whole(c, s):
        return remote(grads.at[rows_b(c)], whole_in.at[s], whole_sem, s, pair_peer)

    def b_load(c, s):
        return pltpu.make_async_copy(grads.at[rows_b(c)], own_b.at[s], load_b_sem.at[s])

    def b_half(c, s):
        return remote(own_b.at[s, pl.ds((1 - side) * unit, unit)], half_in.at[s], half_sem, s, mid_peer)

    def b_side(c, s):
        return remote(own_b.at[s, pl.ds(side * unit, unit)], side_in.at[s], side_sem, s, x_peer)

    def b_store(c, s):
        return pltpu.make_async_copy(total_b.at[s], totals.at[row(c, 2 + side)], store_b_sem.at[s])

    def b_back_mid(c, s):
        return remote(total_b.at[s], totals.at[row(c, 2 + side)], back_mid_sem, s, mid_peer)

    def b_back_pair(c, s):
        return remote(total_b.at[s], totals.at[row(c, 2 + side)], back_pair_sem, s, pair_peer)

    def b_relay(c, s):
        return remote(
            totals.at[row(c, 3 - side)], totals.at[row(c, 3 - side)], relay_sem, s, pair_peer
        )

    def stage(step, offset, guard, body):
        chunk = step - offset
        ok = (chunk >= 0) & (chunk < steps)
        if guard is not None:
            ok = ok & guard

        @pl.when(ok)
        def _():
            body(chunk, lax.rem(chunk, SLOTS))

    def start_all(c, s):
        a_x(c, s).start()
        a_load(c, s).start()

    def start_end(c, s):
        b_whole(c, s).start()

    def start_mid(c, s):
        b_load(c, s).start()

    def a1_end(c, s):
        a_load(c, s).wait()
        a_x(c, s).wait_recv()
        own_a[s] = own_a[s] + x_in[s]
        a_inner(c, s).start()

    def a1_mid(c, s):
        a_load(c, s).wait()
        a_x(c, s).wait_recv()
        own_a[s] = own_a[s] + x_in[s]

    def a2_mid(c, s):
        a_inner(c, s).wait_recv()
        own_a[s] = own_a[s] + inner_in[s]
        a_mid(c, s).start()

    def a3_mid(c, s):
        a_mid(c, s).wait_recv()
        total_a[s] = own_a[s] + mid_in[s]
        a_out_pair(c, s).start()
        a_out_x(c, s).start()
        a_store(c, s).start()

    def a3_end(c, s):
        a_out_pair(c, s).wait_recv()
        a_relay(c, s).start()

    def b1_mid(c, s):
        b_load(c, s).wait()
        b_whole(c, s).wait_recv()
        own_b[s] = own_b[s] + whole_in[s]
        b_half(c, s).start()

    def b2_mid(c, s):
        b_half(c, s).wait_recv()
        mine = pl.ds(pl.multiple_of(side * unit, 8), unit)
        own_b[s, mine] = own_b[s, mine] + half_in[s]
        b_side(c, s).start()

    def b3_mid(c, s):
        b_side(c, s).wait_recv()
        mine = pl.ds(pl.multiple_of(side * unit, 8), unit)
        total_b[s] = own_b[s, mine] + side_in[s]
        b_back_mid(c, s).start()
        b_back_pair(c, s).start()
        b_store(c, s).start()

    def b4_mid(c, s):
        b_back_mid(c, s).wait_recv()
        b_relay(c, s).start()

    def b5_end(c, s):
        b_back_pair(c, s).wait_recv()
        b_relay(c, s).wait_recv()

    def back_all(c, s):
        a_back(c, s).wait_recv()

    def done_end(c, s):
        a_inner(c, s).wait_send()
        b_whole(c, s).wait_send()

    def done_mid(c, s):
        a_mid(c, s).wait_send()
        a_out_pair(c, s).wait_send()
        a_store(c, s).wait()
        b_half(c, s).wait_send()
        b_side(c, s).wait_send()
        b_back_mid(c, s).wait_send()
        b_back_pair(c, s).wait_send()
        b_store(c, s).wait()
        b_relay(c, s).wait_send()

    def done_all(c, s):
        a_x(c, s).wait_send()
        a_out_x(c, s).wait_send()

    def tick(step):
        if not dp_sum:
            return
        stage(step, 0, None, start_all)
        stage(step, 0, is_end, start_end)
        stage(step, 0, is_mid, start_mid)
        stage(step, 8, is_mid, b4_mid)
        stage(step, 6, is_mid, a3_mid)
        stage(step, 6, is_mid, b3_mid)
        stage(step, 8, is_end, a3_end)
        stage(step, 4, is_mid, a2_mid)
        stage(step, 4, is_mid, b2_mid)
        stage(step, 2, is_mid, a1_mid)
        stage(step, 2, is_end, a1_end)
        stage(step, 2, is_mid, b1_mid)
        stage(step, 10, None, back_all)
        stage(step, 10, is_end, b5_end)
        stage(step, 11, is_end, done_end)
        stage(step, 11, is_mid, done_mid)
        stage(step, 11, None, done_all)

    return tick, greet


def tick_scratch(unit, width):
    one = (SLOTS, unit, width)
    two = (SLOTS, 2 * unit, width)
    buffers = [pltpu.VMEM(s, jnp.float32) for s in (one, one, one, two, one, one, one, one, two, one)]
    sems = [pltpu.SemaphoreType.DMA((2, SLOTS))] * 11 + [pltpu.SemaphoreType.DMA((SLOTS,))] * 4
    return buffers, sems


HEAD = 72
EPSILON = 1e-06
UNIT = 8
TAIL_ROWS = 16


CHUNKS = (32, 48, 48, 48, 48, 48, 48, 40, 24)


def tensor_sum_kernel(
    sizes, part, total, core_in, acc, y_in, core_send, core_recv, y_send, y_recv, back_send, back_recv
):
    dp = lax.axis_index("dp")
    tensor = lax.axis_index("tensor")
    core = tensor % 2
    core_peer = (dp, tensor + 1 - 2 * core)
    y_peer = (dp, lax.rem(tensor + 2, 4))
    half = sum(sizes)
    barrier = pltpu.get_barrier_semaphore()
    for peer in (core_peer, y_peer):
        pl.semaphore_signal(barrier, inc=1, device_id=peer, device_id_type=MESH)
    pl.semaphore_wait(barrier, 2)
    starts = [sum(sizes[:i]) for i in range(len(sizes))]

    def mine(i):
        return pl.ds(pl.multiple_of(core * half + starts[i], 8), sizes[i])

    def other(i):
        return pl.ds(pl.multiple_of((1 - core) * half + starts[i], 8), sizes[i])

    def here(i):
        return pl.ds(starts[i], sizes[i])

    def remote(src, dst, send, recv, i, peer):
        return pltpu.make_async_remote_copy(
            src_ref=src, dst_ref=dst, send_sem=send.at[i], recv_sem=recv.at[i],
            device_id=peer, device_id_type=MESH,
        )

    first = [
        remote(part.at[other(i)], core_in.at[here(i)], core_send, core_recv, i, core_peer)
        for i in range(len(sizes))
    ]
    second = [
        remote(acc.at[here(i)], y_in.at[here(i)], y_send, y_recv, i, y_peer) for i in range(len(sizes))
    ]
    third = [
        remote(total.at[mine(i)], total.at[mine(i)], back_send, back_recv, i, core_peer)
        for i in range(len(sizes))
    ]
    for copy in first:
        copy.start()
    for i in range(len(sizes)):
        first[i].wait_recv()
        acc[here(i)] = part[mine(i)] + core_in[here(i)]
        second[i].start()
    for i in range(len(sizes)):
        second[i].wait_recv()
        total[mine(i)] = acc[here(i)] + y_in[here(i)]
        third[i].start()
    for i in range(len(sizes)):
        first[i].wait_send()
        second[i].wait_send()
        third[i].wait_send()
        pltpu.make_async_remote_copy(
            src_ref=total.at[other(i)], dst_ref=total.at[other(i)],
            send_sem=back_send.at[i], recv_sem=back_recv.at[i],
            device_id=core_peer, device_id_type=MESH,
        ).wait_recv()


def tensor_sum(part, collective_id):
    rows, width = part.shape
    sizes = CHUNKS
    half = (rows // 2, width)
    count = len(sizes)
    return pl.pallas_call(
        functools.partial(tensor_sum_kernel, sizes),
        out_shape=jax.ShapeDtypeStruct(part.shape, jnp.float32),
        in_specs=[pl.BlockSpec(memory_space=pltpu.VMEM)],
        out_specs=pl.BlockSpec(memory_space=pltpu.VMEM),
        scratch_shapes=[pltpu.VMEM(half, jnp.float32)] * 3
        + [pltpu.SemaphoreType.DMA((count,))] * 6,
        compiler_params=pltpu.CompilerParams(
            collective_id=collective_id, has_side_effects=True, vmem_limit_bytes=40 << 20
        ),
    )(part)


FIRST = 6
PIECE = 16
LAG = 4
TICK_SPAN = 12
BLOCK = 192


def dot_nn(left, right):
    return lax.dot_general(left, right, (((1,), (0,)), ((), ())), preferred_element_type=jnp.float32)


def dot_nt(left, right):
    return lax.dot_general(left, right, (((1,), (1,)), ((), ())), preferred_element_type=jnp.float32)


def dot_tn(left, right):
    return lax.dot_general(left, right, (((0,), (0,)), ((), ())), preferred_element_type=jnp.float32)


def fold(array):
    return jnp.sum(array, axis=0, keepdims=True)


def gelu_slope(v):
    root = 0.7978845608028654
    inner = jnp.tanh(root * (v + 0.044715 * (v * v * v)))
    return 0.5 * (1.0 + inner) + 0.5 * v * (1.0 - inner * inner) * (root * (1.0 + 0.134145 * (v * v)))


def norm_back(grad_normed, state, gain):
    centred = state - jnp.mean(state, axis=-1, keepdims=True)
    inverse = lax.rsqrt(jnp.mean(centred * centred, axis=-1, keepdims=True) + EPSILON)
    unit = centred * inverse
    grad_unit = grad_normed * gain
    inner = (
        grad_unit
        - jnp.mean(grad_unit, axis=-1, keepdims=True)
        - unit * jnp.mean(grad_unit * unit, axis=-1, keepdims=True)
    )
    return inverse * inner, fold(grad_normed * unit), fold(grad_normed)


def backward_kernel(
    dp_sum, tokens, layers, heads, units_rows, head_dim, send_rows, unit, steps,
    cotangent, hidden, active, normed_two, normed, middle, state, qkv, logsum, mixed,
    down, up, qkv_w, out_w, gain,
    grads, totals, image_grad,
    wide, act_buf, two_buf, qkv_buf, lse_buf, mix_buf, down_buf, up_buf, qkvw_buf, outw_buf, gain_buf,
    flow, flow_low, hid_low, part, total, core_in, acc, y_in, grad_mix, cat, acc_k, acc_v, stage_buf, small,
    x_in, inner_in, mid_in, whole_in, half_in, side_in, own_a, total_a, own_b, total_b,
    load_sem, stage_sem, core_send, core_recv, y_send, y_recv, back_send, back_recv, *tick_sems
):
    width = grads.shape[1]
    rows = part.shape[0]
    blocks = rows // BLOCK
    half = send_rows // 2
    pieces = half // PIECE
    tick, greet = grad_sum_ticks(
        dp_sum, unit, steps, grads, totals,
        (x_in, inner_in, mid_in, whole_in, half_in, side_in, own_a, total_a, own_b, total_b), tick_sems,
    )
    dp = lax.axis_index("dp")
    tensor = lax.axis_index("tensor")
    core = tensor % 2
    core_peer = (dp, tensor + 1 - 2 * core)
    y_peer = (dp, lax.rem(tensor + 2, 4))
    greet((core_peer, y_peer))
    layer_rows = steps * 4 * unit // layers
    off_up = units_rows
    off_out = 2 * units_rows
    off_qkv = off_out + heads * head_dim
    off_small = off_qkv + 3 * heads * head_dim

    def mine(i):
        return pl.ds(pl.multiple_of(core * half + i * PIECE, 8), PIECE)

    def other(i):
        return pl.ds(pl.multiple_of((1 - core) * half + i * PIECE, 8), PIECE)

    def here(i):
        return pl.ds(pl.multiple_of(i * PIECE, 8), PIECE)

    def remote(src, dst, send, recv, peer):
        return pltpu.make_async_remote_copy(
            src_ref=src, dst_ref=dst, send_sem=send, recv_sem=recv, device_id=peer, device_id_type=MESH
        )

    def to_core(p, i):
        return remote(
            part.at[other(i)], core_in.at[here(i)], core_send.at[p, i], core_recv.at[p, i], core_peer
        )

    def to_y(p, i):
        return remote(acc.at[here(i)], y_in.at[p, here(i)], y_send.at[p, i], y_recv.at[p, i], y_peer)

    def to_back(p, i):
        return remote(total.at[mine(i)], total.at[mine(i)], back_send.at[p, i], back_recv.at[p, i], core_peer)

    def from_back(p, i):
        return remote(
            total.at[other(i)], total.at[other(i)], back_send.at[p, i], back_recv.at[p, i], core_peer
        )

    def sum_begin(p):
        def go(i, c):
            to_core(p, i).start()
            return c

        lax.fori_loop(0, pieces, go, 0)

    def sum_step(p, j):
        @pl.when(j < pieces)
        def _():
            to_core(p, j).wait_recv()
            acc[here(j)] = part[mine(j)] + core_in[here(j)]
            to_y(p, j).start()

        late = j - LAG

        @pl.when((late >= 0) & (late < pieces))
        def _():
            to_y(p, late).wait_recv()
            total[mine(late)] = acc[here(late)] + y_in[p, here(late)]
            to_back(p, late).start()

        last = j - LAG - 2

        @pl.when((last >= 0) & (last < pieces))
        def _():
            to_core(p, last).wait_send()
            to_y(p, last).wait_send()
            to_back(p, last).wait_send()
            from_back(p, last).wait_recv()

    sum_steps = pieces + LAG + 2

    def load(source, target, sem):
        return pltpu.make_async_copy(source, target, load_sem.at[sem])

    def stage_copy(slot, row, size):
        return pltpu.make_async_copy(
            stage_buf.at[slot, pl.ds(0, size)], grads.at[pl.ds(pl.multiple_of(row, 8), size)], stage_sem.at[slot]
        )

    layer_ticks = 4 * blocks + 2 * sum_steps + heads * blocks

    def row_block(b):
        return pl.ds(pl.multiple_of(b * BLOCK, 16), BLOCK)

    total[pl.ds(send_rows, rows - send_rows)] = jnp.zeros((rows - send_rows, width), jnp.float32)
    start = load(cotangent, flow_low, 0)
    start.start()
    load(gain, gain_buf, 11).start()
    start.wait()
    load(gain, gain_buf, 11).wait()

    def lift(b, c):
        flow[row_block(b)] = flow_low[row_block(b)].astype(jnp.float32)
        return c

    lax.fori_loop(0, blocks, lift, 0)

    def layer_body(it, carry):
        layer = layers - 1 - it
        base_tick = it * layer_ticks - FIRST
        base_row = it * layer_rows
        hidden_load = load(hidden.at[layer], wide, 0)
        down_load = load(down.at[layer], down_buf, 1)
        up_load = load(up.at[layer], up_buf, 2)
        active_load = load(active.at[layer], act_buf, 3)
        two_load = load(normed_two.at[layer], two_buf, 4)
        outw_load = load(out_w.at[layer], outw_buf, 5)
        qkv_load = load(qkv.at[layer], qkv_buf, 6)
        lse_load = load(logsum.at[layer], lse_buf, 7)
        mix_load = load(mixed.at[layer], mix_buf, 8)
        qkvw_load = load(qkv_w.at[layer], qkvw_buf, 9)
        for copy in (hidden_load, down_load, up_load, active_load, two_load, outw_load, qkv_load, lse_load, mix_load, qkvw_load):
            copy.start()
        small[...] = jnp.zeros_like(small)
        hidden_load.wait()
        down_load.wait()
        up_load.wait()

        def mlp(b, c):
            at = row_block(b)
            grad = flow[at]
            small[4:5] += fold(grad)
            low = grad.astype(jnp.bfloat16)
            flow_low[at] = low
            grad_hidden = dot_nt(low, down_buf[...]) * gelu_slope(wide[at])
            small[3:4] += fold(grad_hidden)
            hid = grad_hidden.astype(jnp.bfloat16)
            hid_low[at] = hid
            part[at] = dot_nt(hid, up_buf[...])
            tick(base_tick + b)
            return c

        lax.fori_loop(0, blocks, mlp, 0)
        sum_begin(0)
        middle_load = load(middle.at[layer], wide, 0)
        middle_load.start()
        active_load.wait()
        two_load.wait()
        tiles = width // 128
        last_rows = units_rows - (tiles - 1) * 128

        def stage_finish(j, count):
            done = j - 1
            whole = (done != tiles - 1) & (done != 2 * tiles - 1)
            slot = lax.rem(done, 2)

            @pl.when((done >= 0) & (done < count) & whole)
            def _():
                stage_copy(slot, base_row, 128).wait()

            @pl.when((done >= 0) & (done < count) & jnp.logical_not(whole))
            def _():
                stage_copy(slot, base_row, last_rows).wait()

        def mlp_weights(j, c):
            sum_step(0, j)
            stage_finish(j, 2 * tiles)
            slot = lax.rem(j, 2)

            @pl.when(j < tiles)
            def _():
                lanes = pl.ds(pl.multiple_of(j * 128, 128), 128)
                stage_buf[slot] = dot_tn(act_buf[:, lanes], flow_low[...])

            @pl.when((j >= tiles) & (j < 2 * tiles))
            def _():
                lanes = pl.ds(pl.multiple_of((j - tiles) * 128, 128), 128)
                stage_buf[slot] = dot_tn(hid_low[:, lanes], two_buf[...])

            second = j >= tiles
            tile = jnp.where(second, j - tiles, j)
            row = base_row + jnp.where(second, off_up, 0) + tile * 128

            @pl.when((j < 2 * tiles) & (tile < tiles - 1))
            def _():
                stage_copy(slot, row, 128).start()

            @pl.when((j < 2 * tiles) & (tile == tiles - 1))
            def _():
                stage_copy(slot, row, last_rows).start()

            tick(base_tick + blocks + j)
            return c

        lax.fori_loop(0, sum_steps, mlp_weights, 0)
        tick_at = base_tick + blocks + sum_steps
        middle_load.wait()
        outw_load.wait()

        def norm_two(b, c):
            at = row_block(b)
            step_grad, gain_grad, shift_grad = norm_back(total[at], wide[at], gain_buf[layer, 1:2])
            small[6:7] += gain_grad
            small[8:9] += shift_grad
            grad = flow[at] + step_grad
            flow[at] = grad
            small[2:3] += fold(grad)
            low = grad.astype(jnp.bfloat16)
            flow_low[at] = low
            grad_mix[at] = dot_nt(low, outw_buf[...]).astype(jnp.bfloat16)
            tick(tick_at + b)
            return c

        lax.fori_loop(0, blocks, norm_two, 0)
        tick_at = tick_at + blocks
        state_load = load(state.at[layer], wide, 0)
        normed_load = load(normed.at[layer], act_buf, 3)
        state_load.start()
        normed_load.start()
        qkv_load.wait()
        lse_load.wait()
        scale = head_dim ** (-0.5)

        def attend(m, c):
            head = m // blocks
            b = lax.rem(m, blocks)
            at = row_block(b)
            lanes = pl.ds(pl.multiple_of(head * 128, 128), 128)
            query = qkv_buf[0, head, at]
            key = qkv_buf[1, head]
            value = qkv_buf[2, head]
            grad = grad_mix[at, lanes]
            scores = dot_nt(query, key) * scale
            probs = jnp.exp(scores - lse_buf[head, at, 0:1])
            column = lax.broadcasted_iota(jnp.int32, probs.shape, 1)
            probs = jnp.where(column < tokens, probs, 0.0)
            grad_weights = dot_nt(grad, value)
            center = jnp.sum(probs * grad_weights, axis=-1, keepdims=True)
            raw = (probs * (grad_weights - center) * scale).astype(jnp.bfloat16)
            grad_query = dot_nn(raw, key)
            small[0:1, lanes] += fold(grad_query)
            cat[at, lanes] = grad_query.astype(jnp.bfloat16)
            add_k = dot_tn(raw, query)
            add_v = dot_tn(probs.astype(jnp.bfloat16), grad)

            @pl.when(b == 0)
            def _():
                acc_k[...] = add_k
                acc_v[...] = add_v

            @pl.when(b > 0)
            def _():
                acc_k[...] += add_k
                acc_v[...] += add_v

            @pl.when(b == blocks - 1)
            def _():
                at_k = pl.ds(pl.multiple_of((heads + head) * 128, 128), 128)
                at_v = pl.ds(pl.multiple_of((2 * heads + head) * 128, 128), 128)
                cat[:, at_k] = acc_k[...].astype(jnp.bfloat16)
                cat[:, at_v] = acc_v[...].astype(jnp.bfloat16)
                small[1:2, lanes] += fold(acc_v[...])

            tick(tick_at + m)
            return c

        lax.fori_loop(0, heads * blocks, attend, 0)
        tick_at = tick_at + heads * blocks
        qkvw_load.wait()

        def project(b, c):
            at = row_block(b)
            part[at] = dot_nt(cat[at], qkvw_buf[...])
            tick(tick_at + b)
            return c

        lax.fori_loop(0, blocks, project, 0)
        tick_at = tick_at + blocks
        sum_begin(1)
        normed_load.wait()
        mix_load.wait()

        def attention_weights(j, c):
            sum_step(1, j)

            @pl.when((j >= 1) & (j < 4 * heads + 1))
            def _():
                stage_copy(lax.rem(j - 1, 2), base_row, head_dim).wait()

            slot = lax.rem(j, 2)

            @pl.when(j < heads)
            def _():
                stage_buf[slot] = dot_tn(mix_buf[j], flow_low[...])

            @pl.when((j >= heads) & (j < 4 * heads))
            def _():
                lanes = pl.ds(pl.multiple_of((j - heads) * 128, 128), 128)
                stage_buf[slot] = dot_tn(cat[:, lanes], act_buf[...])

            @pl.when(j < 4 * heads)
            def _():
                stage_copy(slot, base_row + off_out + j * head_dim, head_dim).start()

            tick(tick_at + j)
            return c

        lax.fori_loop(0, sum_steps, attention_weights, 0)
        tick_at = tick_at + sum_steps
        state_load.wait()

        def norm_one(b, c):
            at = row_block(b)
            step_grad, gain_grad, shift_grad = norm_back(total[at], wide[at], gain_buf[layer, 0:1])
            small[5:6] += gain_grad
            small[7:8] += shift_grad
            flow[at] = flow[at] + step_grad
            tick(tick_at + b)
            return c

        lax.fori_loop(0, blocks, norm_one, 0)
        tail = pltpu.make_async_copy(
            small, grads.at[pl.ds(pl.multiple_of(base_row + off_small, 8), small.shape[0])], load_sem.at[10]
        )
        tail.start()
        tail.wait()
        return carry

    lax.fori_loop(0, layers, layer_body, 0)

    def lower(b, c):
        flow_low[row_block(b)] = flow[row_block(b)].astype(jnp.bfloat16)
        return c

    lax.fori_loop(0, blocks, lower, 0)
    finish = load(flow_low, image_grad, 0)
    finish.start()

    def rest(step, c):
        tick(step)
        return c

    lax.fori_loop(layers * layer_ticks - FIRST, steps + TICK_SPAN, rest, 0)
    finish.wait()


def backward(
    tokens, head_dim, hidden_units, unit, collective_id, dp_sum,
    cotangent, hidden, active, normed_two, normed, middle, state, qkv, logsum, mixed,
    down, up, qkv_w, out_w, gain,
):
    layers, rows, width = hidden.shape
    heads = qkv.shape[2]
    units_rows = -(-hidden_units // 8) * 8
    send_rows = -(-tokens // (2 * PIECE)) * 2 * PIECE
    pieces = send_rows // (2 * PIECE)
    layer_rows = 2 * units_rows + 4 * heads * head_dim + TAIL_ROWS
    steps = layers * layer_rows // (4 * unit)
    buffers, sems = tick_scratch(unit, width)
    f32, low = jnp.float32, jnp.bfloat16
    half = (send_rows // 2, width)
    full = (rows, width)
    any_spec = pl.BlockSpec(memory_space=pl.ANY)
    grads = jax.ShapeDtypeStruct((layers * layer_rows, width), f32)
    return pl.pallas_call(
        functools.partial(
            backward_kernel, dp_sum, tokens, layers, heads, units_rows, head_dim, send_rows, unit, steps
        ),
        out_shape=(grads, grads, jax.ShapeDtypeStruct(full, low)),
        in_specs=[any_spec] * 15,
        out_specs=(any_spec, any_spec, any_spec),
        scratch_shapes=[
            pltpu.VMEM(full, f32),
            pltpu.VMEM(full, low),
            pltpu.VMEM(full, low),
            pltpu.VMEM(qkv.shape[1:], low),
            pltpu.VMEM(logsum.shape[1:], f32),
            pltpu.VMEM(mixed.shape[1:], low),
            pltpu.VMEM(down.shape[1:], low),
            pltpu.VMEM(up.shape[1:], low),
            pltpu.VMEM(qkv_w.shape[1:], low),
            pltpu.VMEM(out_w.shape[1:], low),
            pltpu.VMEM(gain.shape, f32),
            pltpu.VMEM(full, f32),
            pltpu.VMEM(full, low),
            pltpu.VMEM(full, low),
            pltpu.VMEM(full, f32),
            pltpu.VMEM(full, f32),
            pltpu.VMEM(half, f32),
            pltpu.VMEM(half, f32),
            pltpu.VMEM((2,) + half, f32),
            pltpu.VMEM((rows, heads * 128), low),
            pltpu.VMEM((rows, 3 * heads * 128), low),
            pltpu.VMEM((rows, 128), f32),
            pltpu.VMEM((rows, 128), f32),
            pltpu.VMEM((2, 128, width), f32),
            pltpu.VMEM((TAIL_ROWS, width), f32),
        ]
        + buffers
        + [pltpu.SemaphoreType.DMA((12,)), pltpu.SemaphoreType.DMA((2,))]
        + [pltpu.SemaphoreType.DMA((2, pieces))] * 6
        + sems,
        compiler_params=pltpu.CompilerParams(
            collective_id=collective_id, has_side_effects=True, vmem_limit_bytes=60 << 20
        ),
    )(
        cotangent, hidden, active, normed_two, normed, middle, state, qkv, logsum, mixed,
        down, up, qkv_w, out_w, gain,
    )


def standardize(state):
    centred = state - jnp.mean(state, axis=-1, keepdims=True)
    inverse = lax.rsqrt(jnp.mean(centred * centred, axis=-1, keepdims=True) + EPSILON)
    return centred * inverse


def attend_forward(queries, keys, values, tokens):
    scores = jnp.einsum("hqe,hke->hqk", queries, keys, preferred_element_type=jnp.float32) * HEAD ** (-0.5)
    column = lax.broadcasted_iota(jnp.int32, scores.shape, 2)
    scores = jnp.where(column < tokens, scores, -jnp.inf)
    peak = jnp.max(scores, axis=-1, keepdims=True)
    expo = jnp.exp(scores - peak)
    total = jnp.sum(expo, axis=-1, keepdims=True)
    weights = (expo / total).astype(jnp.bfloat16)
    mixed = jnp.einsum("hqk,hke->hqe", weights, values, preferred_element_type=jnp.float32)
    return mixed.astype(jnp.bfloat16), peak + jnp.log(total)


def pad_to(array, axis, size):
    spec = [(0, 0)] * array.ndim
    spec[axis] = (0, size - array.shape[axis])
    return jnp.pad(array, spec)


def by_head(array, axis, heads):
    shape = array.shape[:axis] + (heads, HEAD) + array.shape[axis + 1 :]
    split = pad_to(array.reshape(shape), axis + 1, 128)
    return split.reshape(array.shape[:axis] + (heads * 128,) + array.shape[axis + 1 :])


def local(
    dp_size,
    images,
    qkv_weight,
    qv_bias,
    out_weight,
    out_bias,
    up_weight,
    up_bias,
    down_weight,
    down_bias,
    norm_gain,
    norm_shift,
    cotangent,
):
    count, tokens, width = images.shape
    layers = qkv_weight.shape[0]
    local_width = qkv_weight.shape[3]
    heads = local_width // HEAD
    hidden_units = up_weight.shape[2]
    padded_units = -(-hidden_units // 128) * 128
    rows = -(-tokens // BLOCK) * BLOCK
    up = pad_to(up_weight, 2, padded_units)
    up_b = pad_to(up_bias, 1, padded_units)
    down = pad_to(down_weight, 1, padded_units)
    out_w = by_head(out_weight, 1, heads)
    qkv_w = by_head(qkv_weight, 3, heads).transpose(0, 2, 1, 3).reshape(layers, width, 3 * heads * 128)
    qv_b = by_head(qv_bias, 2, heads)
    qkv_b = jnp.concatenate([qv_b[:, 0], jnp.zeros_like(qv_b[:, 0]), qv_b[:, 1]], axis=1)
    state = pad_to(images[0], 0, rows).astype(jnp.float32)
    kept = []
    for layer in range(layers):
        normed = (standardize(state) * norm_gain[layer, 0] + norm_shift[layer, 0]).astype(jnp.bfloat16)
        qkv = (jnp.dot(normed, qkv_w[layer], preferred_element_type=jnp.float32) + qkv_b[layer]).astype(jnp.bfloat16)
        qkv = qkv.reshape(rows, 3, heads, 128).transpose(1, 2, 0, 3)
        mixed, logsum = attend_forward(qkv[0], qkv[1], qkv[2], tokens)
        partial_out = jnp.einsum(
            "hre,hed->rd", mixed, out_w[layer].reshape(heads, 128, width), preferred_element_type=jnp.float32
        )
        middle = state + tensor_sum(partial_out, 0) + out_bias[layer]
        normed_two = (standardize(middle) * norm_gain[layer, 1] + norm_shift[layer, 1]).astype(jnp.bfloat16)
        hidden = jnp.dot(normed_two, up[layer], preferred_element_type=jnp.float32) + up_b[layer]
        active = jax.nn.gelu(hidden, approximate=True).astype(jnp.bfloat16)
        partial_down = jnp.dot(active, down[layer], preferred_element_type=jnp.float32)
        logsum = jnp.broadcast_to(logsum, (heads, rows, 128))
        kept.append((hidden, active, normed_two, normed, middle, state, qkv, logsum, mixed))
        state = middle + tensor_sum(partial_down, 0) + down_bias[layer]
    encoded = state[:tokens].astype(jnp.bfloat16)[None]
    stacked = [jnp.stack([entry[i] for entry in kept]) for i in range(9)]
    flat, summed, image_grad = backward(
        tokens, HEAD, hidden_units, UNIT, 1, dp_size == 8,
        pad_to(cotangent[0], 0, rows), *stacked, down, up, qkv_w, out_w, norm_gain,
    )
    if dp_size != 8:
        summed = lax.psum(flat, "dp")
    per_layer = summed.reshape(layers, summed.shape[0] // layers, width)[::-1]
    stop = -(-hidden_units // 8) * 8
    down_grad = per_layer[:, :hidden_units]
    up_grad = jnp.swapaxes(per_layer[:, stop : stop + hidden_units], 1, 2)
    out_grad = per_layer[:, 2 * stop : 2 * stop + local_width]
    qkv_grad = per_layer[:, 2 * stop + local_width : 2 * stop + 4 * local_width]
    qkv_grad = jnp.swapaxes(qkv_grad.reshape(layers, 3, local_width, width), 2, 3)
    small = per_layer[:, 2 * stop + 4 * local_width :]
    qv_grad = small[:, 0:2, : heads * 128].reshape(layers, 2, heads, 128)[..., :HEAD]
    return (
        encoded,
        image_grad[:tokens][None],
        qkv_grad,
        qv_grad.reshape(layers, 2, local_width),
        out_grad,
        small[:, 2],
        up_grad,
        small[:, 3, :hidden_units],
        down_grad,
        small[:, 4],
        small[:, 5:7],
        small[:, 7:9],
    )


def solution(mesh):
    in_specs = (
        P("dp", None, None),
        P(None, None, None, "tensor"),
        P(None, None, "tensor"),
        P(None, "tensor", None),
        P(),
        P(None, None, "tensor"),
        P(None, "tensor"),
        P(None, "tensor", None),
        P(),
        P(),
        P(),
        P("dp", None, None),
    )
    out_specs = (
        P("dp", None, None),
        P("dp", None, None),
        P(None, None, None, "tensor"),
        P(None, None, "tensor"),
        P(None, "tensor", None),
        P(),
        P(None, None, "tensor"),
        P(None, "tensor"),
        P(None, "tensor", None),
        P(),
        P(),
        P(),
    )
    return jax.shard_map(
        functools.partial(local, mesh.shape["dp"]), mesh=mesh, in_specs=in_specs, out_specs=out_specs, check_vma=False)
```

```python
import functools

import jax
import jax.numpy as jnp
from jax import lax
from jax.experimental import pallas as pl
from jax.experimental.pallas import tpu as pltpu
from jax.sharding import PartitionSpec as P

MESH = pl.DeviceIdType.MESH
SLOTS = 16


def grad_sum_ticks(dp_sum, unit, steps, layers, grads, totals, buffers, sems):
    (x_in, inner_in, mid_in, whole_in, half_in, side_in, own_a, total_a, own_b, total_b) = buffers
    (
        x_sem, inner_sem, mid_sem, out_pair_sem, out_x_sem, whole_sem, half_sem, side_sem,
        back_mid_sem, back_pair_sem, relay_sem, load_a_sem, load_b_sem, store_a_sem, store_b_sem,
    ) = sems
    dp = lax.axis_index("dp")
    tensor = lax.axis_index("tensor")
    z = dp // 2
    x = dp % 2
    is_mid = (z == 1) | (z == 2)
    is_end = jnp.logical_not(is_mid)
    x_peer = (dp + 1 - 2 * x, tensor)
    pair_peer = (dp + 2 - 4 * (z % 2), tensor)
    mid_z = jnp.where(is_mid, 3 - z, z)
    mid_peer = (mid_z * 2 + x, tensor)
    side = jnp.where(z == 2, 1, 0)

    def greet(others):
        barrier = pltpu.get_barrier_semaphore()
        for peer in others:
            pl.semaphore_signal(barrier, inc=1, device_id=peer, device_id_type=MESH)
        if not dp_sum:
            pl.semaphore_wait(barrier, len(others))
            return
        for peer in (x_peer, pair_peer):
            pl.semaphore_signal(barrier, inc=1, device_id=peer, device_id_type=MESH)

        @pl.when(is_mid)
        def _():
            pl.semaphore_signal(barrier, inc=1, device_id=mid_peer, device_id_type=MESH)
            pl.semaphore_wait(barrier, 3 + len(others))

        @pl.when(is_end)
        def _():
            pl.semaphore_wait(barrier, 2 + len(others))

    layer_steps = steps // layers

    def place(chunk):
        turn = chunk // layer_steps
        return ((layers - 1 - turn) * layer_steps + chunk - turn * layer_steps) * (4 * unit)

    def row(chunk, part):
        return pl.ds(pl.multiple_of(place(chunk) + part * unit, 8), unit)

    def rows_b(chunk):
        return pl.ds(pl.multiple_of(place(chunk) + 2 * unit, 8), 2 * unit)

    def remote(src, dst, sem, slot, peer):
        return pltpu.make_async_remote_copy(
            src_ref=src, dst_ref=dst, send_sem=sem.at[0, slot], recv_sem=sem.at[1, slot],
            device_id=peer, device_id_type=MESH,
        )

    def a_x(c, s):
        return remote(grads.at[row(c, 1 - x)], x_in.at[s], x_sem, s, x_peer)

    def a_load(c, s):
        return pltpu.make_async_copy(grads.at[row(c, x)], own_a.at[s], load_a_sem.at[s])

    def a_inner(c, s):
        return remote(own_a.at[s], inner_in.at[s], inner_sem, s, pair_peer)

    def a_mid(c, s):
        return remote(own_a.at[s], mid_in.at[s], mid_sem, s, mid_peer)

    def a_out_pair(c, s):
        return remote(total_a.at[s], totals.at[row(c, x)], out_pair_sem, s, pair_peer)

    def a_out_x(c, s):
        return remote(total_a.at[s], totals.at[row(c, x)], out_x_sem, s, x_peer)

    def a_store(c, s):
        return pltpu.make_async_copy(total_a.at[s], totals.at[row(c, x)], store_a_sem.at[s])

    def a_relay(c, s):
        return remote(totals.at[row(c, x)], totals.at[row(c, x)], out_x_sem, s, x_peer)

    def a_back(c, s):
        return remote(totals.at[row(c, x)], totals.at[row(c, 1 - x)], out_x_sem, s, x_peer)

    def b_whole(c, s):
        return remote(grads.at[rows_b(c)], whole_in.at[s], whole_sem, s, pair_peer)

    def b_load(c, s):
        return pltpu.make_async_copy(grads.at[rows_b(c)], own_b.at[s], load_b_sem.at[s])

    def b_half(c, s):
        return remote(own_b.at[s, pl.ds((1 - side) * unit, unit)], half_in.at[s], half_sem, s, mid_peer)

    def b_side(c, s):
        return remote(own_b.at[s, pl.ds(side * unit, unit)], side_in.at[s], side_sem, s, x_peer)

    def b_store(c, s):
        return pltpu.make_async_copy(total_b.at[s], totals.at[row(c, 2 + side)], store_b_sem.at[s])

    def b_back_mid(c, s):
        return remote(total_b.at[s], totals.at[row(c, 2 + side)], back_mid_sem, s, mid_peer)

    def b_back_pair(c, s):
        return remote(total_b.at[s], totals.at[row(c, 2 + side)], back_pair_sem, s, pair_peer)

    def b_relay(c, s):
        return remote(
            totals.at[row(c, 3 - side)], totals.at[row(c, 3 - side)], relay_sem, s, pair_peer
        )

    def stage(step, offset, guard, body):
        chunk = step - offset
        ok = (chunk >= 0) & (chunk < steps)
        if guard is not None:
            ok = ok & guard

        @pl.when(ok)
        def _():
            body(chunk, lax.rem(chunk, SLOTS))

    def start_all(c, s):
        a_x(c, s).start()
        a_load(c, s).start()

    def start_end(c, s):
        b_whole(c, s).start()

    def start_mid(c, s):
        b_load(c, s).start()

    def a1_end(c, s):
        a_load(c, s).wait()
        a_x(c, s).wait_recv()
        own_a[s] = own_a[s] + x_in[s]
        a_inner(c, s).start()

    def a1_mid(c, s):
        a_load(c, s).wait()
        a_x(c, s).wait_recv()
        own_a[s] = own_a[s] + x_in[s]

    def a2_mid(c, s):
        a_inner(c, s).wait_recv()
        own_a[s] = own_a[s] + inner_in[s]
        a_mid(c, s).start()

    def a3_mid(c, s):
        a_mid(c, s).wait_recv()
        total_a[s] = own_a[s] + mid_in[s]
        a_out_pair(c, s).start()
        a_out_x(c, s).start()
        a_store(c, s).start()

    def a3_end(c, s):
        a_out_pair(c, s).wait_recv()
        a_relay(c, s).start()

    def b1_mid(c, s):
        b_load(c, s).wait()
        b_whole(c, s).wait_recv()
        own_b[s] = own_b[s] + whole_in[s]
        b_half(c, s).start()

    def b2_mid(c, s):
        b_half(c, s).wait_recv()
        mine = pl.ds(pl.multiple_of(side * unit, 8), unit)
        own_b[s, mine] = own_b[s, mine] + half_in[s]
        b_side(c, s).start()

    def b3_mid(c, s):
        b_side(c, s).wait_recv()
        mine = pl.ds(pl.multiple_of(side * unit, 8), unit)
        total_b[s] = own_b[s, mine] + side_in[s]
        b_back_mid(c, s).start()
        b_back_pair(c, s).start()
        b_store(c, s).start()

    def b4_mid(c, s):
        b_back_mid(c, s).wait_recv()
        b_relay(c, s).start()

    def b5_end(c, s):
        b_back_pair(c, s).wait_recv()
        b_relay(c, s).wait_recv()

    def back_all(c, s):
        a_back(c, s).wait_recv()

    def done_end(c, s):
        a_inner(c, s).wait_send()
        b_whole(c, s).wait_send()

    def done_mid(c, s):
        a_mid(c, s).wait_send()
        a_out_pair(c, s).wait_send()
        a_store(c, s).wait()
        b_half(c, s).wait_send()
        b_side(c, s).wait_send()
        b_back_mid(c, s).wait_send()
        b_back_pair(c, s).wait_send()
        b_store(c, s).wait()
        b_relay(c, s).wait_send()

    def done_all(c, s):
        a_x(c, s).wait_send()
        a_out_x(c, s).wait_send()

    def tick(step):
        if not dp_sum:
            return
        stage(step, 0, None, start_all)
        stage(step, 0, is_end, start_end)
        stage(step, 0, is_mid, start_mid)
        stage(step, 8, is_mid, b4_mid)
        stage(step, 6, is_mid, a3_mid)
        stage(step, 6, is_mid, b3_mid)
        stage(step, 8, is_end, a3_end)
        stage(step, 4, is_mid, a2_mid)
        stage(step, 4, is_mid, b2_mid)
        stage(step, 2, is_mid, a1_mid)
        stage(step, 2, is_end, a1_end)
        stage(step, 2, is_mid, b1_mid)
        stage(step, 10, None, back_all)
        stage(step, 10, is_end, b5_end)
        stage(step, 11, is_end, done_end)
        stage(step, 11, is_mid, done_mid)
        stage(step, 11, None, done_all)

    return tick, greet


def tick_scratch(unit, width):
    one = (SLOTS, unit, width)
    two = (SLOTS, 2 * unit, width)
    buffers = [pltpu.VMEM(s, jnp.float32) for s in (one, one, one, two, one, one, one, one, two, one)]
    sems = [pltpu.SemaphoreType.DMA((2, SLOTS))] * 11 + [pltpu.SemaphoreType.DMA((SLOTS,))] * 4
    return buffers, sems


HEAD = 72
EPSILON = 1e-06
UNIT = 8
TAIL_ROWS = 16


FIRST = 6
PIECE = 16
LAG = 4
TICK_SPAN = 12
BLOCK = 192


def dot_nn(left, right):
    return lax.dot_general(left, right, (((1,), (0,)), ((), ())), preferred_element_type=jnp.float32)


def dot_nt(left, right):
    return lax.dot_general(left, right, (((1,), (1,)), ((), ())), preferred_element_type=jnp.float32)


def dot_tn(left, right):
    return lax.dot_general(left, right, (((0,), (0,)), ((), ())), preferred_element_type=jnp.float32)


def fold(array):
    return jnp.sum(array, axis=0, keepdims=True)


def gelu_slope(v):
    root = 0.7978845608028654
    inner = jnp.tanh(root * (v + 0.044715 * (v * v * v)))
    return 0.5 * (1.0 + inner) + 0.5 * v * (1.0 - inner * inner) * (root * (1.0 + 0.134145 * (v * v)))


def norm_back(grad_normed, state, gain):
    centred = state - jnp.mean(state, axis=-1, keepdims=True)
    inverse = lax.rsqrt(jnp.mean(centred * centred, axis=-1, keepdims=True) + EPSILON)
    unit = centred * inverse
    grad_unit = grad_normed * gain
    inner = (
        grad_unit
        - jnp.mean(grad_unit, axis=-1, keepdims=True)
        - unit * jnp.mean(grad_unit * unit, axis=-1, keepdims=True)
    )
    return inverse * inner, fold(grad_normed * unit), fold(grad_normed)


def backward_kernel(
    dp_sum, tokens, layers, heads, units_rows, head_dim, send_rows, unit, steps,
    cotangent, hidden, active, normed_two, normed, middle, state, qkv, logsum, mixed,
    down, up, qkv_w, out_w, gain, down_b, last_part,
    grads, totals, image_grad, encoded, up_grad, qkv_grad,
    wide, act_buf, two_buf, qkv_buf, lse_buf, mix_buf, down_buf, up_buf, qkvw_buf, outw_buf, gain_buf,
    flow, flow_low, hid_low, part, total, core_in, acc, y_in, grad_mix, cat, tight, acc_k, acc_v, stage_buf, small,
    turned_up, turned_qkv, downb_buf,
    x_in, inner_in, mid_in, whole_in, half_in, side_in, own_a, total_a, own_b, total_b,
    load_sem, stage_sem, turn_sem, core_send, core_recv, y_send, y_recv, back_send, back_recv, *tick_sems
):
    width = grads.shape[1]
    rows = part.shape[0]
    blocks = rows // BLOCK
    half = send_rows // 2
    pieces = half // PIECE
    tick, greet = grad_sum_ticks(
        dp_sum, unit, steps, layers, grads, totals,
        (x_in, inner_in, mid_in, whole_in, half_in, side_in, own_a, total_a, own_b, total_b), tick_sems,
    )
    dp = lax.axis_index("dp")
    tensor = lax.axis_index("tensor")
    core = tensor % 2
    core_peer = (dp, tensor + 1 - 2 * core)
    y_peer = (dp, lax.rem(tensor + 2, 4))
    greet((core_peer, y_peer))
    layer_rows = steps * 4 * unit // layers
    off_up = units_rows
    local_width = heads * head_dim
    off_qkv = 2 * units_rows
    off_out = off_qkv + 3 * local_width
    off_small = off_out + local_width
    spread = spread_matrix(heads, head_dim)

    def mine(i):
        return pl.ds(pl.multiple_of(core * half + i * PIECE, 8), PIECE)

    def other(i):
        return pl.ds(pl.multiple_of((1 - core) * half + i * PIECE, 8), PIECE)

    def here(i):
        return pl.ds(pl.multiple_of(i * PIECE, 8), PIECE)

    def remote(src, dst, send, recv, peer):
        return pltpu.make_async_remote_copy(
            src_ref=src, dst_ref=dst, send_sem=send, recv_sem=recv, device_id=peer, device_id_type=MESH
        )

    def to_core(p, i):
        return remote(
            part.at[other(i)], core_in.at[here(i)], core_send.at[p, i], core_recv.at[p, i], core_peer
        )

    def to_y(p, i):
        return remote(acc.at[here(i)], y_in.at[p, here(i)], y_send.at[p, i], y_recv.at[p, i], y_peer)

    def to_back(p, i):
        return remote(total.at[mine(i)], total.at[mine(i)], back_send.at[p, i], back_recv.at[p, i], core_peer)

    def from_back(p, i):
        return remote(
            total.at[other(i)], total.at[other(i)], back_send.at[p, i], back_recv.at[p, i], core_peer
        )

    def sum_begin(p):
        def go(i, c):
            to_core(p, i).start()
            return c

        lax.fori_loop(0, pieces, go, 0)

    def sum_step(p, j):
        @pl.when(j < pieces)
        def _():
            to_core(p, j).wait_recv()
            acc[here(j)] = part[mine(j)] + core_in[here(j)]
            to_y(p, j).start()

        late = j - LAG

        @pl.when((late >= 0) & (late < pieces))
        def _():
            to_y(p, late).wait_recv()
            total[mine(late)] = acc[here(late)] + y_in[p, here(late)]
            to_back(p, late).start()

        last = j - LAG - 2

        @pl.when((last >= 0) & (last < pieces))
        def _():
            to_core(p, last).wait_send()
            to_y(p, last).wait_send()
            to_back(p, last).wait_send()
            from_back(p, last).wait_recv()

    sum_steps = pieces + LAG + 2

    def load(source, target, sem):
        return pltpu.make_async_copy(source, target, load_sem.at[sem])

    def stage_copy(slot, row, size):
        return pltpu.make_async_copy(
            stage_buf.at[slot, pl.ds(0, size)], grads.at[pl.ds(pl.multiple_of(row, 8), size)], stage_sem.at[slot]
        )

    layer_ticks = 4 * blocks + 2 * sum_steps + heads * blocks

    def row_block(b):
        return pl.ds(pl.multiple_of(b * BLOCK, 16), BLOCK)

    total[pl.ds(send_rows, rows - send_rows)] = jnp.zeros((rows - send_rows, width), jnp.float32)
    start = load(cotangent, flow_low, 0)
    start.start()
    load(gain, gain_buf, 11).start()
    start.wait()
    load(gain, gain_buf, 11).wait()

    def lift(b, c):
        flow[row_block(b)] = flow_low[row_block(b)].astype(jnp.float32)
        return c

    lax.fori_loop(0, blocks, lift, 0)

    def layer_body(it, carry):
        layer = layers - 1 - it
        base_tick = it * layer_ticks - FIRST
        base_row = layer * layer_rows
        hidden_load = load(hidden.at[layer], wide, 0)
        down_load = load(down.at[layer], down_buf, 1)
        up_load = load(up.at[layer], up_buf, 2)
        active_load = load(active.at[layer], act_buf, 3)
        two_load = load(normed_two.at[layer], two_buf, 4)
        outw_load = load(out_w.at[layer], outw_buf, 5)
        qkv_load = load(qkv.at[layer], qkv_buf, 6)
        lse_load = load(logsum.at[layer], lse_buf, 7)
        mix_load = load(mixed.at[layer], mix_buf, 8)
        qkvw_load = load(qkv_w.at[layer], qkvw_buf, 9)
        for copy in (hidden_load, down_load, up_load, active_load, two_load, outw_load, qkv_load, lse_load, mix_load, qkvw_load):
            copy.start()
        small[...] = jnp.zeros_like(small)
        hidden_load.wait()
        down_load.wait()
        up_load.wait()

        def mlp(b, c):
            at = row_block(b)
            grad = flow[at]
            small[4:5] += fold(grad)
            low = grad.astype(jnp.bfloat16)
            flow_low[at] = low
            grad_hidden = dot_nt(low, down_buf[...]) * gelu_slope(wide[at])
            small[3:4] += fold(grad_hidden)
            hid = grad_hidden.astype(jnp.bfloat16)
            hid_low[at] = hid
            part[at] = dot_nt(hid, up_buf[...])
            tick(base_tick + b)
            return c

        lax.fori_loop(0, blocks, mlp, 0)
        sum_begin(0)
        middle_load = load(middle.at[layer], wide, 0)
        middle_load.start()
        active_load.wait()
        two_load.wait()
        tiles = width // 128
        last_rows = units_rows - (tiles - 1) * 128

        def stage_finish(j, count):
            done = j - 1
            whole = (done != tiles - 1) & (done != 2 * tiles - 1)
            slot = lax.rem(done, 2)

            @pl.when((done >= 0) & (done < count) & whole)
            def _():
                stage_copy(slot, base_row, 128).wait()

            @pl.when((done >= 0) & (done < count) & jnp.logical_not(whole))
            def _():
                stage_copy(slot, base_row, last_rows).wait()

        def mlp_weights(j, c):
            sum_step(0, j)
            stage_finish(j, 2 * tiles)
            slot = lax.rem(j, 2)

            @pl.when(j < tiles)
            def _():
                lanes = pl.ds(pl.multiple_of(j * 128, 128), 128)
                stage_buf[slot, pl.ds(0, 128)] = dot_tn(act_buf[:, lanes], flow_low[...])

            @pl.when((j >= tiles) & (j < 2 * tiles))
            def _():
                lanes = pl.ds(pl.multiple_of((j - tiles) * 128, 128), 128)
                stage_buf[slot, pl.ds(0, 128)] = dot_tn(hid_low[:, lanes], two_buf[...])

            second = j >= tiles
            tile = jnp.where(second, j - tiles, j)
            row = base_row + jnp.where(second, off_up, 0) + tile * 128

            @pl.when((j < 2 * tiles) & (tile < tiles - 1))
            def _():
                stage_copy(slot, row, 128).start()

            @pl.when((j < 2 * tiles) & (tile == tiles - 1))
            def _():
                stage_copy(slot, row, last_rows).start()

            tick(base_tick + blocks + j)
            return c

        lax.fori_loop(0, sum_steps, mlp_weights, 0)
        tick_at = base_tick + blocks + sum_steps
        middle_load.wait()
        outw_load.wait()

        def norm_two(b, c):
            at = row_block(b)
            step_grad, gain_grad, shift_grad = norm_back(total[at], wide[at], gain_buf[layer, 1:2])
            small[6:7] += gain_grad
            small[8:9] += shift_grad
            grad = flow[at] + step_grad
            flow[at] = grad
            small[2:3] += fold(grad)
            low = grad.astype(jnp.bfloat16)
            flow_low[at] = low
            grad = dot_nt(low, outw_buf[...]).astype(jnp.bfloat16)
            grad_mix[at] = dot_nn(grad, spread).astype(jnp.bfloat16)
            tick(tick_at + b)
            return c

        lax.fori_loop(0, blocks, norm_two, 0)
        tick_at = tick_at + blocks
        state_load = load(state.at[layer], wide, 0)
        normed_load = load(normed.at[layer], act_buf, 3)
        state_load.start()
        normed_load.start()
        qkv_load.wait()
        lse_load.wait()
        scale = head_dim ** (-0.5)

        def attend(m, c):
            head = m // blocks
            b = lax.rem(m, blocks)
            at = row_block(b)
            lanes = pl.ds(pl.multiple_of(head * 128, 128), 128)
            query = qkv_buf[0, head, at]
            key = qkv_buf[1, head]
            value = qkv_buf[2, head]
            grad = grad_mix[at, lanes]
            scores = dot_nt(query, key) * scale
            probs = jnp.exp(scores - lse_buf[head, at, 0:1])
            column = lax.broadcasted_iota(jnp.int32, probs.shape, 1)
            probs = jnp.where(column < tokens, probs, 0.0)
            grad_weights = dot_nt(grad, value)
            center = jnp.sum(probs * grad_weights, axis=-1, keepdims=True)
            raw = (probs * (grad_weights - center) * scale).astype(jnp.bfloat16)
            grad_query = dot_nn(raw, key)
            small[0:1, lanes] += fold(grad_query)
            cat[at, lanes] = grad_query.astype(jnp.bfloat16)
            add_k = dot_tn(raw, query)
            add_v = dot_tn(probs.astype(jnp.bfloat16), grad)

            @pl.when(b == 0)
            def _():
                acc_k[...] = add_k
                acc_v[...] = add_v

            @pl.when(b > 0)
            def _():
                acc_k[...] += add_k
                acc_v[...] += add_v

            @pl.when(b == blocks - 1)
            def _():
                at_k = pl.ds(pl.multiple_of((heads + head) * 128, 128), 128)
                at_v = pl.ds(pl.multiple_of((2 * heads + head) * 128, 128), 128)
                cat[:, at_k] = acc_k[...].astype(jnp.bfloat16)
                cat[:, at_v] = acc_v[...].astype(jnp.bfloat16)
                small[1:2, lanes] += fold(acc_v[...])

            tick(tick_at + m)
            return c

        lax.fori_loop(0, heads * blocks, attend, 0)
        tick_at = tick_at + heads * blocks
        qkvw_load.wait()

        def project(b, c):
            at = row_block(b)
            out = None
            for i in range(3):
                lanes = pl.ds(i * heads * 128, heads * 128)
                narrow = dot_nt(cat[at, lanes], spread).astype(jnp.bfloat16)
                tight[i, at] = narrow
                term = dot_nt(narrow, qkvw_buf[i])
                out = term if out is None else out + term
            part[at] = out
            tick(tick_at + b)
            return c

        lax.fori_loop(0, blocks, project, 0)
        tick_at = tick_at + blocks
        sum_begin(1)
        normed_load.wait()
        mix_load.wait()

        def attention_weights(j, c):
            sum_step(1, j)

            @pl.when((j >= 1) & (j < 5))
            def _():
                stage_copy(lax.rem(j - 1, 2), base_row, local_width).wait()

            slot = lax.rem(j, 2)

            @pl.when(j < 3)
            def _():
                stage_buf[slot] = dot_tn(tight[j], act_buf[...])

            @pl.when(j == 3)
            def _():
                stage_buf[slot] = dot_tn(mix_buf[...], flow_low[...])

            @pl.when(j < 4)
            def _():
                stage_copy(slot, base_row + off_qkv + j * local_width, local_width).start()

            tick(tick_at + j)
            return c

        lax.fori_loop(0, sum_steps, attention_weights, 0)
        tick_at = tick_at + sum_steps
        state_load.wait()

        def norm_one(b, c):
            at = row_block(b)
            step_grad, gain_grad, shift_grad = norm_back(total[at], wide[at], gain_buf[layer, 0:1])
            small[5:6] += gain_grad
            small[7:8] += shift_grad
            flow[at] = flow[at] + step_grad
            tick(tick_at + b)
            return c

        lax.fori_loop(0, blocks, norm_one, 0)
        tail = pltpu.make_async_copy(
            small, grads.at[pl.ds(pl.multiple_of(base_row + off_small, 8), small.shape[0])], load_sem.at[10]
        )
        tail.start()
        tail.wait()
        return carry

    lax.fori_loop(0, layers, layer_body, 0)

    part_load = load(last_part, part, 1)
    middle_load = load(middle.at[layers - 1], wide, 2)
    bias_load = load(down_b, downb_buf, 3)
    part_load.start()
    middle_load.start()
    bias_load.start()

    def lower(b, c):
        flow_low[row_block(b)] = flow[row_block(b)].astype(jnp.bfloat16)
        return c

    lax.fori_loop(0, blocks, lower, 0)
    image_store = load(flow_low, image_grad, 0)
    image_store.start()
    part_load.wait()
    sum_begin(0)

    tail = layers * layer_ticks - FIRST
    tiles = width // 128
    last_rows = units_rows - (tiles - 1) * 128
    layer_steps = steps // layers

    def landed(turn, row):
        return turn * layer_steps + -(-row // (4 * unit)) + TICK_SPAN

    up_starts, qkv_steps, at_step = [], [], tail
    for turn in range(layers):
        at_step = max(at_step, landed(turn, off_up + units_rows))
        up_starts.append(at_step)
        at_step += tiles + 1
        for i in range(3):
            at_step = max(at_step, landed(turn, off_qkv + (i + 1) * local_width))
            qkv_steps.append((at_step, layers - 1 - turn, i))
            at_step += 1
    stop = max(steps + TICK_SPAN, at_step)

    def up_load(layer, tile, rows_here):
        row = pl.multiple_of(layer * layer_rows + off_up + tile * 128, 8)
        slot = lax.rem(tile, 2)
        return pltpu.make_async_copy(
            totals.at[pl.ds(row, rows_here)], stage_buf.at[slot, pl.ds(0, rows_here)], stage_sem.at[slot]
        )

    def up_store(layer, tile):
        slot = lax.rem(tile, 2)
        lanes = pl.ds(pl.multiple_of(tile * 128, 128), 128)
        return pltpu.make_async_copy(turned_up.at[slot], up_grad.at[layer, :, lanes], turn_sem.at[slot])

    def up_turn(layer, tile):
        @pl.when(tile < tiles - 1)
        def _():
            up_load(layer, tile, 128).start()

        @pl.when(tile == tiles - 1)
        def _():
            up_load(layer, tile, last_rows).start()

        before = tile - 1

        @pl.when(before >= 0)
        def _():
            @pl.when(before < tiles - 1)
            def _():
                up_load(layer, before, 128).wait()

            @pl.when(before == tiles - 1)
            def _():
                up_load(layer, before, last_rows).wait()

            @pl.when(before >= 2)
            def _():
                up_store(layer, before - 2).wait()

            slot = lax.rem(before, 2)
            for i in range(tiles):
                turned_up[slot, pl.ds(i * 128, 128)] = stage_buf[slot, pl.ds(0, 128), pl.ds(i * 128, 128)].T
            up_store(layer, before).start()

        @pl.when(tile == tiles)
        def _():
            up_store(layer, tiles - 2).wait()
            up_store(layer, tiles - 1).wait()

    def qkv_turn(layer, i):
        row = pl.multiple_of(layer * layer_rows + off_qkv + i * local_width, 8)
        fetch = pltpu.make_async_copy(
            totals.at[pl.ds(row, local_width)], stage_buf.at[0, pl.ds(0, local_width)], stage_sem.at[0]
        )
        fetch.start()
        fetch.wait()
        for k in range(tiles):
            turned_qkv[pl.ds(k * 128, 128)] = stage_buf[0, :, pl.ds(k * 128, 128)].T
        store = pltpu.make_async_copy(turned_qkv, qkv_grad.at[layer, i], turn_sem.at[0])
        store.start()
        store.wait()

    def rest(step, c):
        sum_step(0, step - tail)
        tick(step)
        if dp_sum:
            for turn in range(layers):
                tile = step - up_starts[turn]

                @pl.when((tile >= 0) & (tile <= tiles))
                def _():
                    up_turn(layers - 1 - turn, tile)

            hit, layer, index = False, 0, 0
            for when, its_layer, i in qkv_steps:
                here_now = step == when
                hit = here_now | hit
                layer = jnp.where(here_now, its_layer, layer)
                index = jnp.where(here_now, i, index)

            @pl.when(hit)
            def _():
                qkv_turn(layer, index)

        return c

    lax.fori_loop(tail, tail + sum_steps, rest, 0)
    middle_load.wait()
    bias_load.wait()

    def encode(b, c):
        at = row_block(b)
        hid_low[at] = (wide[at] + total[at] + downb_buf[layers - 1 : layers]).astype(jnp.bfloat16)
        return c

    lax.fori_loop(0, blocks, encode, 0)
    encoded_store = load(hid_low, encoded, 1)
    encoded_store.start()
    lax.fori_loop(tail + sum_steps, max(stop, tail + sum_steps), rest, 0)
    image_store.wait()
    encoded_store.wait()


def backward(
    tokens, head_dim, hidden_units, unit, collective_id, dp_sum,
    cotangent, hidden, active, normed_two, normed, middle, state, qkv, logsum, mixed,
    down, up, qkv_w, out_w, gain, down_b, last_part,
):
    layers, rows, width = middle.shape
    heads = qkv.shape[2]
    units_rows = -(-hidden_units // 8) * 8
    send_rows = -(-tokens // (2 * PIECE)) * 2 * PIECE
    pieces = send_rows // (2 * PIECE)
    layer_rows = 2 * units_rows + 4 * heads * head_dim + TAIL_ROWS
    steps = layers * layer_rows // (4 * unit)
    buffers, sems = tick_scratch(unit, width)
    f32, low = jnp.float32, jnp.bfloat16
    half = (send_rows // 2, width)
    full = (rows, width)
    any_spec = pl.BlockSpec(memory_space=pl.ANY)
    grads = jax.ShapeDtypeStruct((layers * layer_rows, width), f32)
    return pl.pallas_call(
        functools.partial(
            backward_kernel, dp_sum, tokens, layers, heads, units_rows, head_dim, send_rows, unit, steps
        ),
        out_shape=(
            grads,
            grads,
            jax.ShapeDtypeStruct(full, low),
            jax.ShapeDtypeStruct(full, low),
            jax.ShapeDtypeStruct((layers, width, width), f32),
            jax.ShapeDtypeStruct((layers, 3, width, heads * head_dim), f32),
        ),
        in_specs=[any_spec] * 17,
        out_specs=(any_spec,) * 6,
        scratch_shapes=[
            pltpu.VMEM(full, f32),
            pltpu.VMEM(full, low),
            pltpu.VMEM(full, low),
            pltpu.VMEM(qkv.shape[1:], low),
            pltpu.VMEM(logsum.shape[1:], f32),
            pltpu.VMEM(mixed.shape[1:], low),
            pltpu.VMEM(down.shape[1:], low),
            pltpu.VMEM(up.shape[1:], low),
            pltpu.VMEM(qkv_w.shape[1:], low),
            pltpu.VMEM(out_w.shape[1:], low),
            pltpu.VMEM(gain.shape, f32),
            pltpu.VMEM(full, f32),
            pltpu.VMEM(full, low),
            pltpu.VMEM(full, low),
            pltpu.VMEM(full, f32),
            pltpu.VMEM(full, f32),
            pltpu.VMEM(half, f32),
            pltpu.VMEM(half, f32),
            pltpu.VMEM((2,) + half, f32),
            pltpu.VMEM((rows, heads * 128), low),
            pltpu.VMEM((rows, 3 * heads * 128), low),
            pltpu.VMEM((3, rows, heads * head_dim), low),
            pltpu.VMEM((rows, 128), f32),
            pltpu.VMEM((rows, 128), f32),
            pltpu.VMEM((2, heads * head_dim, width), f32),
            pltpu.VMEM((TAIL_ROWS, width), f32),
            pltpu.VMEM((2, width, 128), f32),
            pltpu.VMEM((width, heads * head_dim), f32),
            pltpu.VMEM(down_b.shape, f32),
        ]
        + buffers
        + [pltpu.SemaphoreType.DMA((12,)), pltpu.SemaphoreType.DMA((2,)), pltpu.SemaphoreType.DMA((2,))]
        + [pltpu.SemaphoreType.DMA((2, pieces))] * 6
        + sems,
        compiler_params=pltpu.CompilerParams(
            collective_id=collective_id, has_side_effects=True, vmem_limit_bytes=62 << 20
        ),
    )(
        cotangent, hidden, active, normed_two, normed, middle, state, qkv, logsum, mixed,
        down, up, qkv_w, out_w, gain, down_b, last_part,
    )


def spread_matrix(heads, head_dim):
    shape = (heads * head_dim, heads * 128)
    source = lax.broadcasted_iota(jnp.int32, shape, 0)
    lane = lax.broadcasted_iota(jnp.int32, shape, 1)
    hit = (lane // 128 * head_dim + lane % 128 == source) & (lane % 128 < head_dim)
    return jnp.where(hit, 1.0, 0.0).astype(jnp.bfloat16)


def norm_unit(state):
    centred = state - jnp.mean(state, axis=-1, keepdims=True)
    return centred * lax.rsqrt(jnp.mean(centred * centred, axis=-1, keepdims=True) + EPSILON)


def gelu(v):
    return 0.5 * v * (1.0 + jnp.tanh(0.7978845608028654 * (v + 0.044715 * (v * v * v))))


def block_sum(pieces, dp, tensor, part, core_in, y_in, total, sems):
    core = tensor % 2
    core_peer = (dp, tensor + 1 - 2 * core)
    y_peer = (dp, lax.rem(tensor + 2, 4))
    core_sem, y_sem, back_sem = sems
    per_block = BLOCK // (2 * PIECE)

    def mine(i):
        return pl.ds(pl.multiple_of((2 * i + core) * PIECE, 8), PIECE)

    def other(i):
        return pl.ds(pl.multiple_of((2 * i + 1 - core) * PIECE, 8), PIECE)

    def here(i):
        return pl.ds(pl.multiple_of(i * PIECE, 8), PIECE)

    def remote(src, dst, sem, i, peer):
        return pltpu.make_async_remote_copy(
            src_ref=src, dst_ref=dst, send_sem=sem.at[0, i], recv_sem=sem.at[1, i],
            device_id=peer, device_id_type=MESH,
        )

    def to_core(i):
        return remote(part.at[other(i)], core_in.at[here(i)], core_sem, i, core_peer)

    def to_y(i):
        return remote(core_in.at[here(i)], y_in.at[here(i)], y_sem, i, y_peer)

    def to_back(i):
        return remote(total.at[mine(i)], total.at[mine(i)], back_sem, i, core_peer)

    def from_back(i):
        return remote(total.at[other(i)], total.at[other(i)], back_sem, i, core_peer)

    def each(b, body):
        def go(k, c):
            i = b * per_block + k

            @pl.when(i < pieces)
            def _():
                body(i)

            return c

        lax.fori_loop(0, per_block, go, 0)

    def send(b):
        each(b, lambda i: to_core(i).start())

    def meet(b):
        def body(i):
            to_core(i).wait_recv()
            core_in[here(i)] = core_in[here(i)] + part[mine(i)]
            to_y(i).start()

        each(b, body)

    def close(b):
        def body(i):
            to_y(i).wait_recv()
            total[mine(i)] = core_in[here(i)] + y_in[here(i)]
            to_back(i).start()

        each(b, body)

    def finish(b):
        def body(i):
            to_core(i).wait_send()
            to_y(i).wait_send()
            to_back(i).wait_send()
            from_back(i).wait_recv()

        each(b, body)

    return send, meet, close, finish


def forward_kernel(
    tokens, layers, heads, head_dim, send_rows,
    images, qkv_w, qv_b, out_w, out_b, up, up_b, down, down_b, gain, shift,
    hidden, active, normed_two, normed, middle, state, qkv, logsum, mixed, last_part,
    image_buf, flow, normed_buf, qkv_buf, lse_buf, mix_buf, tight_buf, two_buf, hidden_buf, active_buf,
    qkvw_buf, outw_buf, up_buf, down_buf, qvb_buf, outb_buf, upb_buf, downb_buf, gain_buf, shift_buf,
    part_a, core_in_a, y_in_a, total_a, part_b, core_in_b, y_in_b, total_b,
    load_sem, weight_sem, store_sem, middle_sem, *sum_sems
):
    rows, width = flow.shape
    blocks = rows // BLOCK
    pieces = send_rows // (2 * PIECE)
    dp = lax.axis_index("dp")
    tensor = lax.axis_index("tensor")
    core = tensor % 2
    barrier = pltpu.get_barrier_semaphore()
    for peer in ((dp, tensor + 1 - 2 * core), (dp, lax.rem(tensor + 2, 4))):
        pl.semaphore_signal(barrier, inc=1, device_id=peer, device_id_type=MESH)

    def weights(layer):
        return (
            pltpu.make_async_copy(qkv_w.at[layer], qkvw_buf, weight_sem.at[0]),
            pltpu.make_async_copy(out_w.at[layer], outw_buf, weight_sem.at[1]),
            pltpu.make_async_copy(up.at[layer], up_buf, weight_sem.at[2]),
            pltpu.make_async_copy(down.at[layer], down_buf, weight_sem.at[3]),
        )

    singles = [
        pltpu.make_async_copy(source, target, load_sem.at[i])
        for i, (source, target) in enumerate(
            (
                (images, image_buf), (gain, gain_buf), (shift, shift_buf), (qv_b, qvb_buf),
                (out_b, outb_buf), (up_b, upb_buf), (down_b, downb_buf),
            )
        )
    ]
    for copy in singles:
        copy.start()
    current = weights(0)
    for copy in current:
        copy.start()
    spread = spread_matrix(heads, head_dim)
    total_a[pl.ds(send_rows, rows - send_rows)] = jnp.zeros((rows - send_rows, width), jnp.float32)
    total_b[pl.ds(send_rows, rows - send_rows)] = jnp.zeros((rows - send_rows, width), jnp.float32)
    for copy in singles:
        copy.wait()
    pl.semaphore_wait(barrier, 2)

    def row_block(b):
        return pl.ds(pl.multiple_of(b * BLOCK, 16), BLOCK)

    scale = head_dim ** (-0.5)
    stores = {}

    def keep(name, source, target, index):
        copy = pltpu.make_async_copy(source, target, store_sem.at[index])
        copy.start()
        stores[name] = copy

    def settle(*names):
        for name in names:
            if name in stores:
                stores.pop(name).wait()

    def project(layer, b, value):
        at = row_block(b)
        flow[at] = value
        low = (norm_unit(value) * gain_buf[layer, 0:1] + shift_buf[layer, 0:1]).astype(jnp.bfloat16)
        normed_buf[at] = low
        for i in range(3):
            out = dot_nn(low, qkvw_buf[i])
            if i != 1:
                out = out + qvb_buf[layer, i // 2 : i // 2 + 1]
            wide = dot_nn(out.astype(jnp.bfloat16), spread).astype(jnp.bfloat16)
            for head in range(heads):
                qkv_buf[i, head, at] = wide[:, head * 128 : (head + 1) * 128]

    def first(b, c):
        project(0, b, image_buf[row_block(b)].astype(jnp.float32))
        return c

    current[0].wait()
    lax.fori_loop(0, blocks, first, 0)

    for layer in range(layers):
        keep("state", flow, state.at[layer], 0)
        keep("normed", normed_buf, normed.at[layer], 1)
        keep("qkv", qkv_buf, qkv.at[layer], 2)
        settle("logsum", "mixed")
        send_a, meet_a, close_a, finish_a = block_sum(
            pieces, dp, tensor, part_a, core_in_a, y_in_a, total_a, [s.at[layer] for s in sum_sems[:3]]
        )
        send_b, meet_b, close_b, finish_b = block_sum(
            pieces, dp, tensor, part_b, core_in_b, y_in_b, total_b, [s.at[layer] for s in sum_sems[3:]]
        )
        is_last = layer == layers - 1
        if not is_last:
            following = weights(layer + 1)
            following[0].start()

        def attend(m, c):
            head = m // blocks
            at = row_block(lax.rem(m, blocks))
            scores = dot_nt(qkv_buf[0, head, at], qkv_buf[1, head]) * scale
            column = lax.broadcasted_iota(jnp.int32, scores.shape, 1)
            scores = jnp.where(column < tokens, scores, -jnp.inf)
            peak = jnp.max(scores, axis=-1, keepdims=True)
            expo = jnp.exp(scores - peak)
            denominator = jnp.sum(expo, axis=-1, keepdims=True)
            probs = (expo / denominator).astype(jnp.bfloat16)
            lanes = pl.ds(pl.multiple_of(head * 128, 128), 128)
            mix_buf[at, lanes] = dot_nn(probs, qkv_buf[2, head]).astype(jnp.bfloat16)
            lse_buf[head, at] = jnp.broadcast_to(peak + jnp.log(denominator), (BLOCK, 128))
            return c

        lax.fori_loop(0, heads * blocks, attend, 0)
        keep("logsum", lse_buf, logsum.at[layer], 3)
        current[1].wait()

        def output(b, c):
            at = row_block(b)
            tight = dot_nt(mix_buf[at], spread).astype(jnp.bfloat16)
            tight_buf[at] = tight
            part_a[at] = dot_nn(tight, outw_buf[...])
            send_a(b)
            return c

        lax.fori_loop(0, blocks, output, 0)
        keep("mixed", tight_buf, mixed.at[layer], 4)
        if not is_last:
            following[1].start()

        def meet_all(b, c):
            meet_a(b)
            return c

        lax.fori_loop(0, blocks, meet_all, 0)
        settle("state", "normed_two", "hidden", "active")
        current[2].wait()
        current[3].wait()

        def mlp(b, c):
            at = row_block(b)
            close_a(b)
            if not is_last:

                @pl.when(b > 0)
                def _():
                    meet_b(b - 1)

            finish_a(b)
            value = flow[at] + total_a[at] + outb_buf[layer : layer + 1]
            flow[at] = value
            pltpu.make_async_copy(flow.at[at], middle.at[layer, at], middle_sem.at[b]).start()
            low = (norm_unit(value) * gain_buf[layer, 1:2] + shift_buf[layer, 1:2]).astype(jnp.bfloat16)
            two_buf[at] = low
            hid = dot_nn(low, up_buf[...]) + upb_buf[layer : layer + 1]
            hidden_buf[at] = hid
            act = gelu(hid).astype(jnp.bfloat16)
            active_buf[at] = act
            part_b[at] = dot_nn(act, down_buf[...])
            if not is_last:
                send_b(b)
            return c

        lax.fori_loop(0, blocks, mlp, 0)
        keep("normed_two", two_buf, normed_two.at[layer], 5)
        keep("hidden", hidden_buf, hidden.at[layer], 6)
        keep("active", active_buf, active.at[layer], 7)

        def middle_wait(b):
            pltpu.make_async_copy(flow.at[row_block(b)], middle.at[layer, row_block(b)], middle_sem.at[b]).wait()

        if is_last:
            keep("part", part_b, last_part, 8)
            for b in range(blocks):
                middle_wait(b)
        else:
            following[2].start()
            following[3].start()
            following[0].wait()
            meet_b(blocks - 1)
            settle("normed", "qkv")

            def next_project(b, c):
                at = row_block(b)
                close_b(b)
                finish_b(b)
                middle_wait(b)
                project(layer + 1, b, flow[at] + total_b[at] + downb_buf[layer : layer + 1])
                return c

            lax.fori_loop(0, blocks, next_project, 0)
            current = following
    settle(*list(stores))


def forward(
    tokens, head_dim, collective_id,
    images, qkv_w, qv_b, out_w, out_b, up, up_b, down, down_b, gain, shift,
):
    layers = qkv_w.shape[0]
    rows, width = images.shape
    heads = qkv_w.shape[3] // head_dim
    units = up.shape[2]
    send_rows = -(-tokens // (2 * PIECE)) * 2 * PIECE
    pieces = send_rows // (2 * PIECE)
    f32, low = jnp.float32, jnp.bfloat16
    full = (rows, width)
    half = (send_rows // 2, width)
    any_spec = pl.BlockSpec(memory_space=pl.ANY)

    def out(shape, dtype):
        return jax.ShapeDtypeStruct(shape, dtype)

    lanes = heads * 128
    return pl.pallas_call(
        functools.partial(forward_kernel, tokens, layers, heads, head_dim, send_rows),
        out_shape=(
            out((layers, rows, units), f32),
            out((layers, rows, units), low),
            out((layers,) + full, low),
            out((layers,) + full, low),
            out((layers,) + full, f32),
            out((layers,) + full, f32),
            out((layers, 3, heads, rows, 128), low),
            out((layers, heads, rows, 128), f32),
            out((layers, rows, heads * head_dim), low),
            out(full, f32),
        ),
        in_specs=[any_spec] * 11,
        out_specs=(any_spec,) * 10,
        scratch_shapes=[
            pltpu.VMEM(full, low),
            pltpu.VMEM(full, f32),
            pltpu.VMEM(full, low),
            pltpu.VMEM((3, heads, rows, 128), low),
            pltpu.VMEM((heads, rows, 128), f32),
            pltpu.VMEM((rows, lanes), low),
            pltpu.VMEM((rows, heads * head_dim), low),
            pltpu.VMEM(full, low),
            pltpu.VMEM((rows, units), f32),
            pltpu.VMEM((rows, units), low),
            pltpu.VMEM(qkv_w.shape[1:], low),
            pltpu.VMEM(out_w.shape[1:], low),
            pltpu.VMEM(up.shape[1:], low),
            pltpu.VMEM(down.shape[1:], low),
            pltpu.VMEM(qv_b.shape, f32),
            pltpu.VMEM(out_b.shape, f32),
            pltpu.VMEM(up_b.shape, f32),
            pltpu.VMEM(down_b.shape, f32),
            pltpu.VMEM(gain.shape, f32),
            pltpu.VMEM(shift.shape, f32),
        ]
        + [pltpu.VMEM(s, f32) for s in (full, half, half, full)] * 2
        + [
            pltpu.SemaphoreType.DMA((7,)),
            pltpu.SemaphoreType.DMA((4,)),
            pltpu.SemaphoreType.DMA((9,)),
            pltpu.SemaphoreType.DMA((rows // BLOCK,)),
        ]
        + [pltpu.SemaphoreType.DMA((layers, 2, pieces))] * 6,
        compiler_params=pltpu.CompilerParams(
            collective_id=collective_id, has_side_effects=True, vmem_limit_bytes=62 << 20
        ),
    )(images, qkv_w, qv_b, out_w, out_b, up, up_b, down, down_b, gain, shift)


def pad_to(array, axis, size):
    spec = [(0, 0)] * array.ndim
    spec[axis] = (0, size - array.shape[axis])
    return jnp.pad(array, spec)


def local(
    dp_size,
    images,
    qkv_weight,
    qv_bias,
    out_weight,
    out_bias,
    up_weight,
    up_bias,
    down_weight,
    down_bias,
    norm_gain,
    norm_shift,
    cotangent,
):
    tokens, width = images.shape[1:]
    layers = qkv_weight.shape[0]
    local_width = qkv_weight.shape[3]
    heads = local_width // HEAD
    hidden_units = up_weight.shape[2]
    padded_units = -(-hidden_units // 128) * 128
    rows = -(-tokens // BLOCK) * BLOCK
    up = pad_to(up_weight, 2, padded_units)
    up_b = pad_to(up_bias, 1, padded_units)
    down = pad_to(down_weight, 1, padded_units)
    *kept, last_part = forward(
        tokens, HEAD, 0,
        pad_to(images[0], 0, rows), qkv_weight, qv_bias, out_weight, out_bias, up, up_b, down, down_bias,
        norm_gain, norm_shift,
    )
    flat, summed, image_grad, encoded, up_grad, qkv_grad = backward(
        tokens, HEAD, hidden_units, UNIT, 1, dp_size == 8,
        pad_to(cotangent[0], 0, rows), *kept, down, up, qkv_weight, out_weight, norm_gain, down_bias, last_part,
    )
    if dp_size != 8:
        summed = lax.psum(flat, "dp")
    per_layer = summed.reshape(layers, summed.shape[0] // layers, width)
    stop = -(-hidden_units // 8) * 8
    down_grad = per_layer[:, :hidden_units]
    if dp_size == 8:
        up_grad = up_grad[:, :, :hidden_units]
    else:
        up_grad = jnp.swapaxes(per_layer[:, stop : stop + hidden_units], 1, 2)
        qkv_grad = per_layer[:, 2 * stop : 2 * stop + 3 * local_width]
        qkv_grad = jnp.swapaxes(qkv_grad.reshape(layers, 3, local_width, width), 2, 3)
    out_grad = per_layer[:, 2 * stop + 3 * local_width : 2 * stop + 4 * local_width]
    small = per_layer[:, 2 * stop + 4 * local_width :]
    qv_grad = small[:, 0:2, : heads * 128].reshape(layers, 2, heads, 128)[..., :HEAD]
    return (
        encoded[:tokens][None],
        image_grad[:tokens][None],
        qkv_grad,
        qv_grad.reshape(layers, 2, local_width),
        out_grad,
        small[:, 2],
        up_grad,
        small[:, 3, :hidden_units],
        down_grad,
        small[:, 4],
        small[:, 5:7],
        small[:, 7:9],
    )


def solution(mesh):
    in_specs = (
        P("dp", None, None),
        P(None, None, None, "tensor"),
        P(None, None, "tensor"),
        P(None, "tensor", None),
        P(),
        P(None, None, "tensor"),
        P(None, "tensor"),
        P(None, "tensor", None),
        P(),
        P(),
        P(),
        P("dp", None, None),
    )
    out_specs = (
        P("dp", None, None),
        P("dp", None, None),
        P(None, None, None, "tensor"),
        P(None, None, "tensor"),
        P(None, "tensor", None),
        P(),
        P(None, None, "tensor"),
        P(None, "tensor"),
        P(None, "tensor", None),
        P(),
        P(),
        P(),
    )
    return jax.shard_map(
        functools.partial(local, mesh.shape["dp"]), mesh=mesh, in_specs=in_specs, out_specs=out_specs, check_vma=False)
```

```python
import functools

import jax
import jax.numpy as jnp
from jax import lax
from jax.experimental import pallas as pl
from jax.experimental.pallas import tpu as pltpu
from jax.sharding import PartitionSpec as P

MESH = pl.DeviceIdType.MESH
SLOTS = 16


def grad_sum_ticks(dp_sum, unit, steps, layers, grads, totals, buffers, sems):
    (x_in, inner_in, mid_in, whole_in, half_in, side_in, own_a, total_a, own_b, total_b) = buffers
    (
        x_sem, inner_sem, mid_sem, out_pair_sem, out_x_sem, whole_sem, half_sem, side_sem,
        back_mid_sem, back_pair_sem, relay_sem, load_a_sem, load_b_sem, store_a_sem, store_b_sem,
    ) = sems
    dp = lax.axis_index("dp")
    tensor = lax.axis_index("tensor")
    z = dp // 2
    x = dp % 2
    is_mid = (z == 1) | (z == 2)
    is_end = jnp.logical_not(is_mid)
    x_peer = (dp + 1 - 2 * x, tensor)
    pair_peer = (dp + 2 - 4 * (z % 2), tensor)
    mid_z = jnp.where(is_mid, 3 - z, z)
    mid_peer = (mid_z * 2 + x, tensor)
    side = jnp.where(z == 2, 1, 0)

    def greet(others):
        barrier = pltpu.get_barrier_semaphore()
        for peer in others:
            pl.semaphore_signal(barrier, inc=1, device_id=peer, device_id_type=MESH)
        if not dp_sum:
            pl.semaphore_wait(barrier, len(others))
            return
        for peer in (x_peer, pair_peer):
            pl.semaphore_signal(barrier, inc=1, device_id=peer, device_id_type=MESH)

        @pl.when(is_mid)
        def _():
            pl.semaphore_signal(barrier, inc=1, device_id=mid_peer, device_id_type=MESH)
            pl.semaphore_wait(barrier, 3 + len(others))

        @pl.when(is_end)
        def _():
            pl.semaphore_wait(barrier, 2 + len(others))

    layer_steps = steps // layers

    def place(chunk):
        turn = chunk // layer_steps
        return ((layers - 1 - turn) * layer_steps + chunk - turn * layer_steps) * (4 * unit)

    def row(chunk, part):
        return pl.ds(pl.multiple_of(place(chunk) + part * unit, 8), unit)

    def rows_b(chunk):
        return pl.ds(pl.multiple_of(place(chunk) + 2 * unit, 8), 2 * unit)

    def remote(src, dst, sem, slot, peer):
        return pltpu.make_async_remote_copy(
            src_ref=src, dst_ref=dst, send_sem=sem.at[0, slot], recv_sem=sem.at[1, slot],
            device_id=peer, device_id_type=MESH,
        )

    def a_x(c, s):
        return remote(grads.at[row(c, 1 - x)], x_in.at[s], x_sem, s, x_peer)

    def a_load(c, s):
        return pltpu.make_async_copy(grads.at[row(c, x)], own_a.at[s], load_a_sem.at[s])

    def a_inner(c, s):
        return remote(own_a.at[s], inner_in.at[s], inner_sem, s, pair_peer)

    def a_mid(c, s):
        return remote(own_a.at[s], mid_in.at[s], mid_sem, s, mid_peer)

    def a_out_pair(c, s):
        return remote(total_a.at[s], totals.at[row(c, x)], out_pair_sem, s, pair_peer)

    def a_out_x(c, s):
        return remote(total_a.at[s], totals.at[row(c, x)], out_x_sem, s, x_peer)

    def a_store(c, s):
        return pltpu.make_async_copy(total_a.at[s], totals.at[row(c, x)], store_a_sem.at[s])

    def a_relay(c, s):
        return remote(totals.at[row(c, x)], totals.at[row(c, x)], out_x_sem, s, x_peer)

    def a_back(c, s):
        return remote(totals.at[row(c, x)], totals.at[row(c, 1 - x)], out_x_sem, s, x_peer)

    def b_whole(c, s):
        return remote(grads.at[rows_b(c)], whole_in.at[s], whole_sem, s, pair_peer)

    def b_load(c, s):
        return pltpu.make_async_copy(grads.at[rows_b(c)], own_b.at[s], load_b_sem.at[s])

    def b_half(c, s):
        return remote(own_b.at[s, pl.ds((1 - side) * unit, unit)], half_in.at[s], half_sem, s, mid_peer)

    def b_side(c, s):
        return remote(own_b.at[s, pl.ds(side * unit, unit)], side_in.at[s], side_sem, s, x_peer)

    def b_store(c, s):
        return pltpu.make_async_copy(total_b.at[s], totals.at[row(c, 2 + side)], store_b_sem.at[s])

    def b_back_mid(c, s):
        return remote(total_b.at[s], totals.at[row(c, 2 + side)], back_mid_sem, s, mid_peer)

    def b_back_pair(c, s):
        return remote(total_b.at[s], totals.at[row(c, 2 + side)], back_pair_sem, s, pair_peer)

    def b_relay(c, s):
        return remote(
            totals.at[row(c, 3 - side)], totals.at[row(c, 3 - side)], relay_sem, s, pair_peer
        )

    def stage(step, offset, guard, body):
        chunk = step - offset
        ok = (chunk >= 0) & (chunk < steps)
        if guard is not None:
            ok = ok & guard

        @pl.when(ok)
        def _():
            body(chunk, lax.rem(chunk, SLOTS))

    def start_all(c, s):
        a_x(c, s).start()
        a_load(c, s).start()

    def start_end(c, s):
        b_whole(c, s).start()

    def start_mid(c, s):
        b_load(c, s).start()

    def a1_end(c, s):
        a_load(c, s).wait()
        a_x(c, s).wait_recv()
        own_a[s] = own_a[s] + x_in[s]
        a_inner(c, s).start()

    def a1_mid(c, s):
        a_load(c, s).wait()
        a_x(c, s).wait_recv()
        own_a[s] = own_a[s] + x_in[s]

    def a2_mid(c, s):
        a_inner(c, s).wait_recv()
        own_a[s] = own_a[s] + inner_in[s]
        a_mid(c, s).start()

    def a3_mid(c, s):
        a_mid(c, s).wait_recv()
        total_a[s] = own_a[s] + mid_in[s]
        a_out_pair(c, s).start()
        a_out_x(c, s).start()
        a_store(c, s).start()

    def a3_end(c, s):
        a_out_pair(c, s).wait_recv()
        a_relay(c, s).start()

    def b1_mid(c, s):
        b_load(c, s).wait()
        b_whole(c, s).wait_recv()
        own_b[s] = own_b[s] + whole_in[s]
        b_half(c, s).start()

    def b2_mid(c, s):
        b_half(c, s).wait_recv()
        mine = pl.ds(pl.multiple_of(side * unit, 8), unit)
        own_b[s, mine] = own_b[s, mine] + half_in[s]
        b_side(c, s).start()

    def b3_mid(c, s):
        b_side(c, s).wait_recv()
        mine = pl.ds(pl.multiple_of(side * unit, 8), unit)
        total_b[s] = own_b[s, mine] + side_in[s]
        b_back_mid(c, s).start()
        b_back_pair(c, s).start()
        b_store(c, s).start()

    def b4_mid(c, s):
        b_back_mid(c, s).wait_recv()
        b_relay(c, s).start()

    def b5_end(c, s):
        b_back_pair(c, s).wait_recv()
        b_relay(c, s).wait_recv()

    def back_all(c, s):
        a_back(c, s).wait_recv()

    def done_end(c, s):
        a_inner(c, s).wait_send()
        b_whole(c, s).wait_send()

    def done_mid(c, s):
        a_mid(c, s).wait_send()
        a_out_pair(c, s).wait_send()
        a_store(c, s).wait()
        b_half(c, s).wait_send()
        b_side(c, s).wait_send()
        b_back_mid(c, s).wait_send()
        b_back_pair(c, s).wait_send()
        b_store(c, s).wait()
        b_relay(c, s).wait_send()

    def done_all(c, s):
        a_x(c, s).wait_send()
        a_out_x(c, s).wait_send()

    def tick(step):
        if not dp_sum:
            return
        stage(step, 0, None, start_all)
        stage(step, 0, is_end, start_end)
        stage(step, 0, is_mid, start_mid)
        stage(step, 8, is_mid, b4_mid)
        stage(step, 6, is_mid, a3_mid)
        stage(step, 6, is_mid, b3_mid)
        stage(step, 8, is_end, a3_end)
        stage(step, 4, is_mid, a2_mid)
        stage(step, 4, is_mid, b2_mid)
        stage(step, 2, is_mid, a1_mid)
        stage(step, 2, is_end, a1_end)
        stage(step, 2, is_mid, b1_mid)
        stage(step, 10, None, back_all)
        stage(step, 10, is_end, b5_end)
        stage(step, 11, is_end, done_end)
        stage(step, 11, is_mid, done_mid)
        stage(step, 11, None, done_all)

    return tick, greet


def tick_scratch(unit, width):
    one = (SLOTS, unit, width)
    two = (SLOTS, 2 * unit, width)
    buffers = [pltpu.VMEM(s, jnp.float32) for s in (one, one, one, two, one, one, one, one, two, one)]
    sems = [pltpu.SemaphoreType.DMA((2, SLOTS))] * 11 + [pltpu.SemaphoreType.DMA((SLOTS,))] * 4
    return buffers, sems


HEAD = 72
EPSILON = 1e-06
UNIT = 8
TAIL_ROWS = 16


FIRST = 6
PIECE = 16
LAG = 4
TICK_SPAN = 12
BLOCK = 192


def dot_nn(left, right):
    return lax.dot_general(left, right, (((1,), (0,)), ((), ())), preferred_element_type=jnp.float32)


def dot_nt(left, right):
    return lax.dot_general(left, right, (((1,), (1,)), ((), ())), preferred_element_type=jnp.float32)


def dot_tn(left, right):
    return lax.dot_general(left, right, (((0,), (0,)), ((), ())), preferred_element_type=jnp.float32)


def fold(array):
    return jnp.sum(array, axis=0, keepdims=True)


def gelu_slope(v):
    root = 0.7978845608028654
    inner = jnp.tanh(root * (v + 0.044715 * (v * v * v)))
    return 0.5 * (1.0 + inner) + 0.5 * v * (1.0 - inner * inner) * (root * (1.0 + 0.134145 * (v * v)))


def norm_back(grad_normed, state, gain):
    centred = state - jnp.mean(state, axis=-1, keepdims=True)
    inverse = lax.rsqrt(jnp.mean(centred * centred, axis=-1, keepdims=True) + EPSILON)
    unit = centred * inverse
    grad_unit = grad_normed * gain
    inner = (
        grad_unit
        - jnp.mean(grad_unit, axis=-1, keepdims=True)
        - unit * jnp.mean(grad_unit * unit, axis=-1, keepdims=True)
    )
    return inverse * inner, fold(grad_normed * unit), fold(grad_normed)


def backward_kernel(
    dp_sum, tokens, layers, heads, units_rows, head_dim, send_rows, unit, steps,
    cotangent, hidden, active, normed_two, normed, middle, state, qkv, logsum, mixed,
    down, up, qkv_w, out_w, gain, down_b, last_part,
    grads, totals, image_grad, encoded, down_grad, up_grad,
    wide, act_buf, two_buf, qkv_buf, lse_buf, mix_buf, down_buf, up_buf, qkvw_buf, outw_buf, gain_buf,
    flow, flow_low, hid_low, part, total, core_in, acc, y_in, grad_mix, cat, tight, acc_k, acc_v, stage_buf, small,
    downb_buf, woven,
    x_in, inner_in, mid_in, whole_in, half_in, side_in, own_a, total_a, own_b, total_b,
    load_sem, stage_sem, turn_sem, weave_sem, core_send, core_recv, y_send, y_recv, back_send, back_recv, *tick_sems
):
    width = grads.shape[1]
    rows = part.shape[0]
    blocks = rows // BLOCK
    half = send_rows // 2
    pieces = half // PIECE
    tick, greet = grad_sum_ticks(
        dp_sum, unit, steps, layers, grads, totals,
        (x_in, inner_in, mid_in, whole_in, half_in, side_in, own_a, total_a, own_b, total_b), tick_sems,
    )
    dp = lax.axis_index("dp")
    tensor = lax.axis_index("tensor")
    core = tensor % 2
    core_peer = (dp, tensor + 1 - 2 * core)
    y_peer = (dp, lax.rem(tensor + 2, 4))
    greet((core_peer, y_peer))
    layer_rows = steps * 4 * unit // layers
    off_up = units_rows
    local_width = heads * head_dim
    off_qkv = 2 * units_rows
    off_out = off_qkv + 3 * local_width
    off_small = off_out + local_width
    spread = spread_matrix(heads, head_dim)

    def mine(i):
        return pl.ds(pl.multiple_of(core * half + i * PIECE, 8), PIECE)

    def other(i):
        return pl.ds(pl.multiple_of((1 - core) * half + i * PIECE, 8), PIECE)

    def here(i):
        return pl.ds(pl.multiple_of(i * PIECE, 8), PIECE)

    def remote(src, dst, send, recv, peer):
        return pltpu.make_async_remote_copy(
            src_ref=src, dst_ref=dst, send_sem=send, recv_sem=recv, device_id=peer, device_id_type=MESH
        )

    def to_core(p, i):
        return remote(
            part.at[other(i)], core_in.at[here(i)], core_send.at[p, i], core_recv.at[p, i], core_peer
        )

    def to_y(p, i):
        return remote(acc.at[here(i)], y_in.at[p, here(i)], y_send.at[p, i], y_recv.at[p, i], y_peer)

    def to_back(p, i):
        return remote(total.at[mine(i)], total.at[mine(i)], back_send.at[p, i], back_recv.at[p, i], core_peer)

    def from_back(p, i):
        return remote(
            total.at[other(i)], total.at[other(i)], back_send.at[p, i], back_recv.at[p, i], core_peer
        )

    def sum_begin(p):
        def go(i, c):
            to_core(p, i).start()
            return c

        lax.fori_loop(0, pieces, go, 0)

    def sum_step(p, j):
        @pl.when(j < pieces)
        def _():
            to_core(p, j).wait_recv()
            acc[here(j)] = part[mine(j)] + core_in[here(j)]
            to_y(p, j).start()

        late = j - LAG

        @pl.when((late >= 0) & (late < pieces))
        def _():
            to_y(p, late).wait_recv()
            total[mine(late)] = acc[here(late)] + y_in[p, here(late)]
            to_back(p, late).start()

        last = j - LAG - 2

        @pl.when((last >= 0) & (last < pieces))
        def _():
            to_core(p, last).wait_send()
            to_y(p, last).wait_send()
            to_back(p, last).wait_send()
            from_back(p, last).wait_recv()

    sum_steps = pieces + LAG + 2

    def load(source, target, sem):
        return pltpu.make_async_copy(source, target, load_sem.at[sem])

    def stage_copy(slot, row, size):
        return pltpu.make_async_copy(
            stage_buf.at[slot, pl.ds(0, size)], grads.at[pl.ds(pl.multiple_of(row, 8), size)], stage_sem.at[slot]
        )

    layer_ticks = 4 * blocks + 2 * sum_steps + heads * blocks

    def row_block(b):
        return pl.ds(pl.multiple_of(b * BLOCK, 16), BLOCK)

    total[pl.ds(send_rows, rows - send_rows)] = jnp.zeros((rows - send_rows, width), jnp.float32)
    start = load(cotangent, flow_low, 0)
    start.start()
    load(gain, gain_buf, 11).start()
    start.wait()
    load(gain, gain_buf, 11).wait()

    def lift(b, c):
        flow[row_block(b)] = flow_low[row_block(b)].astype(jnp.float32)
        return c

    lax.fori_loop(0, blocks, lift, 0)

    def layer_body(it, carry):
        layer = layers - 1 - it
        base_tick = it * layer_ticks - FIRST
        base_row = layer * layer_rows
        hidden_load = load(hidden.at[layer], wide, 0)
        down_load = load(down.at[layer], down_buf, 1)
        up_load = load(up.at[layer], up_buf, 2)
        active_load = load(active.at[layer], act_buf, 3)
        two_load = load(normed_two.at[layer], two_buf, 4)
        outw_load = load(out_w.at[layer], outw_buf, 5)
        qkv_load = load(qkv.at[layer], qkv_buf, 6)
        lse_load = load(logsum.at[layer], lse_buf, 7)
        mix_load = load(mixed.at[layer], mix_buf, 8)
        qkvw_load = load(qkv_w.at[layer], qkvw_buf, 9)
        for copy in (hidden_load, down_load, up_load, active_load, two_load, outw_load, qkv_load, lse_load, mix_load, qkvw_load):
            copy.start()
        small[...] = jnp.zeros_like(small)
        hidden_load.wait()
        down_load.wait()
        up_load.wait()

        def mlp(b, c):
            at = row_block(b)
            grad = flow[at]
            small[4:5] += fold(grad)
            low = grad.astype(jnp.bfloat16)
            flow_low[at] = low
            grad_hidden = dot_nt(low, down_buf[...]) * gelu_slope(wide[at])
            small[3:4] += fold(grad_hidden)
            hid = grad_hidden.astype(jnp.bfloat16)
            hid_low[at] = hid
            part[at] = dot_nn(hid, up_buf[...])
            tick(base_tick + b)
            return c

        lax.fori_loop(0, blocks, mlp, 0)
        sum_begin(0)
        middle_load = load(middle.at[layer], wide, 0)
        middle_load.start()
        active_load.wait()
        two_load.wait()
        tiles = width // 128
        last_rows = units_rows - (tiles - 1) * 128

        def stage_finish(j, count):
            done = j - 1
            whole = (done != tiles - 1) & (done != 2 * tiles - 1)
            slot = lax.rem(done, 2)

            @pl.when((done >= 0) & (done < count) & whole)
            def _():
                stage_copy(slot, base_row, 128).wait()

            @pl.when((done >= 0) & (done < count) & jnp.logical_not(whole))
            def _():
                stage_copy(slot, base_row, last_rows).wait()

        def mlp_weights(j, c):
            sum_step(0, j)
            stage_finish(j, 2 * tiles)
            slot = lax.rem(j, 2)

            @pl.when(j < tiles)
            def _():
                lanes = pl.ds(pl.multiple_of(j * 128, 128), 128)
                stage_buf[slot, pl.ds(0, 128)] = dot_tn(act_buf[:, lanes], flow_low[...])

            @pl.when((j >= tiles) & (j < 2 * tiles))
            def _():
                lanes = pl.ds(pl.multiple_of((j - tiles) * 128, 128), 128)
                stage_buf[slot, pl.ds(0, 128)] = dot_tn(hid_low[:, lanes], two_buf[...])

            second = j >= tiles
            tile = jnp.where(second, j - tiles, j)
            row = base_row + jnp.where(second, off_up, 0) + tile * 128

            @pl.when((j < 2 * tiles) & (tile < tiles - 1))
            def _():
                stage_copy(slot, row, 128).start()

            @pl.when((j < 2 * tiles) & (tile == tiles - 1))
            def _():
                stage_copy(slot, row, last_rows).start()

            tick(base_tick + blocks + j)
            return c

        lax.fori_loop(0, sum_steps, mlp_weights, 0)
        tick_at = base_tick + blocks + sum_steps
        middle_load.wait()
        outw_load.wait()

        def norm_two(b, c):
            at = row_block(b)
            step_grad, gain_grad, shift_grad = norm_back(total[at], wide[at], gain_buf[layer, 1:2])
            small[6:7] += gain_grad
            small[8:9] += shift_grad
            grad = flow[at] + step_grad
            flow[at] = grad
            small[2:3] += fold(grad)
            low = grad.astype(jnp.bfloat16)
            flow_low[at] = low
            grad = dot_nt(low, outw_buf[...]).astype(jnp.bfloat16)
            grad_mix[at] = dot_nn(grad, spread).astype(jnp.bfloat16)
            tick(tick_at + b)
            return c

        lax.fori_loop(0, blocks, norm_two, 0)
        tick_at = tick_at + blocks
        state_load = load(state.at[layer], wide, 0)
        normed_load = load(normed.at[layer], act_buf, 3)
        state_load.start()
        normed_load.start()
        qkv_load.wait()
        lse_load.wait()
        scale = head_dim ** (-0.5)

        def attend(m, c):
            head = m // blocks
            b = lax.rem(m, blocks)
            at = row_block(b)
            lanes = pl.ds(pl.multiple_of(head * 128, 128), 128)
            query = qkv_buf[0, head, at]
            key = qkv_buf[1, head]
            value = qkv_buf[2, head]
            grad = grad_mix[at, lanes]
            scores = dot_nt(query, key) * scale
            probs = jnp.exp(scores - lse_buf[head, at, 0:1])
            column = lax.broadcasted_iota(jnp.int32, probs.shape, 1)
            probs = jnp.where(column < tokens, probs, 0.0)
            grad_weights = dot_nt(grad, value)
            center = jnp.sum(probs * grad_weights, axis=-1, keepdims=True)
            raw = (probs * (grad_weights - center) * scale).astype(jnp.bfloat16)
            grad_query = dot_nn(raw, key)
            small[0:1, lanes] += fold(grad_query)
            cat[at, lanes] = grad_query.astype(jnp.bfloat16)
            add_k = dot_tn(raw, query)
            add_v = dot_tn(probs.astype(jnp.bfloat16), grad)

            @pl.when(b == 0)
            def _():
                acc_k[...] = add_k
                acc_v[...] = add_v

            @pl.when(b > 0)
            def _():
                acc_k[...] += add_k
                acc_v[...] += add_v

            @pl.when(b == blocks - 1)
            def _():
                at_k = pl.ds(pl.multiple_of((heads + head) * 128, 128), 128)
                at_v = pl.ds(pl.multiple_of((2 * heads + head) * 128, 128), 128)
                cat[:, at_k] = acc_k[...].astype(jnp.bfloat16)
                cat[:, at_v] = acc_v[...].astype(jnp.bfloat16)
                small[1:2, lanes] += fold(acc_v[...])

            tick(tick_at + m)
            return c

        lax.fori_loop(0, heads * blocks, attend, 0)
        tick_at = tick_at + heads * blocks
        qkvw_load.wait()

        def project(b, c):
            at = row_block(b)
            out = None
            for i in range(3):
                lanes = pl.ds(i * heads * 128, heads * 128)
                narrow = dot_nt(cat[at, lanes], spread).astype(jnp.bfloat16)
                tight[i, at] = narrow
                term = dot_nn(narrow, qkvw_buf[i])
                out = term if out is None else out + term
            part[at] = out
            tick(tick_at + b)
            return c

        lax.fori_loop(0, blocks, project, 0)
        tick_at = tick_at + blocks
        sum_begin(1)
        normed_load.wait()
        mix_load.wait()

        def attention_weights(j, c):
            sum_step(1, j)

            @pl.when((j >= 1) & (j < 5))
            def _():
                stage_copy(lax.rem(j - 1, 2), base_row, local_width).wait()

            slot = lax.rem(j, 2)

            @pl.when(j < 3)
            def _():
                stage_buf[slot] = dot_tn(tight[j], act_buf[...])

            @pl.when(j == 3)
            def _():
                stage_buf[slot] = dot_tn(mix_buf[...], flow_low[...])

            @pl.when(j < 4)
            def _():
                stage_copy(slot, base_row + off_qkv + j * local_width, local_width).start()

            tick(tick_at + j)
            return c

        lax.fori_loop(0, sum_steps, attention_weights, 0)
        tick_at = tick_at + sum_steps
        state_load.wait()

        def norm_one(b, c):
            at = row_block(b)
            step_grad, gain_grad, shift_grad = norm_back(total[at], wide[at], gain_buf[layer, 0:1])
            small[5:6] += gain_grad
            small[7:8] += shift_grad
            flow[at] = flow[at] + step_grad
            tick(tick_at + b)
            return c

        lax.fori_loop(0, blocks, norm_one, 0)
        tail = pltpu.make_async_copy(
            small, grads.at[pl.ds(pl.multiple_of(base_row + off_small, 8), small.shape[0])], load_sem.at[10]
        )
        tail.start()
        tail.wait()
        return carry

    lax.fori_loop(0, layers, layer_body, 0)

    part_load = load(last_part, part, 1)
    middle_load = load(middle.at[layers - 1], wide, 2)
    bias_load = load(down_b, downb_buf, 3)
    part_load.start()
    middle_load.start()
    bias_load.start()

    def lower(b, c):
        flow_low[row_block(b)] = flow[row_block(b)].astype(jnp.bfloat16)
        return c

    lax.fori_loop(0, blocks, lower, 0)
    image_store = load(flow_low, image_grad, 0)
    image_store.start()
    part_load.wait()
    sum_begin(0)

    tail = layers * layer_ticks - FIRST
    tiles = width // 128
    last_rows = units_rows - (tiles - 1) * 128
    layer_steps = steps // layers
    weaves, at_step = [], tail
    for k in range(2):
        ready = (layers - 1) * layer_steps + -(-(k + 1) * units_rows // (4 * unit)) + TICK_SPAN
        at_step = max(at_step, ready)
        weaves.append(at_step)
        at_step += tiles + 1

    def each_size(tile, body):
        pl.when(tile < tiles - 1)(lambda: body(128))
        pl.when(tile == tiles - 1)(lambda: body(last_rows))

    def weave_in(k, tile, layer, rows_here):
        row = pl.multiple_of(layer * layer_rows + k * units_rows + tile * 128, 8)
        slot = lax.rem(tile, 2)
        return pltpu.make_async_copy(
            totals.at[pl.ds(row, rows_here)],
            stage_buf.at[slot, pl.ds(layer * 128, rows_here)],
            weave_sem.at[slot, layer],
        )

    def weave_out(target, tile, rows_here):
        slot = lax.rem(tile, 2)
        return pltpu.make_async_copy(
            woven.at[slot, pl.ds(0, rows_here)], target.at[pl.ds(tile * 128, rows_here)], turn_sem.at[slot]
        )

    def weave(k, target, tile):
        def begin(rows_here):
            for layer in range(layers):
                weave_in(k, tile, layer, rows_here).start()

        def arrive(rows_here):
            for layer in range(layers):
                weave_in(k, tile - 1, layer, rows_here).wait()

        each_size(tile, begin)

        @pl.when(tile >= 1)
        def _():
            each_size(tile - 1, arrive)
            slot = lax.rem(tile - 1, 2)

            @pl.when(tile >= 3)
            def _():
                weave_out(target, tile - 3, 128).wait()

            for layer in range(layers):
                woven[slot, :, layer, :] = stage_buf[slot, pl.ds(layer * 128, 128)]
            each_size(tile - 1, lambda rows_here: weave_out(target, tile - 1, rows_here).start())

        @pl.when(tile == tiles)
        def _():
            weave_out(target, tiles - 2, 128).wait()
            weave_out(target, tiles - 1, last_rows).wait()

    def rest(step, c):
        sum_step(0, step - tail)
        tick(step)
        if dp_sum:
            for k, target in enumerate((down_grad, up_grad)):
                tile = step - weaves[k]

                @pl.when((tile >= 0) & (tile <= tiles))
                def _():
                    weave(k, target, tile)

        return c

    lax.fori_loop(tail, tail + sum_steps, rest, 0)
    middle_load.wait()
    bias_load.wait()

    def encode(b, c):
        at = row_block(b)
        hid_low[at] = (wide[at] + total[at] + downb_buf[layers - 1 : layers]).astype(jnp.bfloat16)
        return c

    lax.fori_loop(0, blocks, encode, 0)
    encoded_store = load(hid_low, encoded, 1)
    encoded_store.start()
    lax.fori_loop(tail + sum_steps, max(steps + TICK_SPAN, tail + sum_steps), rest, 0)
    image_store.wait()
    encoded_store.wait()


def backward(
    tokens, head_dim, hidden_units, unit, collective_id, dp_sum,
    cotangent, hidden, active, normed_two, normed, middle, state, qkv, logsum, mixed,
    down, up, qkv_w, out_w, gain, down_b, last_part,
):
    layers, rows, width = middle.shape
    heads = qkv.shape[2]
    units_rows = -(-hidden_units // 8) * 8
    send_rows = -(-tokens // (2 * PIECE)) * 2 * PIECE
    pieces = send_rows // (2 * PIECE)
    layer_rows = 2 * units_rows + 4 * heads * head_dim + TAIL_ROWS
    steps = layers * layer_rows // (4 * unit)
    buffers, sems = tick_scratch(unit, width)
    f32, low = jnp.float32, jnp.bfloat16
    half = (send_rows // 2, width)
    full = (rows, width)
    any_spec = pl.BlockSpec(memory_space=pl.ANY)
    grads = jax.ShapeDtypeStruct((layers * layer_rows, width), f32)
    return pl.pallas_call(
        functools.partial(
            backward_kernel, dp_sum, tokens, layers, heads, units_rows, head_dim, send_rows, unit, steps
        ),
        out_shape=(
            grads,
            grads,
            jax.ShapeDtypeStruct(full, low),
            jax.ShapeDtypeStruct(full, low),
            jax.ShapeDtypeStruct((units_rows, layers, width), f32),
            jax.ShapeDtypeStruct((units_rows, layers, width), f32),
        ),
        in_specs=[any_spec] * 17,
        out_specs=(any_spec,) * 6,
        scratch_shapes=[
            pltpu.VMEM(full, f32),
            pltpu.VMEM(full, low),
            pltpu.VMEM(full, low),
            pltpu.VMEM(qkv.shape[1:], low),
            pltpu.VMEM(logsum.shape[1:], f32),
            pltpu.VMEM(mixed.shape[1:], low),
            pltpu.VMEM(down.shape[1:], low),
            pltpu.VMEM(up.shape[1:], low),
            pltpu.VMEM(qkv_w.shape[1:], low),
            pltpu.VMEM(out_w.shape[1:], low),
            pltpu.VMEM(gain.shape, f32),
            pltpu.VMEM(full, f32),
            pltpu.VMEM(full, low),
            pltpu.VMEM(full, low),
            pltpu.VMEM(full, f32),
            pltpu.VMEM(full, f32),
            pltpu.VMEM(half, f32),
            pltpu.VMEM(half, f32),
            pltpu.VMEM((2,) + half, f32),
            pltpu.VMEM((rows, heads * 128), low),
            pltpu.VMEM((rows, 3 * heads * 128), low),
            pltpu.VMEM((3, rows, heads * head_dim), low),
            pltpu.VMEM((rows, 128), f32),
            pltpu.VMEM((rows, 128), f32),
            pltpu.VMEM((2, heads * head_dim, width), f32),
            pltpu.VMEM((TAIL_ROWS, width), f32),
            pltpu.VMEM(down_b.shape, f32),
            pltpu.VMEM((2, 128, layers, width), f32),
        ]
        + buffers
        + [pltpu.SemaphoreType.DMA((12,)), pltpu.SemaphoreType.DMA((2,)), pltpu.SemaphoreType.DMA((2,)), pltpu.SemaphoreType.DMA((2, layers))]
        + [pltpu.SemaphoreType.DMA((2, pieces))] * 6
        + sems,
        compiler_params=pltpu.CompilerParams(
            collective_id=collective_id, has_side_effects=True, vmem_limit_bytes=62 << 20
        ),
    )(
        cotangent, hidden, active, normed_two, normed, middle, state, qkv, logsum, mixed,
        down, up, qkv_w, out_w, gain, down_b, last_part,
    )


def spread_matrix(heads, head_dim):
    shape = (heads * head_dim, heads * 128)
    source = lax.broadcasted_iota(jnp.int32, shape, 0)
    lane = lax.broadcasted_iota(jnp.int32, shape, 1)
    hit = (lane // 128 * head_dim + lane % 128 == source) & (lane % 128 < head_dim)
    return jnp.where(hit, 1.0, 0.0).astype(jnp.bfloat16)


def norm_unit(state):
    centred = state - jnp.mean(state, axis=-1, keepdims=True)
    return centred * lax.rsqrt(jnp.mean(centred * centred, axis=-1, keepdims=True) + EPSILON)


def gelu(v):
    return 0.5 * v * (1.0 + jnp.tanh(0.7978845608028654 * (v + 0.044715 * (v * v * v))))


def block_sum(pieces, dp, tensor, part, core_in, y_in, total, sems):
    core = tensor % 2
    core_peer = (dp, tensor + 1 - 2 * core)
    y_peer = (dp, lax.rem(tensor + 2, 4))
    core_sem, y_sem, back_sem = sems
    per_block = BLOCK // (2 * PIECE)

    def mine(i):
        return pl.ds(pl.multiple_of((2 * i + core) * PIECE, 8), PIECE)

    def other(i):
        return pl.ds(pl.multiple_of((2 * i + 1 - core) * PIECE, 8), PIECE)

    def here(i):
        return pl.ds(pl.multiple_of(i * PIECE, 8), PIECE)

    def remote(src, dst, sem, i, peer):
        return pltpu.make_async_remote_copy(
            src_ref=src, dst_ref=dst, send_sem=sem.at[0, i], recv_sem=sem.at[1, i],
            device_id=peer, device_id_type=MESH,
        )

    def to_core(i):
        return remote(part.at[other(i)], core_in.at[here(i)], core_sem, i, core_peer)

    def to_y(i):
        return remote(core_in.at[here(i)], y_in.at[here(i)], y_sem, i, y_peer)

    def to_back(i):
        return remote(total.at[mine(i)], total.at[mine(i)], back_sem, i, core_peer)

    def from_back(i):
        return remote(total.at[other(i)], total.at[other(i)], back_sem, i, core_peer)

    def each(b, body):
        def go(k, c):
            i = b * per_block + k

            @pl.when(i < pieces)
            def _():
                body(i)

            return c

        lax.fori_loop(0, per_block, go, 0)

    def send(b):
        each(b, lambda i: to_core(i).start())

    def meet(b):
        def body(i):
            to_core(i).wait_recv()
            core_in[here(i)] = core_in[here(i)] + part[mine(i)]
            to_y(i).start()

        each(b, body)

    def close(b):
        def body(i):
            to_y(i).wait_recv()
            total[mine(i)] = core_in[here(i)] + y_in[here(i)]
            to_back(i).start()

        each(b, body)

    def finish(b):
        def body(i):
            to_core(i).wait_send()
            to_y(i).wait_send()
            to_back(i).wait_send()
            from_back(i).wait_recv()

        each(b, body)

    return send, meet, close, finish


def forward_kernel(
    tokens, layers, heads, head_dim, send_rows,
    images, qkv_w, qv_b, out_w, out_b, up, up_b, down, down_b, gain, shift,
    hidden, active, normed_two, normed, middle, state, qkv, logsum, mixed, last_part,
    image_buf, flow, normed_buf, qkv_buf, lse_buf, mix_buf, tight_buf, two_buf, hidden_buf, active_buf,
    qkvw_buf, outw_buf, up_buf, down_buf, qvb_buf, outb_buf, upb_buf, downb_buf, gain_buf, shift_buf,
    part_a, core_in_a, y_in_a, total_a, part_b, core_in_b, y_in_b, total_b,
    load_sem, weight_sem, store_sem, middle_sem, *sum_sems
):
    rows, width = flow.shape
    blocks = rows // BLOCK
    pieces = send_rows // (2 * PIECE)
    dp = lax.axis_index("dp")
    tensor = lax.axis_index("tensor")
    core = tensor % 2
    barrier = pltpu.get_barrier_semaphore()
    for peer in ((dp, tensor + 1 - 2 * core), (dp, lax.rem(tensor + 2, 4))):
        pl.semaphore_signal(barrier, inc=1, device_id=peer, device_id_type=MESH)

    def weights(layer):
        return (
            pltpu.make_async_copy(qkv_w.at[layer], qkvw_buf, weight_sem.at[0]),
            pltpu.make_async_copy(out_w.at[layer], outw_buf, weight_sem.at[1]),
            pltpu.make_async_copy(up.at[layer], up_buf, weight_sem.at[2]),
            pltpu.make_async_copy(down.at[layer], down_buf, weight_sem.at[3]),
        )

    singles = [
        pltpu.make_async_copy(source, target, load_sem.at[i])
        for i, (source, target) in enumerate(
            (
                (images, image_buf), (gain, gain_buf), (shift, shift_buf), (qv_b, qvb_buf),
                (out_b, outb_buf), (up_b, upb_buf), (down_b, downb_buf),
            )
        )
    ]
    for copy in singles:
        copy.start()
    current = weights(0)
    for copy in current:
        copy.start()
    spread = spread_matrix(heads, head_dim)
    total_a[pl.ds(send_rows, rows - send_rows)] = jnp.zeros((rows - send_rows, width), jnp.float32)
    total_b[pl.ds(send_rows, rows - send_rows)] = jnp.zeros((rows - send_rows, width), jnp.float32)
    for copy in singles:
        copy.wait()
    pl.semaphore_wait(barrier, 2)

    def row_block(b):
        return pl.ds(pl.multiple_of(b * BLOCK, 16), BLOCK)

    scale = head_dim ** (-0.5)
    stores = {}

    def keep(name, source, target, index):
        copy = pltpu.make_async_copy(source, target, store_sem.at[index])
        copy.start()
        stores[name] = copy

    def settle(*names):
        for name in names:
            if name in stores:
                stores.pop(name).wait()

    def project(layer, b, value):
        at = row_block(b)
        flow[at] = value
        low = (norm_unit(value) * gain_buf[layer, 0:1] + shift_buf[layer, 0:1]).astype(jnp.bfloat16)
        normed_buf[at] = low
        for i in range(3):
            out = dot_nt(low, qkvw_buf[i])
            if i != 1:
                out = out + qvb_buf[layer, i // 2 : i // 2 + 1]
            wide = dot_nn(out.astype(jnp.bfloat16), spread).astype(jnp.bfloat16)
            for head in range(heads):
                qkv_buf[i, head, at] = wide[:, head * 128 : (head + 1) * 128]

    def first(b, c):
        project(0, b, image_buf[row_block(b)].astype(jnp.float32))
        return c

    current[0].wait()
    lax.fori_loop(0, blocks, first, 0)

    for layer in range(layers):
        keep("state", flow, state.at[layer], 0)
        keep("normed", normed_buf, normed.at[layer], 1)
        keep("qkv", qkv_buf, qkv.at[layer], 2)
        settle("logsum", "mixed")
        send_a, meet_a, close_a, finish_a = block_sum(
            pieces, dp, tensor, part_a, core_in_a, y_in_a, total_a, [s.at[layer] for s in sum_sems[:3]]
        )
        send_b, meet_b, close_b, finish_b = block_sum(
            pieces, dp, tensor, part_b, core_in_b, y_in_b, total_b, [s.at[layer] for s in sum_sems[3:]]
        )
        is_last = layer == layers - 1
        if not is_last:
            following = weights(layer + 1)
            following[0].start()

        def attend(m, c):
            head = m // blocks
            at = row_block(lax.rem(m, blocks))
            scores = dot_nt(qkv_buf[0, head, at], qkv_buf[1, head]) * scale
            column = lax.broadcasted_iota(jnp.int32, scores.shape, 1)
            scores = jnp.where(column < tokens, scores, -jnp.inf)
            peak = jnp.max(scores, axis=-1, keepdims=True)
            expo = jnp.exp(scores - peak)
            denominator = jnp.sum(expo, axis=-1, keepdims=True)
            probs = (expo / denominator).astype(jnp.bfloat16)
            lanes = pl.ds(pl.multiple_of(head * 128, 128), 128)
            mix_buf[at, lanes] = dot_nn(probs, qkv_buf[2, head]).astype(jnp.bfloat16)
            lse_buf[head, at] = jnp.broadcast_to(peak + jnp.log(denominator), (BLOCK, 128))
            return c

        lax.fori_loop(0, heads * blocks, attend, 0)
        keep("logsum", lse_buf, logsum.at[layer], 3)
        current[1].wait()

        def output(b, c):
            at = row_block(b)
            tight = dot_nt(mix_buf[at], spread).astype(jnp.bfloat16)
            tight_buf[at] = tight
            part_a[at] = dot_nn(tight, outw_buf[...])
            send_a(b)
            return c

        lax.fori_loop(0, blocks, output, 0)
        keep("mixed", tight_buf, mixed.at[layer], 4)
        if not is_last:
            following[1].start()

        def meet_all(b, c):
            meet_a(b)
            return c

        lax.fori_loop(0, blocks, meet_all, 0)
        settle("state", "normed_two", "hidden", "active")
        current[2].wait()
        current[3].wait()

        def mlp(b, c):
            at = row_block(b)
            close_a(b)
            if not is_last:

                @pl.when(b > 0)
                def _():
                    meet_b(b - 1)

            finish_a(b)
            value = flow[at] + total_a[at] + outb_buf[layer : layer + 1]
            flow[at] = value
            pltpu.make_async_copy(flow.at[at], middle.at[layer, at], middle_sem.at[b]).start()
            low = (norm_unit(value) * gain_buf[layer, 1:2] + shift_buf[layer, 1:2]).astype(jnp.bfloat16)
            two_buf[at] = low
            hid = dot_nt(low, up_buf[...]) + upb_buf[layer : layer + 1]
            hidden_buf[at] = hid
            act = gelu(hid).astype(jnp.bfloat16)
            active_buf[at] = act
            part_b[at] = dot_nn(act, down_buf[...])
            if not is_last:
                send_b(b)
            return c

        lax.fori_loop(0, blocks, mlp, 0)
        keep("normed_two", two_buf, normed_two.at[layer], 5)
        keep("hidden", hidden_buf, hidden.at[layer], 6)
        keep("active", active_buf, active.at[layer], 7)

        def middle_wait(b):
            pltpu.make_async_copy(flow.at[row_block(b)], middle.at[layer, row_block(b)], middle_sem.at[b]).wait()

        if is_last:
            keep("part", part_b, last_part, 8)
            for b in range(blocks):
                middle_wait(b)
        else:
            following[2].start()
            following[3].start()
            following[0].wait()
            meet_b(blocks - 1)
            settle("normed", "qkv")

            def next_project(b, c):
                at = row_block(b)
                close_b(b)
                finish_b(b)
                middle_wait(b)
                project(layer + 1, b, flow[at] + total_b[at] + downb_buf[layer : layer + 1])
                return c

            lax.fori_loop(0, blocks, next_project, 0)
            current = following
    settle(*list(stores))


def forward(
    tokens, head_dim, collective_id,
    images, qkv_w, qv_b, out_w, out_b, up, up_b, down, down_b, gain, shift,
):
    layers = qkv_w.shape[0]
    rows, width = images.shape
    heads = qkv_w.shape[2] // head_dim
    units = up.shape[1]
    send_rows = -(-tokens // (2 * PIECE)) * 2 * PIECE
    pieces = send_rows // (2 * PIECE)
    f32, low = jnp.float32, jnp.bfloat16
    full = (rows, width)
    half = (send_rows // 2, width)
    any_spec = pl.BlockSpec(memory_space=pl.ANY)

    def out(shape, dtype):
        return jax.ShapeDtypeStruct(shape, dtype)

    lanes = heads * 128
    return pl.pallas_call(
        functools.partial(forward_kernel, tokens, layers, heads, head_dim, send_rows),
        out_shape=(
            out((layers, rows, units), f32),
            out((layers, rows, units), low),
            out((layers,) + full, low),
            out((layers,) + full, low),
            out((layers,) + full, f32),
            out((layers,) + full, f32),
            out((layers, 3, heads, rows, 128), low),
            out((layers, heads, rows, 128), f32),
            out((layers, rows, heads * head_dim), low),
            out(full, f32),
        ),
        in_specs=[any_spec] * 11,
        out_specs=(any_spec,) * 10,
        scratch_shapes=[
            pltpu.VMEM(full, low),
            pltpu.VMEM(full, f32),
            pltpu.VMEM(full, low),
            pltpu.VMEM((3, heads, rows, 128), low),
            pltpu.VMEM((heads, rows, 128), f32),
            pltpu.VMEM((rows, lanes), low),
            pltpu.VMEM((rows, heads * head_dim), low),
            pltpu.VMEM(full, low),
            pltpu.VMEM((rows, units), f32),
            pltpu.VMEM((rows, units), low),
            pltpu.VMEM(qkv_w.shape[1:], low),
            pltpu.VMEM(out_w.shape[1:], low),
            pltpu.VMEM(up.shape[1:], low),
            pltpu.VMEM(down.shape[1:], low),
            pltpu.VMEM(qv_b.shape, f32),
            pltpu.VMEM(out_b.shape, f32),
            pltpu.VMEM(up_b.shape, f32),
            pltpu.VMEM(down_b.shape, f32),
            pltpu.VMEM(gain.shape, f32),
            pltpu.VMEM(shift.shape, f32),
        ]
        + [pltpu.VMEM(s, f32) for s in (full, half, half, full)] * 2
        + [
            pltpu.SemaphoreType.DMA((7,)),
            pltpu.SemaphoreType.DMA((4,)),
            pltpu.SemaphoreType.DMA((9,)),
            pltpu.SemaphoreType.DMA((rows // BLOCK,)),
        ]
        + [pltpu.SemaphoreType.DMA((layers, 2, pieces))] * 6,
        compiler_params=pltpu.CompilerParams(
            collective_id=collective_id, has_side_effects=True, vmem_limit_bytes=62 << 20
        ),
    )(images, qkv_w, qv_b, out_w, out_b, up, up_b, down, down_b, gain, shift)


def pad_to(array, axis, size):
    spec = [(0, 0)] * array.ndim
    spec[axis] = (0, size - array.shape[axis])
    return jnp.pad(array, spec)


def local(
    dp_size,
    images,
    qkv_weight,
    qv_bias,
    out_weight,
    out_bias,
    up_weight,
    up_bias,
    down_weight,
    down_bias,
    norm_gain,
    norm_shift,
    cotangent,
):
    tokens, width = images.shape[1:]
    layers = qkv_weight.shape[0]
    local_width = qkv_weight.shape[3]
    heads = local_width // HEAD
    hidden_units = up_weight.shape[2]
    padded_units = -(-hidden_units // 128) * 128
    rows = -(-tokens // BLOCK) * BLOCK
    up = pad_to(jnp.swapaxes(up_weight, 1, 2), 1, padded_units)
    qkv_rows = jnp.swapaxes(qkv_weight, 2, 3)
    up_b = pad_to(up_bias, 1, padded_units)
    down = pad_to(down_weight, 1, padded_units)
    *kept, last_part = forward(
        tokens, HEAD, 0,
        pad_to(images[0], 0, rows), qkv_rows, qv_bias, out_weight, out_bias, up, up_b, down, down_bias,
        norm_gain, norm_shift,
    )
    flat, summed, image_grad, encoded, down_rows, up_rows = backward(
        tokens, HEAD, hidden_units, UNIT, 1, dp_size == 8,
        pad_to(cotangent[0], 0, rows), *kept, down, up, qkv_rows, out_weight, norm_gain, down_bias, last_part,
    )
    if dp_size != 8:
        summed = lax.psum(flat, "dp")
    per_layer = summed.reshape(layers, summed.shape[0] // layers, width)
    stop = -(-hidden_units // 8) * 8
    if dp_size == 8:
        down_grad = jnp.swapaxes(down_rows[:hidden_units], 0, 1)
        up_grad = jnp.transpose(up_rows[:hidden_units], (1, 2, 0))
    else:
        down_grad = per_layer[:, :hidden_units]
        up_grad = jnp.swapaxes(per_layer[:, stop : stop + hidden_units], 1, 2)
    qkv_grad = per_layer[:, 2 * stop : 2 * stop + 3 * local_width]
    qkv_grad = jnp.swapaxes(qkv_grad.reshape(layers, 3, local_width, width), 2, 3)
    out_grad = per_layer[:, 2 * stop + 3 * local_width : 2 * stop + 4 * local_width]
    small = per_layer[:, 2 * stop + 4 * local_width :]
    qv_grad = small[:, 0:2, : heads * 128].reshape(layers, 2, heads, 128)[..., :HEAD]
    return (
        encoded[:tokens][None],
        image_grad[:tokens][None],
        qkv_grad,
        qv_grad.reshape(layers, 2, local_width),
        out_grad,
        small[:, 2],
        up_grad,
        small[:, 3, :hidden_units],
        down_grad,
        small[:, 4],
        small[:, 5:7],
        small[:, 7:9],
    )


def solution(mesh):
    in_specs = (
        P("dp", None, None),
        P(None, None, None, "tensor"),
        P(None, None, "tensor"),
        P(None, "tensor", None),
        P(),
        P(None, None, "tensor"),
        P(None, "tensor"),
        P(None, "tensor", None),
        P(),
        P(),
        P(),
        P("dp", None, None),
    )
    out_specs = (
        P("dp", None, None),
        P("dp", None, None),
        P(None, None, None, "tensor"),
        P(None, None, "tensor"),
        P(None, "tensor", None),
        P(),
        P(None, None, "tensor"),
        P(None, "tensor"),
        P(None, "tensor", None),
        P(),
        P(),
        P(),
    )
    return jax.shard_map(
        functools.partial(local, mesh.shape["dp"]), mesh=mesh, in_specs=in_specs, out_specs=out_specs, check_vma=False)
```

```python
import functools

import jax
import jax.numpy as jnp
from jax import lax
from jax.experimental import pallas as pl
from jax.experimental.pallas import tpu as pltpu
from jax.sharding import PartitionSpec as P

MESH = pl.DeviceIdType.MESH
SLOTS = 16


def grad_sum_ticks(dp_sum, unit, steps, layers, grads, totals, buffers, sems):
    (x_in, inner_in, mid_in, whole_in, half_in, side_in, own_a, total_a, own_b, total_b) = buffers
    (
        x_sem, inner_sem, mid_sem, out_pair_sem, out_x_sem, whole_sem, half_sem, side_sem,
        back_mid_sem, back_pair_sem, relay_sem, load_a_sem, load_b_sem, store_a_sem, store_b_sem,
    ) = sems
    dp = lax.axis_index("dp")
    tensor = lax.axis_index("tensor")
    z = dp // 2
    x = dp % 2
    is_mid = (z == 1) | (z == 2)
    is_end = jnp.logical_not(is_mid)
    x_peer = (dp + 1 - 2 * x, tensor)
    pair_peer = (dp + 2 - 4 * (z % 2), tensor)
    mid_z = jnp.where(is_mid, 3 - z, z)
    mid_peer = (mid_z * 2 + x, tensor)
    side = jnp.where(z == 2, 1, 0)

    def greet(others):
        barrier = pltpu.get_barrier_semaphore()
        for peer in others:
            pl.semaphore_signal(barrier, inc=1, device_id=peer, device_id_type=MESH)
        if not dp_sum:
            pl.semaphore_wait(barrier, len(others))
            return
        for peer in (x_peer, pair_peer):
            pl.semaphore_signal(barrier, inc=1, device_id=peer, device_id_type=MESH)

        @pl.when(is_mid)
        def _():
            pl.semaphore_signal(barrier, inc=1, device_id=mid_peer, device_id_type=MESH)
            pl.semaphore_wait(barrier, 3 + len(others))

        @pl.when(is_end)
        def _():
            pl.semaphore_wait(barrier, 2 + len(others))

    layer_steps = steps // layers

    def place(chunk):
        turn = chunk // layer_steps
        return ((layers - 1 - turn) * layer_steps + chunk - turn * layer_steps) * (4 * unit)

    def row(chunk, part):
        return pl.ds(pl.multiple_of(place(chunk) + part * unit, 8), unit)

    def rows_b(chunk):
        return pl.ds(pl.multiple_of(place(chunk) + 2 * unit, 8), 2 * unit)

    def remote(src, dst, sem, slot, peer):
        return pltpu.make_async_remote_copy(
            src_ref=src, dst_ref=dst, send_sem=sem.at[0, slot], recv_sem=sem.at[1, slot],
            device_id=peer, device_id_type=MESH,
        )

    def a_x(c, s):
        return remote(grads.at[row(c, 1 - x)], x_in.at[s], x_sem, s, x_peer)

    def a_load(c, s):
        return pltpu.make_async_copy(grads.at[row(c, x)], own_a.at[s], load_a_sem.at[s])

    def a_inner(c, s):
        return remote(own_a.at[s], inner_in.at[s], inner_sem, s, pair_peer)

    def a_mid(c, s):
        return remote(own_a.at[s], mid_in.at[s], mid_sem, s, mid_peer)

    def a_out_pair(c, s):
        return remote(total_a.at[s], totals.at[row(c, x)], out_pair_sem, s, pair_peer)

    def a_out_x(c, s):
        return remote(total_a.at[s], totals.at[row(c, x)], out_x_sem, s, x_peer)

    def a_store(c, s):
        return pltpu.make_async_copy(total_a.at[s], totals.at[row(c, x)], store_a_sem.at[s])

    def a_relay(c, s):
        return remote(totals.at[row(c, x)], totals.at[row(c, x)], out_x_sem, s, x_peer)

    def a_back(c, s):
        return remote(totals.at[row(c, x)], totals.at[row(c, 1 - x)], out_x_sem, s, x_peer)

    def b_whole(c, s):
        return remote(grads.at[rows_b(c)], whole_in.at[s], whole_sem, s, pair_peer)

    def b_load(c, s):
        return pltpu.make_async_copy(grads.at[rows_b(c)], own_b.at[s], load_b_sem.at[s])

    def b_half(c, s):
        return remote(own_b.at[s, pl.ds((1 - side) * unit, unit)], half_in.at[s], half_sem, s, mid_peer)

    def b_side(c, s):
        return remote(own_b.at[s, pl.ds(side * unit, unit)], side_in.at[s], side_sem, s, x_peer)

    def b_store(c, s):
        return pltpu.make_async_copy(total_b.at[s], totals.at[row(c, 2 + side)], store_b_sem.at[s])

    def b_back_mid(c, s):
        return remote(total_b.at[s], totals.at[row(c, 2 + side)], back_mid_sem, s, mid_peer)

    def b_back_pair(c, s):
        return remote(total_b.at[s], totals.at[row(c, 2 + side)], back_pair_sem, s, pair_peer)

    def b_relay(c, s):
        return remote(
            totals.at[row(c, 3 - side)], totals.at[row(c, 3 - side)], relay_sem, s, pair_peer
        )

    def stage(step, offset, guard, body):
        chunk = step - offset
        ok = (chunk >= 0) & (chunk < steps)
        if guard is not None:
            ok = ok & guard

        @pl.when(ok)
        def _():
            body(chunk, lax.rem(chunk, SLOTS))

    def start_all(c, s):
        a_x(c, s).start()
        a_load(c, s).start()

    def start_end(c, s):
        b_whole(c, s).start()

    def start_mid(c, s):
        b_load(c, s).start()

    def a1_end(c, s):
        a_load(c, s).wait()
        a_x(c, s).wait_recv()
        own_a[s] = own_a[s] + x_in[s]
        a_inner(c, s).start()

    def a1_mid(c, s):
        a_load(c, s).wait()
        a_x(c, s).wait_recv()
        own_a[s] = own_a[s] + x_in[s]

    def a2_mid(c, s):
        a_inner(c, s).wait_recv()
        own_a[s] = own_a[s] + inner_in[s]
        a_mid(c, s).start()

    def a3_mid(c, s):
        a_mid(c, s).wait_recv()
        total_a[s] = own_a[s] + mid_in[s]
        a_out_pair(c, s).start()
        a_out_x(c, s).start()
        a_store(c, s).start()

    def a3_end(c, s):
        a_out_pair(c, s).wait_recv()
        a_relay(c, s).start()

    def b1_mid(c, s):
        b_load(c, s).wait()
        b_whole(c, s).wait_recv()
        own_b[s] = own_b[s] + whole_in[s]
        b_half(c, s).start()

    def b2_mid(c, s):
        b_half(c, s).wait_recv()
        mine = pl.ds(pl.multiple_of(side * unit, 8), unit)
        own_b[s, mine] = own_b[s, mine] + half_in[s]
        b_side(c, s).start()

    def b3_mid(c, s):
        b_side(c, s).wait_recv()
        mine = pl.ds(pl.multiple_of(side * unit, 8), unit)
        total_b[s] = own_b[s, mine] + side_in[s]
        b_back_mid(c, s).start()
        b_back_pair(c, s).start()
        b_store(c, s).start()

    def b4_mid(c, s):
        b_back_mid(c, s).wait_recv()
        b_relay(c, s).start()

    def b5_end(c, s):
        b_back_pair(c, s).wait_recv()
        b_relay(c, s).wait_recv()

    def back_all(c, s):
        a_back(c, s).wait_recv()

    def done_end(c, s):
        a_inner(c, s).wait_send()
        b_whole(c, s).wait_send()

    def done_mid(c, s):
        a_mid(c, s).wait_send()
        a_out_pair(c, s).wait_send()
        a_store(c, s).wait()
        b_half(c, s).wait_send()
        b_side(c, s).wait_send()
        b_back_mid(c, s).wait_send()
        b_back_pair(c, s).wait_send()
        b_store(c, s).wait()
        b_relay(c, s).wait_send()

    def done_all(c, s):
        a_x(c, s).wait_send()
        a_out_x(c, s).wait_send()

    def tick(step):
        if not dp_sum:
            return
        stage(step, 0, None, start_all)
        stage(step, 0, is_end, start_end)
        stage(step, 0, is_mid, start_mid)
        stage(step, 8, is_mid, b4_mid)
        stage(step, 6, is_mid, a3_mid)
        stage(step, 6, is_mid, b3_mid)
        stage(step, 8, is_end, a3_end)
        stage(step, 4, is_mid, a2_mid)
        stage(step, 4, is_mid, b2_mid)
        stage(step, 2, is_mid, a1_mid)
        stage(step, 2, is_end, a1_end)
        stage(step, 2, is_mid, b1_mid)
        stage(step, 10, None, back_all)
        stage(step, 10, is_end, b5_end)
        stage(step, 11, is_end, done_end)
        stage(step, 11, is_mid, done_mid)
        stage(step, 11, None, done_all)

    return tick, greet


def tick_scratch(unit, width):
    one = (SLOTS, unit, width)
    two = (SLOTS, 2 * unit, width)
    buffers = [pltpu.VMEM(s, jnp.float32) for s in (one, one, one, two, one, one, one, one, two, one)]
    sems = [pltpu.SemaphoreType.DMA((2, SLOTS))] * 11 + [pltpu.SemaphoreType.DMA((SLOTS,))] * 4
    return buffers, sems


HEAD = 72
EPSILON = 1e-06
UNIT = 8
TAIL_ROWS = 16


FIRST = 2
PIECE = 16
LAG = 4
TICK_SPAN = 12
BLOCK = 192


def dot_nn(left, right):
    return lax.dot_general(left, right, (((1,), (0,)), ((), ())), preferred_element_type=jnp.float32)


def dot_nt(left, right):
    return lax.dot_general(left, right, (((1,), (1,)), ((), ())), preferred_element_type=jnp.float32)


def dot_tn(left, right):
    return lax.dot_general(left, right, (((0,), (0,)), ((), ())), preferred_element_type=jnp.float32)


def fold(array):
    return jnp.sum(array, axis=0, keepdims=True)


def gelu_slope(v):
    root = 0.7978845608028654
    inner = jnp.tanh(root * (v + 0.044715 * (v * v * v)))
    return 0.5 * (1.0 + inner) + 0.5 * v * (1.0 - inner * inner) * (root * (1.0 + 0.134145 * (v * v)))


def norm_back(grad_normed, state, gain):
    centred = state - jnp.mean(state, axis=-1, keepdims=True)
    inverse = lax.rsqrt(jnp.mean(centred * centred, axis=-1, keepdims=True) + EPSILON)
    unit = centred * inverse
    grad_unit = grad_normed * gain
    inner = (
        grad_unit
        - jnp.mean(grad_unit, axis=-1, keepdims=True)
        - unit * jnp.mean(grad_unit * unit, axis=-1, keepdims=True)
    )
    return inverse * inner, fold(grad_normed * unit), fold(grad_normed)


def backward_kernel(
    dp_sum, tokens, layers, heads, units_rows, head_dim, send_rows, unit, steps,
    cotangent, hidden, active, normed_two, normed, middle, state, qkv, logsum, mixed,
    down, up, qkv_w, out_w, gain, last_part,
    grads, totals, image_grad, encoded, down_grad, up_grad,
    raw_buf, wide, act_buf, two_buf, qkv_buf, lse_buf, mix_buf, down_buf, up_buf, qkvw_buf, outw_buf, gain_buf,
    flow, flow_low, hid_low, part, total, core_in, acc, y_in, grad_mix, cat, tight, acc_k, acc_v, stage_buf, small,
    woven,
    x_in, inner_in, mid_in, whole_in, half_in, side_in, own_a, total_a, own_b, total_b,
    load_sem, stage_sem, turn_sem, weave_sem, core_send, core_recv, y_send, y_recv, back_send, back_recv, *tick_sems
):
    width = grads.shape[1]
    rows = part.shape[0]
    blocks = rows // BLOCK
    half = send_rows // 2
    pieces = half // PIECE
    tick, greet = grad_sum_ticks(
        dp_sum, unit, steps, layers, grads, totals,
        (x_in, inner_in, mid_in, whole_in, half_in, side_in, own_a, total_a, own_b, total_b), tick_sems,
    )
    dp = lax.axis_index("dp")
    tensor = lax.axis_index("tensor")
    core = tensor % 2
    core_peer = (dp, tensor + 1 - 2 * core)
    y_peer = (dp, lax.rem(tensor + 2, 4))
    greet((core_peer, y_peer))
    layer_rows = steps * 4 * unit // layers
    off_up = units_rows
    local_width = heads * head_dim
    off_qkv = 2 * units_rows
    off_out = off_qkv + 3 * local_width
    off_small = off_out + local_width
    spread = spread_matrix(heads, head_dim)

    def mine(i):
        return pl.ds(pl.multiple_of(core * half + i * PIECE, 8), PIECE)

    def other(i):
        return pl.ds(pl.multiple_of((1 - core) * half + i * PIECE, 8), PIECE)

    def here(i):
        return pl.ds(pl.multiple_of(i * PIECE, 8), PIECE)

    def remote(src, dst, send, recv, peer):
        return pltpu.make_async_remote_copy(
            src_ref=src, dst_ref=dst, send_sem=send, recv_sem=recv, device_id=peer, device_id_type=MESH
        )

    def to_core(p, i):
        return remote(
            part.at[other(i)], core_in.at[here(i)], core_send.at[p, i], core_recv.at[p, i], core_peer
        )

    def to_y(p, i):
        return remote(acc.at[here(i)], y_in.at[p, here(i)], y_send.at[p, i], y_recv.at[p, i], y_peer)

    def to_back(p, i):
        return remote(total.at[mine(i)], total.at[mine(i)], back_send.at[p, i], back_recv.at[p, i], core_peer)

    def from_back(p, i):
        return remote(
            total.at[other(i)], total.at[other(i)], back_send.at[p, i], back_recv.at[p, i], core_peer
        )

    def sum_begin(p):
        def go(i, c):
            to_core(p, i).start()
            return c

        lax.fori_loop(0, pieces, go, 0)

    def sum_step(p, j):
        @pl.when(j < pieces)
        def _():
            to_core(p, j).wait_recv()
            acc[here(j)] = part[mine(j)] + core_in[here(j)]
            to_y(p, j).start()

        late = j - LAG

        @pl.when((late >= 0) & (late < pieces))
        def _():
            to_y(p, late).wait_recv()
            total[mine(late)] = acc[here(late)] + y_in[p, here(late)]
            to_back(p, late).start()

        last = j - LAG - 2

        @pl.when((last >= 0) & (last < pieces))
        def _():
            to_core(p, last).wait_send()
            to_y(p, last).wait_send()
            to_back(p, last).wait_send()
            from_back(p, last).wait_recv()

    sum_steps = pieces + LAG + 2

    def load(source, target, sem):
        return pltpu.make_async_copy(source, target, load_sem.at[sem])

    def stage_copy(slot, row, size):
        return pltpu.make_async_copy(
            stage_buf.at[slot, pl.ds(0, size)], grads.at[pl.ds(pl.multiple_of(row, 8), size)], stage_sem.at[slot]
        )

    tiles = width // 128
    last_rows = units_rows - (tiles - 1) * 128
    layer_ticks = tiles + 1 + 4 * blocks + 2 * sum_steps + heads * blocks

    def row_block(b):
        return pl.ds(pl.multiple_of(b * BLOCK, 16), BLOCK)

    total[pl.ds(send_rows, rows - send_rows)] = jnp.zeros((rows - send_rows, width), jnp.float32)
    start = load(cotangent, raw_buf, 11)
    start.start()
    gain_load = load(gain, gain_buf, 10)
    gain_load.start()

    def layer_body(it, carry):
        layer = layers - 1 - it
        base_tick = it * layer_ticks - FIRST
        base_row = layer * layer_rows
        hidden_load = load(hidden.at[layer], wide, 0)
        down_load = load(down.at[layer], down_buf, 1)
        up_load = load(up.at[layer], up_buf, 2)
        active_load = load(active.at[layer], act_buf, 3)
        two_load = load(normed_two.at[layer], two_buf, 4)
        outw_load = load(out_w.at[layer], outw_buf, 5)
        qkv_load = load(qkv.at[layer], qkv_buf, 6)
        lse_load = load(logsum.at[layer], lse_buf, 7)
        mix_load = load(mixed.at[layer], mix_buf, 8)
        qkvw_load = load(qkv_w.at[layer], qkvw_buf, 9)
        for copy in (active_load, hidden_load, down_load, up_load, two_load, outw_load, qkv_load, lse_load, mix_load, qkvw_load):
            copy.start()
        small[...] = jnp.zeros_like(small)

        @pl.when(it == 0)
        def _():
            start.wait()
            gain_load.wait()

            lift_rows(raw_buf, flow, tokens)

        def lower(b, c):
            at = row_block(b)
            grad = flow[at]
            small[4:5] += fold(grad)
            flow_low[at] = grad.astype(jnp.bfloat16)
            return c

        lax.fori_loop(0, blocks, lower, 0)
        active_load.wait()

        def tile_copy(tile, row):
            slot = lax.rem(tile, 2)
            pl.when(tile < tiles - 1)(lambda: stage_copy(slot, row, 128).start())
            pl.when(tile == tiles - 1)(lambda: stage_copy(slot, row, last_rows).start())

        def tile_done(tile):
            slot = lax.rem(tile, 2)
            pl.when((tile >= 0) & (tile < tiles - 1))(lambda: stage_copy(slot, base_row, 128).wait())
            pl.when(tile == tiles - 1)(lambda: stage_copy(slot, base_row, last_rows).wait())

        def down_weights(j, c):
            tile_done(j - 1)

            @pl.when(j < tiles)
            def _():
                lanes = pl.ds(pl.multiple_of(j * 128, 128), 128)
                stage_buf[lax.rem(j, 2), pl.ds(0, 128)] = dot_tn(act_buf[:, lanes], flow_low[...])
                tile_copy(j, base_row + j * 128)

            tick(base_tick + j)
            return c

        lax.fori_loop(0, tiles + 1, down_weights, 0)
        tick_at = base_tick + tiles + 1
        hidden_load.wait()
        down_load.wait()
        up_load.wait()

        def mlp(b, c):
            at = row_block(b)
            grad_hidden = dot_nt(flow_low[at], down_buf[...]) * gelu_slope(wide[at])
            small[3:4] += fold(grad_hidden)
            hid = grad_hidden.astype(jnp.bfloat16)
            hid_low[at] = hid
            part[at] = dot_nn(hid, up_buf[...])
            tick(tick_at + b)
            return c

        lax.fori_loop(0, blocks, mlp, 0)
        sum_begin(0)
        middle_load = load(middle.at[layer], wide, 0)
        middle_load.start()
        two_load.wait()
        tick_at = tick_at + blocks

        def up_weights(j, c):
            sum_step(0, j)
            tile_done(j - 1)

            @pl.when(j < tiles)
            def _():
                lanes = pl.ds(pl.multiple_of(j * 128, 128), 128)
                stage_buf[lax.rem(j, 2), pl.ds(0, 128)] = dot_tn(hid_low[:, lanes], two_buf[...])
                tile_copy(j, base_row + off_up + j * 128)

            tick(tick_at + j)
            return c

        lax.fori_loop(0, sum_steps, up_weights, 0)
        tick_at = tick_at + sum_steps
        part_load = load(last_part, part, 1)
        pl.when(it == 0)(part_load.start)
        middle_load.wait()
        outw_load.wait()

        def norm_two(b, c):
            at = row_block(b)
            step_grad, gain_grad, shift_grad = norm_back(total[at], wide[at], gain_buf[layer, 1:2])
            small[6:7] += gain_grad
            small[8:9] += shift_grad
            grad = flow[at] + step_grad
            flow[at] = grad
            small[2:3] += fold(grad)
            low = grad.astype(jnp.bfloat16)
            flow_low[at] = low
            grad = dot_nt(low, outw_buf[...]).astype(jnp.bfloat16)
            grad_mix[at] = dot_nn(grad, spread).astype(jnp.bfloat16)
            tick(tick_at + b)
            return c

        lax.fori_loop(0, blocks, norm_two, 0)
        tick_at = tick_at + blocks
        state_load = load(state.at[layer], wide, 0)
        normed_load = load(normed.at[layer], act_buf, 3)
        state_load.start()
        normed_load.start()
        qkv_load.wait()
        lse_load.wait()
        scale = head_dim ** (-0.5)

        @pl.when(it == 0)
        def _():
            part_load.wait()
            sum_begin(2)


        def attend(m, c):
            head = m // blocks
            b = lax.rem(m, blocks)
            at = row_block(b)
            lanes = pl.ds(pl.multiple_of(head * 128, 128), 128)
            query = qkv_buf[0, head, at]
            key = qkv_buf[1, head]
            value = qkv_buf[2, head]
            grad = grad_mix[at, lanes]
            scores = dot_nt(query, key) * scale
            probs = jnp.exp(scores - lse_buf[head, at, 0:1])
            column = lax.broadcasted_iota(jnp.int32, probs.shape, 1)
            probs = jnp.where(column < tokens, probs, 0.0)
            grad_weights = dot_nt(grad, value)
            center = jnp.sum(probs * grad_weights, axis=-1, keepdims=True)
            raw = (probs * (grad_weights - center) * scale).astype(jnp.bfloat16)
            grad_query = dot_nn(raw, key)
            small[0:1, lanes] += fold(grad_query)
            cat[at, lanes] = grad_query.astype(jnp.bfloat16)
            add_k = dot_tn(raw, query)
            add_v = dot_tn(probs.astype(jnp.bfloat16), grad)

            @pl.when(b == 0)
            def _():
                acc_k[...] = add_k
                acc_v[...] = add_v

            @pl.when(b > 0)
            def _():
                acc_k[...] += add_k
                acc_v[...] += add_v

            @pl.when(b == blocks - 1)
            def _():
                at_k = pl.ds(pl.multiple_of((heads + head) * 128, 128), 128)
                at_v = pl.ds(pl.multiple_of((2 * heads + head) * 128, 128), 128)
                cat[:, at_k] = acc_k[...].astype(jnp.bfloat16)
                cat[:, at_v] = acc_v[...].astype(jnp.bfloat16)
                small[1:2, lanes] += fold(acc_v[...])

            @pl.when(it == 0)
            def _():
                sum_step(2, 2 * m)
                sum_step(2, 2 * m + 1)

            tick(tick_at + m)
            return c

        lax.fori_loop(0, heads * blocks, attend, 0)
        tick_at = tick_at + heads * blocks
        qkvw_load.wait()

        def project(b, c):
            at = row_block(b)
            out = None
            for i in range(3):
                lanes = pl.ds(i * heads * 128, heads * 128)
                narrow = dot_nt(cat[at, lanes], spread).astype(jnp.bfloat16)
                tight[i, at] = narrow
                term = dot_nn(narrow, qkvw_buf[i])
                out = term if out is None else out + term
            part[at] = out

            @pl.when(it == 0)
            def _():
                hid_low[at] = total[at].astype(jnp.bfloat16)

            tick(tick_at + b)
            return c

        lax.fori_loop(0, blocks, project, 0)
        tick_at = tick_at + blocks
        sum_begin(1)
        encoded_store = load(hid_low, encoded, 1)
        pl.when(it == 0)(encoded_store.start)
        normed_load.wait()
        mix_load.wait()

        def attention_weights(j, c):
            sum_step(1, j)

            @pl.when((j >= 1) & (j < 5))
            def _():
                stage_copy(lax.rem(j - 1, 2), base_row, local_width).wait()

            slot = lax.rem(j, 2)

            @pl.when(j < 3)
            def _():
                stage_buf[slot] = dot_tn(tight[j], act_buf[...])

            @pl.when(j == 3)
            def _():
                stage_buf[slot] = dot_tn(mix_buf[...], flow_low[...])

            @pl.when(j < 4)
            def _():
                stage_copy(slot, base_row + off_qkv + j * local_width, local_width).start()

            tick(tick_at + j)
            return c

        lax.fori_loop(0, sum_steps, attention_weights, 0)
        tick_at = tick_at + sum_steps
        state_load.wait()

        def norm_one(b, c):
            at = row_block(b)
            step_grad, gain_grad, shift_grad = norm_back(total[at], wide[at], gain_buf[layer, 0:1])
            small[5:6] += gain_grad
            small[7:8] += shift_grad
            flow[at] = flow[at] + step_grad
            tick(tick_at + b)
            return c

        lax.fori_loop(0, blocks, norm_one, 0)
        tail = pltpu.make_async_copy(
            small, grads.at[pl.ds(pl.multiple_of(base_row + off_small, 8), small.shape[0])], load_sem.at[10]
        )
        tail.start()
        tail.wait()
        pl.when(it == 0)(encoded_store.wait)
        return carry

    lax.fori_loop(0, layers, layer_body, 0)

    def lower(b, c):
        flow_low[row_block(b)] = flow[row_block(b)].astype(jnp.bfloat16)
        return c

    lax.fori_loop(0, blocks, lower, 0)
    image_store = load(flow_low, image_grad, 0)
    image_store.start()

    tail = layers * layer_ticks - FIRST
    layer_steps = steps // layers
    weaves, at_step = [], tail
    for k in range(2):
        ready = (layers - 1) * layer_steps + -(-(k + 1) * units_rows // (4 * unit)) + TICK_SPAN
        at_step = max(at_step, ready)
        weaves.append(at_step)
        at_step += tiles + 1

    def each_size(tile, body):
        pl.when(tile < tiles - 1)(lambda: body(128))
        pl.when(tile == tiles - 1)(lambda: body(last_rows))

    def weave_in(k, tile, layer, rows_here):
        row = pl.multiple_of(layer * layer_rows + k * units_rows + tile * 128, 8)
        slot = lax.rem(tile, 2)
        return pltpu.make_async_copy(
            totals.at[pl.ds(row, rows_here)],
            stage_buf.at[slot, pl.ds(layer * 128, rows_here)],
            weave_sem.at[slot, layer],
        )

    def weave_out(target, tile, rows_here):
        slot = lax.rem(tile, 2)
        return pltpu.make_async_copy(
            woven.at[slot, pl.ds(0, rows_here)], target.at[pl.ds(tile * 128, rows_here)], turn_sem.at[slot]
        )

    def weave(k, target, tile):
        def begin(rows_here):
            for layer in range(layers):
                weave_in(k, tile, layer, rows_here).start()

        def arrive(rows_here):
            for layer in range(layers):
                weave_in(k, tile - 1, layer, rows_here).wait()

        each_size(tile, begin)

        @pl.when(tile >= 1)
        def _():
            each_size(tile - 1, arrive)
            slot = lax.rem(tile - 1, 2)

            @pl.when(tile >= 3)
            def _():
                weave_out(target, tile - 3, 128).wait()

            for layer in range(layers):
                woven[slot, :, layer, :] = stage_buf[slot, pl.ds(layer * 128, 128)]
            each_size(tile - 1, lambda rows_here: weave_out(target, tile - 1, rows_here).start())

        @pl.when(tile == tiles)
        def _():
            weave_out(target, tiles - 2, 128).wait()
            weave_out(target, tiles - 1, last_rows).wait()

    def rest(step, c):
        tick(step)
        if dp_sum:
            for k, target in enumerate((down_grad, up_grad)):
                tile = step - weaves[k]

                @pl.when((tile >= 0) & (tile <= tiles))
                def _():
                    weave(k, target, tile)

        return c

    lax.fori_loop(tail, max(steps + TICK_SPAN, at_step), rest, 0)
    image_store.wait()


def backward(
    tokens, head_dim, hidden_units, unit, collective_id, dp_sum,
    cotangent, hidden, active, normed_two, normed, middle, state, qkv, logsum, mixed,
    down, up, qkv_w, out_w, gain, last_part,
):
    layers, rows, width = middle.shape
    heads = qkv.shape[2]
    units_rows = -(-hidden_units // 8) * 8
    send_rows = -(-tokens // (2 * PIECE)) * 2 * PIECE
    pieces = send_rows // (2 * PIECE)
    layer_rows = 2 * units_rows + 4 * heads * head_dim + TAIL_ROWS
    steps = layers * layer_rows // (4 * unit)
    buffers, sems = tick_scratch(unit, width)
    f32, low = jnp.float32, jnp.bfloat16
    half = (send_rows // 2, width)
    full = (rows, width)
    any_spec = pl.BlockSpec(memory_space=pl.ANY)
    grads = jax.ShapeDtypeStruct((layers * layer_rows, width), f32)
    return pl.pallas_call(
        functools.partial(
            backward_kernel, dp_sum, tokens, layers, heads, units_rows, head_dim, send_rows, unit, steps
        ),
        out_shape=(
            grads,
            grads,
            jax.ShapeDtypeStruct(full, low),
            jax.ShapeDtypeStruct(full, low),
            jax.ShapeDtypeStruct((units_rows, layers, width), f32),
            jax.ShapeDtypeStruct((units_rows, layers, width), f32),
        ),
        in_specs=[any_spec] * 16,
        out_specs=(any_spec,) * 6,
        scratch_shapes=[
            pltpu.VMEM(cotangent.shape, low),
            pltpu.VMEM(full, f32),
            pltpu.VMEM(full, low),
            pltpu.VMEM(full, low),
            pltpu.VMEM(qkv.shape[1:], low),
            pltpu.VMEM(logsum.shape[1:], f32),
            pltpu.VMEM(mixed.shape[1:], low),
            pltpu.VMEM(down.shape[1:], low),
            pltpu.VMEM(up.shape[1:], low),
            pltpu.VMEM(qkv_w.shape[1:], low),
            pltpu.VMEM(out_w.shape[1:], low),
            pltpu.VMEM(gain.shape, f32),
            pltpu.VMEM(full, f32),
            pltpu.VMEM(full, low),
            pltpu.VMEM(full, low),
            pltpu.VMEM(full, f32),
            pltpu.VMEM(full, f32),
            pltpu.VMEM(half, f32),
            pltpu.VMEM(half, f32),
            pltpu.VMEM((3,) + half, f32),
            pltpu.VMEM((rows, heads * 128), low),
            pltpu.VMEM((rows, 3 * heads * 128), low),
            pltpu.VMEM((3, rows, heads * head_dim), low),
            pltpu.VMEM((rows, 128), f32),
            pltpu.VMEM((rows, 128), f32),
            pltpu.VMEM((2, heads * head_dim, width), f32),
            pltpu.VMEM((TAIL_ROWS, width), f32),
            pltpu.VMEM((2, 128, layers, width), f32),
        ]
        + buffers
        + [pltpu.SemaphoreType.DMA((12,)), pltpu.SemaphoreType.DMA((2,)), pltpu.SemaphoreType.DMA((2,)), pltpu.SemaphoreType.DMA((2, layers))]
        + [pltpu.SemaphoreType.DMA((3, pieces))] * 6
        + sems,
        compiler_params=pltpu.CompilerParams(
            collective_id=collective_id, has_side_effects=True, vmem_limit_bytes=62 << 20
        ),
    )(
        cotangent, hidden, active, normed_two, normed, middle, state, qkv, logsum, mixed,
        down, up, qkv_w, out_w, gain, last_part,
    )


def lift_rows(source, target, tokens):
    blocks = target.shape[0] // BLOCK

    def one(b, c):
        at = pl.ds(pl.multiple_of(b * BLOCK, 16), BLOCK)
        target[at] = source[at].astype(jnp.float32)
        return c

    lax.fori_loop(0, blocks - 1, one, 0)
    begin = (blocks - 1) * BLOCK
    target[pl.ds(begin, BLOCK)] = jnp.zeros((BLOCK, target.shape[1]), jnp.float32)
    last = pl.ds(begin, tokens - begin)
    target[last] = source[last].astype(jnp.float32)


def spread_matrix(heads, head_dim):
    shape = (heads * head_dim, heads * 128)
    source = lax.broadcasted_iota(jnp.int32, shape, 0)
    lane = lax.broadcasted_iota(jnp.int32, shape, 1)
    hit = (lane // 128 * head_dim + lane % 128 == source) & (lane % 128 < head_dim)
    return jnp.where(hit, 1.0, 0.0).astype(jnp.bfloat16)


def norm_unit(state):
    centred = state - jnp.mean(state, axis=-1, keepdims=True)
    return centred * lax.rsqrt(jnp.mean(centred * centred, axis=-1, keepdims=True) + EPSILON)


def gelu(v):
    return 0.5 * v * (1.0 + jnp.tanh(0.7978845608028654 * (v + 0.044715 * (v * v * v))))


def block_sum(pieces, dp, tensor, part, core_in, y_in, total, sems):
    core = tensor % 2
    core_peer = (dp, tensor + 1 - 2 * core)
    y_peer = (dp, lax.rem(tensor + 2, 4))
    core_sem, y_sem, back_sem = sems
    per_block = BLOCK // (2 * PIECE)

    def mine(i):
        return pl.ds(pl.multiple_of((2 * i + core) * PIECE, 8), PIECE)

    def other(i):
        return pl.ds(pl.multiple_of((2 * i + 1 - core) * PIECE, 8), PIECE)

    def here(i):
        return pl.ds(pl.multiple_of(i * PIECE, 8), PIECE)

    def remote(src, dst, sem, i, peer):
        return pltpu.make_async_remote_copy(
            src_ref=src, dst_ref=dst, send_sem=sem.at[0, i], recv_sem=sem.at[1, i],
            device_id=peer, device_id_type=MESH,
        )

    def to_core(i):
        return remote(part.at[other(i)], core_in.at[here(i)], core_sem, i, core_peer)

    def to_y(i):
        return remote(core_in.at[here(i)], y_in.at[here(i)], y_sem, i, y_peer)

    def to_back(i):
        return remote(total.at[mine(i)], total.at[mine(i)], back_sem, i, core_peer)

    def from_back(i):
        return remote(total.at[other(i)], total.at[other(i)], back_sem, i, core_peer)

    def each(b, body):
        def go(k, c):
            i = b * per_block + k

            @pl.when(i < pieces)
            def _():
                body(i)

            return c

        lax.fori_loop(0, per_block, go, 0)

    def send(b):
        each(b, lambda i: to_core(i).start())

    def meet(b):
        def body(i):
            to_core(i).wait_recv()
            core_in[here(i)] = core_in[here(i)] + part[mine(i)]
            to_y(i).start()

        each(b, body)

    def close(b):
        def body(i):
            to_y(i).wait_recv()
            total[mine(i)] = core_in[here(i)] + y_in[here(i)]
            to_back(i).start()

        each(b, body)

    def finish(b):
        def body(i):
            to_core(i).wait_send()
            to_y(i).wait_send()
            to_back(i).wait_send()
            from_back(i).wait_recv()

        each(b, body)

    return send, meet, close, finish


def forward_kernel(
    tokens, layers, heads, head_dim, send_rows,
    images, qkv_w, qv_b, out_w, out_b, up, up_b, down, down_b, gain, shift,
    hidden, active, normed_two, normed, middle, state, qkv, logsum, mixed, last_part,
    image_buf, upb_raw, flow, normed_buf, qkv_buf, lse_buf, mix_buf, tight_buf, two_buf, hidden_buf, active_buf,
    qkvw_buf, outw_buf, up_buf, down_buf, qvb_buf, outb_buf, upb_buf, downb_buf, gain_buf, shift_buf,
    part_a, core_in_a, y_in_a, total_a, part_b, core_in_b, y_in_b, total_b,
    load_sem, weight_sem, store_sem, middle_sem, *sum_sems
):
    rows, width = flow.shape
    blocks = rows // BLOCK
    pieces = send_rows // (2 * PIECE)
    dp = lax.axis_index("dp")
    tensor = lax.axis_index("tensor")
    core = tensor % 2
    barrier = pltpu.get_barrier_semaphore()
    for peer in ((dp, tensor + 1 - 2 * core), (dp, lax.rem(tensor + 2, 4))):
        pl.semaphore_signal(barrier, inc=1, device_id=peer, device_id_type=MESH)

    def weights(layer):
        return (
            pltpu.make_async_copy(qkv_w.at[layer], qkvw_buf, weight_sem.at[0]),
            pltpu.make_async_copy(out_w.at[layer], outw_buf, weight_sem.at[1]),
            pltpu.make_async_copy(up.at[layer], up_buf, weight_sem.at[2]),
            pltpu.make_async_copy(down.at[layer], down_buf, weight_sem.at[3]),
        )

    singles = [
        pltpu.make_async_copy(source, target, load_sem.at[i])
        for i, (source, target) in enumerate(
            (
                (images, image_buf), (gain, gain_buf), (shift, shift_buf), (qv_b, qvb_buf),
                (out_b, outb_buf), (up_b, upb_raw), (down_b, downb_buf),
            )
        )
    ]
    for copy in singles:
        copy.start()
    current = weights(0)
    for copy in current:
        copy.start()
    spread = spread_matrix(heads, head_dim)
    total_a[pl.ds(send_rows, rows - send_rows)] = jnp.zeros((rows - send_rows, width), jnp.float32)
    total_b[pl.ds(send_rows, rows - send_rows)] = jnp.zeros((rows - send_rows, width), jnp.float32)
    for copy in singles:
        copy.wait()
    pl.semaphore_wait(barrier, 2)

    def row_block(b):
        return pl.ds(pl.multiple_of(b * BLOCK, 16), BLOCK)

    scale = head_dim ** (-0.5)
    stores = {}

    def keep(name, source, target, index):
        copy = pltpu.make_async_copy(source, target, store_sem.at[index])
        copy.start()
        stores[name] = copy

    def settle(*names):
        for name in names:
            if name in stores:
                stores.pop(name).wait()

    def project(layer, b, value):
        at = row_block(b)
        flow[at] = value
        low = (norm_unit(value) * gain_buf[layer, 0:1] + shift_buf[layer, 0:1]).astype(jnp.bfloat16)
        normed_buf[at] = low
        for i in range(3):
            out = dot_nt(low, qkvw_buf[i])
            if i != 1:
                out = out + qvb_buf[layer, i // 2 : i // 2 + 1]
            wide = dot_nn(out.astype(jnp.bfloat16), spread).astype(jnp.bfloat16)
            for head in range(heads):
                qkv_buf[i, head, at] = wide[:, head * 128 : (head + 1) * 128]

    def first(b, c):
        project(0, b, flow[row_block(b)])
        return c

    lift_rows(image_buf, flow, tokens)
    upb_buf[...] = jnp.zeros_like(upb_buf)
    upb_buf[:, pl.ds(0, upb_raw.shape[1])] = upb_raw[...]
    current[0].wait()
    lax.fori_loop(0, blocks, first, 0)

    for layer in range(layers):
        keep("state", flow, state.at[layer], 0)
        keep("normed", normed_buf, normed.at[layer], 1)
        keep("qkv", qkv_buf, qkv.at[layer], 2)
        settle("logsum", "mixed")
        send_a, meet_a, close_a, finish_a = block_sum(
            pieces, dp, tensor, part_a, core_in_a, y_in_a, total_a, [s.at[layer] for s in sum_sems[:3]]
        )
        send_b, meet_b, close_b, finish_b = block_sum(
            pieces, dp, tensor, part_b, core_in_b, y_in_b, total_b, [s.at[layer] for s in sum_sems[3:]]
        )
        is_last = layer == layers - 1
        if not is_last:
            following = weights(layer + 1)
            following[0].start()

        current[1].wait()

        def attend(b, c):
            at = row_block(b)

            def one_head(head, c):
                scores = dot_nt(qkv_buf[0, head, at], qkv_buf[1, head]) * scale
                column = lax.broadcasted_iota(jnp.int32, scores.shape, 1)
                scores = jnp.where(column < tokens, scores, -jnp.inf)
                peak = jnp.max(scores, axis=-1, keepdims=True)
                expo = jnp.exp(scores - peak)
                denominator = jnp.sum(expo, axis=-1, keepdims=True)
                probs = (expo / denominator).astype(jnp.bfloat16)
                lanes = pl.ds(pl.multiple_of(head * 128, 128), 128)
                mix_buf[:, lanes] = dot_nn(probs, qkv_buf[2, head]).astype(jnp.bfloat16)
                lse_buf[head, at] = jnp.broadcast_to(peak + jnp.log(denominator), (BLOCK, 128))
                return c

            lax.fori_loop(0, heads, one_head, 0)
            tight = dot_nt(mix_buf[...], spread).astype(jnp.bfloat16)
            tight_buf[at] = tight
            part_a[at] = dot_nn(tight, outw_buf[...])
            send_a(b)

            @pl.when(b > 0)
            def _():
                meet_a(b - 1)

            return c

        lax.fori_loop(0, blocks, attend, 0)
        meet_a(blocks - 1)
        keep("logsum", lse_buf, logsum.at[layer], 3)
        keep("mixed", tight_buf, mixed.at[layer], 4)
        if not is_last:
            following[1].start()

        settle("state", "normed_two", "hidden", "active")
        current[2].wait()
        current[3].wait()

        def mlp(b, c):
            at = row_block(b)
            close_a(b)
            if not is_last:

                @pl.when(b > 0)
                def _():
                    meet_b(b - 1)

            finish_a(b)
            value = flow[at] + total_a[at] + outb_buf[layer : layer + 1]
            flow[at] = value
            pltpu.make_async_copy(flow.at[at], middle.at[layer, at], middle_sem.at[b]).start()
            low = (norm_unit(value) * gain_buf[layer, 1:2] + shift_buf[layer, 1:2]).astype(jnp.bfloat16)
            two_buf[at] = low
            hid = dot_nt(low, up_buf[...]) + upb_buf[layer : layer + 1]
            hidden_buf[at] = hid
            act = gelu(hid).astype(jnp.bfloat16)
            active_buf[at] = act
            partial = dot_nn(act, down_buf[...])
            if is_last:
                lead = jnp.where(tensor == 0, 1.0, 0.0)
                partial = partial + lead * (value + downb_buf[layer : layer + 1])
            part_b[at] = partial
            if not is_last:
                send_b(b)
            return c

        lax.fori_loop(0, blocks, mlp, 0)
        keep("normed_two", two_buf, normed_two.at[layer], 5)
        keep("hidden", hidden_buf, hidden.at[layer], 6)
        keep("active", active_buf, active.at[layer], 7)

        def middle_wait(b):
            pltpu.make_async_copy(flow.at[row_block(b)], middle.at[layer, row_block(b)], middle_sem.at[b]).wait()

        if is_last:
            keep("part", part_b, last_part, 8)
            for b in range(blocks):
                middle_wait(b)
        else:
            following[2].start()
            following[3].start()
            following[0].wait()
            meet_b(blocks - 1)
            settle("normed", "qkv")

            def next_project(b, c):
                at = row_block(b)
                close_b(b)
                finish_b(b)
                middle_wait(b)
                project(layer + 1, b, flow[at] + total_b[at] + downb_buf[layer : layer + 1])
                return c

            lax.fori_loop(0, blocks, next_project, 0)
            current = following
    settle(*list(stores))


def forward(
    tokens, head_dim, collective_id,
    images, qkv_w, qv_b, out_w, out_b, up, up_b, down, down_b, gain, shift,
):
    layers = qkv_w.shape[0]
    width = images.shape[1]
    rows = -(-tokens // BLOCK) * BLOCK
    heads = qkv_w.shape[2] // head_dim
    units = up.shape[1]
    send_rows = -(-tokens // (2 * PIECE)) * 2 * PIECE
    pieces = send_rows // (2 * PIECE)
    f32, low = jnp.float32, jnp.bfloat16
    full = (rows, width)
    half = (send_rows // 2, width)
    any_spec = pl.BlockSpec(memory_space=pl.ANY)

    def out(shape, dtype):
        return jax.ShapeDtypeStruct(shape, dtype)

    lanes = heads * 128
    return pl.pallas_call(
        functools.partial(forward_kernel, tokens, layers, heads, head_dim, send_rows),
        out_shape=(
            out((layers, rows, units), f32),
            out((layers, rows, units), low),
            out((layers,) + full, low),
            out((layers,) + full, low),
            out((layers,) + full, f32),
            out((layers,) + full, f32),
            out((layers, 3, heads, rows, 128), low),
            out((layers, heads, rows, 128), f32),
            out((layers, rows, heads * head_dim), low),
            out(full, f32),
        ),
        in_specs=[any_spec] * 11,
        out_specs=(any_spec,) * 10,
        scratch_shapes=[
            pltpu.VMEM(images.shape, low),
            pltpu.VMEM(up_b.shape, f32),
            pltpu.VMEM(full, f32),
            pltpu.VMEM(full, low),
            pltpu.VMEM((3, heads, rows, 128), low),
            pltpu.VMEM((heads, rows, 128), f32),
            pltpu.VMEM((BLOCK, lanes), low),
            pltpu.VMEM((rows, heads * head_dim), low),
            pltpu.VMEM(full, low),
            pltpu.VMEM((rows, units), f32),
            pltpu.VMEM((rows, units), low),
            pltpu.VMEM(qkv_w.shape[1:], low),
            pltpu.VMEM(out_w.shape[1:], low),
            pltpu.VMEM(up.shape[1:], low),
            pltpu.VMEM(down.shape[1:], low),
            pltpu.VMEM(qv_b.shape, f32),
            pltpu.VMEM(out_b.shape, f32),
            pltpu.VMEM((layers, units), f32),
            pltpu.VMEM(down_b.shape, f32),
            pltpu.VMEM(gain.shape, f32),
            pltpu.VMEM(shift.shape, f32),
        ]
        + [pltpu.VMEM(s, f32) for s in (full, half, half, full)] * 2
        + [
            pltpu.SemaphoreType.DMA((7,)),
            pltpu.SemaphoreType.DMA((4,)),
            pltpu.SemaphoreType.DMA((9,)),
            pltpu.SemaphoreType.DMA((rows // BLOCK,)),
        ]
        + [pltpu.SemaphoreType.DMA((layers, 2, pieces))] * 6,
        compiler_params=pltpu.CompilerParams(
            collective_id=collective_id, has_side_effects=True, vmem_limit_bytes=62 << 20
        ),
    )(images, qkv_w, qv_b, out_w, out_b, up, up_b, down, down_b, gain, shift)


def finish_kernel(
    layers, heads, head_dim, hidden_units, layer_rows, off_qkv,
    totals, down_rows, up_rows, image_rows, encoded_rows,
    encoded, image_grad, qkv_grad, qv_grad, out_grad, out_b, up_grad, up_b, down_grad, down_b, gain, shift,
    down_buf, up_wide, rows_buf, long_a, long_b, short_a, short_b, small, qv_buf, up_buf, plain, pair, sem,
):
    width = totals.shape[1]
    local_width = heads * head_dim
    count = [0]

    def move(source, target):
        copy = pltpu.make_async_copy(source, target, sem.at[count[0]])
        count[0] += 1
        copy.start()
        return copy

    small_rows = small.shape[1]
    off_small = off_qkv + 4 * local_width
    fetch = [move(totals.at[pl.ds(l * layer_rows + off_small, small_rows)], small.at[l]) for l in range(layers)]
    fetch_a = move(encoded_rows, long_a)
    fetch_b = move(image_rows, long_b)
    through = []
    for source, buffer, target in ((down_rows, down_buf, down_grad), (up_rows, up_wide, up_grad)):
        for at in range(0, hidden_units, 128):
            here = pl.ds(at, min(128, hidden_units - at))
            through.append((move(source.at[here], buffer.at[here]), buffer.at[here], target.at[here]))
    for l in range(layers):
        begin = l * layer_rows + off_qkv
        for i in range(4):
            rows = pl.ds(begin + i * local_width, local_width)
            target = qkv_grad.at[l, i] if i < 3 else out_grad.at[l]
            through.append((move(totals.at[rows], rows_buf.at[l, i]), rows_buf.at[l, i], target))
    moves = []
    for arrived, buffer, target in through:
        arrived.wait()
        moves.append(move(buffer, target))
    for copy in fetch:
        copy.wait()
    for l in range(layers):
        for i in range(2):
            for h in range(heads):
                qv_buf[l, i : i + 1, h * head_dim : (h + 1) * head_dim] = small[
                    l, i : i + 1, h * 128 : h * 128 + head_dim
                ]
        plain[0, l : l + 1] = small[l, 2:3]
        up_buf[l : l + 1] = small[l, 3:4, :hidden_units]
        plain[1, l : l + 1] = small[l, 4:5]
        pair[0, l] = small[l, 5:7]
        pair[1, l] = small[l, 7:9]
    moves += [
        move(qv_buf, qv_grad), move(plain.at[0], out_b), move(up_buf, up_b), move(plain.at[1], down_b),
        move(pair.at[0], gain), move(pair.at[1], shift),
    ]
    tokens = short_a.shape[0]
    fetch_a.wait()
    short_a[...] = long_a[:tokens]
    moves.append(move(short_a, encoded))
    fetch_b.wait()
    short_b[...] = long_b[:tokens]
    moves.append(move(short_b, image_grad))
    for copy in moves:
        copy.wait()


def finish(tokens, heads, head_dim, hidden_units, totals, down_rows, up_rows, image_rows, encoded_rows):
    layers = down_rows.shape[1]
    width = totals.shape[1]
    rows = image_rows.shape[0]
    layer_rows = totals.shape[0] // layers
    off_qkv = 2 * down_rows.shape[0]
    local_width = heads * head_dim
    f32, low = jnp.float32, jnp.bfloat16
    any_spec = pl.BlockSpec(memory_space=pl.ANY)

    def out(shape, dtype=f32):
        return jax.ShapeDtypeStruct(shape, dtype)

    copies = 4 * -(-hidden_units // 128) + 9 * layers + 10
    return pl.pallas_call(
        functools.partial(finish_kernel, layers, heads, head_dim, hidden_units, layer_rows, off_qkv),
        out_shape=(
            out((tokens, width), low),
            out((tokens, width), low),
            out((layers, 3, local_width, width)),
            out((layers, 2, local_width)),
            out((layers, local_width, width)),
            out((layers, width)),
            out((hidden_units, layers, width)),
            out((layers, hidden_units)),
            out((hidden_units, layers, width)),
            out((layers, width)),
            out((layers, 2, width)),
            out((layers, 2, width)),
        ),
        in_specs=[any_spec] * 5,
        out_specs=(any_spec,) * 12,
        scratch_shapes=[
            pltpu.VMEM((hidden_units, layers, width), f32),
            pltpu.VMEM((hidden_units, layers, width), f32),
            pltpu.VMEM((layers, 4, local_width, width), f32),
            pltpu.VMEM((rows, width), low),
            pltpu.VMEM((rows, width), low),
            pltpu.VMEM((tokens, width), low),
            pltpu.VMEM((tokens, width), low),
            pltpu.VMEM((layers, TAIL_ROWS, width), f32),
            pltpu.VMEM((layers, 2, local_width), f32),
            pltpu.VMEM((layers, hidden_units), f32),
            pltpu.VMEM((2, layers, width), f32),
            pltpu.VMEM((2, layers, 2, width), f32),
            pltpu.SemaphoreType.DMA((copies,)),
        ],
        compiler_params=pltpu.CompilerParams(has_side_effects=True, vmem_limit_bytes=56 << 20),
    )(totals, down_rows, up_rows, image_rows, encoded_rows)


def pad_to(array, axis, size):
    spec = [(0, 0)] * array.ndim
    spec[axis] = (0, size - array.shape[axis])
    return jnp.pad(array, spec)


def local(
    dp_size,
    images,
    qkv_weight,
    qv_bias,
    out_weight,
    out_bias,
    up_weight,
    up_bias,
    down_weight,
    down_bias,
    norm_gain,
    norm_shift,
    cotangent,
):
    tokens, width = images.shape[1:]
    layers = qkv_weight.shape[0]
    local_width = qkv_weight.shape[3]
    heads = local_width // HEAD
    hidden_units = up_weight.shape[2]
    padded_units = -(-hidden_units // 128) * 128
    up = pad_to(jnp.swapaxes(up_weight, 1, 2), 1, padded_units)
    qkv_rows = jnp.swapaxes(qkv_weight, 2, 3)
    down = pad_to(down_weight, 1, padded_units)
    *kept, last_part = forward(
        tokens, HEAD, 0,
        images[0], qkv_rows, qv_bias, out_weight, out_bias, up, up_bias, down, down_bias,
        norm_gain, norm_shift,
    )
    flat, summed, image_grad, encoded, down_rows, up_rows = backward(
        tokens, HEAD, hidden_units, UNIT, 1, dp_size == 8,
        cotangent[0], *kept, down, up, qkv_rows, out_weight, norm_gain, last_part,
    )
    if dp_size != 8:
        summed = lax.psum(flat, "dp")
        per_layer = summed.reshape(layers, summed.shape[0] // layers, width)
        stop = down_rows.shape[0]
        down_rows = jnp.swapaxes(per_layer[:, :stop], 0, 1)
        up_rows = jnp.swapaxes(per_layer[:, stop : 2 * stop], 0, 1)
    encoded, image_grad, qkv_grad, qv_grad, out_grad, out_b, up_grad, up_b, down_grad, down_b, gain, shift = finish(
        tokens, heads, HEAD, hidden_units, summed, down_rows, up_rows, image_grad, encoded
    )
    return (
        encoded[None],
        image_grad[None],
        jnp.swapaxes(qkv_grad, 2, 3),
        qv_grad,
        out_grad,
        out_b,
        jnp.transpose(up_grad, (1, 2, 0)),
        up_b,
        jnp.swapaxes(down_grad, 0, 1),
        down_b,
        gain,
        shift,
    )


def solution(mesh):
    in_specs = (
        P("dp", None, None),
        P(None, None, None, "tensor"),
        P(None, None, "tensor"),
        P(None, "tensor", None),
        P(),
        P(None, None, "tensor"),
        P(None, "tensor"),
        P(None, "tensor", None),
        P(),
        P(),
        P(),
        P("dp", None, None),
    )
    out_specs = (
        P("dp", None, None),
        P("dp", None, None),
        P(None, None, None, "tensor"),
        P(None, None, "tensor"),
        P(None, "tensor", None),
        P(),
        P(None, None, "tensor"),
        P(None, "tensor"),
        P(None, "tensor", None),
        P(),
        P(),
        P(),
    )
    return jax.shard_map(
        functools.partial(local, mesh.shape["dp"]), mesh=mesh, in_specs=in_specs, out_specs=out_specs, check_vma=False)
```

```python
import functools

import jax
import jax.numpy as jnp
from jax import lax
from jax.experimental import pallas as pl
from jax.experimental.pallas import tpu as pltpu
from jax.sharding import PartitionSpec as P

MESH = pl.DeviceIdType.MESH
SLOTS = 24
FEW = 8
HOP = 3
ROUND = 3
PARTS = 10
TICK_SPAN = 7 * HOP + 2
TICK_BUFFERS = 17


def grad_sum_ticks(dp_sum, unit, steps, layers, grads, totals, buffers, sems):
    (
        x_in, inner_in, mid_in, own_a, total_a,
        whole_in, half_in, side_in, own_b, total_b,
        far_in, cross_in, near_in, end_in, own_f, own_n, total_e,
    ) = buffers
    (
        x_sem, inner_sem, mid_sem, out_pair_sem, out_x_sem,
        whole_sem, half_sem, side_sem, back_mid_sem, back_pair_sem, relay_sem,
        far_sem, cross_sem, near_sem, end_sem, back_one_sem, back_two_sem, back_three_sem,
        load_a_sem, store_a_sem, load_b_sem, store_b_sem, load_f_sem, load_n_sem, store_e_sem,
    ) = sems
    dp = lax.axis_index("dp")
    tensor = lax.axis_index("tensor")
    z = dp // 2
    x = dp % 2
    is_mid = (z == 1) | (z == 2)
    is_end = jnp.logical_not(is_mid)
    x_peer = (dp + 1 - 2 * x, tensor)
    pair_peer = (dp + 2 - 4 * (z % 2), tensor)
    mid_z = jnp.where(is_mid, 3 - z, z)
    mid_peer = (mid_z * 2 + x, tensor)
    side = jnp.where(z == 2, 1, 0)
    near = jnp.where(z >= 2, 1, 0)

    def greet(others):
        barrier = pltpu.get_barrier_semaphore()
        for peer in others:
            pl.semaphore_signal(barrier, inc=1, device_id=peer, device_id_type=MESH)
        if not dp_sum:
            pl.semaphore_wait(barrier, len(others))
            return
        for peer in (x_peer, pair_peer):
            pl.semaphore_signal(barrier, inc=1, device_id=peer, device_id_type=MESH)

        @pl.when(is_mid)
        def _():
            pl.semaphore_signal(barrier, inc=1, device_id=mid_peer, device_id_type=MESH)
            pl.semaphore_wait(barrier, 3 + len(others))

        @pl.when(is_end)
        def _():
            pl.semaphore_wait(barrier, 2 + len(others))

    rounds = steps // ROUND // layers

    def rows(turn_of, part, count=1):
        turn = turn_of // rounds
        first = ((layers - 1 - turn) * rounds + turn_of - turn * rounds) * (PARTS * unit)
        return pl.ds(pl.multiple_of(first + part * unit, 8), count * unit)

    def row_a(c, part):
        return rows(c // ROUND, 2 * lax.rem(c, ROUND) + part)

    def row_m(c, part, count=1):
        return rows(c, 6 + part, count)

    def row_e(c, part):
        return rows(c, 8 + part)

    def remote(src, dst, sem, slot, peer):
        return pltpu.make_async_remote_copy(
            src_ref=src, dst_ref=dst, send_sem=sem.at[0, slot], recv_sem=sem.at[1, slot],
            device_id=peer, device_id_type=MESH,
        )

    def local_copy(src, dst, sem, slot):
        return pltpu.make_async_copy(src, dst, sem.at[slot])

    def a_x(c, s):
        return remote(grads.at[row_a(c, 1 - x)], x_in.at[s], x_sem, s, x_peer)

    def a_load(c, s):
        return local_copy(grads.at[row_a(c, x)], own_a.at[s], load_a_sem, s)

    def a_inner(c, s):
        return remote(own_a.at[s], inner_in.at[s], inner_sem, s, pair_peer)

    def a_mid(c, s):
        return remote(own_a.at[s], mid_in.at[s], mid_sem, s, mid_peer)

    def a_out_pair(c, s):
        return remote(total_a.at[s], totals.at[row_a(c, x)], out_pair_sem, s, pair_peer)

    def a_out_x(c, s):
        return remote(total_a.at[s], totals.at[row_a(c, x)], out_x_sem, s, x_peer)

    def a_store(c, s):
        return local_copy(total_a.at[s], totals.at[row_a(c, x)], store_a_sem, s)

    def a_relay(c, s):
        return remote(totals.at[row_a(c, x)], totals.at[row_a(c, x)], out_x_sem, s, x_peer)

    def a_back(c, s):
        return remote(totals.at[row_a(c, x)], totals.at[row_a(c, 1 - x)], out_x_sem, s, x_peer)

    def m_whole(c, s):
        return remote(grads.at[row_m(c, 0, 2)], whole_in.at[s], whole_sem, s, pair_peer)

    def m_load(c, s):
        return local_copy(grads.at[row_m(c, 0, 2)], own_b.at[s], load_b_sem, s)

    def m_half(c, s):
        return remote(own_b.at[s, pl.ds((1 - side) * unit, unit)], half_in.at[s], half_sem, s, mid_peer)

    def m_side(c, s):
        return remote(own_b.at[s, pl.ds(side * unit, unit)], side_in.at[s], side_sem, s, x_peer)

    def m_store(c, s):
        return local_copy(total_b.at[s], totals.at[row_m(c, side)], store_b_sem, s)

    def m_back_mid(c, s):
        return remote(total_b.at[s], totals.at[row_m(c, side)], back_mid_sem, s, mid_peer)

    def m_back_pair(c, s):
        return remote(total_b.at[s], totals.at[row_m(c, side)], back_pair_sem, s, pair_peer)

    def m_relay(c, s):
        return remote(totals.at[row_m(c, 1 - side)], totals.at[row_m(c, 1 - side)], relay_sem, s, pair_peer)

    def e_far(c, s):
        return remote(grads.at[row_e(c, 1 - near)], far_in.at[s], far_sem, s, pair_peer)

    def e_load_far(c, s):
        return local_copy(grads.at[row_e(c, 1 - near)], own_f.at[s], load_f_sem, s)

    def e_load_near(c, s):
        return local_copy(grads.at[row_e(c, near)], own_n.at[s], load_n_sem, s)

    def e_cross(c, s):
        return remote(own_f.at[s], cross_in.at[s], cross_sem, s, mid_peer)

    def e_near(c, s):
        return remote(own_n.at[s], near_in.at[s], near_sem, s, pair_peer)

    def e_end(c, s):
        return remote(own_n.at[s], end_in.at[s], end_sem, s, x_peer)

    def e_store(c, s):
        return local_copy(total_e.at[s], totals.at[row_e(c, near)], store_e_sem, s)

    def e_back_one(c, s):
        return remote(total_e.at[s], totals.at[row_e(c, near)], back_one_sem, s, pair_peer)

    def e_back_two(c, s):
        return remote(totals.at[row_e(c, near)], totals.at[row_e(c, near)], back_two_sem, s, mid_peer)

    def e_back_three(c, s):
        return remote(totals.at[row_e(c, 1 - near)], totals.at[row_e(c, 1 - near)], back_three_sem, s, pair_peer)

    def a_start(c, s):
        a_x(c, s).start()
        a_load(c, s).start()

    def a_one(c, s):
        a_load(c, s).wait()
        a_x(c, s).wait_recv()
        own_a[s] = own_a[s] + x_in[s]
        pl.when(is_end)(lambda: a_inner(c, s).start())

    def a_two(c, s):
        a_inner(c, s).wait_recv()
        own_a[s] = own_a[s] + inner_in[s]
        a_mid(c, s).start()

    def a_three(c, s):
        a_mid(c, s).wait_recv()
        total_a[s] = own_a[s] + mid_in[s]
        a_out_pair(c, s).start()
        a_out_x(c, s).start()
        a_store(c, s).start()

    def a_four(c, s):
        a_out_pair(c, s).wait_recv()
        a_relay(c, s).start()

    def a_five(c, s):
        a_back(c, s).wait_recv()

    def a_done(c, s):
        a_x(c, s).wait_send()
        a_out_x(c, s).wait_send()
        pl.when(is_end)(lambda: a_inner(c, s).wait_send())

        @pl.when(is_mid)
        def _():
            a_mid(c, s).wait_send()
            a_out_pair(c, s).wait_send()
            a_store(c, s).wait()

    def m_start(c, s):
        pl.when(is_end)(lambda: m_whole(c, s).start())
        pl.when(is_mid)(lambda: m_load(c, s).start())

    def m_one(c, s):
        m_load(c, s).wait()
        m_whole(c, s).wait_recv()
        own_b[s] = own_b[s] + whole_in[s]
        m_half(c, s).start()

    def m_two(c, s):
        m_half(c, s).wait_recv()
        mine = pl.ds(pl.multiple_of(side * unit, 8), unit)
        own_b[s, mine] = own_b[s, mine] + half_in[s]
        m_side(c, s).start()

    def m_three(c, s):
        m_side(c, s).wait_recv()
        mine = pl.ds(pl.multiple_of(side * unit, 8), unit)
        total_b[s] = own_b[s, mine] + side_in[s]
        m_back_mid(c, s).start()
        m_back_pair(c, s).start()
        m_store(c, s).start()

    def m_four(c, s):
        m_back_mid(c, s).wait_recv()
        m_relay(c, s).start()

    def m_five(c, s):
        m_back_pair(c, s).wait_recv()
        m_relay(c, s).wait_recv()

    def m_done(c, s):
        pl.when(is_end)(lambda: m_whole(c, s).wait_send())

        @pl.when(is_mid)
        def _():
            m_half(c, s).wait_send()
            m_side(c, s).wait_send()
            m_back_mid(c, s).wait_send()
            m_back_pair(c, s).wait_send()
            m_store(c, s).wait()
            m_relay(c, s).wait_send()

    def e_start(c, s):
        e_load_near(c, s).start()
        pl.when(is_end)(lambda: e_far(c, s).start())
        pl.when(is_mid)(lambda: e_load_far(c, s).start())

    def e_one(c, s):
        e_load_far(c, s).wait()
        e_far(c, s).wait_recv()
        own_f[s] = own_f[s] + far_in[s]
        e_cross(c, s).start()

    def e_two(c, s):
        e_load_near(c, s).wait()
        e_cross(c, s).wait_recv()
        own_n[s] = own_n[s] + cross_in[s]
        e_near(c, s).start()

    def e_three(c, s):
        e_load_near(c, s).wait()
        e_near(c, s).wait_recv()
        own_n[s] = own_n[s] + near_in[s]
        e_end(c, s).start()

    def e_four(c, s):
        e_end(c, s).wait_recv()
        total_e[s] = own_n[s] + end_in[s]
        e_back_one(c, s).start()
        e_store(c, s).start()

    def e_five(c, s):
        e_back_one(c, s).wait_recv()
        e_back_two(c, s).start()

    def e_six(c, s):
        e_back_two(c, s).wait_recv()
        e_back_three(c, s).start()

    def e_seven(c, s):
        e_back_three(c, s).wait_recv()

    def e_done(c, s):
        @pl.when(is_end)
        def _():
            e_far(c, s).wait_send()
            e_end(c, s).wait_send()
            e_back_one(c, s).wait_send()
            e_store(c, s).wait()

        @pl.when(is_mid)
        def _():
            e_cross(c, s).wait_send()
            e_near(c, s).wait_send()
            e_back_two(c, s).wait_send()
            e_back_three(c, s).wait_send()

    def stage(step, offset, phase, guard, body):
        at = step - offset
        ok = (at >= 0) & (at < steps)
        if guard is not None:
            ok = ok & guard
        if phase is None:
            chunk, slots = at, SLOTS
        else:
            ok = ok & (lax.rem(at, ROUND) == phase)
            chunk, slots = at // ROUND, FEW

        @pl.when(ok)
        def _():
            body(chunk, lax.rem(chunk, slots))

    def tick(step):
        if not dp_sum:
            return
        stage(step, 0, None, None, a_start)
        stage(step, 0, 0, None, m_start)
        stage(step, 0, 1, None, e_start)
        stage(step, 6 * HOP, 1, is_mid, e_six)
        stage(step, 5 * HOP, 1, is_mid, e_five)
        stage(step, 4 * HOP, 1, is_end, e_four)
        stage(step, 4 * HOP, 0, is_mid, m_four)
        stage(step, 3 * HOP, None, is_mid, a_three)
        stage(step, 3 * HOP, 0, is_mid, m_three)
        stage(step, 4 * HOP, None, is_end, a_four)
        stage(step, 3 * HOP, 1, is_end, e_three)
        stage(step, 2 * HOP, None, is_mid, a_two)
        stage(step, 2 * HOP, 0, is_mid, m_two)
        stage(step, 2 * HOP, 1, is_mid, e_two)
        stage(step, HOP, None, None, a_one)
        stage(step, HOP, 0, is_mid, m_one)
        stage(step, HOP, 1, is_mid, e_one)
        stage(step, 5 * HOP, None, None, a_five)
        stage(step, 5 * HOP, 0, is_end, m_five)
        stage(step, 7 * HOP, 1, is_end, e_seven)
        stage(step, 5 * HOP + 1, None, None, a_done)
        stage(step, 5 * HOP + 1, 0, None, m_done)
        stage(step, 7 * HOP + 1, 1, None, e_done)

    return tick, greet


def tick_scratch(unit, width):
    many, few, double = (SLOTS, unit, width), (FEW, unit, width), (FEW, 2 * unit, width)
    shapes = [many] * 5 + [double, few, few, double, few] + [few] * 7
    buffers = [pltpu.VMEM(shape, jnp.float32) for shape in shapes]
    sems = [pltpu.SemaphoreType.DMA((2, SLOTS))] * 5 + [pltpu.SemaphoreType.DMA((2, FEW))] * 13
    sems += [pltpu.SemaphoreType.DMA((SLOTS,))] * 2 + [pltpu.SemaphoreType.DMA((FEW,))] * 5
    return buffers, sems


HEAD = 72
EPSILON = 1e-06
UNIT = 8
TAIL_ROWS = 48


FIRST = 1
PIECE = 16
LAG = 4
BLOCK = 128
WIDE_BLOCK = 192


def dot_nn(left, right):
    return lax.dot_general(left, right, (((1,), (0,)), ((), ())), preferred_element_type=jnp.float32)


def dot_nt(left, right):
    return lax.dot_general(left, right, (((1,), (1,)), ((), ())), preferred_element_type=jnp.float32)


def dot_tn(left, right):
    return lax.dot_general(left, right, (((0,), (0,)), ((), ())), preferred_element_type=jnp.float32)


def fold(array):
    return jnp.sum(array, axis=0, keepdims=True)


def gelu_slope(v):
    root = 0.7978845608028654
    inner = jnp.tanh(root * (v + 0.044715 * (v * v * v)))
    return 0.5 * (1.0 + inner) + 0.5 * v * (1.0 - inner * inner) * (root * (1.0 + 0.134145 * (v * v)))


def norm_back(grad_normed, state, gain):
    centred = state - jnp.mean(state, axis=-1, keepdims=True)
    inverse = lax.rsqrt(jnp.mean(centred * centred, axis=-1, keepdims=True) + EPSILON)
    unit = centred * inverse
    grad_unit = grad_normed * gain
    inner = (
        grad_unit
        - jnp.mean(grad_unit, axis=-1, keepdims=True)
        - unit * jnp.mean(grad_unit * unit, axis=-1, keepdims=True)
    )
    return inverse * inner, fold(grad_normed * unit), fold(grad_normed)


def backward_kernel(
    dp_sum, tokens, layers, heads, units_rows, head_dim, send_rows, unit, steps,
    cotangent, hidden, active, normed_two, normed, middle, state, qkv, logsum, mixed,
    down, up, qkv_w, out_w, gain, last_part,
    grads, totals, image_grad, encoded, down_grad, up_grad,
    raw_buf, wide, act_buf, two_buf, qkv_buf, lse_buf, mix_buf, down_buf, up_buf, qkvw_buf, outw_buf, gain_buf,
    flow, flow_low, hid_low, part, total, core_in, acc, y_in, grad_mix, cat, tight, acc_k, acc_v, stage_buf, small,
    woven, load_sem, stage_sem, turn_sem, weave_sem, core_send, core_recv, y_send, y_recv, back_send, back_recv,
    *tick_refs
):
    width = grads.shape[1]
    rows = part.shape[0]
    blocks = rows // BLOCK
    half = send_rows // 2
    pieces = half // PIECE
    tick, greet = grad_sum_ticks(
        dp_sum, unit, steps, layers, grads, totals, tick_refs[:TICK_BUFFERS], tick_refs[TICK_BUFFERS:]
    )
    dp = lax.axis_index("dp")
    tensor = lax.axis_index("tensor")
    core = tensor % 2
    core_peer = (dp, tensor + 1 - 2 * core)
    y_peer = (dp, lax.rem(tensor + 2, 4))
    greet((core_peer, y_peer))
    layer_rows = steps // ROUND * PARTS * unit // layers
    off_up = units_rows
    local_width = heads * head_dim
    off_qkv = 2 * units_rows
    off_out = off_qkv + 3 * local_width
    off_small = off_out + local_width
    spread = spread_matrix(heads, head_dim)

    def mine(i):
        return pl.ds(pl.multiple_of(core * half + i * PIECE, 8), PIECE)

    def other(i):
        return pl.ds(pl.multiple_of((1 - core) * half + i * PIECE, 8), PIECE)

    def here(i):
        return pl.ds(pl.multiple_of(i * PIECE, 8), PIECE)

    def remote(src, dst, send, recv, peer):
        return pltpu.make_async_remote_copy(
            src_ref=src, dst_ref=dst, send_sem=send, recv_sem=recv, device_id=peer, device_id_type=MESH
        )

    def to_core(p, i):
        return remote(
            part.at[other(i)], core_in.at[here(i)], core_send.at[p, i], core_recv.at[p, i], core_peer
        )

    def to_y(p, i):
        return remote(acc.at[here(i)], y_in.at[p, here(i)], y_send.at[p, i], y_recv.at[p, i], y_peer)

    def to_back(p, i):
        return remote(total.at[mine(i)], total.at[mine(i)], back_send.at[p, i], back_recv.at[p, i], core_peer)

    def from_back(p, i):
        return remote(
            total.at[other(i)], total.at[other(i)], back_send.at[p, i], back_recv.at[p, i], core_peer
        )

    def sum_begin(p):
        def go(i, c):
            to_core(p, i).start()
            return c

        lax.fori_loop(0, pieces, go, 0)

    def sum_step(p, j):
        @pl.when(j < pieces)
        def _():
            to_core(p, j).wait_recv()
            acc[here(j)] = part[mine(j)] + core_in[here(j)]
            to_y(p, j).start()

        late = j - LAG

        @pl.when((late >= 0) & (late < pieces))
        def _():
            to_y(p, late).wait_recv()
            total[mine(late)] = acc[here(late)] + y_in[p, here(late)]
            to_back(p, late).start()

        last = j - LAG - 2

        @pl.when((last >= 0) & (last < pieces))
        def _():
            to_core(p, last).wait_send()
            to_y(p, last).wait_send()
            to_back(p, last).wait_send()
            from_back(p, last).wait_recv()

    sum_steps = pieces + LAG + 2

    def load(source, target, sem):
        return pltpu.make_async_copy(source, target, load_sem.at[sem])

    def stage_copy(slot, row, size):
        return pltpu.make_async_copy(
            stage_buf.at[slot, pl.ds(0, size)], grads.at[pl.ds(pl.multiple_of(row, 8), size)], stage_sem.at[slot]
        )

    tiles = width // 128
    last_rows = units_rows - (tiles - 1) * 128
    layer_ticks = tiles + 1 + 4 * blocks + 2 * sum_steps + heads * blocks

    def row_block(b):
        return pl.ds(pl.multiple_of(b * BLOCK, 16), BLOCK)

    total[pl.ds(send_rows, rows - send_rows)] = jnp.zeros((rows - send_rows, width), jnp.float32)
    start = load(cotangent, raw_buf, 11)
    start.start()
    gain_load = load(gain, gain_buf, 10)
    gain_load.start()

    def layer_body(it, carry):
        layer = layers - 1 - it
        base_tick = it * layer_ticks - FIRST
        base_row = layer * layer_rows
        hidden_load = load(hidden.at[layer], wide, 0)
        down_load = load(down.at[layer], down_buf, 1)
        up_load = load(up.at[layer], up_buf, 2)
        active_load = load(active.at[layer], act_buf, 3)
        two_load = load(normed_two.at[layer], two_buf, 4)
        outw_load = load(out_w.at[layer], outw_buf, 5)
        qkv_load = load(qkv.at[layer], qkv_buf, 6)
        lse_load = load(logsum.at[layer], lse_buf, 7)
        mix_load = load(mixed.at[layer], mix_buf, 8)
        qkvw_load = load(qkv_w.at[layer], qkvw_buf, 9)
        for copy in (active_load, hidden_load, down_load, up_load, two_load, outw_load, qkv_load, lse_load, mix_load, qkvw_load):
            copy.start()
        small[...] = jnp.zeros_like(small)

        @pl.when(it == 0)
        def _():
            start.wait()
            gain_load.wait()

            lift_rows(raw_buf, flow, tokens, BLOCK)

        def lower(b, c):
            at = row_block(b)
            grad = flow[at]
            small[4:5] += fold(grad)
            flow_low[at] = grad.astype(jnp.bfloat16)
            return c

        lax.fori_loop(0, blocks, lower, 0)
        active_load.wait()

        def tile_copy(tile, row):
            slot = lax.rem(tile, 2)
            pl.when(tile < tiles - 1)(lambda: stage_copy(slot, row, 128).start())
            pl.when(tile == tiles - 1)(lambda: stage_copy(slot, row, last_rows).start())

        def tile_done(tile):
            slot = lax.rem(tile, 2)
            pl.when((tile >= 0) & (tile < tiles - 1))(lambda: stage_copy(slot, base_row, 128).wait())
            pl.when(tile == tiles - 1)(lambda: stage_copy(slot, base_row, last_rows).wait())

        def down_weights(j, c):
            tile_done(j - 1)

            @pl.when(j < tiles)
            def _():
                lanes = pl.ds(pl.multiple_of(j * 128, 128), 128)
                stage_buf[lax.rem(j, 2), pl.ds(0, 128)] = dot_tn(act_buf[:, lanes], flow_low[...])
                tile_copy(j, base_row + j * 128)

            tick(base_tick + j)
            return c

        lax.fori_loop(0, tiles + 1, down_weights, 0)
        tick_at = base_tick + tiles + 1
        hidden_load.wait()
        down_load.wait()
        up_load.wait()

        def mlp(b, c):
            at = row_block(b)
            grad_hidden = dot_nt(flow_low[at], down_buf[...]) * gelu_slope(wide[at])
            small[3:4] += fold(grad_hidden)
            hid = grad_hidden.astype(jnp.bfloat16)
            hid_low[at] = hid
            part[at] = dot_nn(hid, up_buf[...])
            tick(tick_at + b)
            return c

        lax.fori_loop(0, blocks, mlp, 0)
        sum_begin(0)
        middle_load = load(middle.at[layer], wide, 0)
        middle_load.start()
        two_load.wait()
        tick_at = tick_at + blocks

        def up_weights(j, c):
            sum_step(0, j)
            tile_done(j - 1)

            @pl.when(j < tiles)
            def _():
                lanes = pl.ds(pl.multiple_of(j * 128, 128), 128)
                stage_buf[lax.rem(j, 2), pl.ds(0, 128)] = dot_tn(hid_low[:, lanes], two_buf[...])
                tile_copy(j, base_row + off_up + j * 128)

            tick(tick_at + j)
            return c

        lax.fori_loop(0, sum_steps, up_weights, 0)
        tick_at = tick_at + sum_steps
        part_load = load(last_part, part, 1)
        pl.when(it == 0)(part_load.start)
        middle_load.wait()
        outw_load.wait()

        def norm_two(b, c):
            at = row_block(b)
            step_grad, gain_grad, shift_grad = norm_back(total[at], wide[at], gain_buf[layer, 1:2])
            small[6:7] += gain_grad
            small[8:9] += shift_grad
            grad = flow[at] + step_grad
            flow[at] = grad
            small[2:3] += fold(grad)
            low = grad.astype(jnp.bfloat16)
            flow_low[at] = low
            grad = dot_nt(low, outw_buf[...]).astype(jnp.bfloat16)
            grad_mix[at] = dot_nn(grad, spread).astype(jnp.bfloat16)
            tick(tick_at + b)
            return c

        lax.fori_loop(0, blocks, norm_two, 0)
        tick_at = tick_at + blocks
        state_load = load(state.at[layer], wide, 0)
        normed_load = load(normed.at[layer], act_buf, 3)
        state_load.start()
        normed_load.start()
        qkv_load.wait()
        lse_load.wait()
        scale = head_dim ** (-0.5)

        @pl.when(it == 0)
        def _():
            part_load.wait()
            sum_begin(2)


        def attend(m, c):
            head = m // blocks
            b = lax.rem(m, blocks)
            at = row_block(b)
            lanes = pl.ds(pl.multiple_of(head * 128, 128), 128)
            query = qkv_buf[0, head, at]
            key = qkv_buf[1, head]
            value = qkv_buf[2, head]
            grad = grad_mix[at, lanes]
            scores = dot_nt(query, key) * scale
            probs = jnp.exp(scores - lse_buf[head, at, 0:1])
            column = lax.broadcasted_iota(jnp.int32, probs.shape, 1)
            probs = jnp.where(column < tokens, probs, 0.0)
            grad_weights = dot_nt(grad, value)
            center = jnp.sum(probs * grad_weights, axis=-1, keepdims=True)
            raw = (probs * (grad_weights - center) * scale).astype(jnp.bfloat16)
            grad_query = dot_nn(raw, key)
            small[0:1, lanes] += fold(grad_query)
            cat[at, lanes] = grad_query.astype(jnp.bfloat16)
            add_k = dot_tn(raw, query)
            add_v = dot_tn(probs.astype(jnp.bfloat16), grad)

            @pl.when(b == 0)
            def _():
                acc_k[...] = add_k
                acc_v[...] = add_v

            @pl.when(b > 0)
            def _():
                acc_k[...] += add_k
                acc_v[...] += add_v

            @pl.when(b == blocks - 1)
            def _():
                at_k = pl.ds(pl.multiple_of((heads + head) * 128, 128), 128)
                at_v = pl.ds(pl.multiple_of((2 * heads + head) * 128, 128), 128)
                cat[:, at_k] = acc_k[...].astype(jnp.bfloat16)
                cat[:, at_v] = acc_v[...].astype(jnp.bfloat16)
                small[1:2, lanes] += fold(acc_v[...])

            @pl.when(it == 0)
            def _():
                sum_step(2, 2 * m)
                sum_step(2, 2 * m + 1)

            tick(tick_at + m)
            return c

        lax.fori_loop(0, heads * blocks, attend, 0)
        tick_at = tick_at + heads * blocks
        qkvw_load.wait()

        def project(b, c):
            at = row_block(b)
            out = None
            for i in range(3):
                lanes = pl.ds(i * heads * 128, heads * 128)
                narrow = dot_nt(cat[at, lanes], spread).astype(jnp.bfloat16)
                tight[i, at] = narrow
                term = dot_nn(narrow, qkvw_buf[i])
                out = term if out is None else out + term
            part[at] = out

            @pl.when(it == 0)
            def _():
                hid_low[at] = total[at].astype(jnp.bfloat16)

            tick(tick_at + b)
            return c

        lax.fori_loop(0, blocks, project, 0)
        tick_at = tick_at + blocks
        sum_begin(1)
        encoded_store = load(hid_low, encoded, 1)
        pl.when(it == 0)(encoded_store.start)
        normed_load.wait()
        mix_load.wait()

        def attention_weights(j, c):
            sum_step(1, j)

            @pl.when((j >= 1) & (j < 5))
            def _():
                stage_copy(lax.rem(j - 1, 2), base_row, local_width).wait()

            slot = lax.rem(j, 2)

            @pl.when(j < 3)
            def _():
                stage_buf[slot] = dot_tn(tight[j], act_buf[...])

            @pl.when(j == 3)
            def _():
                stage_buf[slot] = dot_tn(mix_buf[...], flow_low[...])

            @pl.when(j < 4)
            def _():
                stage_copy(slot, base_row + off_qkv + j * local_width, local_width).start()

            tick(tick_at + j)
            return c

        lax.fori_loop(0, sum_steps, attention_weights, 0)
        tick_at = tick_at + sum_steps
        state_load.wait()

        def norm_one(b, c):
            at = row_block(b)
            step_grad, gain_grad, shift_grad = norm_back(total[at], wide[at], gain_buf[layer, 0:1])
            small[5:6] += gain_grad
            small[7:8] += shift_grad
            flow[at] = flow[at] + step_grad
            tick(tick_at + b)
            return c

        lax.fori_loop(0, blocks, norm_one, 0)
        tail = pltpu.make_async_copy(
            small, grads.at[pl.ds(pl.multiple_of(base_row + off_small, 8), small.shape[0])], load_sem.at[10]
        )
        tail.start()
        tail.wait()
        pl.when(it == 0)(encoded_store.wait)
        return carry

    lax.fori_loop(0, layers, layer_body, 0)

    def lower(b, c):
        flow_low[row_block(b)] = flow[row_block(b)].astype(jnp.bfloat16)
        return c

    lax.fori_loop(0, blocks, lower, 0)
    image_store = load(flow_low, image_grad, 0)
    image_store.start()

    tail = layers * layer_ticks - FIRST
    layer_steps = steps // layers
    weaves, at_step = [], tail
    for k in range(2):
        ready = (layers - 1) * layer_steps + -(-(k + 1) * units_rows // (PARTS * unit)) * ROUND + TICK_SPAN
        at_step = max(at_step, ready)
        weaves.append(at_step)
        at_step += tiles + 1

    def each_size(tile, body):
        pl.when(tile < tiles - 1)(lambda: body(128))
        pl.when(tile == tiles - 1)(lambda: body(last_rows))

    def weave_in(k, tile, layer, rows_here):
        row = pl.multiple_of(layer * layer_rows + k * units_rows + tile * 128, 8)
        slot = lax.rem(tile, 2)
        return pltpu.make_async_copy(
            totals.at[pl.ds(row, rows_here)],
            stage_buf.at[slot, pl.ds(layer * 128, rows_here)],
            weave_sem.at[slot, layer],
        )

    def weave_out(target, tile, rows_here):
        slot = lax.rem(tile, 2)
        return pltpu.make_async_copy(
            woven.at[slot, pl.ds(0, rows_here)], target.at[pl.ds(tile * 128, rows_here)], turn_sem.at[slot]
        )

    def weave(k, target, tile):
        def begin(rows_here):
            for layer in range(layers):
                weave_in(k, tile, layer, rows_here).start()

        def arrive(rows_here):
            for layer in range(layers):
                weave_in(k, tile - 1, layer, rows_here).wait()

        each_size(tile, begin)

        @pl.when(tile >= 1)
        def _():
            each_size(tile - 1, arrive)
            slot = lax.rem(tile - 1, 2)

            @pl.when(tile >= 3)
            def _():
                weave_out(target, tile - 3, 128).wait()

            for layer in range(layers):
                woven[slot, :, layer, :] = stage_buf[slot, pl.ds(layer * 128, 128)]
            each_size(tile - 1, lambda rows_here: weave_out(target, tile - 1, rows_here).start())

        @pl.when(tile == tiles)
        def _():
            weave_out(target, tiles - 2, 128).wait()
            weave_out(target, tiles - 1, last_rows).wait()

    def rest(step, c):
        tick(step)
        if dp_sum:
            for k, target in enumerate((down_grad, up_grad)):
                tile = step - weaves[k]

                @pl.when((tile >= 0) & (tile <= tiles))
                def _():
                    weave(k, target, tile)

        return c

    lax.fori_loop(tail, max(steps + TICK_SPAN, at_step), rest, 0)
    image_store.wait()


def backward(
    tokens, head_dim, hidden_units, unit, collective_id, dp_sum,
    cotangent, hidden, active, normed_two, normed, middle, state, qkv, logsum, mixed,
    down, up, qkv_w, out_w, gain, last_part,
):
    layers, rows, width = middle.shape
    heads = qkv.shape[2]
    units_rows = -(-hidden_units // 8) * 8
    send_rows = -(-tokens // (2 * PIECE)) * 2 * PIECE
    pieces = send_rows // (2 * PIECE)
    layer_rows = 2 * units_rows + 4 * heads * head_dim + TAIL_ROWS
    steps = layers * layer_rows // (PARTS * unit) * ROUND
    buffers, sems = tick_scratch(unit, width)
    f32, low = jnp.float32, jnp.bfloat16
    half = (send_rows // 2, width)
    full = (rows, width)
    any_spec = pl.BlockSpec(memory_space=pl.ANY)
    grads = jax.ShapeDtypeStruct((layers * layer_rows, width), f32)
    return pl.pallas_call(
        functools.partial(
            backward_kernel, dp_sum, tokens, layers, heads, units_rows, head_dim, send_rows, unit, steps
        ),
        out_shape=(
            grads,
            grads,
            jax.ShapeDtypeStruct(full, low),
            jax.ShapeDtypeStruct(full, low),
            jax.ShapeDtypeStruct((units_rows, layers, width), f32),
            jax.ShapeDtypeStruct((units_rows, layers, width), f32),
        ),
        in_specs=[any_spec] * 16,
        out_specs=(any_spec,) * 6,
        scratch_shapes=[
            pltpu.VMEM(cotangent.shape, low),
            pltpu.VMEM(full, f32),
            pltpu.VMEM(full, low),
            pltpu.VMEM(full, low),
            pltpu.VMEM(qkv.shape[1:], low),
            pltpu.VMEM(logsum.shape[1:], f32),
            pltpu.VMEM(mixed.shape[1:], low),
            pltpu.VMEM(down.shape[1:], low),
            pltpu.VMEM(up.shape[1:], low),
            pltpu.VMEM(qkv_w.shape[1:], low),
            pltpu.VMEM(out_w.shape[1:], low),
            pltpu.VMEM(gain.shape, f32),
            pltpu.VMEM(full, f32),
            pltpu.VMEM(full, low),
            pltpu.VMEM(full, low),
            pltpu.VMEM(full, f32),
            pltpu.VMEM(full, f32),
            pltpu.VMEM(half, f32),
            pltpu.VMEM(half, f32),
            pltpu.VMEM((3,) + half, f32),
            pltpu.VMEM((rows, heads * 128), low),
            pltpu.VMEM((rows, 3 * heads * 128), low),
            pltpu.VMEM((3, rows, heads * head_dim), low),
            pltpu.VMEM((rows, 128), f32),
            pltpu.VMEM((rows, 128), f32),
            pltpu.VMEM((2, heads * head_dim, width), f32),
            pltpu.VMEM((TAIL_ROWS, width), f32),
            pltpu.VMEM((2, 128, layers, width), f32),
        ]
        + [pltpu.SemaphoreType.DMA((12,)), pltpu.SemaphoreType.DMA((2,)), pltpu.SemaphoreType.DMA((2,)), pltpu.SemaphoreType.DMA((2, layers))]
        + [pltpu.SemaphoreType.DMA((3, pieces))] * 6
        + buffers
        + sems,
        compiler_params=pltpu.CompilerParams(
            collective_id=collective_id, has_side_effects=True, vmem_limit_bytes=63 << 20
        ),
    )(
        cotangent, hidden, active, normed_two, normed, middle, state, qkv, logsum, mixed,
        down, up, qkv_w, out_w, gain, last_part,
    )


def lift_rows(source, target, tokens, size):
    blocks = target.shape[0] // size

    def one(b, c):
        at = pl.ds(pl.multiple_of(b * size, 16), size)
        target[at] = source[at].astype(jnp.float32)
        return c

    lax.fori_loop(0, blocks - 1, one, 0)
    begin = (blocks - 1) * size
    target[pl.ds(begin, size)] = jnp.zeros((size, target.shape[1]), jnp.float32)
    last = pl.ds(begin, tokens - begin)
    target[last] = source[last].astype(jnp.float32)


def spread_matrix(heads, head_dim):
    shape = (heads * head_dim, heads * 128)
    source = lax.broadcasted_iota(jnp.int32, shape, 0)
    lane = lax.broadcasted_iota(jnp.int32, shape, 1)
    hit = (lane // 128 * head_dim + lane % 128 == source) & (lane % 128 < head_dim)
    return jnp.where(hit, 1.0, 0.0).astype(jnp.bfloat16)


def norm_unit(state):
    centred = state - jnp.mean(state, axis=-1, keepdims=True)
    return centred * lax.rsqrt(jnp.mean(centred * centred, axis=-1, keepdims=True) + EPSILON)


def gelu(v):
    return 0.5 * v * (1.0 + jnp.tanh(0.7978845608028654 * (v + 0.044715 * (v * v * v))))


def block_sum(pieces, dp, tensor, part, core_in, y_in, total, sems):
    core = tensor % 2
    core_peer = (dp, tensor + 1 - 2 * core)
    y_peer = (dp, lax.rem(tensor + 2, 4))
    core_sem, y_sem, back_sem = sems
    per_block = WIDE_BLOCK // (2 * PIECE)

    def mine(i):
        return pl.ds(pl.multiple_of((2 * i + core) * PIECE, 8), PIECE)

    def other(i):
        return pl.ds(pl.multiple_of((2 * i + 1 - core) * PIECE, 8), PIECE)

    def here(i):
        return pl.ds(pl.multiple_of(i * PIECE, 8), PIECE)

    def remote(src, dst, sem, i, peer):
        return pltpu.make_async_remote_copy(
            src_ref=src, dst_ref=dst, send_sem=sem.at[0, i], recv_sem=sem.at[1, i],
            device_id=peer, device_id_type=MESH,
        )

    def to_core(i):
        return remote(part.at[other(i)], core_in.at[here(i)], core_sem, i, core_peer)

    def to_y(i):
        return remote(core_in.at[here(i)], y_in.at[here(i)], y_sem, i, y_peer)

    def to_back(i):
        return remote(total.at[mine(i)], total.at[mine(i)], back_sem, i, core_peer)

    def from_back(i):
        return remote(total.at[other(i)], total.at[other(i)], back_sem, i, core_peer)

    def each(b, body):
        def go(k, c):
            i = b * per_block + k

            @pl.when(i < pieces)
            def _():
                body(i)

            return c

        lax.fori_loop(0, per_block, go, 0)

    def send(b):
        each(b, lambda i: to_core(i).start())

    def meet(b):
        def body(i):
            to_core(i).wait_recv()
            core_in[here(i)] = core_in[here(i)] + part[mine(i)]
            to_y(i).start()

        each(b, body)

    def close(b):
        def body(i):
            to_y(i).wait_recv()
            total[mine(i)] = core_in[here(i)] + y_in[here(i)]
            to_back(i).start()

        each(b, body)

    def finish(b):
        def body(i):
            to_core(i).wait_send()
            to_y(i).wait_send()
            to_back(i).wait_send()
            from_back(i).wait_recv()

        each(b, body)

    return send, meet, close, finish


def forward_kernel(
    tokens, layers, heads, head_dim, send_rows,
    images, qkv_w, qv_b, out_w, out_b, up, up_b, down, down_b, gain, shift,
    hidden, active, normed_two, normed, middle, state, qkv, logsum, mixed, last_part,
    image_buf, upb_raw, flow, normed_buf, qkv_buf, lse_buf, mix_buf, tight_buf, two_buf, hidden_buf, active_buf,
    qkvw_buf, outw_buf, up_buf, down_buf, qvb_buf, outb_buf, upb_buf, downb_buf, gain_buf, shift_buf,
    part_a, core_in_a, y_in_a, total_a, part_b, core_in_b, y_in_b, total_b,
    load_sem, weight_sem, store_sem, middle_sem, *sum_sems
):
    rows, width = flow.shape
    blocks = rows // WIDE_BLOCK
    pieces = send_rows // (2 * PIECE)
    dp = lax.axis_index("dp")
    tensor = lax.axis_index("tensor")
    core = tensor % 2
    barrier = pltpu.get_barrier_semaphore()
    for peer in ((dp, tensor + 1 - 2 * core), (dp, lax.rem(tensor + 2, 4))):
        pl.semaphore_signal(barrier, inc=1, device_id=peer, device_id_type=MESH)

    def weights(layer):
        return (
            pltpu.make_async_copy(qkv_w.at[layer], qkvw_buf, weight_sem.at[0]),
            pltpu.make_async_copy(out_w.at[layer], outw_buf, weight_sem.at[1]),
            pltpu.make_async_copy(up.at[layer], up_buf, weight_sem.at[2]),
            pltpu.make_async_copy(down.at[layer], down_buf, weight_sem.at[3]),
        )

    singles = [
        pltpu.make_async_copy(source, target, load_sem.at[i])
        for i, (source, target) in enumerate(
            (
                (images, image_buf), (gain, gain_buf), (shift, shift_buf), (qv_b, qvb_buf),
                (out_b, outb_buf), (up_b, upb_raw), (down_b, downb_buf),
            )
        )
    ]
    for copy in singles:
        copy.start()
    current = weights(0)
    for copy in current:
        copy.start()
    spread = spread_matrix(heads, head_dim)
    total_a[pl.ds(send_rows, rows - send_rows)] = jnp.zeros((rows - send_rows, width), jnp.float32)
    total_b[pl.ds(send_rows, rows - send_rows)] = jnp.zeros((rows - send_rows, width), jnp.float32)
    for copy in singles:
        copy.wait()
    pl.semaphore_wait(barrier, 2)

    def row_block(b):
        return pl.ds(pl.multiple_of(b * WIDE_BLOCK, 16), WIDE_BLOCK)

    scale = head_dim ** (-0.5)
    stores = {}

    def keep(name, source, target, index):
        copy = pltpu.make_async_copy(source, target, store_sem.at[index])
        copy.start()
        stores[name] = copy

    def settle(*names):
        for name in names:
            if name in stores:
                stores.pop(name).wait()

    def project(layer, b, value):
        at = row_block(b)
        flow[at] = value
        low = (norm_unit(value) * gain_buf[layer, 0:1] + shift_buf[layer, 0:1]).astype(jnp.bfloat16)
        normed_buf[at] = low
        for i in range(3):
            out = dot_nt(low, qkvw_buf[i])
            if i != 1:
                out = out + qvb_buf[layer, i // 2 : i // 2 + 1]
            wide = dot_nn(out.astype(jnp.bfloat16), spread).astype(jnp.bfloat16)
            for head in range(heads):
                qkv_buf[i, head, at] = wide[:, head * 128 : (head + 1) * 128]

    def first(b, c):
        project(0, b, flow[row_block(b)])
        return c

    lift_rows(image_buf, flow, tokens, WIDE_BLOCK)
    upb_buf[...] = jnp.zeros_like(upb_buf)
    upb_buf[:, pl.ds(0, upb_raw.shape[1])] = upb_raw[...]
    current[0].wait()
    lax.fori_loop(0, blocks, first, 0)

    for layer in range(layers):
        keep("state", flow, state.at[layer], 0)
        keep("normed", normed_buf, normed.at[layer], 1)
        keep("qkv", qkv_buf, qkv.at[layer], 2)
        settle("logsum", "mixed")
        send_a, meet_a, close_a, finish_a = block_sum(
            pieces, dp, tensor, part_a, core_in_a, y_in_a, total_a, [s.at[layer] for s in sum_sems[:3]]
        )
        send_b, meet_b, close_b, finish_b = block_sum(
            pieces, dp, tensor, part_b, core_in_b, y_in_b, total_b, [s.at[layer] for s in sum_sems[3:]]
        )
        is_last = layer == layers - 1
        if not is_last:
            following = weights(layer + 1)
            following[0].start()

        current[1].wait()

        def attend(b, c):
            at = row_block(b)

            def one_head(head, c):
                scores = dot_nt(qkv_buf[0, head, at], qkv_buf[1, head]) * scale
                column = lax.broadcasted_iota(jnp.int32, scores.shape, 1)
                scores = jnp.where(column < tokens, scores, -jnp.inf)
                peak = jnp.max(scores, axis=-1, keepdims=True)
                expo = jnp.exp(scores - peak)
                denominator = jnp.sum(expo, axis=-1, keepdims=True)
                probs = (expo / denominator).astype(jnp.bfloat16)
                lanes = pl.ds(pl.multiple_of(head * 128, 128), 128)
                mix_buf[:, lanes] = dot_nn(probs, qkv_buf[2, head]).astype(jnp.bfloat16)
                lse_buf[head, at] = jnp.broadcast_to(peak + jnp.log(denominator), (WIDE_BLOCK, 128))
                return c

            lax.fori_loop(0, heads, one_head, 0)
            tight = dot_nt(mix_buf[...], spread).astype(jnp.bfloat16)
            tight_buf[at] = tight
            part_a[at] = dot_nn(tight, outw_buf[...])
            send_a(b)

            @pl.when(b > 0)
            def _():
                meet_a(b - 1)

            return c

        lax.fori_loop(0, blocks, attend, 0)
        meet_a(blocks - 1)
        keep("logsum", lse_buf, logsum.at[layer], 3)
        keep("mixed", tight_buf, mixed.at[layer], 4)
        if not is_last:
            following[1].start()

        settle("state", "normed_two", "hidden", "active")
        current[2].wait()
        current[3].wait()

        def mlp(b, c):
            at = row_block(b)
            close_a(b)
            if not is_last:

                @pl.when(b > 0)
                def _():
                    meet_b(b - 1)

            finish_a(b)
            value = flow[at] + total_a[at] + outb_buf[layer : layer + 1]
            flow[at] = value
            pltpu.make_async_copy(flow.at[at], middle.at[layer, at], middle_sem.at[b]).start()
            low = (norm_unit(value) * gain_buf[layer, 1:2] + shift_buf[layer, 1:2]).astype(jnp.bfloat16)
            two_buf[at] = low
            hid = dot_nt(low, up_buf[...]) + upb_buf[layer : layer + 1]
            hidden_buf[at] = hid
            act = gelu(hid).astype(jnp.bfloat16)
            active_buf[at] = act
            partial = dot_nn(act, down_buf[...])
            if is_last:
                lead = jnp.where(tensor == 0, 1.0, 0.0)
                partial = partial + lead * (value + downb_buf[layer : layer + 1])
            part_b[at] = partial
            if not is_last:
                send_b(b)
            return c

        lax.fori_loop(0, blocks, mlp, 0)
        keep("normed_two", two_buf, normed_two.at[layer], 5)
        keep("hidden", hidden_buf, hidden.at[layer], 6)
        keep("active", active_buf, active.at[layer], 7)

        def middle_wait(b):
            pltpu.make_async_copy(flow.at[row_block(b)], middle.at[layer, row_block(b)], middle_sem.at[b]).wait()

        if is_last:
            keep("part", part_b, last_part, 8)
            for b in range(blocks):
                middle_wait(b)
        else:
            following[2].start()
            following[3].start()
            following[0].wait()
            meet_b(blocks - 1)
            settle("normed", "qkv")

            def next_project(b, c):
                at = row_block(b)
                close_b(b)
                finish_b(b)
                middle_wait(b)
                project(layer + 1, b, flow[at] + total_b[at] + downb_buf[layer : layer + 1])
                return c

            lax.fori_loop(0, blocks, next_project, 0)
            current = following
    settle(*list(stores))


def forward(
    tokens, head_dim, collective_id,
    images, qkv_w, qv_b, out_w, out_b, up, up_b, down, down_b, gain, shift,
):
    layers = qkv_w.shape[0]
    width = images.shape[1]
    rows = -(-tokens // WIDE_BLOCK) * WIDE_BLOCK
    heads = qkv_w.shape[2] // head_dim
    units = up.shape[1]
    send_rows = -(-tokens // (2 * PIECE)) * 2 * PIECE
    pieces = send_rows // (2 * PIECE)
    f32, low = jnp.float32, jnp.bfloat16
    full = (rows, width)
    half = (send_rows // 2, width)
    any_spec = pl.BlockSpec(memory_space=pl.ANY)

    def out(shape, dtype):
        return jax.ShapeDtypeStruct(shape, dtype)

    lanes = heads * 128
    return pl.pallas_call(
        functools.partial(forward_kernel, tokens, layers, heads, head_dim, send_rows),
        out_shape=(
            out((layers, rows, units), f32),
            out((layers, rows, units), low),
            out((layers,) + full, low),
            out((layers,) + full, low),
            out((layers,) + full, f32),
            out((layers,) + full, f32),
            out((layers, 3, heads, rows, 128), low),
            out((layers, heads, rows, 128), f32),
            out((layers, rows, heads * head_dim), low),
            out(full, f32),
        ),
        in_specs=[any_spec] * 11,
        out_specs=(any_spec,) * 10,
        scratch_shapes=[
            pltpu.VMEM(images.shape, low),
            pltpu.VMEM(up_b.shape, f32),
            pltpu.VMEM(full, f32),
            pltpu.VMEM(full, low),
            pltpu.VMEM((3, heads, rows, 128), low),
            pltpu.VMEM((heads, rows, 128), f32),
            pltpu.VMEM((WIDE_BLOCK, lanes), low),
            pltpu.VMEM((rows, heads * head_dim), low),
            pltpu.VMEM(full, low),
            pltpu.VMEM((rows, units), f32),
            pltpu.VMEM((rows, units), low),
            pltpu.VMEM(qkv_w.shape[1:], low),
            pltpu.VMEM(out_w.shape[1:], low),
            pltpu.VMEM(up.shape[1:], low),
            pltpu.VMEM(down.shape[1:], low),
            pltpu.VMEM(qv_b.shape, f32),
            pltpu.VMEM(out_b.shape, f32),
            pltpu.VMEM((layers, units), f32),
            pltpu.VMEM(down_b.shape, f32),
            pltpu.VMEM(gain.shape, f32),
            pltpu.VMEM(shift.shape, f32),
        ]
        + [pltpu.VMEM(s, f32) for s in (full, half, half, full)] * 2
        + [
            pltpu.SemaphoreType.DMA((7,)),
            pltpu.SemaphoreType.DMA((4,)),
            pltpu.SemaphoreType.DMA((9,)),
            pltpu.SemaphoreType.DMA((rows // WIDE_BLOCK,)),
        ]
        + [pltpu.SemaphoreType.DMA((layers, 2, pieces))] * 6,
        compiler_params=pltpu.CompilerParams(
            collective_id=collective_id, has_side_effects=True, vmem_limit_bytes=63 << 20
        ),
    )(images, qkv_w, qv_b, out_w, out_b, up, up_b, down, down_b, gain, shift)


def finish_kernel(
    layers, heads, head_dim, hidden_units, layer_rows, off_qkv,
    totals, down_rows, up_rows, image_rows, encoded_rows,
    encoded, image_grad, qkv_grad, qv_grad, out_grad, out_b, up_grad, up_b, down_grad, down_b, gain, shift,
    down_buf, up_wide, rows_buf, long_a, long_b, short_a, short_b, small, qv_buf, up_buf, plain, pair, sem,
):
    width = totals.shape[1]
    local_width = heads * head_dim
    count = [0]

    def move(source, target):
        copy = pltpu.make_async_copy(source, target, sem.at[count[0]])
        count[0] += 1
        copy.start()
        return copy

    small_rows = small.shape[1]
    off_small = off_qkv + 4 * local_width
    fetch = [move(totals.at[pl.ds(l * layer_rows + off_small, small_rows)], small.at[l]) for l in range(layers)]
    fetch_a = move(encoded_rows, long_a)
    fetch_b = move(image_rows, long_b)
    through = []
    for source, buffer, target in ((down_rows, down_buf, down_grad), (up_rows, up_wide, up_grad)):
        for at in range(0, hidden_units, 128):
            here = pl.ds(at, min(128, hidden_units - at))
            through.append((move(source.at[here], buffer.at[here]), buffer.at[here], target.at[here]))
    for l in range(layers):
        begin = l * layer_rows + off_qkv
        for i in range(4):
            rows = pl.ds(begin + i * local_width, local_width)
            target = qkv_grad.at[l, i] if i < 3 else out_grad.at[l]
            through.append((move(totals.at[rows], rows_buf.at[l, i]), rows_buf.at[l, i], target))
    moves = []
    for arrived, buffer, target in through:
        arrived.wait()
        moves.append(move(buffer, target))
    for copy in fetch:
        copy.wait()
    for l in range(layers):
        for i in range(2):
            for h in range(heads):
                qv_buf[l, i : i + 1, h * head_dim : (h + 1) * head_dim] = small[
                    l, i : i + 1, h * 128 : h * 128 + head_dim
                ]
        plain[0, l : l + 1] = small[l, 2:3]
        up_buf[l : l + 1] = small[l, 3:4, :hidden_units]
        plain[1, l : l + 1] = small[l, 4:5]
        pair[0, l] = small[l, 5:7]
        pair[1, l] = small[l, 7:9]
    moves += [
        move(qv_buf, qv_grad), move(plain.at[0], out_b), move(up_buf, up_b), move(plain.at[1], down_b),
        move(pair.at[0], gain), move(pair.at[1], shift),
    ]
    tokens = short_a.shape[0]
    fetch_a.wait()
    short_a[...] = long_a[:tokens]
    moves.append(move(short_a, encoded))
    fetch_b.wait()
    short_b[...] = long_b[:tokens]
    moves.append(move(short_b, image_grad))
    for copy in moves:
        copy.wait()


def finish(tokens, heads, head_dim, hidden_units, totals, down_rows, up_rows, image_rows, encoded_rows):
    layers = down_rows.shape[1]
    width = totals.shape[1]
    rows = image_rows.shape[0]
    layer_rows = totals.shape[0] // layers
    off_qkv = 2 * down_rows.shape[0]
    local_width = heads * head_dim
    f32, low = jnp.float32, jnp.bfloat16
    any_spec = pl.BlockSpec(memory_space=pl.ANY)

    def out(shape, dtype=f32):
        return jax.ShapeDtypeStruct(shape, dtype)

    copies = 4 * -(-hidden_units // 128) + 9 * layers + 10
    return pl.pallas_call(
        functools.partial(finish_kernel, layers, heads, head_dim, hidden_units, layer_rows, off_qkv),
        out_shape=(
            out((tokens, width), low),
            out((tokens, width), low),
            out((layers, 3, local_width, width)),
            out((layers, 2, local_width)),
            out((layers, local_width, width)),
            out((layers, width)),
            out((hidden_units, layers, width)),
            out((layers, hidden_units)),
            out((hidden_units, layers, width)),
            out((layers, width)),
            out((layers, 2, width)),
            out((layers, 2, width)),
        ),
        in_specs=[any_spec] * 5,
        out_specs=(any_spec,) * 12,
        scratch_shapes=[
            pltpu.VMEM((hidden_units, layers, width), f32),
            pltpu.VMEM((hidden_units, layers, width), f32),
            pltpu.VMEM((layers, 4, local_width, width), f32),
            pltpu.VMEM((rows, width), low),
            pltpu.VMEM((rows, width), low),
            pltpu.VMEM((tokens, width), low),
            pltpu.VMEM((tokens, width), low),
            pltpu.VMEM((layers, TAIL_ROWS, width), f32),
            pltpu.VMEM((layers, 2, local_width), f32),
            pltpu.VMEM((layers, hidden_units), f32),
            pltpu.VMEM((2, layers, width), f32),
            pltpu.VMEM((2, layers, 2, width), f32),
            pltpu.SemaphoreType.DMA((copies,)),
        ],
        compiler_params=pltpu.CompilerParams(has_side_effects=True, vmem_limit_bytes=56 << 20),
    )(totals, down_rows, up_rows, image_rows, encoded_rows)


def pad_to(array, axis, size):
    spec = [(0, 0)] * array.ndim
    spec[axis] = (0, size - array.shape[axis])
    return jnp.pad(array, spec)


def local(
    dp_size,
    images,
    qkv_weight,
    qv_bias,
    out_weight,
    out_bias,
    up_weight,
    up_bias,
    down_weight,
    down_bias,
    norm_gain,
    norm_shift,
    cotangent,
):
    tokens, width = images.shape[1:]
    layers = qkv_weight.shape[0]
    local_width = qkv_weight.shape[3]
    heads = local_width // HEAD
    hidden_units = up_weight.shape[2]
    padded_units = -(-hidden_units // 128) * 128
    up = pad_to(jnp.swapaxes(up_weight, 1, 2), 1, padded_units)
    qkv_rows = jnp.swapaxes(qkv_weight, 2, 3)
    down = pad_to(down_weight, 1, padded_units)
    *kept, last_part = forward(
        tokens, HEAD, 0,
        images[0], qkv_rows, qv_bias, out_weight, out_bias, up, up_bias, down, down_bias,
        norm_gain, norm_shift,
    )
    flat, summed, image_grad, encoded, down_rows, up_rows = backward(
        tokens, HEAD, hidden_units, UNIT, 1, dp_size == 8,
        cotangent[0], *kept, down, up, qkv_rows, out_weight, norm_gain, last_part,
    )
    if dp_size != 8:
        summed = lax.psum(flat, "dp")
        per_layer = summed.reshape(layers, summed.shape[0] // layers, width)
        stop = down_rows.shape[0]
        down_rows = jnp.swapaxes(per_layer[:, :stop], 0, 1)
        up_rows = jnp.swapaxes(per_layer[:, stop : 2 * stop], 0, 1)
    encoded, image_grad, qkv_grad, qv_grad, out_grad, out_b, up_grad, up_b, down_grad, down_b, gain, shift = finish(
        tokens, heads, HEAD, hidden_units, summed, down_rows, up_rows, image_grad, encoded
    )
    return (
        encoded[None],
        image_grad[None],
        jnp.swapaxes(qkv_grad, 2, 3),
        qv_grad,
        out_grad,
        out_b,
        jnp.transpose(up_grad, (1, 2, 0)),
        up_b,
        jnp.swapaxes(down_grad, 0, 1),
        down_b,
        gain,
        shift,
    )


def solution(mesh):
    in_specs = (
        P("dp", None, None),
        P(None, None, None, "tensor"),
        P(None, None, "tensor"),
        P(None, "tensor", None),
        P(),
        P(None, None, "tensor"),
        P(None, "tensor"),
        P(None, "tensor", None),
        P(),
        P(),
        P(),
        P("dp", None, None),
    )
    out_specs = (
        P("dp", None, None),
        P("dp", None, None),
        P(None, None, None, "tensor"),
        P(None, None, "tensor"),
        P(None, "tensor", None),
        P(),
        P(None, None, "tensor"),
        P(None, "tensor"),
        P(None, "tensor", None),
        P(),
        P(),
        P(),
    )
    return jax.shard_map(
        functools.partial(local, mesh.shape["dp"]), mesh=mesh, in_specs=in_specs, out_specs=out_specs, check_vma=False)
```

```python
import functools

import jax
import jax.numpy as jnp
from jax import lax
from jax.experimental import pallas as pl
from jax.experimental.pallas import tpu as pltpu
from jax.sharding import PartitionSpec as P

MESH = pl.DeviceIdType.MESH
SLOTS = 24
FEW = 8
HOP = 3
ROUND = 3
PARTS = 10
TICK_SPAN = 7 * HOP + 2
TICK_BUFFERS = 17


def grad_sum_ticks(dp_sum, unit, steps, grads, totals, buffers, sems):
    (
        x_in, inner_in, mid_in, own_a, total_a,
        whole_in, half_in, side_in, own_b, total_b,
        far_in, cross_in, near_in, end_in, own_f, own_n, total_e,
    ) = buffers
    (
        x_sem, inner_sem, mid_sem, out_pair_sem, out_x_sem,
        whole_sem, half_sem, side_sem, back_mid_sem, back_pair_sem, relay_sem,
        far_sem, cross_sem, near_sem, end_sem, back_one_sem, back_two_sem, back_three_sem,
        load_a_sem, store_a_sem, load_b_sem, store_b_sem, load_f_sem, load_n_sem, store_e_sem,
    ) = sems
    dp = lax.axis_index("dp")
    tensor = lax.axis_index("tensor")
    z = dp // 2
    x = dp % 2
    is_mid = (z == 1) | (z == 2)
    is_end = jnp.logical_not(is_mid)
    x_peer = (dp + 1 - 2 * x, tensor)
    pair_peer = (dp + 2 - 4 * (z % 2), tensor)
    mid_z = jnp.where(is_mid, 3 - z, z)
    mid_peer = (mid_z * 2 + x, tensor)
    side = jnp.where(z == 2, 1, 0)
    near = jnp.where(z >= 2, 1, 0)

    def greet(others):
        barrier = pltpu.get_barrier_semaphore()
        for peer in others:
            pl.semaphore_signal(barrier, inc=1, device_id=peer, device_id_type=MESH)
        if not dp_sum:
            pl.semaphore_wait(barrier, len(others))
            return
        for peer in (x_peer, pair_peer):
            pl.semaphore_signal(barrier, inc=1, device_id=peer, device_id_type=MESH)

        @pl.when(is_mid)
        def _():
            pl.semaphore_signal(barrier, inc=1, device_id=mid_peer, device_id_type=MESH)
            pl.semaphore_wait(barrier, 3 + len(others))

        @pl.when(is_end)
        def _():
            pl.semaphore_wait(barrier, 2 + len(others))

    def rows(chunk, part, count=1):
        return pl.ds(pl.multiple_of((chunk * PARTS + part) * unit, 8), count * unit)

    def row_a(c, part):
        return rows(c // ROUND, 2 * lax.rem(c, ROUND) + part)

    def row_m(c, part, count=1):
        return rows(c, 6 + part, count)

    def row_e(c, part):
        return rows(c, 8 + part)

    def remote(src, dst, sem, slot, peer):
        return pltpu.make_async_remote_copy(
            src_ref=src, dst_ref=dst, send_sem=sem.at[0, slot], recv_sem=sem.at[1, slot],
            device_id=peer, device_id_type=MESH,
        )

    def local_copy(src, dst, sem, slot):
        return pltpu.make_async_copy(src, dst, sem.at[slot])

    def a_x(c, s):
        return remote(grads.at[row_a(c, 1 - x)], x_in.at[s], x_sem, s, x_peer)

    def a_load(c, s):
        return local_copy(grads.at[row_a(c, x)], own_a.at[s], load_a_sem, s)

    def a_inner(c, s):
        return remote(own_a.at[s], inner_in.at[s], inner_sem, s, pair_peer)

    def a_mid(c, s):
        return remote(own_a.at[s], mid_in.at[s], mid_sem, s, mid_peer)

    def a_out_pair(c, s):
        return remote(total_a.at[s], totals.at[row_a(c, x)], out_pair_sem, s, pair_peer)

    def a_out_x(c, s):
        return remote(total_a.at[s], totals.at[row_a(c, x)], out_x_sem, s, x_peer)

    def a_store(c, s):
        return local_copy(total_a.at[s], totals.at[row_a(c, x)], store_a_sem, s)

    def a_relay(c, s):
        return remote(totals.at[row_a(c, x)], totals.at[row_a(c, x)], out_x_sem, s, x_peer)

    def a_back(c, s):
        return remote(totals.at[row_a(c, x)], totals.at[row_a(c, 1 - x)], out_x_sem, s, x_peer)

    def m_whole(c, s):
        return remote(grads.at[row_m(c, 0, 2)], whole_in.at[s], whole_sem, s, pair_peer)

    def m_load(c, s):
        return local_copy(grads.at[row_m(c, 0, 2)], own_b.at[s], load_b_sem, s)

    def m_half(c, s):
        return remote(own_b.at[s, pl.ds((1 - side) * unit, unit)], half_in.at[s], half_sem, s, mid_peer)

    def m_side(c, s):
        return remote(own_b.at[s, pl.ds(side * unit, unit)], side_in.at[s], side_sem, s, x_peer)

    def m_store(c, s):
        return local_copy(total_b.at[s], totals.at[row_m(c, side)], store_b_sem, s)

    def m_back_mid(c, s):
        return remote(total_b.at[s], totals.at[row_m(c, side)], back_mid_sem, s, mid_peer)

    def m_back_pair(c, s):
        return remote(total_b.at[s], totals.at[row_m(c, side)], back_pair_sem, s, pair_peer)

    def m_relay(c, s):
        return remote(totals.at[row_m(c, 1 - side)], totals.at[row_m(c, 1 - side)], relay_sem, s, pair_peer)

    def e_far(c, s):
        return remote(grads.at[row_e(c, 1 - near)], far_in.at[s], far_sem, s, pair_peer)

    def e_load_far(c, s):
        return local_copy(grads.at[row_e(c, 1 - near)], own_f.at[s], load_f_sem, s)

    def e_load_near(c, s):
        return local_copy(grads.at[row_e(c, near)], own_n.at[s], load_n_sem, s)

    def e_cross(c, s):
        return remote(own_f.at[s], cross_in.at[s], cross_sem, s, mid_peer)

    def e_near(c, s):
        return remote(own_n.at[s], near_in.at[s], near_sem, s, pair_peer)

    def e_end(c, s):
        return remote(own_n.at[s], end_in.at[s], end_sem, s, x_peer)

    def e_store(c, s):
        return local_copy(total_e.at[s], totals.at[row_e(c, near)], store_e_sem, s)

    def e_back_one(c, s):
        return remote(total_e.at[s], totals.at[row_e(c, near)], back_one_sem, s, pair_peer)

    def e_back_two(c, s):
        return remote(totals.at[row_e(c, near)], totals.at[row_e(c, near)], back_two_sem, s, mid_peer)

    def e_back_three(c, s):
        return remote(totals.at[row_e(c, 1 - near)], totals.at[row_e(c, 1 - near)], back_three_sem, s, pair_peer)

    def a_start(c, s):
        a_x(c, s).start()
        a_load(c, s).start()

    def a_one(c, s):
        a_load(c, s).wait()
        a_x(c, s).wait_recv()
        own_a[s] = own_a[s] + x_in[s]
        pl.when(is_end)(lambda: a_inner(c, s).start())

    def a_two(c, s):
        a_inner(c, s).wait_recv()
        own_a[s] = own_a[s] + inner_in[s]
        a_mid(c, s).start()

    def a_three(c, s):
        a_mid(c, s).wait_recv()
        total_a[s] = own_a[s] + mid_in[s]
        a_out_pair(c, s).start()
        a_out_x(c, s).start()
        a_store(c, s).start()

    def a_four(c, s):
        a_out_pair(c, s).wait_recv()
        a_relay(c, s).start()

    def a_five(c, s):
        a_back(c, s).wait_recv()

    def a_done(c, s):
        a_x(c, s).wait_send()
        a_out_x(c, s).wait_send()
        pl.when(is_end)(lambda: a_inner(c, s).wait_send())

        @pl.when(is_mid)
        def _():
            a_mid(c, s).wait_send()
            a_out_pair(c, s).wait_send()
            a_store(c, s).wait()

    def m_start(c, s):
        pl.when(is_end)(lambda: m_whole(c, s).start())
        pl.when(is_mid)(lambda: m_load(c, s).start())

    def m_one(c, s):
        m_load(c, s).wait()
        m_whole(c, s).wait_recv()
        own_b[s] = own_b[s] + whole_in[s]
        m_half(c, s).start()

    def m_two(c, s):
        m_half(c, s).wait_recv()
        mine = pl.ds(pl.multiple_of(side * unit, 8), unit)
        own_b[s, mine] = own_b[s, mine] + half_in[s]
        m_side(c, s).start()

    def m_three(c, s):
        m_side(c, s).wait_recv()
        mine = pl.ds(pl.multiple_of(side * unit, 8), unit)
        total_b[s] = own_b[s, mine] + side_in[s]
        m_back_mid(c, s).start()
        m_back_pair(c, s).start()
        m_store(c, s).start()

    def m_four(c, s):
        m_back_mid(c, s).wait_recv()
        m_relay(c, s).start()

    def m_five(c, s):
        m_back_pair(c, s).wait_recv()
        m_relay(c, s).wait_recv()

    def m_done(c, s):
        pl.when(is_end)(lambda: m_whole(c, s).wait_send())

        @pl.when(is_mid)
        def _():
            m_half(c, s).wait_send()
            m_side(c, s).wait_send()
            m_back_mid(c, s).wait_send()
            m_back_pair(c, s).wait_send()
            m_store(c, s).wait()
            m_relay(c, s).wait_send()

    def e_start(c, s):
        e_load_near(c, s).start()
        pl.when(is_end)(lambda: e_far(c, s).start())
        pl.when(is_mid)(lambda: e_load_far(c, s).start())

    def e_one(c, s):
        e_load_far(c, s).wait()
        e_far(c, s).wait_recv()
        own_f[s] = own_f[s] + far_in[s]
        e_cross(c, s).start()

    def e_two(c, s):
        e_load_near(c, s).wait()
        e_cross(c, s).wait_recv()
        own_n[s] = own_n[s] + cross_in[s]
        e_near(c, s).start()

    def e_three(c, s):
        e_load_near(c, s).wait()
        e_near(c, s).wait_recv()
        own_n[s] = own_n[s] + near_in[s]
        e_end(c, s).start()

    def e_four(c, s):
        e_end(c, s).wait_recv()
        total_e[s] = own_n[s] + end_in[s]
        e_back_one(c, s).start()
        e_store(c, s).start()

    def e_five(c, s):
        e_back_one(c, s).wait_recv()
        e_back_two(c, s).start()

    def e_six(c, s):
        e_back_two(c, s).wait_recv()
        e_back_three(c, s).start()

    def e_seven(c, s):
        e_back_three(c, s).wait_recv()

    def e_done(c, s):
        @pl.when(is_end)
        def _():
            e_far(c, s).wait_send()
            e_end(c, s).wait_send()
            e_back_one(c, s).wait_send()
            e_store(c, s).wait()

        @pl.when(is_mid)
        def _():
            e_cross(c, s).wait_send()
            e_near(c, s).wait_send()
            e_back_two(c, s).wait_send()
            e_back_three(c, s).wait_send()

    def stage(step, offset, phase, guard, body):
        at = step - offset
        ok = (at >= 0) & (at < steps)
        if guard is not None:
            ok = ok & guard
        if phase is None:
            chunk, slots = at, SLOTS
        else:
            ok = ok & (lax.rem(at, ROUND) == phase)
            chunk, slots = at // ROUND, FEW

        @pl.when(ok)
        def _():
            body(chunk, lax.rem(chunk, slots))

    def tick(step):
        if not dp_sum:
            return
        stage(step, 0, None, None, a_start)
        stage(step, 0, 0, None, m_start)
        stage(step, 0, 1, None, e_start)
        stage(step, 6 * HOP, 1, is_mid, e_six)
        stage(step, 5 * HOP, 1, is_mid, e_five)
        stage(step, 4 * HOP, 1, is_end, e_four)
        stage(step, 4 * HOP, 0, is_mid, m_four)
        stage(step, 3 * HOP, None, is_mid, a_three)
        stage(step, 3 * HOP, 0, is_mid, m_three)
        stage(step, 4 * HOP, None, is_end, a_four)
        stage(step, 3 * HOP, 1, is_end, e_three)
        stage(step, 2 * HOP, None, is_mid, a_two)
        stage(step, 2 * HOP, 0, is_mid, m_two)
        stage(step, 2 * HOP, 1, is_mid, e_two)
        stage(step, HOP, None, None, a_one)
        stage(step, HOP, 0, is_mid, m_one)
        stage(step, HOP, 1, is_mid, e_one)
        stage(step, 5 * HOP, None, None, a_five)
        stage(step, 5 * HOP, 0, is_end, m_five)
        stage(step, 7 * HOP, 1, is_end, e_seven)
        stage(step, 5 * HOP + 1, None, None, a_done)
        stage(step, 5 * HOP + 1, 0, None, m_done)
        stage(step, 7 * HOP + 1, 1, None, e_done)

    return tick, greet


def tick_scratch(unit, width):
    many, few, double = (SLOTS, unit, width), (FEW, unit, width), (FEW, 2 * unit, width)
    shapes = [many] * 5 + [double, few, few, double, few] + [few] * 7
    buffers = [pltpu.VMEM(shape, jnp.float32) for shape in shapes]
    sems = [pltpu.SemaphoreType.DMA((2, SLOTS))] * 5 + [pltpu.SemaphoreType.DMA((2, FEW))] * 13
    sems += [pltpu.SemaphoreType.DMA((SLOTS,))] * 2 + [pltpu.SemaphoreType.DMA((FEW,))] * 5
    return buffers, sems


HEAD = 72
EPSILON = 1e-06
UNIT = 8
TAIL_ROWS = 8


FIRST = 1
PIECE = 16
LAG = 4
BLOCK = 128
WIDE_BLOCK = 192


def dot_nn(left, right):
    return lax.dot_general(left, right, (((1,), (0,)), ((), ())), preferred_element_type=jnp.float32)


def dot_nt(left, right):
    return lax.dot_general(left, right, (((1,), (1,)), ((), ())), preferred_element_type=jnp.float32)


def dot_tn(left, right):
    return lax.dot_general(left, right, (((0,), (0,)), ((), ())), preferred_element_type=jnp.float32)


def fold(array):
    return jnp.sum(array, axis=0, keepdims=True)


def gelu_slope(v):
    root = 0.7978845608028654
    inner = jnp.tanh(root * (v + 0.044715 * (v * v * v)))
    return 0.5 * (1.0 + inner) + 0.5 * v * (1.0 - inner * inner) * (root * (1.0 + 0.134145 * (v * v)))


def norm_back(grad_normed, state, gain):
    centred = state - jnp.mean(state, axis=-1, keepdims=True)
    inverse = lax.rsqrt(jnp.mean(centred * centred, axis=-1, keepdims=True) + EPSILON)
    unit = centred * inverse
    grad_unit = grad_normed * gain
    inner = (
        grad_unit
        - jnp.mean(grad_unit, axis=-1, keepdims=True)
        - unit * jnp.mean(grad_unit * unit, axis=-1, keepdims=True)
    )
    return inverse * inner, fold(grad_normed * unit), fold(grad_normed)


def backward_kernel(
    dp_sum, tokens, layers, heads, units_rows, head_dim, send_rows, unit, steps,
    cotangent, hidden, active, normed_two, normed, middle, state, qkv, logsum, mixed,
    down, up, qkv_w, out_w, gain, last_part,
    grads, totals, image_grad, encoded, down_grad, up_grad,
    raw_buf, wide, act_buf, two_buf, qkv_buf, lse_buf, mix_buf, down_buf, up_buf, qkvw_buf, outw_buf, gain_buf,
    flow, flow_low, hid_low, part, total, core_in, acc, y_in, grad_mix, cat, tight, acc_k, acc_v, stage_buf, small,
    woven, load_sem, stage_sem, turn_sem, weave_sem, core_send, core_recv, y_send, y_recv, back_send, back_recv,
    *tick_refs
):
    width = grads.shape[1]
    rows = part.shape[0]
    blocks = rows // BLOCK
    half = send_rows // 2
    pieces = half // PIECE
    tick, greet = grad_sum_ticks(
        dp_sum, unit, steps, grads, totals, tick_refs[:TICK_BUFFERS], tick_refs[TICK_BUFFERS:]
    )
    dp = lax.axis_index("dp")
    tensor = lax.axis_index("tensor")
    core = tensor % 2
    core_peer = (dp, tensor + 1 - 2 * core)
    y_peer = (dp, lax.rem(tensor + 2, 4))
    greet((core_peer, y_peer))
    layer_rows = grads.shape[0] // layers
    off_up = units_rows
    local_width = heads * head_dim
    off_qkv = 2 * units_rows
    off_out = off_qkv + 3 * local_width
    off_small = off_out + local_width
    spread = spread_matrix(heads, head_dim)

    def mine(i):
        return pl.ds(pl.multiple_of(core * half + i * PIECE, 8), PIECE)

    def other(i):
        return pl.ds(pl.multiple_of((1 - core) * half + i * PIECE, 8), PIECE)

    def here(i):
        return pl.ds(pl.multiple_of(i * PIECE, 8), PIECE)

    def remote(src, dst, send, recv, peer):
        return pltpu.make_async_remote_copy(
            src_ref=src, dst_ref=dst, send_sem=send, recv_sem=recv, device_id=peer, device_id_type=MESH
        )

    def to_core(p, i):
        return remote(
            part.at[other(i)], core_in.at[here(i)], core_send.at[p, i], core_recv.at[p, i], core_peer
        )

    def to_y(p, i):
        return remote(acc.at[here(i)], y_in.at[p, here(i)], y_send.at[p, i], y_recv.at[p, i], y_peer)

    def to_back(p, i):
        return remote(total.at[mine(i)], total.at[mine(i)], back_send.at[p, i], back_recv.at[p, i], core_peer)

    def from_back(p, i):
        return remote(
            total.at[other(i)], total.at[other(i)], back_send.at[p, i], back_recv.at[p, i], core_peer
        )

    def sum_begin(p):
        def go(i, c):
            to_core(p, i).start()
            return c

        lax.fori_loop(0, pieces, go, 0)

    def sum_step(p, j):
        @pl.when(j < pieces)
        def _():
            to_core(p, j).wait_recv()
            acc[here(j)] = part[mine(j)] + core_in[here(j)]
            to_y(p, j).start()

        late = j - LAG

        @pl.when((late >= 0) & (late < pieces))
        def _():
            to_y(p, late).wait_recv()
            total[mine(late)] = acc[here(late)] + y_in[p, here(late)]
            to_back(p, late).start()

        last = j - LAG - 2

        @pl.when((last >= 0) & (last < pieces))
        def _():
            to_core(p, last).wait_send()
            to_y(p, last).wait_send()
            to_back(p, last).wait_send()
            from_back(p, last).wait_recv()

    sum_steps = pieces + LAG + 2

    def load(source, target, sem):
        return pltpu.make_async_copy(source, target, load_sem.at[sem])

    def stage_copy(slot, row, size):
        return pltpu.make_async_copy(
            stage_buf.at[slot, pl.ds(0, size)], grads.at[pl.ds(pl.multiple_of(row, 8), size)], stage_sem.at[slot]
        )

    tiles = width // 128
    last_rows = units_rows - (tiles - 1) * 128
    layer_ticks = tiles + 1 + 4 * blocks + 2 * sum_steps + heads * blocks

    def row_block(b):
        return pl.ds(pl.multiple_of(b * BLOCK, 16), BLOCK)

    total[pl.ds(send_rows, rows - send_rows)] = jnp.zeros((rows - send_rows, width), jnp.float32)
    start = load(cotangent, raw_buf, 11)
    start.start()
    load(active.at[layers - 1], act_buf, 3).start()
    gain_load = load(gain, gain_buf, 10)
    gain_load.start()

    def layer_body(it, carry):
        layer = layers - 1 - it
        base_tick = it * layer_ticks - FIRST
        base_row = it * layer_rows
        hidden_load = load(hidden.at[layer], wide, 0)
        down_load = load(down.at[layer], down_buf, 1)
        up_load = load(up.at[layer], up_buf, 2)
        active_load = load(active.at[layer], act_buf, 3)
        two_load = load(normed_two.at[layer], two_buf, 4)
        outw_load = load(out_w.at[layer], outw_buf, 5)
        qkv_load = load(qkv.at[layer], qkv_buf, 6)
        lse_load = load(logsum.at[layer], lse_buf, 7)
        mix_load = load(mixed.at[layer], mix_buf, 8)
        qkvw_load = load(qkv_w.at[layer], qkvw_buf, 9)
        pl.when(it > 0)(active_load.start)
        small[...] = jnp.zeros_like(small)

        @pl.when(it == 0)
        def _():
            start.wait()
            lower_rows(raw_buf, flow_low, wide, tokens)

        def lower(b, c):
            at = row_block(b)
            flow_low[at] = flow[at].astype(jnp.bfloat16)
            return c

        @pl.when(it > 0)
        def _():
            lax.fori_loop(0, blocks, lower, 0)

        active_load.wait()
        for copy in (hidden_load, down_load, up_load, two_load, outw_load, qkv_load, lse_load, mix_load, qkvw_load):
            copy.start()

        def tile_copy(tile, row):
            slot = lax.rem(tile, 2)
            pl.when(tile < tiles - 1)(lambda: stage_copy(slot, row, 128).start())
            pl.when(tile == tiles - 1)(lambda: stage_copy(slot, row, last_rows).start())

        def tile_done(tile):
            slot = lax.rem(tile, 2)
            pl.when((tile >= 0) & (tile < tiles - 1))(lambda: stage_copy(slot, base_row, 128).wait())
            pl.when(tile == tiles - 1)(lambda: stage_copy(slot, base_row, last_rows).wait())

        def down_weights(j, c):
            tile_done(j - 1)

            @pl.when(j < tiles)
            def _():
                lanes = pl.ds(pl.multiple_of(j * 128, 128), 128)
                stage_buf[lax.rem(j, 2), pl.ds(0, 128)] = dot_tn(act_buf[:, lanes], flow_low[...])
                tile_copy(j, base_row + j * 128)

            tick(base_tick + j)
            return c

        lax.fori_loop(0, tiles + 1, down_weights, 0)
        tick_at = base_tick + tiles + 1

        @pl.when(it == 0)
        def _():
            gain_load.wait()
            lift_rows(raw_buf, flow, tokens, BLOCK)

        hidden_load.wait()
        down_load.wait()
        up_load.wait()

        def mlp(b, c):
            at = row_block(b)
            small[3:4] += fold(flow[at])
            grad_hidden = dot_nt(flow_low[at], down_buf[...]) * gelu_slope(wide[at])
            small[2:3] += fold(grad_hidden)
            hid = grad_hidden.astype(jnp.bfloat16)
            hid_low[at] = hid
            part[at] = dot_nn(hid, up_buf[...])
            tick(tick_at + b)
            return c

        lax.fori_loop(0, blocks, mlp, 0)
        sum_begin(0)
        middle_load = load(middle.at[layer], wide, 0)
        middle_load.start()
        two_load.wait()
        tick_at = tick_at + blocks

        def up_weights(j, c):
            sum_step(0, j)
            tile_done(j - 1)

            @pl.when(j < tiles)
            def _():
                lanes = pl.ds(pl.multiple_of(j * 128, 128), 128)
                stage_buf[lax.rem(j, 2), pl.ds(0, 128)] = dot_tn(hid_low[:, lanes], two_buf[...])
                tile_copy(j, base_row + off_up + j * 128)

            tick(tick_at + j)
            return c

        lax.fori_loop(0, sum_steps, up_weights, 0)
        tick_at = tick_at + sum_steps
        part_load = load(last_part, part, 1)
        pl.when(it == 0)(part_load.start)
        middle_load.wait()
        outw_load.wait()

        def norm_two(b, c):
            at = row_block(b)
            step_grad, gain_grad, shift_grad = norm_back(total[at], wide[at], gain_buf[layer, 1:2])
            small[5:6] += gain_grad
            small[7:8] += shift_grad
            grad = flow[at] + step_grad
            flow[at] = grad
            small[1:2] += fold(grad)
            low = grad.astype(jnp.bfloat16)
            flow_low[at] = low
            grad = dot_nt(low, outw_buf[...]).astype(jnp.bfloat16)
            grad_mix[at] = dot_nn(grad, spread).astype(jnp.bfloat16)
            tick(tick_at + b)
            return c

        lax.fori_loop(0, blocks, norm_two, 0)
        tick_at = tick_at + blocks
        state_load = load(state.at[layer], wide, 0)
        normed_load = load(normed.at[layer], act_buf, 3)
        state_load.start()
        normed_load.start()
        qkv_load.wait()
        lse_load.wait()
        scale = head_dim ** (-0.5)

        @pl.when(it == 0)
        def _():
            part_load.wait()
            sum_begin(2)


        def attend(m, c):
            head = m // blocks
            b = lax.rem(m, blocks)
            at = row_block(b)
            lanes = pl.ds(pl.multiple_of(head * 128, 128), 128)
            query = qkv_buf[0, head, at]
            key = qkv_buf[1, head]
            value = qkv_buf[2, head]
            grad = grad_mix[at, lanes]
            scores = dot_nt(query, key) * scale
            probs = jnp.exp(scores - lse_buf[head, at, 0:1])
            column = lax.broadcasted_iota(jnp.int32, probs.shape, 1)
            probs = jnp.where(column < tokens, probs, 0.0)
            grad_weights = dot_nt(grad, value)
            center = jnp.sum(probs * grad_weights, axis=-1, keepdims=True)
            raw = (probs * (grad_weights - center) * scale).astype(jnp.bfloat16)
            grad_query = dot_nn(raw, key)
            small[0:1, lanes] += fold(grad_query)
            cat[at, lanes] = grad_query.astype(jnp.bfloat16)
            add_k = dot_tn(raw, query)
            add_v = dot_tn(probs.astype(jnp.bfloat16), grad)

            @pl.when(b == 0)
            def _():
                acc_k[...] = add_k
                acc_v[...] = add_v

            @pl.when(b > 0)
            def _():
                acc_k[...] += add_k
                acc_v[...] += add_v

            @pl.when(b == blocks - 1)
            def _():
                at_k = pl.ds(pl.multiple_of((heads + head) * 128, 128), 128)
                at_v = pl.ds(pl.multiple_of((2 * heads + head) * 128, 128), 128)
                cat[:, at_k] = acc_k[...].astype(jnp.bfloat16)
                cat[:, at_v] = acc_v[...].astype(jnp.bfloat16)
                small[0:1, pl.ds(pl.multiple_of((heads + head) * 128, 128), 128)] += fold(acc_v[...])

            @pl.when(it == 0)
            def _():
                sum_step(2, 2 * m)
                sum_step(2, 2 * m + 1)

            tick(tick_at + m)
            return c

        lax.fori_loop(0, heads * blocks, attend, 0)
        tick_at = tick_at + heads * blocks
        qkvw_load.wait()

        def project(b, c):
            at = row_block(b)
            out = None
            for i in range(3):
                lanes = pl.ds(i * heads * 128, heads * 128)
                narrow = dot_nt(cat[at, lanes], spread).astype(jnp.bfloat16)
                tight[i, at] = narrow
                term = dot_nn(narrow, qkvw_buf[i])
                out = term if out is None else out + term
            part[at] = out

            @pl.when(it == 0)
            def _():
                hid_low[at] = total[at].astype(jnp.bfloat16)

            tick(tick_at + b)
            return c

        lax.fori_loop(0, blocks, project, 0)
        tick_at = tick_at + blocks
        sum_begin(1)
        encoded_store = load(hid_low, encoded, 1)
        pl.when(it == 0)(encoded_store.start)
        normed_load.wait()
        mix_load.wait()

        def attention_weights(j, c):
            sum_step(1, j)

            @pl.when((j >= 1) & (j < 5))
            def _():
                stage_copy(lax.rem(j - 1, 2), base_row, local_width).wait()

            slot = lax.rem(j, 2)

            @pl.when(j < 3)
            def _():
                stage_buf[slot] = dot_tn(tight[j], act_buf[...])

            @pl.when(j == 3)
            def _():
                stage_buf[slot] = dot_tn(mix_buf[...], flow_low[...])

            @pl.when(j < 4)
            def _():
                stage_copy(slot, base_row + off_qkv + j * local_width, local_width).start()

            tick(tick_at + j)
            return c

        lax.fori_loop(0, sum_steps, attention_weights, 0)
        tick_at = tick_at + sum_steps
        state_load.wait()

        def norm_one(b, c):
            at = row_block(b)
            step_grad, gain_grad, shift_grad = norm_back(total[at], wide[at], gain_buf[layer, 0:1])
            small[4:5] += gain_grad
            small[6:7] += shift_grad
            flow[at] = flow[at] + step_grad
            tick(tick_at + b)
            return c

        lax.fori_loop(0, blocks, norm_one, 0)
        tail = pltpu.make_async_copy(
            small, grads.at[pl.ds(pl.multiple_of(base_row + off_small, 8), small.shape[0])], load_sem.at[10]
        )
        tail.start()
        tail.wait()
        pl.when(it == 0)(encoded_store.wait)
        return carry

    lax.fori_loop(0, layers, layer_body, 0)

    def lower(b, c):
        flow_low[row_block(b)] = flow[row_block(b)].astype(jnp.bfloat16)
        return c

    lax.fori_loop(0, blocks, lower, 0)
    image_store = load(flow_low, image_grad, 0)
    image_store.start()

    tail = layers * layer_ticks - FIRST
    weaves, at_step = [], tail
    for k in range(2):
        last_row = (layers - 1) * layer_rows + (k + 1) * units_rows
        ready = -(-last_row // (PARTS * unit)) * ROUND + TICK_SPAN
        at_step = max(at_step, ready)
        weaves.append(at_step)
        at_step += tiles + 1

    def each_size(tile, body):
        pl.when(tile < tiles - 1)(lambda: body(128))
        pl.when(tile == tiles - 1)(lambda: body(last_rows))

    def weave_in(k, tile, layer, rows_here):
        row = pl.multiple_of((layers - 1 - layer) * layer_rows + k * units_rows + tile * 128, 8)
        slot = lax.rem(tile, 2)
        return pltpu.make_async_copy(
            totals.at[pl.ds(row, rows_here)],
            stage_buf.at[slot, pl.ds(layer * 128, rows_here)],
            weave_sem.at[slot, layer],
        )

    def weave_out(target, tile, rows_here):
        slot = lax.rem(tile, 2)
        return pltpu.make_async_copy(
            woven.at[slot, pl.ds(0, rows_here)], target.at[pl.ds(tile * 128, rows_here)], turn_sem.at[slot]
        )

    def weave(k, target, tile):
        def begin(rows_here):
            for layer in range(layers):
                weave_in(k, tile, layer, rows_here).start()

        def arrive(rows_here):
            for layer in range(layers):
                weave_in(k, tile - 1, layer, rows_here).wait()

        each_size(tile, begin)

        @pl.when(tile >= 1)
        def _():
            each_size(tile - 1, arrive)
            slot = lax.rem(tile - 1, 2)

            @pl.when(tile >= 3)
            def _():
                weave_out(target, tile - 3, 128).wait()

            for layer in range(layers):
                woven[slot, :, layer, :] = stage_buf[slot, pl.ds(layer * 128, 128)]
            each_size(tile - 1, lambda rows_here: weave_out(target, tile - 1, rows_here).start())

        @pl.when(tile == tiles)
        def _():
            weave_out(target, tiles - 2, 128).wait()
            weave_out(target, tiles - 1, last_rows).wait()

    def rest(step, c):
        tick(step)
        if dp_sum:
            for k, target in enumerate((down_grad, up_grad)):
                tile = step - weaves[k]

                @pl.when((tile >= 0) & (tile <= tiles))
                def _():
                    weave(k, target, tile)

        return c

    lax.fori_loop(tail, max(steps + TICK_SPAN, at_step), rest, 0)
    image_store.wait()


def backward(
    tokens, head_dim, hidden_units, unit, collective_id, dp_sum,
    cotangent, hidden, active, normed_two, normed, middle, state, qkv, logsum, mixed,
    down, up, qkv_w, out_w, gain, last_part,
):
    layers, rows, width = middle.shape
    heads = qkv.shape[2]
    units_rows = -(-hidden_units // 8) * 8
    send_rows = -(-tokens // (2 * PIECE)) * 2 * PIECE
    pieces = send_rows // (2 * PIECE)
    layer_rows = 2 * units_rows + 4 * heads * head_dim + TAIL_ROWS
    steps = layers * layer_rows // (PARTS * unit) * ROUND
    assert steps * PARTS * unit == layers * layer_rows * ROUND
    buffers, sems = tick_scratch(unit, width)
    f32, low = jnp.float32, jnp.bfloat16
    half = (send_rows // 2, width)
    full = (rows, width)
    any_spec = pl.BlockSpec(memory_space=pl.ANY)
    grads = jax.ShapeDtypeStruct((layers * layer_rows, width), f32)
    return pl.pallas_call(
        functools.partial(
            backward_kernel, dp_sum, tokens, layers, heads, units_rows, head_dim, send_rows, unit, steps
        ),
        out_shape=(
            grads,
            grads,
            jax.ShapeDtypeStruct(full, low),
            jax.ShapeDtypeStruct(full, low),
            jax.ShapeDtypeStruct((units_rows, layers, width), f32),
            jax.ShapeDtypeStruct((units_rows, layers, width), f32),
        ),
        in_specs=[any_spec] * 16,
        out_specs=(any_spec,) * 6,
        scratch_shapes=[
            pltpu.VMEM(cotangent.shape, low),
            pltpu.VMEM(full, f32),
            pltpu.VMEM(full, low),
            pltpu.VMEM(full, low),
            pltpu.VMEM(qkv.shape[1:], low),
            pltpu.VMEM(logsum.shape[1:], f32),
            pltpu.VMEM(mixed.shape[1:], low),
            pltpu.VMEM(down.shape[1:], low),
            pltpu.VMEM(up.shape[1:], low),
            pltpu.VMEM(qkv_w.shape[1:], low),
            pltpu.VMEM(out_w.shape[1:], low),
            pltpu.VMEM(gain.shape, f32),
            pltpu.VMEM(full, f32),
            pltpu.VMEM(full, low),
            pltpu.VMEM(full, low),
            pltpu.VMEM(full, f32),
            pltpu.VMEM(full, f32),
            pltpu.VMEM(half, f32),
            pltpu.VMEM(half, f32),
            pltpu.VMEM((3,) + half, f32),
            pltpu.VMEM((rows, heads * 128), low),
            pltpu.VMEM((rows, 3 * heads * 128), low),
            pltpu.VMEM((3, rows, heads * head_dim), low),
            pltpu.VMEM((rows, 128), f32),
            pltpu.VMEM((rows, 128), f32),
            pltpu.VMEM((2, heads * head_dim, width), f32),
            pltpu.VMEM((TAIL_ROWS, width), f32),
            pltpu.VMEM((2, 128, layers, width), f32),
        ]
        + [pltpu.SemaphoreType.DMA((12,)), pltpu.SemaphoreType.DMA((2,)), pltpu.SemaphoreType.DMA((2,)), pltpu.SemaphoreType.DMA((2, layers))]
        + [pltpu.SemaphoreType.DMA((3, pieces))] * 6
        + buffers
        + sems,
        compiler_params=pltpu.CompilerParams(
            collective_id=collective_id, has_side_effects=True, vmem_limit_bytes=63 << 20
        ),
    )(
        cotangent, hidden, active, normed_two, normed, middle, state, qkv, logsum, mixed,
        down, up, qkv_w, out_w, gain, last_part,
    )


def lift_rows(source, target, tokens, size):
    blocks = target.shape[0] // size

    def one(b, c):
        at = pl.ds(pl.multiple_of(b * size, 16), size)
        target[at] = source[at].astype(jnp.float32)
        return c

    lax.fori_loop(0, blocks - 1, one, 0)
    begin = (blocks - 1) * size
    target[pl.ds(begin, size)] = jnp.zeros((size, target.shape[1]), jnp.float32)
    last = pl.ds(begin, tokens - begin)
    target[last] = source[last].astype(jnp.float32)


def lower_rows(source, target, wide, tokens):
    full = tokens // BLOCK

    def one(b, c):
        at = pl.ds(pl.multiple_of(b * BLOCK, 16), BLOCK)
        target[at] = source[at]
        return c

    lax.fori_loop(0, full, one, 0)
    tail = pl.ds(full * BLOCK, target.shape[0] - full * BLOCK)
    wide[tail] = jnp.zeros((target.shape[0] - full * BLOCK, target.shape[1]), jnp.float32)
    some = pl.ds(full * BLOCK, tokens - full * BLOCK)
    wide[some] = source[some].astype(jnp.float32)
    target[tail] = wide[tail].astype(jnp.bfloat16)


def spread_matrix(heads, head_dim):
    shape = (heads * head_dim, heads * 128)
    source = lax.broadcasted_iota(jnp.int32, shape, 0)
    lane = lax.broadcasted_iota(jnp.int32, shape, 1)
    hit = (lane // 128 * head_dim + lane % 128 == source) & (lane % 128 < head_dim)
    return jnp.where(hit, 1.0, 0.0).astype(jnp.bfloat16)


def norm_unit(state):
    centred = state - jnp.mean(state, axis=-1, keepdims=True)
    return centred * lax.rsqrt(jnp.mean(centred * centred, axis=-1, keepdims=True) + EPSILON)


def gelu(v):
    return 0.5 * v * (1.0 + jnp.tanh(0.7978845608028654 * (v + 0.044715 * (v * v * v))))


def block_sum(pieces, dp, tensor, part, core_in, y_in, total, sems):
    core = tensor % 2
    core_peer = (dp, tensor + 1 - 2 * core)
    y_peer = (dp, lax.rem(tensor + 2, 4))
    core_sem, y_sem, back_sem = sems
    per_block = WIDE_BLOCK // (2 * PIECE)

    def mine(i):
        return pl.ds(pl.multiple_of((2 * i + core) * PIECE, 8), PIECE)

    def other(i):
        return pl.ds(pl.multiple_of((2 * i + 1 - core) * PIECE, 8), PIECE)

    def here(i):
        return pl.ds(pl.multiple_of(i * PIECE, 8), PIECE)

    def remote(src, dst, sem, i, peer):
        return pltpu.make_async_remote_copy(
            src_ref=src, dst_ref=dst, send_sem=sem.at[0, i], recv_sem=sem.at[1, i],
            device_id=peer, device_id_type=MESH,
        )

    def to_core(i):
        return remote(part.at[other(i)], core_in.at[here(i)], core_sem, i, core_peer)

    def to_y(i):
        return remote(core_in.at[here(i)], y_in.at[here(i)], y_sem, i, y_peer)

    def to_back(i):
        return remote(total.at[mine(i)], total.at[mine(i)], back_sem, i, core_peer)

    def from_back(i):
        return remote(total.at[other(i)], total.at[other(i)], back_sem, i, core_peer)

    def each(b, body):
        def go(k, c):
            i = b * per_block + k

            @pl.when(i < pieces)
            def _():
                body(i)

            return c

        lax.fori_loop(0, per_block, go, 0)

    def send(b):
        each(b, lambda i: to_core(i).start())

    def meet(b):
        def body(i):
            to_core(i).wait_recv()
            core_in[here(i)] = core_in[here(i)] + part[mine(i)]
            to_y(i).start()

        each(b, body)

    def close(b):
        def body(i):
            to_y(i).wait_recv()
            total[mine(i)] = core_in[here(i)] + y_in[here(i)]
            to_back(i).start()

        each(b, body)

    def finish(b):
        def body(i):
            to_core(i).wait_send()
            to_y(i).wait_send()
            to_back(i).wait_send()
            from_back(i).wait_recv()

        each(b, body)

    return send, meet, close, finish


def forward_kernel(
    tokens, layers, heads, head_dim, send_rows,
    images, qkv_w, qv_b, out_w, out_b, up, up_b, down, down_b, gain, shift,
    hidden, active, normed_two, normed, middle, state, qkv, logsum, mixed, down_rows, up_rows, last_part,
    image_buf, upb_raw, flow, normed_buf, qkv_buf, lse_buf, mix_buf, tight_buf, two_buf, hidden_buf, active_buf,
    qkvw_buf, outw_buf, up_buf, down_buf, qvb_buf, outb_buf, upb_buf, downb_buf, gain_buf, shift_buf,
    part_a, core_in_a, y_in_a, total_a, part_b, core_in_b, y_in_b, total_b,
    pair_buf, split_buf, edge_buf, load_sem, weight_sem, store_sem, block_sem, split_sem, split_out_sem, *sum_sems
):
    rows, width = flow.shape
    blocks = rows // WIDE_BLOCK
    pieces = send_rows // (2 * PIECE)
    dp = lax.axis_index("dp")
    tensor = lax.axis_index("tensor")
    core = tensor % 2
    barrier = pltpu.get_barrier_semaphore()
    for peer in ((dp, tensor + 1 - 2 * core), (dp, lax.rem(tensor + 2, 4))):
        pl.semaphore_signal(barrier, inc=1, device_id=peer, device_id_type=MESH)

    def weights(layer):
        return (
            pltpu.make_async_copy(qkv_w.at[layer], qkvw_buf, weight_sem.at[0]),
            pltpu.make_async_copy(out_w.at[layer], outw_buf, weight_sem.at[1]),
            pltpu.make_async_copy(up_rows.at[layer], up_buf, weight_sem.at[2]),
            pltpu.make_async_copy(down_rows.at[layer], down_buf, weight_sem.at[3]),
        )

    tiles = up_buf.shape[0] // 128
    units = up.shape[0]
    last_units = units - (tiles - 1) * 128

    def split_in(k, tile, size):
        slot = lax.rem(k * tiles + tile, 2)
        source = (up, down)[k]
        return pltpu.make_async_copy(
            source.at[pl.ds(tile * 128, size)], pair_buf.at[slot, pl.ds(0, size)], split_sem.at[0, slot]
        )

    def split_size(tile, body):
        pl.when(tile < tiles - 1)(lambda: body(128))
        pl.when(tile == tiles - 1)(lambda: body(last_units))

    def split_out(k, tile, layer):
        slot = lax.rem(k * tiles + tile, 2)
        target = (up_rows, down_rows)[k]
        return pltpu.make_async_copy(
            split_buf.at[slot, layer], target.at[layer, pl.ds(pl.multiple_of(tile * 128, 128), 128)],
            split_out_sem.at[slot, layer],
        )

    def split(k):
        first_buf = (up_buf, down_buf)[k]

        def one(tile, c):
            slot = lax.rem(k * tiles + tile, 2)
            pl.when(tile + 1 < tiles)(lambda: split_size(tile + 1, lambda size: split_in(k, tile + 1, size).start()))
            if k == 0:
                pl.when(tile == tiles - 1)(lambda: split_in(1, 0, 128).start())
            split_size(tile, lambda size: split_in(k, tile, size).wait())
            for layer in range(layers):
                if k == 0:
                    pl.when(tile >= 2)(lambda: split_out(k, tile - 2, layer).wait())
                else:
                    pl.when(tile >= 2)(lambda: split_out(k, tile - 2, layer).wait())
                    pl.when(tile < 2)(lambda: split_out(0, tile + tiles - 2, layer).wait())

                @pl.when(tile < tiles - 1)
                def _():
                    split_buf[slot, layer] = pair_buf[slot, :, layer, :]

                @pl.when(tile == tiles - 1)
                def _():
                    edge_buf[...] = jnp.zeros_like(edge_buf)
                    edge_buf[pl.ds(0, last_units)] = pair_buf[slot, pl.ds(0, last_units), layer, :].astype(jnp.float32)
                    split_buf[slot, layer] = edge_buf[...].astype(jnp.bfloat16)

                split_out(k, tile, layer).start()
            first_buf[pl.ds(pl.multiple_of(tile * 128, 128), 128)] = split_buf[slot, 0]
            return c

        lax.fori_loop(0, tiles, one, 0)

    singles = [
        pltpu.make_async_copy(source, target, load_sem.at[i])
        for i, (source, target) in enumerate(
            (
                (images, image_buf), (gain, gain_buf), (shift, shift_buf), (qv_b, qvb_buf),
                (out_b, outb_buf), (up_b, upb_raw), (down_b, downb_buf),
            )
        )
    ]
    for copy in singles:
        copy.start()
    current = weights(0)
    current[0].start()
    current[1].start()
    split_in(0, 0, 128).start()
    spread = spread_matrix(heads, head_dim)
    total_a[pl.ds(send_rows, rows - send_rows)] = jnp.zeros((rows - send_rows, width), jnp.float32)
    total_b[pl.ds(send_rows, rows - send_rows)] = jnp.zeros((rows - send_rows, width), jnp.float32)
    for copy in singles:
        copy.wait()
    pl.semaphore_wait(barrier, 2)

    def row_block(b):
        return pl.ds(pl.multiple_of(b * WIDE_BLOCK, 16), WIDE_BLOCK)

    scale = head_dim ** (-0.5)
    stores = {}

    def block_store(layer, b, kind):
        at = row_block(b)
        source, target = (
            (flow, middle.at[layer, at]),
            (two_buf, normed_two.at[layer, at]),
            (hidden_buf, hidden.at[layer, at]),
            (active_buf, active.at[layer, at]),
            (part_b, last_part.at[at]),
        )[kind]
        return pltpu.make_async_copy(source.at[at], target, block_sem.at[kind, b])

    def keep(name, source, target, index):
        copy = pltpu.make_async_copy(source, target, store_sem.at[index])
        copy.start()
        stores[name] = copy

    def settle(*names):
        for name in names:
            if name in stores:
                stores.pop(name).wait()

    def project(layer, b, value):
        at = row_block(b)
        flow[at] = value
        low = (norm_unit(value) * gain_buf[layer, 0:1] + shift_buf[layer, 0:1]).astype(jnp.bfloat16)
        normed_buf[at] = low
        for i in range(3):
            out = dot_nt(low, qkvw_buf[i])
            if i != 1:
                out = out + qvb_buf[layer, i // 2 : i // 2 + 1]
            wide = dot_nn(out.astype(jnp.bfloat16), spread).astype(jnp.bfloat16)
            for head in range(heads):
                qkv_buf[i, head, at] = wide[:, head * 128 : (head + 1) * 128]

    def first(b, c):
        project(0, b, flow[row_block(b)])
        return c

    lift_rows(image_buf, flow, tokens, WIDE_BLOCK)
    upb_buf[...] = jnp.zeros_like(upb_buf)
    upb_buf[:, pl.ds(0, upb_raw.shape[1])] = upb_raw[...]
    current[0].wait()
    lax.fori_loop(0, blocks, first, 0)

    for layer in range(layers):
        keep("state", flow, state.at[layer], 0)
        keep("normed", normed_buf, normed.at[layer], 1)
        keep("qkv", qkv_buf, qkv.at[layer], 2)
        settle("logsum", "mixed")
        send_a, meet_a, close_a, finish_a = block_sum(
            pieces, dp, tensor, part_a, core_in_a, y_in_a, total_a, [s.at[layer] for s in sum_sems[:3]]
        )
        send_b, meet_b, close_b, finish_b = block_sum(
            pieces, dp, tensor, part_b, core_in_b, y_in_b, total_b, [s.at[layer] for s in sum_sems[3:]]
        )
        is_last = layer == layers - 1
        if not is_last:
            following = weights(layer + 1)
            following[0].start()

        current[1].wait()

        def attend(b, c):
            at = row_block(b)

            def one_head(head, c):
                scores = dot_nt(qkv_buf[0, head, at], qkv_buf[1, head]) * scale
                column = lax.broadcasted_iota(jnp.int32, scores.shape, 1)
                scores = jnp.where(column < tokens, scores, -jnp.inf)
                peak = jnp.max(scores, axis=-1, keepdims=True)
                expo = jnp.exp(scores - peak)
                denominator = jnp.sum(expo, axis=-1, keepdims=True)
                probs = (expo / denominator).astype(jnp.bfloat16)
                lanes = pl.ds(pl.multiple_of(head * 128, 128), 128)
                mix_buf[:, lanes] = dot_nn(probs, qkv_buf[2, head]).astype(jnp.bfloat16)
                lse_buf[head, at] = jnp.broadcast_to(peak + jnp.log(denominator), (WIDE_BLOCK, 128))
                return c

            lax.fori_loop(0, heads, one_head, 0)
            tight = dot_nt(mix_buf[...], spread).astype(jnp.bfloat16)
            tight_buf[at] = tight
            part_a[at] = dot_nn(tight, outw_buf[...])
            send_a(b)

            @pl.when(b > 0)
            def _():
                meet_a(b - 1)

            return c

        lax.fori_loop(0, blocks, attend, 0)
        meet_a(blocks - 1)
        keep("logsum", lse_buf, logsum.at[layer], 3)
        keep("mixed", tight_buf, mixed.at[layer], 4)
        if not is_last:
            following[1].start()

        settle("state")
        if layer == 0:
            split(0)
            split(1)
        else:
            current[2].wait()
            current[3].wait()

        def mlp(b, c):
            at = row_block(b)
            close_a(b)
            if not is_last:

                @pl.when(b > 0)
                def _():
                    meet_b(b - 1)

            finish_a(b)
            value = flow[at] + total_a[at] + outb_buf[layer : layer + 1]
            flow[at] = value
            block_store(layer, b, 0).start()
            low = (norm_unit(value) * gain_buf[layer, 1:2] + shift_buf[layer, 1:2]).astype(jnp.bfloat16)
            two_buf[at] = low
            hid = dot_nt(low, up_buf[...]) + upb_buf[layer : layer + 1]
            hidden_buf[at] = hid
            act = gelu(hid).astype(jnp.bfloat16)
            active_buf[at] = act
            partial = dot_nn(act, down_buf[...])
            if is_last:
                lead = jnp.where(tensor == 0, 1.0, 0.0)
                partial = partial + lead * (value + downb_buf[layer : layer + 1])
            part_b[at] = partial
            for kind in range(1, 5 if is_last else 4):
                block_store(layer, b, kind).start()
            if not is_last:
                send_b(b)
            return c

        lax.fori_loop(0, blocks, mlp, 0)

        def stored(*kinds):
            def one(b, c):
                for kind in kinds:
                    block_store(layer, b, kind).wait()
                return c

            lax.fori_loop(0, blocks, one, 0)

        if is_last:
            stored(0, 1, 2, 3, 4)
        else:
            for tile in (tiles - 2, tiles - 1):
                for l in range(layers):
                    split_out(1, tile, l).wait()
            following[2].start()
            following[3].start()
            following[0].wait()
            meet_b(blocks - 1)
            settle("normed", "qkv")

            def next_project(b, c):
                at = row_block(b)
                close_b(b)
                finish_b(b)
                block_store(layer, b, 0).wait()
                project(layer + 1, b, flow[at] + total_b[at] + downb_buf[layer : layer + 1])
                return c

            lax.fori_loop(0, blocks, next_project, 0)
            stored(1, 2, 3)
            current = following
    settle(*list(stores))


def forward(
    tokens, head_dim, collective_id,
    images, qkv_w, qv_b, out_w, out_b, up, up_b, down, down_b, gain, shift,
):
    layers = qkv_w.shape[0]
    width = images.shape[1]
    rows = -(-tokens // WIDE_BLOCK) * WIDE_BLOCK
    heads = qkv_w.shape[2] // head_dim
    units = -(-up.shape[0] // 128) * 128
    send_rows = -(-tokens // (2 * PIECE)) * 2 * PIECE
    pieces = send_rows // (2 * PIECE)
    f32, low = jnp.float32, jnp.bfloat16
    full = (rows, width)
    half = (send_rows // 2, width)
    any_spec = pl.BlockSpec(memory_space=pl.ANY)

    def out(shape, dtype):
        return jax.ShapeDtypeStruct(shape, dtype)

    lanes = heads * 128
    return pl.pallas_call(
        functools.partial(forward_kernel, tokens, layers, heads, head_dim, send_rows),
        out_shape=(
            out((layers, rows, units), f32),
            out((layers, rows, units), low),
            out((layers,) + full, low),
            out((layers,) + full, low),
            out((layers,) + full, f32),
            out((layers,) + full, f32),
            out((layers, 3, heads, rows, 128), low),
            out((layers, heads, rows, 128), f32),
            out((layers, rows, heads * head_dim), low),
            out((layers, units, width), low),
            out((layers, units, width), low),
            out(full, f32),
        ),
        in_specs=[any_spec] * 11,
        out_specs=(any_spec,) * 12,
        scratch_shapes=[
            pltpu.VMEM(images.shape, low),
            pltpu.VMEM(up_b.shape, f32),
            pltpu.VMEM(full, f32),
            pltpu.VMEM(full, low),
            pltpu.VMEM((3, heads, rows, 128), low),
            pltpu.VMEM((heads, rows, 128), f32),
            pltpu.VMEM((WIDE_BLOCK, lanes), low),
            pltpu.VMEM((rows, heads * head_dim), low),
            pltpu.VMEM(full, low),
            pltpu.VMEM((rows, units), f32),
            pltpu.VMEM((rows, units), low),
            pltpu.VMEM(qkv_w.shape[1:], low),
            pltpu.VMEM(out_w.shape[1:], low),
            pltpu.VMEM((units, width), low),
            pltpu.VMEM((units, width), low),
            pltpu.VMEM(qv_b.shape, f32),
            pltpu.VMEM(out_b.shape, f32),
            pltpu.VMEM((layers, units), f32),
            pltpu.VMEM(down_b.shape, f32),
            pltpu.VMEM(gain.shape, f32),
            pltpu.VMEM(shift.shape, f32),
        ]
        + [pltpu.VMEM(s, f32) for s in (full, half, half, full)] * 2
        + [
            pltpu.VMEM((2, 128, layers, width), low),
            pltpu.VMEM((2, layers, 128, width), low),
            pltpu.VMEM((128, width), f32),
            pltpu.SemaphoreType.DMA((7,)),
            pltpu.SemaphoreType.DMA((4,)),
            pltpu.SemaphoreType.DMA((9,)),
            pltpu.SemaphoreType.DMA((5, rows // WIDE_BLOCK)),
            pltpu.SemaphoreType.DMA((1, 2)),
            pltpu.SemaphoreType.DMA((2, layers)),
        ]
        + [pltpu.SemaphoreType.DMA((layers, 2, pieces))] * 6,
        compiler_params=pltpu.CompilerParams(
            collective_id=collective_id, has_side_effects=True, vmem_limit_bytes=63 << 20
        ),
    )(images, qkv_w, qv_b, out_w, out_b, up, up_b, down, down_b, gain, shift)


def finish_kernel(
    layers, heads, head_dim, hidden_units, layer_rows, off_qkv,
    totals, down_rows, up_rows, image_rows, encoded_rows,
    encoded, image_grad, qkv_grad, qv_grad, out_grad, out_b, up_grad, up_b, down_grad, down_b, gain, shift,
    down_buf, up_wide, rows_buf, long_a, long_b, short_a, short_b, small, qv_buf, up_buf, plain, pair, sem,
):
    width = totals.shape[1]
    local_width = heads * head_dim
    count = [0]

    def move(source, target):
        copy = pltpu.make_async_copy(source, target, sem.at[count[0]])
        count[0] += 1
        copy.start()
        return copy

    small_rows = small.shape[1]
    off_small = off_qkv + 4 * local_width
    firsts = [(layers - 1 - l) * layer_rows for l in range(layers)]
    fetch = [move(totals.at[pl.ds(firsts[l] + off_small, small_rows)], small.at[l]) for l in range(layers)]
    fetch_a = move(encoded_rows, long_a)
    fetch_b = move(image_rows, long_b)
    through = []
    for source, buffer, target in ((down_rows, down_buf, down_grad), (up_rows, up_wide, up_grad)):
        for at in range(0, hidden_units, 128):
            here = pl.ds(at, min(128, hidden_units - at))
            through.append((move(source.at[here], buffer.at[here]), buffer.at[here], target.at[here]))
    for l in range(layers):
        begin = firsts[l] + off_qkv
        for i in range(4):
            rows = pl.ds(begin + i * local_width, local_width)
            target = qkv_grad.at[l, i] if i < 3 else out_grad.at[l]
            through.append((move(totals.at[rows], rows_buf.at[l, i]), rows_buf.at[l, i], target))
    moves = []
    for arrived, buffer, target in through:
        arrived.wait()
        moves.append(move(buffer, target))
    for copy in fetch:
        copy.wait()
    for l in range(layers):
        for i in range(2):
            for h in range(heads):
                lane = (i * heads + h) * 128
                qv_buf[l, i : i + 1, h * head_dim : (h + 1) * head_dim] = small[l, 0:1, lane : lane + head_dim]
        plain[0, l : l + 1] = small[l, 1:2]
        up_buf[l : l + 1] = small[l, 2:3, :hidden_units]
        plain[1, l : l + 1] = small[l, 3:4]
        pair[0, l] = small[l, 4:6]
        pair[1, l] = small[l, 6:8]
    moves += [
        move(qv_buf, qv_grad), move(plain.at[0], out_b), move(up_buf, up_b), move(plain.at[1], down_b),
        move(pair.at[0], gain), move(pair.at[1], shift),
    ]
    tokens = short_a.shape[0]
    fetch_a.wait()
    short_a[...] = long_a[:tokens]
    moves.append(move(short_a, encoded))
    fetch_b.wait()
    short_b[...] = long_b[:tokens]
    moves.append(move(short_b, image_grad))
    for copy in moves:
        copy.wait()


def finish(tokens, heads, head_dim, hidden_units, totals, down_rows, up_rows, image_rows, encoded_rows):
    layers = down_rows.shape[1]
    width = totals.shape[1]
    rows = image_rows.shape[0]
    layer_rows = totals.shape[0] // layers
    off_qkv = 2 * down_rows.shape[0]
    local_width = heads * head_dim
    f32, low = jnp.float32, jnp.bfloat16
    any_spec = pl.BlockSpec(memory_space=pl.ANY)

    def out(shape, dtype=f32):
        return jax.ShapeDtypeStruct(shape, dtype)

    copies = 4 * -(-hidden_units // 128) + 9 * layers + 10
    return pl.pallas_call(
        functools.partial(finish_kernel, layers, heads, head_dim, hidden_units, layer_rows, off_qkv),
        out_shape=(
            out((tokens, width), low),
            out((tokens, width), low),
            out((layers, 3, local_width, width)),
            out((layers, 2, local_width)),
            out((layers, local_width, width)),
            out((layers, width)),
            out((hidden_units, layers, width)),
            out((layers, hidden_units)),
            out((hidden_units, layers, width)),
            out((layers, width)),
            out((layers, 2, width)),
            out((layers, 2, width)),
        ),
        in_specs=[any_spec] * 5,
        out_specs=(any_spec,) * 12,
        scratch_shapes=[
            pltpu.VMEM((hidden_units, layers, width), f32),
            pltpu.VMEM((hidden_units, layers, width), f32),
            pltpu.VMEM((layers, 4, local_width, width), f32),
            pltpu.VMEM((rows, width), low),
            pltpu.VMEM((rows, width), low),
            pltpu.VMEM((tokens, width), low),
            pltpu.VMEM((tokens, width), low),
            pltpu.VMEM((layers, TAIL_ROWS, width), f32),
            pltpu.VMEM((layers, 2, local_width), f32),
            pltpu.VMEM((layers, hidden_units), f32),
            pltpu.VMEM((2, layers, width), f32),
            pltpu.VMEM((2, layers, 2, width), f32),
            pltpu.SemaphoreType.DMA((copies,)),
        ],
        compiler_params=pltpu.CompilerParams(has_side_effects=True, vmem_limit_bytes=56 << 20),
    )(totals, down_rows, up_rows, image_rows, encoded_rows)


def local(
    dp_size,
    images,
    qkv_weight,
    qv_bias,
    out_weight,
    out_bias,
    up_weight,
    up_bias,
    down_weight,
    down_bias,
    norm_gain,
    norm_shift,
    cotangent,
):
    tokens, width = images.shape[1:]
    layers = qkv_weight.shape[0]
    local_width = qkv_weight.shape[3]
    heads = local_width // HEAD
    hidden_units = up_weight.shape[2]
    qkv_rows = jnp.swapaxes(qkv_weight, 2, 3)
    up = jnp.transpose(up_weight, (2, 0, 1))
    down = jnp.swapaxes(down_weight, 0, 1)
    *kept, last_part = forward(
        tokens, HEAD, 0,
        images[0], qkv_rows, qv_bias, out_weight, out_bias, up, up_bias, down, down_bias,
        norm_gain, norm_shift,
    )
    flat, summed, image_grad, encoded, down_rows, up_rows = backward(
        tokens, HEAD, hidden_units, UNIT, 1, dp_size == 8,
        cotangent[0], *kept, qkv_rows, out_weight, norm_gain, last_part,
    )
    if dp_size != 8:
        summed = lax.psum(flat, "dp")
        per_layer = summed.reshape(layers, summed.shape[0] // layers, width)[::-1]
        stop = down_rows.shape[0]
        down_rows = jnp.swapaxes(per_layer[:, :stop], 0, 1)
        up_rows = jnp.swapaxes(per_layer[:, stop : 2 * stop], 0, 1)
    encoded, image_grad, qkv_grad, qv_grad, out_grad, out_b, up_grad, up_b, down_grad, down_b, gain, shift = finish(
        tokens, heads, HEAD, hidden_units, summed, down_rows, up_rows, image_grad, encoded
    )
    return (
        encoded[None],
        image_grad[None],
        jnp.swapaxes(qkv_grad, 2, 3),
        qv_grad,
        out_grad,
        out_b,
        jnp.transpose(up_grad, (1, 2, 0)),
        up_b,
        jnp.swapaxes(down_grad, 0, 1),
        down_b,
        gain,
        shift,
    )


def solution(mesh):
    in_specs = (
        P("dp", None, None),
        P(None, None, None, "tensor"),
        P(None, None, "tensor"),
        P(None, "tensor", None),
        P(),
        P(None, None, "tensor"),
        P(None, "tensor"),
        P(None, "tensor", None),
        P(),
        P(),
        P(),
        P("dp", None, None),
    )
    out_specs = (
        P("dp", None, None),
        P("dp", None, None),
        P(None, None, None, "tensor"),
        P(None, None, "tensor"),
        P(None, "tensor", None),
        P(),
        P(None, None, "tensor"),
        P(None, "tensor"),
        P(None, "tensor", None),
        P(),
        P(),
        P(),
    )
    return jax.shard_map(
        functools.partial(local, mesh.shape["dp"]), mesh=mesh, in_specs=in_specs, out_specs=out_specs, check_vma=False)
```

```python
import functools

import jax
import jax.numpy as jnp
from jax import lax
from jax.experimental import pallas as pl
from jax.experimental.pallas import tpu as pltpu
from jax.sharding import PartitionSpec as P

MESH = pl.DeviceIdType.MESH
SLOTS = 24
FEW = 8
HOP = 3
ROUND = 3
PARTS = 10
TICK_SPAN = 7 * HOP + 2
TICK_BUFFERS = 17


def grad_sum_ticks(dp_sum, unit, steps, grads, totals, buffers, sems):
    (
        x_in, inner_in, mid_in, own_a, total_a,
        whole_in, half_in, side_in, own_b, total_b,
        far_in, cross_in, near_in, end_in, own_f, own_n, total_e,
    ) = buffers
    (
        x_sem, inner_sem, mid_sem, out_pair_sem, out_x_sem,
        whole_sem, half_sem, side_sem, back_mid_sem, back_pair_sem, relay_sem,
        far_sem, cross_sem, near_sem, end_sem, back_one_sem, back_two_sem, back_three_sem,
        load_a_sem, store_a_sem, load_b_sem, store_b_sem, load_f_sem, load_n_sem, store_e_sem,
    ) = sems
    dp = lax.axis_index("dp")
    tensor = lax.axis_index("tensor")
    z = dp // 2
    x = dp % 2
    is_mid = (z == 1) | (z == 2)
    is_end = jnp.logical_not(is_mid)
    x_peer = (dp + 1 - 2 * x, tensor)
    pair_peer = (dp + 2 - 4 * (z % 2), tensor)
    mid_z = jnp.where(is_mid, 3 - z, z)
    mid_peer = (mid_z * 2 + x, tensor)
    side = jnp.where(z == 2, 1, 0)
    near = jnp.where(z >= 2, 1, 0)

    def greet(others):
        barrier = pltpu.get_barrier_semaphore()
        for peer in others:
            pl.semaphore_signal(barrier, inc=1, device_id=peer, device_id_type=MESH)
        if not dp_sum:
            pl.semaphore_wait(barrier, len(others))
            return
        for peer in (x_peer, pair_peer):
            pl.semaphore_signal(barrier, inc=1, device_id=peer, device_id_type=MESH)

        @pl.when(is_mid)
        def _():
            pl.semaphore_signal(barrier, inc=1, device_id=mid_peer, device_id_type=MESH)
            pl.semaphore_wait(barrier, 3 + len(others))

        @pl.when(is_end)
        def _():
            pl.semaphore_wait(barrier, 2 + len(others))

    def rows(chunk, part, count=1):
        return pl.ds(pl.multiple_of((chunk * PARTS + part) * unit, 8), count * unit)

    def row_a(c, part):
        return rows(c // ROUND, 2 * lax.rem(c, ROUND) + part)

    def row_m(c, part, count=1):
        return rows(c, 6 + part, count)

    def row_e(c, part):
        return rows(c, 8 + part)

    def remote(src, dst, sem, slot, peer):
        return pltpu.make_async_remote_copy(
            src_ref=src, dst_ref=dst, send_sem=sem.at[0, slot], recv_sem=sem.at[1, slot],
            device_id=peer, device_id_type=MESH,
        )

    def local_copy(src, dst, sem, slot):
        return pltpu.make_async_copy(src, dst, sem.at[slot])

    def a_x(c, s):
        return remote(grads.at[row_a(c, 1 - x)], x_in.at[s], x_sem, s, x_peer)

    def a_load(c, s):
        return local_copy(grads.at[row_a(c, x)], own_a.at[s], load_a_sem, s)

    def a_inner(c, s):
        return remote(own_a.at[s], inner_in.at[s], inner_sem, s, pair_peer)

    def a_mid(c, s):
        return remote(own_a.at[s], mid_in.at[s], mid_sem, s, mid_peer)

    def a_out_pair(c, s):
        return remote(total_a.at[s], totals.at[row_a(c, x)], out_pair_sem, s, pair_peer)

    def a_out_x(c, s):
        return remote(total_a.at[s], totals.at[row_a(c, x)], out_x_sem, s, x_peer)

    def a_store(c, s):
        return local_copy(total_a.at[s], totals.at[row_a(c, x)], store_a_sem, s)

    def a_relay(c, s):
        return remote(totals.at[row_a(c, x)], totals.at[row_a(c, x)], out_x_sem, s, x_peer)

    def a_back(c, s):
        return remote(totals.at[row_a(c, x)], totals.at[row_a(c, 1 - x)], out_x_sem, s, x_peer)

    def m_whole(c, s):
        return remote(grads.at[row_m(c, 0, 2)], whole_in.at[s], whole_sem, s, pair_peer)

    def m_load(c, s):
        return local_copy(grads.at[row_m(c, 0, 2)], own_b.at[s], load_b_sem, s)

    def m_half(c, s):
        return remote(own_b.at[s, pl.ds((1 - side) * unit, unit)], half_in.at[s], half_sem, s, mid_peer)

    def m_side(c, s):
        return remote(own_b.at[s, pl.ds(side * unit, unit)], side_in.at[s], side_sem, s, x_peer)

    def m_store(c, s):
        return local_copy(total_b.at[s], totals.at[row_m(c, side)], store_b_sem, s)

    def m_back_mid(c, s):
        return remote(total_b.at[s], totals.at[row_m(c, side)], back_mid_sem, s, mid_peer)

    def m_back_pair(c, s):
        return remote(total_b.at[s], totals.at[row_m(c, side)], back_pair_sem, s, pair_peer)

    def m_relay(c, s):
        return remote(totals.at[row_m(c, 1 - side)], totals.at[row_m(c, 1 - side)], relay_sem, s, pair_peer)

    def e_far(c, s):
        return remote(grads.at[row_e(c, 1 - near)], far_in.at[s], far_sem, s, pair_peer)

    def e_load_far(c, s):
        return local_copy(grads.at[row_e(c, 1 - near)], own_f.at[s], load_f_sem, s)

    def e_load_near(c, s):
        return local_copy(grads.at[row_e(c, near)], own_n.at[s], load_n_sem, s)

    def e_cross(c, s):
        return remote(own_f.at[s], cross_in.at[s], cross_sem, s, mid_peer)

    def e_near(c, s):
        return remote(own_n.at[s], near_in.at[s], near_sem, s, pair_peer)

    def e_end(c, s):
        return remote(own_n.at[s], end_in.at[s], end_sem, s, x_peer)

    def e_store(c, s):
        return local_copy(total_e.at[s], totals.at[row_e(c, near)], store_e_sem, s)

    def e_back_one(c, s):
        return remote(total_e.at[s], totals.at[row_e(c, near)], back_one_sem, s, pair_peer)

    def e_back_two(c, s):
        return remote(totals.at[row_e(c, near)], totals.at[row_e(c, near)], back_two_sem, s, mid_peer)

    def e_back_three(c, s):
        return remote(totals.at[row_e(c, 1 - near)], totals.at[row_e(c, 1 - near)], back_three_sem, s, pair_peer)

    def a_start(c, s):
        a_x(c, s).start()
        a_load(c, s).start()

    def a_one(c, s):
        a_load(c, s).wait()
        a_x(c, s).wait_recv()
        own_a[s] = own_a[s] + x_in[s]
        pl.when(is_end)(lambda: a_inner(c, s).start())

    def a_two(c, s):
        a_inner(c, s).wait_recv()
        own_a[s] = own_a[s] + inner_in[s]
        a_mid(c, s).start()

    def a_three(c, s):
        a_mid(c, s).wait_recv()
        total_a[s] = own_a[s] + mid_in[s]
        a_out_pair(c, s).start()
        a_out_x(c, s).start()
        a_store(c, s).start()

    def a_four(c, s):
        a_out_pair(c, s).wait_recv()
        a_relay(c, s).start()

    def a_five(c, s):
        a_back(c, s).wait_recv()

    def a_done(c, s):
        a_x(c, s).wait_send()
        a_out_x(c, s).wait_send()
        pl.when(is_end)(lambda: a_inner(c, s).wait_send())

        @pl.when(is_mid)
        def _():
            a_mid(c, s).wait_send()
            a_out_pair(c, s).wait_send()
            a_store(c, s).wait()

    def m_start(c, s):
        pl.when(is_end)(lambda: m_whole(c, s).start())
        pl.when(is_mid)(lambda: m_load(c, s).start())

    def m_one(c, s):
        m_load(c, s).wait()
        m_whole(c, s).wait_recv()
        own_b[s] = own_b[s] + whole_in[s]
        m_half(c, s).start()

    def m_two(c, s):
        m_half(c, s).wait_recv()
        mine = pl.ds(pl.multiple_of(side * unit, 8), unit)
        own_b[s, mine] = own_b[s, mine] + half_in[s]
        m_side(c, s).start()

    def m_three(c, s):
        m_side(c, s).wait_recv()
        mine = pl.ds(pl.multiple_of(side * unit, 8), unit)
        total_b[s] = own_b[s, mine] + side_in[s]
        m_back_mid(c, s).start()
        m_back_pair(c, s).start()
        m_store(c, s).start()

    def m_four(c, s):
        m_back_mid(c, s).wait_recv()
        m_relay(c, s).start()

    def m_five(c, s):
        m_back_pair(c, s).wait_recv()
        m_relay(c, s).wait_recv()

    def m_done(c, s):
        pl.when(is_end)(lambda: m_whole(c, s).wait_send())

        @pl.when(is_mid)
        def _():
            m_half(c, s).wait_send()
            m_side(c, s).wait_send()
            m_back_mid(c, s).wait_send()
            m_back_pair(c, s).wait_send()
            m_store(c, s).wait()
            m_relay(c, s).wait_send()

    def e_start(c, s):
        e_load_near(c, s).start()
        pl.when(is_end)(lambda: e_far(c, s).start())
        pl.when(is_mid)(lambda: e_load_far(c, s).start())

    def e_one(c, s):
        e_load_far(c, s).wait()
        e_far(c, s).wait_recv()
        own_f[s] = own_f[s] + far_in[s]
        e_cross(c, s).start()

    def e_two(c, s):
        e_load_near(c, s).wait()
        e_cross(c, s).wait_recv()
        own_n[s] = own_n[s] + cross_in[s]
        e_near(c, s).start()

    def e_three(c, s):
        e_load_near(c, s).wait()
        e_near(c, s).wait_recv()
        own_n[s] = own_n[s] + near_in[s]
        e_end(c, s).start()

    def e_four(c, s):
        e_end(c, s).wait_recv()
        total_e[s] = own_n[s] + end_in[s]
        e_back_one(c, s).start()
        e_store(c, s).start()

    def e_five(c, s):
        e_back_one(c, s).wait_recv()
        e_back_two(c, s).start()

    def e_six(c, s):
        e_back_two(c, s).wait_recv()
        e_back_three(c, s).start()

    def e_seven(c, s):
        e_back_three(c, s).wait_recv()

    def e_done(c, s):
        @pl.when(is_end)
        def _():
            e_far(c, s).wait_send()
            e_end(c, s).wait_send()
            e_back_one(c, s).wait_send()
            e_store(c, s).wait()

        @pl.when(is_mid)
        def _():
            e_cross(c, s).wait_send()
            e_near(c, s).wait_send()
            e_back_two(c, s).wait_send()
            e_back_three(c, s).wait_send()

    def stage(step, offset, phase, guard, body):
        at = step - offset
        ok = (at >= 0) & (at < steps)
        if guard is not None:
            ok = ok & guard
        if phase is None:
            chunk, slots = at, SLOTS
        else:
            ok = ok & (lax.rem(at, ROUND) == phase)
            chunk, slots = at // ROUND, FEW

        @pl.when(ok)
        def _():
            body(chunk, lax.rem(chunk, slots))

    def tick(step):
        if not dp_sum:
            return
        stage(step, 0, None, None, a_start)
        stage(step, 0, 0, None, m_start)
        stage(step, 0, 1, None, e_start)
        stage(step, 6 * HOP, 1, is_mid, e_six)
        stage(step, 5 * HOP, 1, is_mid, e_five)
        stage(step, 4 * HOP, 1, is_end, e_four)
        stage(step, 4 * HOP, 0, is_mid, m_four)
        stage(step, 3 * HOP, None, is_mid, a_three)
        stage(step, 3 * HOP, 0, is_mid, m_three)
        stage(step, 4 * HOP, None, is_end, a_four)
        stage(step, 3 * HOP, 1, is_end, e_three)
        stage(step, 2 * HOP, None, is_mid, a_two)
        stage(step, 2 * HOP, 0, is_mid, m_two)
        stage(step, 2 * HOP, 1, is_mid, e_two)
        stage(step, HOP, None, None, a_one)
        stage(step, HOP, 0, is_mid, m_one)
        stage(step, HOP, 1, is_mid, e_one)
        stage(step, 5 * HOP, None, None, a_five)
        stage(step, 5 * HOP, 0, is_end, m_five)
        stage(step, 7 * HOP, 1, is_end, e_seven)
        stage(step, 5 * HOP + 1, None, None, a_done)
        stage(step, 5 * HOP + 1, 0, None, m_done)
        stage(step, 7 * HOP + 1, 1, None, e_done)

    return tick, greet


def tick_scratch(unit, width):
    many, few, double = (SLOTS, unit, width), (FEW, unit, width), (FEW, 2 * unit, width)
    shapes = [many] * 5 + [double, few, few, double, few] + [few] * 7
    buffers = [pltpu.VMEM(shape, jnp.float32) for shape in shapes]
    sems = [pltpu.SemaphoreType.DMA((2, SLOTS))] * 5 + [pltpu.SemaphoreType.DMA((2, FEW))] * 13
    sems += [pltpu.SemaphoreType.DMA((SLOTS,))] * 2 + [pltpu.SemaphoreType.DMA((FEW,))] * 5
    return buffers, sems


HEAD = 72
EPSILON = 1e-06
UNIT = 8
TAIL_ROWS = 8


FIRST = 1
PIECE = 16
LAG = 4
BLOCK = 128
WIDE_BLOCK = 192


def dot_nn(left, right):
    return lax.dot_general(left, right, (((1,), (0,)), ((), ())), preferred_element_type=jnp.float32)


def dot_nt(left, right):
    return lax.dot_general(left, right, (((1,), (1,)), ((), ())), preferred_element_type=jnp.float32)


def dot_tn(left, right):
    return lax.dot_general(left, right, (((0,), (0,)), ((), ())), preferred_element_type=jnp.float32)


def fold(array):
    return jnp.sum(array, axis=0, keepdims=True)


def gelu_slope(v):
    root = 0.7978845608028654
    inner = jnp.tanh(root * (v + 0.044715 * (v * v * v)))
    return 0.5 * (1.0 + inner) + 0.5 * v * (1.0 - inner * inner) * (root * (1.0 + 0.134145 * (v * v)))


def norm_back(grad_normed, state, gain):
    centred = state - jnp.mean(state, axis=-1, keepdims=True)
    inverse = lax.rsqrt(jnp.mean(centred * centred, axis=-1, keepdims=True) + EPSILON)
    unit = centred * inverse
    grad_unit = grad_normed * gain
    inner = (
        grad_unit
        - jnp.mean(grad_unit, axis=-1, keepdims=True)
        - unit * jnp.mean(grad_unit * unit, axis=-1, keepdims=True)
    )
    return inverse * inner, fold(grad_normed * unit), fold(grad_normed)


def backward_kernel(
    dp_sum, tokens, layers, heads, units_rows, head_dim, send_rows, unit, steps,
    cotangent, hidden, active, normed_two, normed, middle, state, qkv, logsum, mixed,
    down, up, qkv_w, out_w, gain, last_part,
    grads, totals, image_grad, encoded, down_grad, up_grad,
    raw_buf, wide, act_buf, two_buf, qkv_buf, lse_buf, mix_buf, down_buf, up_buf, qkvw_buf, outw_buf, gain_buf,
    flow, flow_low, hid_low, part, total, core_in, acc, y_in, grad_mix, cat, tight, acc_k, acc_v, stage_buf, small,
    woven, load_sem, stage_sem, turn_sem, weave_sem, core_send, core_recv, y_send, y_recv, back_send, back_recv,
    *tick_refs
):
    width = grads.shape[1]
    rows = part.shape[0]
    blocks = rows // BLOCK
    half = send_rows // 2
    pieces = half // PIECE
    tick, greet = grad_sum_ticks(
        dp_sum, unit, steps, grads, totals, tick_refs[:TICK_BUFFERS], tick_refs[TICK_BUFFERS:]
    )
    dp = lax.axis_index("dp")
    tensor = lax.axis_index("tensor")
    core = tensor % 2
    core_peer = (dp, tensor + 1 - 2 * core)
    y_peer = (dp, lax.rem(tensor + 2, 4))
    greet((core_peer, y_peer))
    layer_rows = grads.shape[0] // layers
    off_up = units_rows
    local_width = heads * head_dim
    off_qkv = 2 * units_rows
    off_out = off_qkv + 3 * local_width
    off_small = off_out + local_width
    spread = spread_matrix(heads, head_dim)

    def mine(i):
        return pl.ds(pl.multiple_of(core * half + i * PIECE, 8), PIECE)

    def other(i):
        return pl.ds(pl.multiple_of((1 - core) * half + i * PIECE, 8), PIECE)

    def here(i):
        return pl.ds(pl.multiple_of(i * PIECE, 8), PIECE)

    def remote(src, dst, send, recv, peer):
        return pltpu.make_async_remote_copy(
            src_ref=src, dst_ref=dst, send_sem=send, recv_sem=recv, device_id=peer, device_id_type=MESH
        )

    def to_core(p, i):
        return remote(
            part.at[other(i)], core_in.at[here(i)], core_send.at[p, i], core_recv.at[p, i], core_peer
        )

    def to_y(p, i):
        return remote(acc.at[here(i)], y_in.at[p, here(i)], y_send.at[p, i], y_recv.at[p, i], y_peer)

    def to_back(p, i):
        return remote(total.at[mine(i)], total.at[mine(i)], back_send.at[p, i], back_recv.at[p, i], core_peer)

    def from_back(p, i):
        return remote(
            total.at[other(i)], total.at[other(i)], back_send.at[p, i], back_recv.at[p, i], core_peer
        )

    def sum_begin(p):
        def go(i, c):
            to_core(p, i).start()
            return c

        lax.fori_loop(0, pieces, go, 0)

    def sum_step(p, j):
        @pl.when(j < pieces)
        def _():
            to_core(p, j).wait_recv()
            acc[here(j)] = part[mine(j)] + core_in[here(j)]
            to_y(p, j).start()

        late = j - LAG

        @pl.when((late >= 0) & (late < pieces))
        def _():
            to_y(p, late).wait_recv()
            total[mine(late)] = acc[here(late)] + y_in[p, here(late)]
            to_back(p, late).start()

        last = j - LAG - 2

        @pl.when((last >= 0) & (last < pieces))
        def _():
            to_core(p, last).wait_send()
            to_y(p, last).wait_send()
            to_back(p, last).wait_send()
            from_back(p, last).wait_recv()

    sum_steps = pieces + LAG + 2

    def load(source, target, sem):
        return pltpu.make_async_copy(source, target, load_sem.at[sem])

    def stage_copy(slot, row, size):
        return pltpu.make_async_copy(
            stage_buf.at[slot, pl.ds(0, size)], grads.at[pl.ds(pl.multiple_of(row, 8), size)], stage_sem.at[slot]
        )

    tiles = width // 128
    last_rows = units_rows - (tiles - 1) * 128
    layer_ticks = tiles + 1 + 4 * blocks + 2 * sum_steps + heads * blocks

    def row_block(b):
        return pl.ds(pl.multiple_of(b * BLOCK, 16), BLOCK)

    total[pl.ds(send_rows, rows - send_rows)] = jnp.zeros((rows - send_rows, width), jnp.float32)
    start = load(cotangent, raw_buf, 11)
    start.start()
    load(active.at[layers - 1], act_buf, 3).start()
    gain_load = load(gain, gain_buf, 10)
    gain_load.start()

    def layer_body(it, carry):
        layer = layers - 1 - it
        base_tick = it * layer_ticks - FIRST
        base_row = it * layer_rows
        hidden_load = load(hidden.at[layer], wide, 0)
        down_load = load(down.at[layer], down_buf, 1)
        up_load = load(up.at[layer], up_buf, 2)
        active_load = load(active.at[layer], act_buf, 3)
        two_load = load(normed_two.at[layer], two_buf, 4)
        outw_load = load(out_w.at[layer], outw_buf, 5)
        qkv_load = load(qkv.at[layer], qkv_buf, 6)
        lse_load = load(logsum.at[layer], lse_buf, 7)
        mix_load = load(mixed.at[layer], mix_buf, 8)
        qkvw_load = load(qkv_w.at[layer], qkvw_buf, 9)
        pl.when(it > 0)(active_load.start)
        small[...] = jnp.zeros_like(small)

        @pl.when(it == 0)
        def _():
            start.wait()
            lower_rows(raw_buf, flow_low, wide, tokens)

        def lower(b, c):
            at = row_block(b)
            flow_low[at] = flow[at].astype(jnp.bfloat16)
            return c

        @pl.when(it > 0)
        def _():
            lax.fori_loop(0, blocks, lower, 0)

        active_load.wait()
        for copy in (hidden_load, down_load, up_load, two_load, outw_load, qkv_load, lse_load, mix_load, qkvw_load):
            copy.start()

        def tile_copy(tile, row):
            slot = lax.rem(tile, 2)
            pl.when(tile < tiles - 1)(lambda: stage_copy(slot, row, 128).start())
            pl.when(tile == tiles - 1)(lambda: stage_copy(slot, row, last_rows).start())

        def tile_done(tile):
            slot = lax.rem(tile, 2)
            pl.when((tile >= 0) & (tile < tiles - 1))(lambda: stage_copy(slot, base_row, 128).wait())
            pl.when(tile == tiles - 1)(lambda: stage_copy(slot, base_row, last_rows).wait())

        def down_weights(j, c):
            tile_done(j - 1)

            @pl.when(j < tiles)
            def _():
                lanes = pl.ds(pl.multiple_of(j * 128, 128), 128)
                stage_buf[lax.rem(j, 2), pl.ds(0, 128)] = dot_tn(act_buf[:, lanes], flow_low[...])
                tile_copy(j, base_row + j * 128)

            tick(base_tick + j)
            return c

        lax.fori_loop(0, tiles + 1, down_weights, 0)
        tick_at = base_tick + tiles + 1

        @pl.when(it == 0)
        def _():
            gain_load.wait()
            lift_rows(raw_buf, flow, tokens, BLOCK)

        hidden_load.wait()
        down_load.wait()
        up_load.wait()

        def mlp(b, c):
            at = row_block(b)
            small[3:4] += fold(flow[at])
            grad_hidden = dot_nt(flow_low[at], down_buf[...]) * gelu_slope(wide[at])
            small[2:3] += fold(grad_hidden)
            hid = grad_hidden.astype(jnp.bfloat16)
            hid_low[at] = hid
            part[at] = dot_nn(hid, up_buf[...])
            tick(tick_at + b)
            return c

        lax.fori_loop(0, blocks, mlp, 0)
        sum_begin(0)
        middle_load = load(middle.at[layer], wide, 0)
        middle_load.start()
        two_load.wait()
        tick_at = tick_at + blocks

        def up_weights(j, c):
            sum_step(0, j)
            tile_done(j - 1)

            @pl.when(j < tiles)
            def _():
                lanes = pl.ds(pl.multiple_of(j * 128, 128), 128)
                stage_buf[lax.rem(j, 2), pl.ds(0, 128)] = dot_tn(hid_low[:, lanes], two_buf[...])
                tile_copy(j, base_row + off_up + j * 128)

            tick(tick_at + j)
            return c

        lax.fori_loop(0, sum_steps, up_weights, 0)
        tick_at = tick_at + sum_steps
        part_load = load(last_part, part, 1)
        pl.when(it == 0)(part_load.start)
        middle_load.wait()
        outw_load.wait()

        def norm_two(b, c):
            at = row_block(b)
            step_grad, gain_grad, shift_grad = norm_back(total[at], wide[at], gain_buf[layer, 1:2])
            small[5:6] += gain_grad
            small[7:8] += shift_grad
            grad = flow[at] + step_grad
            flow[at] = grad
            small[1:2] += fold(grad)
            low = grad.astype(jnp.bfloat16)
            flow_low[at] = low
            grad = dot_nt(low, outw_buf[...]).astype(jnp.bfloat16)
            grad_mix[at] = dot_nn(grad, spread).astype(jnp.bfloat16)
            tick(tick_at + b)
            return c

        lax.fori_loop(0, blocks, norm_two, 0)
        tick_at = tick_at + blocks
        state_load = load(state.at[layer], wide, 0)
        normed_load = load(normed.at[layer], act_buf, 3)
        state_load.start()
        normed_load.start()
        qkv_load.wait()
        lse_load.wait()
        scale = head_dim ** (-0.5)

        @pl.when(it == 0)
        def _():
            part_load.wait()
            sum_begin(2)


        def attend(m, c):
            head = m // blocks
            b = lax.rem(m, blocks)
            at = row_block(b)
            lanes = pl.ds(pl.multiple_of(head * 128, 128), 128)
            query = qkv_buf[0, head, at]
            key = qkv_buf[1, head]
            value = qkv_buf[2, head]
            grad = grad_mix[at, lanes]
            scores = dot_nt(query, key) * scale
            probs = jnp.exp(scores - lse_buf[head, at, 0:1])
            column = lax.broadcasted_iota(jnp.int32, probs.shape, 1)
            probs = jnp.where(column < tokens, probs, 0.0)
            grad_weights = dot_nt(grad, value)
            center = jnp.sum(probs * grad_weights, axis=-1, keepdims=True)
            raw = (probs * (grad_weights - center) * scale).astype(jnp.bfloat16)
            grad_query = dot_nn(raw, key)
            small[0:1, lanes] += fold(grad_query)
            cat[at, lanes] = grad_query.astype(jnp.bfloat16)
            add_k = dot_tn(raw, query)
            add_v = dot_tn(probs.astype(jnp.bfloat16), grad)

            @pl.when(b == 0)
            def _():
                acc_k[...] = add_k
                acc_v[...] = add_v

            @pl.when(b > 0)
            def _():
                acc_k[...] += add_k
                acc_v[...] += add_v

            @pl.when(b == blocks - 1)
            def _():
                at_k = pl.ds(pl.multiple_of((heads + head) * 128, 128), 128)
                at_v = pl.ds(pl.multiple_of((2 * heads + head) * 128, 128), 128)
                cat[:, at_k] = acc_k[...].astype(jnp.bfloat16)
                cat[:, at_v] = acc_v[...].astype(jnp.bfloat16)
                small[0:1, pl.ds(pl.multiple_of((heads + head) * 128, 128), 128)] += fold(acc_v[...])

            @pl.when(it == 0)
            def _():
                sum_step(2, 2 * m)
                sum_step(2, 2 * m + 1)

            tick(tick_at + m)
            return c

        lax.fori_loop(0, heads * blocks, attend, 0)
        tick_at = tick_at + heads * blocks
        qkvw_load.wait()

        def project(b, c):
            at = row_block(b)
            out = None
            for i in range(3):
                lanes = pl.ds(i * heads * 128, heads * 128)
                narrow = dot_nt(cat[at, lanes], spread).astype(jnp.bfloat16)
                tight[i, at] = narrow
                term = dot_nn(narrow, qkvw_buf[i])
                out = term if out is None else out + term
            part[at] = out

            @pl.when(it == 0)
            def _():
                hid_low[at] = total[at].astype(jnp.bfloat16)

            tick(tick_at + b)
            return c

        lax.fori_loop(0, blocks, project, 0)
        tick_at = tick_at + blocks
        sum_begin(1)
        encoded_store = load(hid_low, encoded, 1)
        pl.when(it == 0)(encoded_store.start)
        normed_load.wait()
        mix_load.wait()

        def attention_weights(j, c):
            sum_step(1, j)

            @pl.when((j >= 1) & (j < 5))
            def _():
                stage_copy(lax.rem(j - 1, 2), base_row, local_width).wait()

            slot = lax.rem(j, 2)

            @pl.when(j < 3)
            def _():
                stage_buf[slot] = dot_tn(tight[j], act_buf[...])

            @pl.when(j == 3)
            def _():
                stage_buf[slot] = dot_tn(mix_buf[...], flow_low[...])

            @pl.when(j < 4)
            def _():
                stage_copy(slot, base_row + off_qkv + j * local_width, local_width).start()

            tick(tick_at + j)
            return c

        lax.fori_loop(0, sum_steps, attention_weights, 0)
        tick_at = tick_at + sum_steps
        state_load.wait()

        def norm_one(b, c):
            at = row_block(b)
            step_grad, gain_grad, shift_grad = norm_back(total[at], wide[at], gain_buf[layer, 0:1])
            small[4:5] += gain_grad
            small[6:7] += shift_grad
            flow[at] = flow[at] + step_grad
            tick(tick_at + b)
            return c

        lax.fori_loop(0, blocks, norm_one, 0)
        tail = pltpu.make_async_copy(
            small, grads.at[pl.ds(pl.multiple_of(base_row + off_small, 8), small.shape[0])], load_sem.at[10]
        )
        tail.start()
        tail.wait()
        pl.when(it == 0)(encoded_store.wait)
        return carry

    lax.fori_loop(0, layers, layer_body, 0)

    def lower(b, c):
        flow_low[row_block(b)] = flow[row_block(b)].astype(jnp.bfloat16)
        return c

    lax.fori_loop(0, blocks, lower, 0)
    image_store = load(flow_low, image_grad, 0)
    image_store.start()

    tail = layers * layer_ticks - FIRST
    weaves, at_step = [], tail
    for k in range(2):
        last_row = (layers - 1) * layer_rows + (k + 1) * units_rows
        ready = -(-last_row // (PARTS * unit)) * ROUND + TICK_SPAN
        at_step = max(at_step, ready)
        weaves.append(at_step)
        at_step += tiles + 1

    def each_size(tile, body):
        pl.when(tile < tiles - 1)(lambda: body(128))
        pl.when(tile == tiles - 1)(lambda: body(last_rows))

    def weave_in(k, tile, layer, rows_here):
        row = pl.multiple_of((layers - 1 - layer) * layer_rows + k * units_rows + tile * 128, 8)
        slot = lax.rem(tile, 2)
        return pltpu.make_async_copy(
            totals.at[pl.ds(row, rows_here)],
            stage_buf.at[slot, pl.ds(layer * 128, rows_here)],
            weave_sem.at[slot, layer],
        )

    def weave_out(target, tile, rows_here):
        slot = lax.rem(tile, 2)
        return pltpu.make_async_copy(
            woven.at[slot, pl.ds(0, rows_here)], target.at[pl.ds(tile * 128, rows_here)], turn_sem.at[slot]
        )

    def weave(k, target, tile):
        def begin(rows_here):
            for layer in range(layers):
                weave_in(k, tile, layer, rows_here).start()

        def arrive(rows_here):
            for layer in range(layers):
                weave_in(k, tile - 1, layer, rows_here).wait()

        each_size(tile, begin)

        @pl.when(tile >= 1)
        def _():
            each_size(tile - 1, arrive)
            slot = lax.rem(tile - 1, 2)

            @pl.when(tile >= 3)
            def _():
                weave_out(target, tile - 3, 128).wait()

            for layer in range(layers):
                woven[slot, :, layer, :] = stage_buf[slot, pl.ds(layer * 128, 128)]
            each_size(tile - 1, lambda rows_here: weave_out(target, tile - 1, rows_here).start())

        @pl.when(tile == tiles)
        def _():
            weave_out(target, tiles - 2, 128).wait()
            weave_out(target, tiles - 1, last_rows).wait()

    def rest(step, c):
        tick(step)
        if dp_sum:
            for k, target in enumerate((down_grad, up_grad)):
                tile = step - weaves[k]

                @pl.when((tile >= 0) & (tile <= tiles))
                def _():
                    weave(k, target, tile)

        return c

    lax.fori_loop(tail, max(steps + TICK_SPAN, at_step), rest, 0)
    image_store.wait()


def backward(
    tokens, head_dim, hidden_units, unit, collective_id, dp_sum,
    cotangent, hidden, active, normed_two, normed, middle, state, qkv, logsum, mixed,
    down, up, qkv_w, out_w, gain, last_part,
):
    layers, rows, width = middle.shape
    heads = qkv.shape[2]
    units_rows = -(-hidden_units // 8) * 8
    send_rows = -(-tokens // (2 * PIECE)) * 2 * PIECE
    pieces = send_rows // (2 * PIECE)
    layer_rows = 2 * units_rows + 4 * heads * head_dim + TAIL_ROWS
    steps = layers * layer_rows // (PARTS * unit) * ROUND
    assert steps * PARTS * unit == layers * layer_rows * ROUND
    buffers, sems = tick_scratch(unit, width)
    f32, low = jnp.float32, jnp.bfloat16
    half = (send_rows // 2, width)
    full = (rows, width)
    any_spec = pl.BlockSpec(memory_space=pl.ANY)
    grads = jax.ShapeDtypeStruct((layers * layer_rows, width), f32)
    return pl.pallas_call(
        functools.partial(
            backward_kernel, dp_sum, tokens, layers, heads, units_rows, head_dim, send_rows, unit, steps
        ),
        out_shape=(
            grads,
            grads,
            jax.ShapeDtypeStruct(full, low),
            jax.ShapeDtypeStruct(full, low),
            jax.ShapeDtypeStruct((units_rows, layers, width), f32),
            jax.ShapeDtypeStruct((units_rows, layers, width), f32),
        ),
        in_specs=[any_spec] * 16,
        out_specs=(any_spec,) * 6,
        scratch_shapes=[
            pltpu.VMEM(cotangent.shape, low),
            pltpu.VMEM(full, f32),
            pltpu.VMEM(full, low),
            pltpu.VMEM(full, low),
            pltpu.VMEM(qkv.shape[1:], low),
            pltpu.VMEM(logsum.shape[1:], f32),
            pltpu.VMEM(mixed.shape[1:], low),
            pltpu.VMEM(down.shape[1:], low),
            pltpu.VMEM(up.shape[1:], low),
            pltpu.VMEM(qkv_w.shape[1:], low),
            pltpu.VMEM(out_w.shape[1:], low),
            pltpu.VMEM(gain.shape, f32),
            pltpu.VMEM(full, f32),
            pltpu.VMEM(full, low),
            pltpu.VMEM(full, low),
            pltpu.VMEM(full, f32),
            pltpu.VMEM(full, f32),
            pltpu.VMEM(half, f32),
            pltpu.VMEM(half, f32),
            pltpu.VMEM((3,) + half, f32),
            pltpu.VMEM((rows, heads * 128), low),
            pltpu.VMEM((rows, 3 * heads * 128), low),
            pltpu.VMEM((3, rows, heads * head_dim), low),
            pltpu.VMEM((rows, 128), f32),
            pltpu.VMEM((rows, 128), f32),
            pltpu.VMEM((2, heads * head_dim, width), f32),
            pltpu.VMEM((TAIL_ROWS, width), f32),
            pltpu.VMEM((2, 128, layers, width), f32),
        ]
        + [pltpu.SemaphoreType.DMA((12,)), pltpu.SemaphoreType.DMA((2,)), pltpu.SemaphoreType.DMA((2,)), pltpu.SemaphoreType.DMA((2, layers))]
        + [pltpu.SemaphoreType.DMA((3, pieces))] * 6
        + buffers
        + sems,
        compiler_params=pltpu.CompilerParams(
            collective_id=collective_id, has_side_effects=True, vmem_limit_bytes=63 << 20
        ),
    )(
        cotangent, hidden, active, normed_two, normed, middle, state, qkv, logsum, mixed,
        down, up, qkv_w, out_w, gain, last_part,
    )


def lift_rows(source, target, tokens, size):
    blocks = target.shape[0] // size

    def one(b, c):
        at = pl.ds(pl.multiple_of(b * size, 16), size)
        target[at] = source[at].astype(jnp.float32)
        return c

    lax.fori_loop(0, blocks - 1, one, 0)
    begin = (blocks - 1) * size
    target[pl.ds(begin, size)] = jnp.zeros((size, target.shape[1]), jnp.float32)
    last = pl.ds(begin, tokens - begin)
    target[last] = source[last].astype(jnp.float32)


def lower_rows(source, target, wide, tokens):
    full = tokens // BLOCK

    def one(b, c):
        at = pl.ds(pl.multiple_of(b * BLOCK, 16), BLOCK)
        target[at] = source[at]
        return c

    lax.fori_loop(0, full, one, 0)
    tail = pl.ds(full * BLOCK, target.shape[0] - full * BLOCK)
    wide[tail] = jnp.zeros((target.shape[0] - full * BLOCK, target.shape[1]), jnp.float32)
    some = pl.ds(full * BLOCK, tokens - full * BLOCK)
    wide[some] = source[some].astype(jnp.float32)
    target[tail] = wide[tail].astype(jnp.bfloat16)


def spread_matrix(heads, head_dim):
    shape = (heads * head_dim, heads * 128)
    source = lax.broadcasted_iota(jnp.int32, shape, 0)
    lane = lax.broadcasted_iota(jnp.int32, shape, 1)
    hit = (lane // 128 * head_dim + lane % 128 == source) & (lane % 128 < head_dim)
    return jnp.where(hit, 1.0, 0.0).astype(jnp.bfloat16)


def norm_unit(state):
    centred = state - jnp.mean(state, axis=-1, keepdims=True)
    return centred * lax.rsqrt(jnp.mean(centred * centred, axis=-1, keepdims=True) + EPSILON)


def gelu(v):
    return 0.5 * v * (1.0 + jnp.tanh(0.7978845608028654 * (v + 0.044715 * (v * v * v))))


def block_sum(pieces, dp, tensor, part, core_in, y_in, total, sems):
    core = tensor % 2
    core_peer = (dp, tensor + 1 - 2 * core)
    y_peer = (dp, lax.rem(tensor + 2, 4))
    core_sem, y_sem, back_sem = sems
    per_block = WIDE_BLOCK // (2 * PIECE)

    def mine(i):
        return pl.ds(pl.multiple_of((2 * i + core) * PIECE, 8), PIECE)

    def other(i):
        return pl.ds(pl.multiple_of((2 * i + 1 - core) * PIECE, 8), PIECE)

    def here(i):
        return pl.ds(pl.multiple_of(i * PIECE, 8), PIECE)

    def remote(src, dst, sem, i, peer):
        return pltpu.make_async_remote_copy(
            src_ref=src, dst_ref=dst, send_sem=sem.at[0, i], recv_sem=sem.at[1, i],
            device_id=peer, device_id_type=MESH,
        )

    def to_core(i):
        return remote(part.at[other(i)], core_in.at[here(i)], core_sem, i, core_peer)

    def to_y(i):
        return remote(core_in.at[here(i)], y_in.at[here(i)], y_sem, i, y_peer)

    def to_back(i):
        return remote(total.at[mine(i)], total.at[mine(i)], back_sem, i, core_peer)

    def from_back(i):
        return remote(total.at[other(i)], total.at[other(i)], back_sem, i, core_peer)

    def each(b, body):
        def go(k, c):
            i = b * per_block + k

            @pl.when(i < pieces)
            def _():
                body(i)

            return c

        lax.fori_loop(0, per_block, go, 0)

    def send(b):
        each(b, lambda i: to_core(i).start())

    def meet(b):
        def body(i):
            to_core(i).wait_recv()
            core_in[here(i)] = core_in[here(i)] + part[mine(i)]
            to_y(i).start()

        each(b, body)

    def close(b):
        def body(i):
            to_y(i).wait_recv()
            total[mine(i)] = core_in[here(i)] + y_in[here(i)]
            to_back(i).start()

        each(b, body)

    def finish(b):
        def body(i):
            to_core(i).wait_send()
            to_y(i).wait_send()
            to_back(i).wait_send()
            from_back(i).wait_recv()

        each(b, body)

    return send, meet, close, finish


def pair_sum(pieces, dp, tensor, part, core_in, total, sems):
    core = tensor % 2
    core_peer = (dp, tensor + 1 - 2 * core)
    core_sem, back_sem = sems
    per_block = WIDE_BLOCK // (2 * PIECE)

    def mine(i):
        return pl.ds(pl.multiple_of((2 * i + core) * PIECE, 8), PIECE)

    def other(i):
        return pl.ds(pl.multiple_of((2 * i + 1 - core) * PIECE, 8), PIECE)

    def here(i):
        return pl.ds(pl.multiple_of(i * PIECE, 8), PIECE)

    def remote(src, dst, sem, i):
        return pltpu.make_async_remote_copy(
            src_ref=src, dst_ref=dst, send_sem=sem.at[0, i], recv_sem=sem.at[1, i],
            device_id=core_peer, device_id_type=MESH,
        )

    def to_core(i):
        return remote(part.at[other(i)], core_in.at[here(i)], core_sem, i)

    def to_back(i):
        return remote(total.at[mine(i)], total.at[mine(i)], back_sem, i)

    def from_back(i):
        return remote(total.at[other(i)], total.at[other(i)], back_sem, i)

    def each(b, body):
        def go(k, c):
            i = b * per_block + k

            @pl.when(i < pieces)
            def _():
                body(i)

            return c

        lax.fori_loop(0, per_block, go, 0)

    def send(b):
        each(b, lambda i: to_core(i).start())

    def meet(b):
        def body(i):
            to_core(i).wait_recv()
            total[mine(i)] = core_in[here(i)] + part[mine(i)]
            to_back(i).start()

        each(b, body)

    def finish(b):
        def body(i):
            to_core(i).wait_send()
            to_back(i).wait_send()
            from_back(i).wait_recv()

        each(b, body)

    return send, meet, finish


def forward_kernel(
    dp_size, tokens, layers, heads, head_dim, send_rows,
    images, qkv_w, qv_b, out_w, out_b, up, up_b, down, down_b, gain, shift,
    hidden, active, normed_two, normed, middle, state, qkv, logsum, mixed, down_rows, up_rows, last_part,
    image_buf, upb_raw, flow, normed_buf, qkv_buf, lse_buf, mix_buf, tight_buf, two_buf, hidden_buf, active_buf,
    qkvw_buf, outw_buf, up_buf, down_buf, qvb_buf, outb_buf, upb_buf, downb_buf, gain_buf, shift_buf,
    part_a, core_in_a, total_a, part_b, core_in_b, y_in_b, total_b,
    quarter_buf, y_rows, both_w, both_mix, packed, y_packed,
    pair_buf, edge_buf, load_sem, weight_sem, store_sem, block_sem, split_sem, split_out_sem,
    quarter_sem, rows_sem, packed_sem, *sum_sems
):
    rows, width = flow.shape
    local_width = heads * head_dim
    blocks = rows // WIDE_BLOCK
    pieces = send_rows // (2 * PIECE)
    dp = lax.axis_index("dp")
    tensor = lax.axis_index("tensor")
    core = tensor % 2
    barrier = pltpu.get_barrier_semaphore()
    y_peer = (dp, lax.rem(tensor + 2, 4))
    upper = tensor // 2
    stride = dp_size // 4
    spot = dp // stride
    others = [(lax.rem(spot + k, 4) * stride + lax.rem(dp, stride), tensor) for k in (1, 2, 3)]
    for peer in [(dp, tensor + 1 - 2 * core), y_peer] + others:
        pl.semaphore_signal(barrier, inc=1, device_id=peer, device_id_type=MESH)
    quarter = quarter_buf.shape[1]
    group = packed.shape[1]

    def remote(src, dst, sem, peer):
        return pltpu.make_async_remote_copy(
            src_ref=src, dst_ref=dst, send_sem=sem[0], recv_sem=sem[1], device_id=peer, device_id_type=MESH
        )

    def quarter_rows(at):
        return pl.ds(pl.multiple_of(at * quarter, 8), quarter)

    def quarter_out(layer):
        return remote(
            quarter_buf.at[layer], y_rows.at[layer, quarter_rows(spot)],
            (quarter_sem.at[0, layer], quarter_sem.at[1, layer]), y_peer,
        )

    def rows_out(layer, k):
        here = y_rows.at[layer, quarter_rows(spot)]
        return remote(here, here, (rows_sem.at[0, layer, k - 1], rows_sem.at[1, layer, k - 1]), others[k - 1])

    def rows_back(layer, k):
        here = y_rows.at[layer, quarter_rows(lax.rem(spot + 4 - k, 4))]
        return remote(here, here, (rows_sem.at[0, layer, k - 1], rows_sem.at[1, layer, k - 1]), others[k - 1])

    def packed_out(layer, b):
        return remote(
            packed.at[b], y_packed.at[layer, b], (packed_sem.at[0, layer, b], packed_sem.at[1, layer, b]), y_peer
        )

    def weights(layer):
        return (pltpu.make_async_copy(qkv_w.at[layer], qkvw_buf, weight_sem.at[0]),)

    tiles = up_buf.shape[0] // 128
    units = up.shape[0]
    last_units = units - (tiles - 1) * 128

    def split_in(k, tile, size):
        slot = lax.rem(k * tiles + tile, 2)
        source = (up, down)[k]
        return pltpu.make_async_copy(
            source.at[pl.ds(tile * 128, size)], pair_buf.at[slot, pl.ds(0, size)], split_sem.at[0, slot]
        )

    def split_size(tile, body):
        pl.when(tile < tiles - 1)(lambda: body(128))
        pl.when(tile == tiles - 1)(lambda: body(last_units))

    def split_out(k, layer):
        source, target = ((up_buf, up_rows), (down_buf, down_rows))[k]
        return pltpu.make_async_copy(source, target.at[layer], split_out_sem.at[k])

    def split(layer):
        for k, target in enumerate((up_buf, down_buf)):

            def one(tile, c):
                slot = lax.rem(k * tiles + tile, 2)
                pl.when(tile + 1 < tiles)(
                    lambda: split_size(tile + 1, lambda size: split_in(k, tile + 1, size).start())
                )
                if k == 0:
                    pl.when(tile == tiles - 1)(lambda: split_in(1, 0, 128).start())
                split_size(tile, lambda size: split_in(k, tile, size).wait())
                at = pl.ds(pl.multiple_of(tile * 128, 128), 128)

                @pl.when(tile < tiles - 1)
                def _():
                    target[at] = pair_buf[slot, :, layer, :]

                @pl.when(tile == tiles - 1)
                def _():
                    edge_buf[...] = jnp.zeros_like(edge_buf)
                    edge_buf[pl.ds(0, last_units)] = pair_buf[slot, pl.ds(0, last_units), layer, :].astype(jnp.float32)
                    target[at] = edge_buf[...].astype(jnp.bfloat16)

                return c

            lax.fori_loop(0, tiles, one, 0)
            split_out(k, layer).start()


    singles = [
        pltpu.make_async_copy(source, target, load_sem.at[i])
        for i, (source, target) in enumerate(
            (
                (out_w, outw_buf), (images, image_buf), (gain, gain_buf), (shift, shift_buf), (qv_b, qvb_buf),
                (out_b, outb_buf), (up_b, upb_raw), (down_b, downb_buf),
            )
        )
    ]
    for copy in singles:
        copy.start()
    current = weights(0)
    current[0].start()
    split_in(0, 0, 128).start()
    spread = spread_matrix(heads, head_dim)
    total_a[pl.ds(send_rows, rows - send_rows)] = jnp.zeros((rows - send_rows, width), jnp.float32)
    total_b[pl.ds(send_rows, rows - send_rows)] = jnp.zeros((rows - send_rows, width), jnp.float32)
    singles[0].wait()
    for k in range(4):

        @pl.when(spot == k)
        def _():
            lead_rows = k * quarter % 16
            for layer in range(layers):
                some = outw_buf[layer, pl.ds(k * quarter - lead_rows, quarter + 8)].astype(jnp.float32)
                quarter_buf[layer] = some[lead_rows : lead_rows + quarter]

    pl.semaphore_wait(barrier, 5)
    quarter_out(0).start()
    for copy in singles[1:]:
        copy.wait()

    def row_block(b):
        return pl.ds(pl.multiple_of(b * WIDE_BLOCK, 16), WIDE_BLOCK)

    scale = head_dim ** (-0.5)
    stores = {}

    def block_store(layer, b, kind):
        at = row_block(b)
        source, target = (
            (flow, middle.at[layer, at]),
            (two_buf, normed_two.at[layer, at]),
            (hidden_buf, hidden.at[layer, at]),
            (active_buf, active.at[layer, at]),
            (part_b, last_part.at[at]),
        )[kind]
        return pltpu.make_async_copy(source.at[at], target, block_sem.at[kind, b])

    def keep(name, source, target, index):
        copy = pltpu.make_async_copy(source, target, store_sem.at[index])
        copy.start()
        stores[name] = copy

    def settle(*names):
        for name in names:
            if name in stores:
                stores.pop(name).wait()

    def project(layer, b, value):
        at = row_block(b)
        flow[at] = value
        low = (norm_unit(value) * gain_buf[layer, 0:1] + shift_buf[layer, 0:1]).astype(jnp.bfloat16)
        normed_buf[at] = low
        for i in range(3):
            out = dot_nt(low, qkvw_buf[i])
            if i != 1:
                out = out + qvb_buf[layer, i // 2 : i // 2 + 1]
            wide = dot_nn(out.astype(jnp.bfloat16), spread).astype(jnp.bfloat16)
            for head in range(heads):
                qkv_buf[i, head, at] = wide[:, head * 128 : (head + 1) * 128]

    def first(b, c):
        project(0, b, flow[row_block(b)])
        return c

    lift_rows(image_buf, flow, tokens, WIDE_BLOCK)
    upb_buf[...] = jnp.zeros_like(upb_buf)
    upb_buf[:, pl.ds(0, upb_raw.shape[1])] = upb_raw[...]
    current[0].wait()
    lax.fori_loop(0, blocks, first, 0)

    for layer in range(layers):
        keep("state", flow, state.at[layer], 0)
        keep("normed", normed_buf, normed.at[layer], 1)
        keep("qkv", qkv_buf, qkv.at[layer], 2)
        settle("logsum", "mixed")
        send_a, meet_a, finish_a = pair_sum(
            pieces, dp, tensor, part_a, core_in_a, total_a, [s.at[layer] for s in sum_sems[:2]]
        )
        send_b, meet_b, close_b, finish_b = block_sum(
            pieces, dp, tensor, part_b, core_in_b, y_in_b, total_b, [s.at[layer] for s in sum_sems[2:]]
        )
        is_last = layer == layers - 1
        if not is_last:
            following = weights(layer + 1)
            following[0].start()

        both_w[upper] = outw_buf[layer]
        if layer == 0:
            quarter_out(0).wait_recv()
            for k in (1, 2, 3):
                rows_out(0, k).start()

        def attend(b, c):
            at = row_block(b)

            def one_head(head, c):
                scores = dot_nt(qkv_buf[0, head, at], qkv_buf[1, head]) * scale
                column = lax.broadcasted_iota(jnp.int32, scores.shape, 1)
                scores = jnp.where(column < tokens, scores, -jnp.inf)
                peak = jnp.max(scores, axis=-1, keepdims=True)
                expo = jnp.exp(scores - peak)
                denominator = jnp.sum(expo, axis=-1, keepdims=True)
                probs = (expo / denominator).astype(jnp.bfloat16)
                lanes = pl.ds(pl.multiple_of(head * 128, 128), 128)
                mix_buf[:, lanes] = dot_nn(probs, qkv_buf[2, head]).astype(jnp.bfloat16)
                lse_buf[head, at] = jnp.broadcast_to(peak + jnp.log(denominator), (WIDE_BLOCK, 128))
                return c

            lax.fori_loop(0, heads, one_head, 0)
            tight = dot_nt(mix_buf[...], spread).astype(jnp.bfloat16)
            tight_buf[at] = tight
            loose = tight.astype(jnp.float32)
            for g in range(heads):
                packed[b, :, g * local_width : (g + 1) * local_width] = loose[g * group : (g + 1) * group]
            packed_out(layer, b).start()
            return c

        lax.fori_loop(0, blocks, attend, 0)
        if not is_last:
            quarter_out(layer + 1).start()
        keep("logsum", lse_buf, logsum.at[layer], 3)
        keep("mixed", tight_buf, mixed.at[layer], 4)
        settle("state")
        if layer == 0:
            split(0)
        for k in (1, 2, 3):
            rows_back(layer, k).wait_recv()
        both_w[1 - upper] = y_rows[layer].astype(jnp.bfloat16)

        def output(b):
            packed_out(layer, b).wait_recv()
            both_mix[upper] = tight_buf[row_block(b)]
            for g in range(heads):
                both_mix[1 - upper, pl.ds(g * group, group)] = y_packed[
                    layer, b, :, g * local_width : (g + 1) * local_width
                ].astype(jnp.bfloat16)
            part_a[row_block(b)] = dot_nn(both_mix[0], both_w[0]) + dot_nn(both_mix[1], both_w[1])
            send_a(b)

        def mlp(b):
            at = row_block(b)
            if not is_last:

                @pl.when(b > 0)
                def _():
                    meet_b(b - 1)

            finish_a(b)
            value = flow[at] + total_a[at] + outb_buf[layer : layer + 1]
            flow[at] = value
            block_store(layer, b, 0).start()
            low = (norm_unit(value) * gain_buf[layer, 1:2] + shift_buf[layer, 1:2]).astype(jnp.bfloat16)
            two_buf[at] = low
            hid = dot_nt(low, up_buf[...]) + upb_buf[layer : layer + 1]
            hidden_buf[at] = hid
            act = gelu(hid).astype(jnp.bfloat16)
            active_buf[at] = act
            partial = dot_nn(act, down_buf[...])
            if is_last:
                lead = jnp.where(tensor == 0, 1.0, 0.0)
                partial = partial + lead * (value + downb_buf[layer : layer + 1])
            part_b[at] = partial
            for kind in range(1, 5 if is_last else 4):
                block_store(layer, b, kind).start()
            if not is_last:
                send_b(b)

        def output_and_mlp(b, c):
            pl.when(b < blocks)(lambda: output(b))
            pl.when((b > 0) & (b <= blocks))(lambda: meet_a(b - 1))
            pl.when(b > 1)(lambda: mlp(b - 2))
            return c

        lax.fori_loop(0, blocks + 2, output_and_mlp, 0)
        quarter_out(layer).wait_send()
        for k in (1, 2, 3):
            rows_out(layer, k).wait_send()
        for b in range(blocks):
            packed_out(layer, b).wait_send()
        if not is_last:
            quarter_out(layer + 1).wait_recv()
            for k in (1, 2, 3):
                rows_out(layer + 1, k).start()

        def stored(*kinds):
            def one(b, c):
                for kind in kinds:
                    block_store(layer, b, kind).wait()
                return c

            lax.fori_loop(0, blocks, one, 0)

        if is_last:
            stored(0, 1, 2, 3, 4)
        else:
            meet_b(blocks - 1)
            for k in range(2):
                split_out(k, layer).wait()
            split_in(0, 0, 128).start()
            split(layer + 1)
            following[0].wait()
            settle("normed", "qkv")

            def next_project(b, c):
                at = row_block(b)
                close_b(b)
                finish_b(b)
                block_store(layer, b, 0).wait()
                project(layer + 1, b, flow[at] + total_b[at] + downb_buf[layer : layer + 1])
                return c

            lax.fori_loop(0, blocks, next_project, 0)
            stored(1, 2, 3)
            current = following
    for k in range(2):
        split_out(k, layers - 1).wait()
    settle(*list(stores))


def forward(
    dp_size, tokens, head_dim, collective_id,
    images, qkv_w, qv_b, out_w, out_b, up, up_b, down, down_b, gain, shift,
):
    layers = qkv_w.shape[0]
    width = images.shape[1]
    rows = -(-tokens // WIDE_BLOCK) * WIDE_BLOCK
    heads = qkv_w.shape[2] // head_dim
    units = -(-up.shape[0] // 128) * 128
    send_rows = -(-tokens // (2 * PIECE)) * 2 * PIECE
    pieces = send_rows // (2 * PIECE)
    f32, low = jnp.float32, jnp.bfloat16
    full = (rows, width)
    half = (send_rows // 2, width)
    any_spec = pl.BlockSpec(memory_space=pl.ANY)

    def out(shape, dtype):
        return jax.ShapeDtypeStruct(shape, dtype)

    lanes = heads * 128
    blocks = rows // WIDE_BLOCK
    local_width = heads * head_dim
    return pl.pallas_call(
        functools.partial(forward_kernel, dp_size, tokens, layers, heads, head_dim, send_rows),
        out_shape=(
            out((layers, rows, units), f32),
            out((layers, rows, units), low),
            out((layers,) + full, low),
            out((layers,) + full, low),
            out((layers,) + full, f32),
            out((layers,) + full, f32),
            out((layers, 3, heads, rows, 128), low),
            out((layers, heads, rows, 128), f32),
            out((layers, rows, heads * head_dim), low),
            out((layers, units, width), low),
            out((layers, units, width), low),
            out(full, f32),
        ),
        in_specs=[any_spec] * 11,
        out_specs=(any_spec,) * 12,
        scratch_shapes=[
            pltpu.VMEM(images.shape, low),
            pltpu.VMEM(up_b.shape, f32),
            pltpu.VMEM(full, f32),
            pltpu.VMEM(full, low),
            pltpu.VMEM((3, heads, rows, 128), low),
            pltpu.VMEM((heads, rows, 128), f32),
            pltpu.VMEM((WIDE_BLOCK, lanes), low),
            pltpu.VMEM((rows, heads * head_dim), low),
            pltpu.VMEM(full, low),
            pltpu.VMEM((rows, units), f32),
            pltpu.VMEM((rows, units), low),
            pltpu.VMEM(qkv_w.shape[1:], low),
            pltpu.VMEM(out_w.shape, low),
            pltpu.VMEM((units, width), low),
            pltpu.VMEM((units, width), low),
            pltpu.VMEM(qv_b.shape, f32),
            pltpu.VMEM(out_b.shape, f32),
            pltpu.VMEM((layers, units), f32),
            pltpu.VMEM(down_b.shape, f32),
            pltpu.VMEM(gain.shape, f32),
            pltpu.VMEM(shift.shape, f32),
        ]
        + [pltpu.VMEM(s, f32) for s in (full, half, full, full, half, half, full)]
        + [
            pltpu.VMEM((layers, local_width // 4, width), f32),
            pltpu.VMEM((layers, local_width, width), f32),
            pltpu.VMEM((2, local_width, width), low),
            pltpu.VMEM((2, WIDE_BLOCK, local_width), low),
            pltpu.VMEM((blocks, WIDE_BLOCK // heads, heads * local_width), f32),
            pltpu.VMEM((layers, blocks, WIDE_BLOCK // heads, heads * local_width), f32),
            pltpu.VMEM((2, 128, layers, width), low),
            pltpu.VMEM((128, width), f32),
            pltpu.SemaphoreType.DMA((8,)),
            pltpu.SemaphoreType.DMA((1,)),
            pltpu.SemaphoreType.DMA((9,)),
            pltpu.SemaphoreType.DMA((5, rows // WIDE_BLOCK)),
            pltpu.SemaphoreType.DMA((1, 2)),
            pltpu.SemaphoreType.DMA((2,)),
            pltpu.SemaphoreType.DMA((2, layers)),
            pltpu.SemaphoreType.DMA((2, layers, 3)),
            pltpu.SemaphoreType.DMA((2, layers, blocks)),
        ]
        + [pltpu.SemaphoreType.DMA((layers, 2, pieces))] * 5,
        compiler_params=pltpu.CompilerParams(
            collective_id=collective_id, has_side_effects=True, vmem_limit_bytes=63 << 20
        ),
    )(images, qkv_w, qv_b, out_w, out_b, up, up_b, down, down_b, gain, shift)


def finish_kernel(
    layers, heads, head_dim, hidden_units, layer_rows, off_qkv,
    totals, down_rows, up_rows, image_rows, encoded_rows,
    encoded, image_grad, qkv_grad, qv_grad, out_grad, out_b, up_grad, up_b, down_grad, down_b, gain, shift,
    down_buf, up_wide, rows_buf, long_a, long_b, short_a, short_b, small, qv_buf, up_buf, plain, pair, sem,
):
    width = totals.shape[1]
    local_width = heads * head_dim
    count = [0]

    def move(source, target):
        copy = pltpu.make_async_copy(source, target, sem.at[count[0]])
        count[0] += 1
        copy.start()
        return copy

    small_rows = small.shape[1]
    off_small = off_qkv + 4 * local_width
    firsts = [(layers - 1 - l) * layer_rows for l in range(layers)]
    fetch = [move(totals.at[pl.ds(firsts[l] + off_small, small_rows)], small.at[l]) for l in range(layers)]
    fetch_a = move(encoded_rows, long_a)
    fetch_b = move(image_rows, long_b)
    through = []
    for source, buffer, target in ((down_rows, down_buf, down_grad), (up_rows, up_wide, up_grad)):
        for at in range(0, hidden_units, 128):
            here = pl.ds(at, min(128, hidden_units - at))
            through.append((move(source.at[here], buffer.at[here]), buffer.at[here], target.at[here]))
    for l in range(layers):
        begin = firsts[l] + off_qkv
        for i in range(4):
            rows = pl.ds(begin + i * local_width, local_width)
            target = qkv_grad.at[l, i] if i < 3 else out_grad.at[l]
            through.append((move(totals.at[rows], rows_buf.at[l, i]), rows_buf.at[l, i], target))
    moves = []
    for arrived, buffer, target in through:
        arrived.wait()
        moves.append(move(buffer, target))
    for copy in fetch:
        copy.wait()
    for l in range(layers):
        for i in range(2):
            for h in range(heads):
                lane = (i * heads + h) * 128
                qv_buf[l, i : i + 1, h * head_dim : (h + 1) * head_dim] = small[l, 0:1, lane : lane + head_dim]
        plain[0, l : l + 1] = small[l, 1:2]
        up_buf[l : l + 1] = small[l, 2:3, :hidden_units]
        plain[1, l : l + 1] = small[l, 3:4]
        pair[0, l] = small[l, 4:6]
        pair[1, l] = small[l, 6:8]
    moves += [
        move(qv_buf, qv_grad), move(plain.at[0], out_b), move(up_buf, up_b), move(plain.at[1], down_b),
        move(pair.at[0], gain), move(pair.at[1], shift),
    ]
    tokens = short_a.shape[0]
    fetch_a.wait()
    short_a[...] = long_a[:tokens]
    moves.append(move(short_a, encoded))
    fetch_b.wait()
    short_b[...] = long_b[:tokens]
    moves.append(move(short_b, image_grad))
    for copy in moves:
        copy.wait()


def finish(tokens, heads, head_dim, hidden_units, totals, down_rows, up_rows, image_rows, encoded_rows):
    layers = down_rows.shape[1]
    width = totals.shape[1]
    rows = image_rows.shape[0]
    layer_rows = totals.shape[0] // layers
    off_qkv = 2 * down_rows.shape[0]
    local_width = heads * head_dim
    f32, low = jnp.float32, jnp.bfloat16
    any_spec = pl.BlockSpec(memory_space=pl.ANY)

    def out(shape, dtype=f32):
        return jax.ShapeDtypeStruct(shape, dtype)

    copies = 4 * -(-hidden_units // 128) + 9 * layers + 10
    return pl.pallas_call(
        functools.partial(finish_kernel, layers, heads, head_dim, hidden_units, layer_rows, off_qkv),
        out_shape=(
            out((tokens, width), low),
            out((tokens, width), low),
            out((layers, 3, local_width, width)),
            out((layers, 2, local_width)),
            out((layers, local_width, width)),
            out((layers, width)),
            out((hidden_units, layers, width)),
            out((layers, hidden_units)),
            out((hidden_units, layers, width)),
            out((layers, width)),
            out((layers, 2, width)),
            out((layers, 2, width)),
        ),
        in_specs=[any_spec] * 5,
        out_specs=(any_spec,) * 12,
        scratch_shapes=[
            pltpu.VMEM((hidden_units, layers, width), f32),
            pltpu.VMEM((hidden_units, layers, width), f32),
            pltpu.VMEM((layers, 4, local_width, width), f32),
            pltpu.VMEM((rows, width), low),
            pltpu.VMEM((rows, width), low),
            pltpu.VMEM((tokens, width), low),
            pltpu.VMEM((tokens, width), low),
            pltpu.VMEM((layers, TAIL_ROWS, width), f32),
            pltpu.VMEM((layers, 2, local_width), f32),
            pltpu.VMEM((layers, hidden_units), f32),
            pltpu.VMEM((2, layers, width), f32),
            pltpu.VMEM((2, layers, 2, width), f32),
            pltpu.SemaphoreType.DMA((copies,)),
        ],
        compiler_params=pltpu.CompilerParams(has_side_effects=True, vmem_limit_bytes=56 << 20),
    )(totals, down_rows, up_rows, image_rows, encoded_rows)


def local(
    dp_size,
    images,
    qkv_weight,
    qv_bias,
    out_weight,
    out_bias,
    up_weight,
    up_bias,
    down_weight,
    down_bias,
    norm_gain,
    norm_shift,
    cotangent,
):
    tokens, width = images.shape[1:]
    layers = qkv_weight.shape[0]
    local_width = qkv_weight.shape[3]
    heads = local_width // HEAD
    hidden_units = up_weight.shape[2]
    qkv_rows = jnp.swapaxes(qkv_weight, 2, 3)
    up = jnp.transpose(up_weight, (2, 0, 1))
    down = jnp.swapaxes(down_weight, 0, 1)
    *kept, last_part = forward(
        dp_size, tokens, HEAD, 0,
        images[0], qkv_rows, qv_bias, out_weight, out_bias, up, up_bias, down, down_bias,
        norm_gain, norm_shift,
    )
    flat, summed, image_grad, encoded, down_rows, up_rows = backward(
        tokens, HEAD, hidden_units, UNIT, 1, dp_size == 8,
        cotangent[0], *kept, qkv_rows, out_weight, norm_gain, last_part,
    )
    if dp_size != 8:
        summed = lax.psum(flat, "dp")
        per_layer = summed.reshape(layers, summed.shape[0] // layers, width)[::-1]
        stop = down_rows.shape[0]
        down_rows = jnp.swapaxes(per_layer[:, :stop], 0, 1)
        up_rows = jnp.swapaxes(per_layer[:, stop : 2 * stop], 0, 1)
    encoded, image_grad, qkv_grad, qv_grad, out_grad, out_b, up_grad, up_b, down_grad, down_b, gain, shift = finish(
        tokens, heads, HEAD, hidden_units, summed, down_rows, up_rows, image_grad, encoded
    )
    return (
        encoded[None],
        image_grad[None],
        jnp.swapaxes(qkv_grad, 2, 3),
        qv_grad,
        out_grad,
        out_b,
        jnp.transpose(up_grad, (1, 2, 0)),
        up_b,
        jnp.swapaxes(down_grad, 0, 1),
        down_b,
        gain,
        shift,
    )


def solution(mesh):
    in_specs = (
        P("dp", None, None),
        P(None, None, None, "tensor"),
        P(None, None, "tensor"),
        P(None, "tensor", None),
        P(),
        P(None, None, "tensor"),
        P(None, "tensor"),
        P(None, "tensor", None),
        P(),
        P(),
        P(),
        P("dp", None, None),
    )
    out_specs = (
        P("dp", None, None),
        P("dp", None, None),
        P(None, None, None, "tensor"),
        P(None, None, "tensor"),
        P(None, "tensor", None),
        P(),
        P(None, None, "tensor"),
        P(None, "tensor"),
        P(None, "tensor", None),
        P(),
        P(),
        P(),
    )
    return jax.shard_map(
        functools.partial(local, mesh.shape["dp"]), mesh=mesh, in_specs=in_specs, out_specs=out_specs, check_vma=False)
```

```python
import functools

import jax
import jax.numpy as jnp
from jax import lax
from jax.experimental import pallas as pl
from jax.experimental.pallas import tpu as pltpu
from jax.sharding import PartitionSpec as P

MESH = pl.DeviceIdType.MESH
SLOTS = 24
FEW = 8
HOP = 3
ROUND = 3
PARTS = 10
TICK_SPAN = 7 * HOP + 2
TICK_BUFFERS = 17


def grad_sum_ticks(dp_sum, unit, steps, grads, totals, buffers, sems):
    (
        x_in, inner_in, mid_in, own_a, total_a,
        whole_in, half_in, side_in, own_b, total_b,
        far_in, cross_in, near_in, end_in, own_f, own_n, total_e,
    ) = buffers
    (
        x_sem, inner_sem, mid_sem, out_pair_sem, out_x_sem,
        whole_sem, half_sem, side_sem, back_mid_sem, back_pair_sem, relay_sem,
        far_sem, cross_sem, near_sem, end_sem, back_one_sem, back_two_sem, back_three_sem,
        load_a_sem, store_a_sem, load_b_sem, store_b_sem, load_f_sem, load_n_sem, store_e_sem,
    ) = sems
    dp = lax.axis_index("dp")
    tensor = lax.axis_index("tensor")
    z = dp // 2
    x = dp % 2
    is_mid = (z == 1) | (z == 2)
    is_end = jnp.logical_not(is_mid)
    x_peer = (dp + 1 - 2 * x, tensor)
    pair_peer = (dp + 2 - 4 * (z % 2), tensor)
    mid_z = jnp.where(is_mid, 3 - z, z)
    mid_peer = (mid_z * 2 + x, tensor)
    side = jnp.where(z == 2, 1, 0)
    near = jnp.where(z >= 2, 1, 0)

    def greet(others):
        barrier = pltpu.get_barrier_semaphore()
        for peer in others + ((x_peer, pair_peer) if dp_sum else ()):
            pl.semaphore_signal(barrier, inc=1, device_id=peer, device_id_type=MESH)
        if dp_sum:

            @pl.when(is_mid)
            def _():
                pl.semaphore_signal(barrier, inc=1, device_id=mid_peer, device_id_type=MESH)

    def met(others):
        barrier = pltpu.get_barrier_semaphore()
        if dp_sum:
            pl.when(is_mid)(lambda: pl.semaphore_wait(barrier, 3 + len(others)))
            pl.when(is_end)(lambda: pl.semaphore_wait(barrier, 2 + len(others)))
        else:
            pl.semaphore_wait(barrier, len(others))

    def rows(chunk, part, count=1):
        return pl.ds(pl.multiple_of((chunk * PARTS + part) * unit, 8), count * unit)

    def row_a(c, part):
        return rows(c // ROUND, 2 * lax.rem(c, ROUND) + part)

    def row_m(c, part, count=1):
        return rows(c, 6 + part, count)

    def row_e(c, part):
        return rows(c, 8 + part)

    def remote(src, dst, sem, slot, peer):
        return pltpu.make_async_remote_copy(
            src_ref=src, dst_ref=dst, send_sem=sem.at[0, slot], recv_sem=sem.at[1, slot],
            device_id=peer, device_id_type=MESH,
        )

    def local_copy(src, dst, sem, slot):
        return pltpu.make_async_copy(src, dst, sem.at[slot])

    def a_x(c, s):
        return remote(grads.at[row_a(c, 1 - x)], x_in.at[s], x_sem, s, x_peer)

    def a_load(c, s):
        return local_copy(grads.at[row_a(c, x)], own_a.at[s], load_a_sem, s)

    def a_inner(c, s):
        return remote(own_a.at[s], inner_in.at[s], inner_sem, s, pair_peer)

    def a_mid(c, s):
        return remote(own_a.at[s], mid_in.at[s], mid_sem, s, mid_peer)

    def a_out_pair(c, s):
        return remote(total_a.at[s], totals.at[row_a(c, x)], out_pair_sem, s, pair_peer)

    def a_out_x(c, s):
        return remote(total_a.at[s], totals.at[row_a(c, x)], out_x_sem, s, x_peer)

    def a_store(c, s):
        return local_copy(total_a.at[s], totals.at[row_a(c, x)], store_a_sem, s)

    def a_relay(c, s):
        return remote(totals.at[row_a(c, x)], totals.at[row_a(c, x)], out_x_sem, s, x_peer)

    def a_back(c, s):
        return remote(totals.at[row_a(c, x)], totals.at[row_a(c, 1 - x)], out_x_sem, s, x_peer)

    def m_whole(c, s):
        return remote(grads.at[row_m(c, 0, 2)], whole_in.at[s], whole_sem, s, pair_peer)

    def m_load(c, s):
        return local_copy(grads.at[row_m(c, 0, 2)], own_b.at[s], load_b_sem, s)

    def m_half(c, s):
        return remote(own_b.at[s, pl.ds((1 - side) * unit, unit)], half_in.at[s], half_sem, s, mid_peer)

    def m_side(c, s):
        return remote(own_b.at[s, pl.ds(side * unit, unit)], side_in.at[s], side_sem, s, x_peer)

    def m_store(c, s):
        return local_copy(total_b.at[s], totals.at[row_m(c, side)], store_b_sem, s)

    def m_back_mid(c, s):
        return remote(total_b.at[s], totals.at[row_m(c, side)], back_mid_sem, s, mid_peer)

    def m_back_pair(c, s):
        return remote(total_b.at[s], totals.at[row_m(c, side)], back_pair_sem, s, pair_peer)

    def m_relay(c, s):
        return remote(totals.at[row_m(c, 1 - side)], totals.at[row_m(c, 1 - side)], relay_sem, s, pair_peer)

    def e_far(c, s):
        return remote(grads.at[row_e(c, 1 - near)], far_in.at[s], far_sem, s, pair_peer)

    def e_load_far(c, s):
        return local_copy(grads.at[row_e(c, 1 - near)], own_f.at[s], load_f_sem, s)

    def e_load_near(c, s):
        return local_copy(grads.at[row_e(c, near)], own_n.at[s], load_n_sem, s)

    def e_cross(c, s):
        return remote(own_f.at[s], cross_in.at[s], cross_sem, s, mid_peer)

    def e_near(c, s):
        return remote(own_n.at[s], near_in.at[s], near_sem, s, pair_peer)

    def e_end(c, s):
        return remote(own_n.at[s], end_in.at[s], end_sem, s, x_peer)

    def e_store(c, s):
        return local_copy(total_e.at[s], totals.at[row_e(c, near)], store_e_sem, s)

    def e_back_one(c, s):
        return remote(total_e.at[s], totals.at[row_e(c, near)], back_one_sem, s, pair_peer)

    def e_back_two(c, s):
        return remote(totals.at[row_e(c, near)], totals.at[row_e(c, near)], back_two_sem, s, mid_peer)

    def e_back_three(c, s):
        return remote(totals.at[row_e(c, 1 - near)], totals.at[row_e(c, 1 - near)], back_three_sem, s, pair_peer)

    def a_start(c, s):
        a_x(c, s).start()
        a_load(c, s).start()

    def a_one(c, s):
        a_load(c, s).wait()
        a_x(c, s).wait_recv()
        own_a[s] = own_a[s] + x_in[s]
        pl.when(is_end)(lambda: a_inner(c, s).start())

    def a_two(c, s):
        a_inner(c, s).wait_recv()
        own_a[s] = own_a[s] + inner_in[s]
        a_mid(c, s).start()

    def a_three(c, s):
        a_mid(c, s).wait_recv()
        total_a[s] = own_a[s] + mid_in[s]
        a_out_pair(c, s).start()
        a_out_x(c, s).start()
        a_store(c, s).start()

    def a_four(c, s):
        a_out_pair(c, s).wait_recv()
        a_relay(c, s).start()

    def a_five(c, s):
        a_back(c, s).wait_recv()

    def a_done(c, s):
        a_x(c, s).wait_send()
        a_out_x(c, s).wait_send()
        pl.when(is_end)(lambda: a_inner(c, s).wait_send())

        @pl.when(is_mid)
        def _():
            a_mid(c, s).wait_send()
            a_out_pair(c, s).wait_send()
            a_store(c, s).wait()

    def m_start(c, s):
        pl.when(is_end)(lambda: m_whole(c, s).start())
        pl.when(is_mid)(lambda: m_load(c, s).start())

    def m_one(c, s):
        m_load(c, s).wait()
        m_whole(c, s).wait_recv()
        own_b[s] = own_b[s] + whole_in[s]
        m_half(c, s).start()

    def m_two(c, s):
        m_half(c, s).wait_recv()
        mine = pl.ds(pl.multiple_of(side * unit, 8), unit)
        own_b[s, mine] = own_b[s, mine] + half_in[s]
        m_side(c, s).start()

    def m_three(c, s):
        m_side(c, s).wait_recv()
        mine = pl.ds(pl.multiple_of(side * unit, 8), unit)
        total_b[s] = own_b[s, mine] + side_in[s]
        m_back_mid(c, s).start()
        m_back_pair(c, s).start()
        m_store(c, s).start()

    def m_four(c, s):
        m_back_mid(c, s).wait_recv()
        m_relay(c, s).start()

    def m_five(c, s):
        m_back_pair(c, s).wait_recv()
        m_relay(c, s).wait_recv()

    def m_done(c, s):
        pl.when(is_end)(lambda: m_whole(c, s).wait_send())

        @pl.when(is_mid)
        def _():
            m_half(c, s).wait_send()
            m_side(c, s).wait_send()
            m_back_mid(c, s).wait_send()
            m_back_pair(c, s).wait_send()
            m_store(c, s).wait()
            m_relay(c, s).wait_send()

    def e_start(c, s):
        e_load_near(c, s).start()
        pl.when(is_end)(lambda: e_far(c, s).start())
        pl.when(is_mid)(lambda: e_load_far(c, s).start())

    def e_one(c, s):
        e_load_far(c, s).wait()
        e_far(c, s).wait_recv()
        own_f[s] = own_f[s] + far_in[s]
        e_cross(c, s).start()

    def e_two(c, s):
        e_load_near(c, s).wait()
        e_cross(c, s).wait_recv()
        own_n[s] = own_n[s] + cross_in[s]
        e_near(c, s).start()

    def e_three(c, s):
        e_load_near(c, s).wait()
        e_near(c, s).wait_recv()
        own_n[s] = own_n[s] + near_in[s]
        e_end(c, s).start()

    def e_four(c, s):
        e_end(c, s).wait_recv()
        total_e[s] = own_n[s] + end_in[s]
        e_back_one(c, s).start()
        e_store(c, s).start()

    def e_five(c, s):
        e_back_one(c, s).wait_recv()
        e_back_two(c, s).start()

    def e_six(c, s):
        e_back_two(c, s).wait_recv()
        e_back_three(c, s).start()

    def e_seven(c, s):
        e_back_three(c, s).wait_recv()

    def e_done(c, s):
        @pl.when(is_end)
        def _():
            e_far(c, s).wait_send()
            e_end(c, s).wait_send()
            e_back_one(c, s).wait_send()
            e_store(c, s).wait()

        @pl.when(is_mid)
        def _():
            e_cross(c, s).wait_send()
            e_near(c, s).wait_send()
            e_back_two(c, s).wait_send()
            e_back_three(c, s).wait_send()

    def stage(step, offset, phase, guard, body):
        at = step - offset
        ok = (at >= 0) & (at < steps)
        if guard is not None:
            ok = ok & guard
        if phase is None:
            chunk, slots = at, SLOTS
        else:
            ok = ok & (lax.rem(at, ROUND) == phase)
            chunk, slots = at // ROUND, FEW

        @pl.when(ok)
        def _():
            body(chunk, lax.rem(chunk, slots))

    def tick(step):
        if not dp_sum:
            return
        stage(step, 0, None, None, a_start)
        stage(step, 0, 0, None, m_start)
        stage(step, 0, 1, None, e_start)
        stage(step, 6 * HOP, 1, is_mid, e_six)
        stage(step, 5 * HOP, 1, is_mid, e_five)
        stage(step, 4 * HOP, 1, is_end, e_four)
        stage(step, 4 * HOP, 0, is_mid, m_four)
        stage(step, 3 * HOP, None, is_mid, a_three)
        stage(step, 3 * HOP, 0, is_mid, m_three)
        stage(step, 4 * HOP, None, is_end, a_four)
        stage(step, 3 * HOP, 1, is_end, e_three)
        stage(step, 2 * HOP, None, is_mid, a_two)
        stage(step, 2 * HOP, 0, is_mid, m_two)
        stage(step, 2 * HOP, 1, is_mid, e_two)
        stage(step, HOP, None, None, a_one)
        stage(step, HOP, 0, is_mid, m_one)
        stage(step, HOP, 1, is_mid, e_one)
        stage(step, 5 * HOP, None, None, a_five)
        stage(step, 5 * HOP, 0, is_end, m_five)
        stage(step, 7 * HOP, 1, is_end, e_seven)
        stage(step, 5 * HOP + 1, None, None, a_done)
        stage(step, 5 * HOP + 1, 0, None, m_done)
        stage(step, 7 * HOP + 1, 1, None, e_done)

    return tick, greet, met


def tick_scratch(unit, width):
    many, few, double = (SLOTS, unit, width), (FEW, unit, width), (FEW, 2 * unit, width)
    shapes = [many] * 5 + [double, few, few, double, few] + [few] * 7
    buffers = [pltpu.VMEM(shape, jnp.float32) for shape in shapes]
    sems = [pltpu.SemaphoreType.DMA((2, SLOTS))] * 5 + [pltpu.SemaphoreType.DMA((2, FEW))] * 13
    sems += [pltpu.SemaphoreType.DMA((SLOTS,))] * 2 + [pltpu.SemaphoreType.DMA((FEW,))] * 5
    return buffers, sems


HEAD = 72
EPSILON = 1e-06
UNIT = 8
TAIL_ROWS = 8


FIRST = 1
PIECE = 16
LAG = 4
BLOCK = 128
WIDE_BLOCK = 192
SPLIT_SLOTS = 4


def dot_nn(left, right):
    return lax.dot_general(left, right, (((1,), (0,)), ((), ())), preferred_element_type=jnp.float32)


def dot_nt(left, right):
    return lax.dot_general(left, right, (((1,), (1,)), ((), ())), preferred_element_type=jnp.float32)


def dot_tn(left, right):
    return lax.dot_general(left, right, (((0,), (0,)), ((), ())), preferred_element_type=jnp.float32)


def fold(array):
    return jnp.sum(array, axis=0, keepdims=True)


def gelu_slope(v):
    root = 0.7978845608028654
    inner = jnp.tanh(root * (v + 0.044715 * (v * v * v)))
    return 0.5 * (1.0 + inner) + 0.5 * v * (1.0 - inner * inner) * (root * (1.0 + 0.134145 * (v * v)))


def norm_back(grad_normed, state, gain):
    centred = state - jnp.mean(state, axis=-1, keepdims=True)
    inverse = lax.rsqrt(jnp.mean(centred * centred, axis=-1, keepdims=True) + EPSILON)
    unit = centred * inverse
    grad_unit = grad_normed * gain
    inner = (
        grad_unit
        - jnp.mean(grad_unit, axis=-1, keepdims=True)
        - unit * jnp.mean(grad_unit * unit, axis=-1, keepdims=True)
    )
    return inverse * inner, fold(grad_normed * unit), fold(grad_normed)


def backward_kernel(
    dp_sum, tokens, layers, heads, units_rows, head_dim, send_rows, unit, steps,
    cotangent, hidden, active, normed_two, normed, middle, state, qkv, logsum, mixed,
    down, up, qkv_w, out_w, gain, last_part,
    grads, totals, image_grad, encoded, down_grad, up_grad,
    raw_buf, wide, act_buf, two_buf, qkv_buf, lse_buf, mix_buf, down_buf, up_buf, qkvw_buf, outw_buf, gain_buf,
    flow, flow_low, hid_low, part, total, core_in, acc, y_in, grad_mix, cat, tight, acc_k, acc_v, stage_buf, small,
    woven, load_sem, stage_sem, turn_sem, weave_sem, core_send, core_recv, y_send, y_recv, back_send, back_recv,
    *tick_refs
):
    width = grads.shape[1]
    rows = part.shape[0]
    blocks = rows // BLOCK
    half = send_rows // 2
    pieces = half // PIECE
    tick, greet, met = grad_sum_ticks(
        dp_sum, unit, steps, grads, totals, tick_refs[:TICK_BUFFERS], tick_refs[TICK_BUFFERS:]
    )
    dp = lax.axis_index("dp")
    tensor = lax.axis_index("tensor")
    core = tensor % 2
    core_peer = (dp, tensor + 1 - 2 * core)
    y_peer = (dp, lax.rem(tensor + 2, 4))
    greet((core_peer, y_peer))
    layer_rows = grads.shape[0] // layers
    off_up = units_rows
    local_width = heads * head_dim
    off_qkv = 2 * units_rows
    off_out = off_qkv + 3 * local_width
    off_small = off_out + local_width
    spread = spread_matrix(heads, head_dim)

    def mine(i):
        return pl.ds(pl.multiple_of(core * half + i * PIECE, 8), PIECE)

    def other(i):
        return pl.ds(pl.multiple_of((1 - core) * half + i * PIECE, 8), PIECE)

    def here(i):
        return pl.ds(pl.multiple_of(i * PIECE, 8), PIECE)

    def remote(src, dst, send, recv, peer):
        return pltpu.make_async_remote_copy(
            src_ref=src, dst_ref=dst, send_sem=send, recv_sem=recv, device_id=peer, device_id_type=MESH
        )

    def to_core(p, i):
        return remote(
            part.at[other(i)], core_in.at[here(i)], core_send.at[p, i], core_recv.at[p, i], core_peer
        )

    def to_y(p, i):
        return remote(acc.at[here(i)], y_in.at[p, here(i)], y_send.at[p, i], y_recv.at[p, i], y_peer)

    def to_back(p, i):
        return remote(total.at[mine(i)], total.at[mine(i)], back_send.at[p, i], back_recv.at[p, i], core_peer)

    def from_back(p, i):
        return remote(
            total.at[other(i)], total.at[other(i)], back_send.at[p, i], back_recv.at[p, i], core_peer
        )

    def sum_begin(p):
        def go(i, c):
            to_core(p, i).start()
            return c

        lax.fori_loop(0, pieces, go, 0)

    def sum_step(p, j):
        @pl.when(j < pieces)
        def _():
            to_core(p, j).wait_recv()
            acc[here(j)] = part[mine(j)] + core_in[here(j)]
            to_y(p, j).start()

        late = j - LAG

        @pl.when((late >= 0) & (late < pieces))
        def _():
            to_y(p, late).wait_recv()
            total[mine(late)] = acc[here(late)] + y_in[p, here(late)]
            to_back(p, late).start()

        last = j - LAG - 2

        @pl.when((last >= 0) & (last < pieces))
        def _():
            to_core(p, last).wait_send()
            to_y(p, last).wait_send()
            to_back(p, last).wait_send()
            from_back(p, last).wait_recv()

    sum_steps = pieces + LAG + 2

    def load(source, target, sem):
        return pltpu.make_async_copy(source, target, load_sem.at[sem])

    def stage_copy(slot, row, size):
        return pltpu.make_async_copy(
            stage_buf.at[slot, pl.ds(0, size)], grads.at[pl.ds(pl.multiple_of(row, 8), size)], stage_sem.at[slot]
        )

    tiles = width // 128
    last_rows = units_rows - (tiles - 1) * 128
    layer_ticks = tiles + 1 + 4 * blocks + 2 * sum_steps + heads * blocks

    def row_block(b):
        return pl.ds(pl.multiple_of(b * BLOCK, 16), BLOCK)

    total[pl.ds(send_rows, rows - send_rows)] = jnp.zeros((rows - send_rows, width), jnp.float32)
    start = load(cotangent, raw_buf, 11)
    start.start()
    load(active.at[layers - 1], act_buf, 3).start()
    gain_load = load(gain, gain_buf, 10)
    gain_load.start()
    start.wait()
    lower_rows(raw_buf, flow_low, wide, tokens)
    met((core_peer, y_peer))

    def layer_body(it, carry):
        layer = layers - 1 - it
        base_tick = it * layer_ticks - FIRST
        base_row = it * layer_rows
        hidden_load = load(hidden.at[layer], wide, 0)
        down_load = load(down.at[layer], down_buf, 1)
        up_load = load(up.at[layer], up_buf, 2)
        active_load = load(active.at[layer], act_buf, 3)
        two_load = load(normed_two.at[layer], two_buf, 4)
        outw_load = load(out_w.at[layer], outw_buf, 5)
        qkv_load = load(qkv.at[layer], qkv_buf, 6)
        lse_load = load(logsum.at[layer], lse_buf, 7)
        mix_load = load(mixed.at[layer], mix_buf, 8)
        qkvw_load = load(qkv_w.at[layer], qkvw_buf, 9)
        pl.when(it > 0)(active_load.start)
        small[...] = jnp.zeros_like(small)

        def lower(b, c):
            at = row_block(b)
            flow_low[at] = flow[at].astype(jnp.bfloat16)
            return c

        @pl.when(it > 0)
        def _():
            lax.fori_loop(0, blocks, lower, 0)

        active_load.wait()
        for copy in (hidden_load, down_load, up_load, two_load, outw_load, qkv_load, lse_load, mix_load, qkvw_load):
            copy.start()

        def tile_copy(tile, row):
            slot = lax.rem(tile, 2)
            pl.when(tile < tiles - 1)(lambda: stage_copy(slot, row, 128).start())
            pl.when(tile == tiles - 1)(lambda: stage_copy(slot, row, last_rows).start())

        def tile_done(tile):
            slot = lax.rem(tile, 2)
            pl.when((tile >= 0) & (tile < tiles - 1))(lambda: stage_copy(slot, base_row, 128).wait())
            pl.when(tile == tiles - 1)(lambda: stage_copy(slot, base_row, last_rows).wait())

        def down_weights(j, c):
            tile_done(j - 1)
            tick(base_tick + j)

            @pl.when(j < tiles)
            def _():
                lanes = pl.ds(pl.multiple_of(j * 128, 128), 128)
                stage_buf[lax.rem(j, 2), pl.ds(0, 128)] = dot_tn(act_buf[:, lanes], flow_low[...])
                tile_copy(j, base_row + j * 128)

            return c

        lax.fori_loop(0, tiles + 1, down_weights, 0)
        tick_at = base_tick + tiles + 1

        @pl.when(it == 0)
        def _():
            gain_load.wait()
            lift_rows(raw_buf, flow, tokens, BLOCK)

        hidden_load.wait()
        down_load.wait()
        up_load.wait()

        def mlp(b, c):
            at = row_block(b)
            small[3:4] += fold(flow[at])
            grad_hidden = dot_nt(flow_low[at], down_buf[...]) * gelu_slope(wide[at])
            small[2:3] += fold(grad_hidden)
            hid = grad_hidden.astype(jnp.bfloat16)
            hid_low[at] = hid
            part[at] = dot_nn(hid, up_buf[...])
            tick(tick_at + b)
            return c

        lax.fori_loop(0, blocks, mlp, 0)
        sum_begin(0)
        middle_load = load(middle.at[layer], wide, 0)
        middle_load.start()
        two_load.wait()
        tick_at = tick_at + blocks

        def up_weights(j, c):
            sum_step(0, j)
            tile_done(j - 1)

            @pl.when(j < tiles)
            def _():
                lanes = pl.ds(pl.multiple_of(j * 128, 128), 128)
                stage_buf[lax.rem(j, 2), pl.ds(0, 128)] = dot_tn(hid_low[:, lanes], two_buf[...])
                tile_copy(j, base_row + off_up + j * 128)

            tick(tick_at + j)
            return c

        lax.fori_loop(0, sum_steps, up_weights, 0)
        tick_at = tick_at + sum_steps
        part_load = load(last_part, part, 1)
        pl.when(it == 0)(part_load.start)
        middle_load.wait()
        outw_load.wait()

        def norm_two(b, c):
            at = row_block(b)
            step_grad, gain_grad, shift_grad = norm_back(total[at], wide[at], gain_buf[layer, 1:2])
            small[5:6] += gain_grad
            small[7:8] += shift_grad
            grad = flow[at] + step_grad
            flow[at] = grad
            small[1:2] += fold(grad)
            low = grad.astype(jnp.bfloat16)
            flow_low[at] = low
            grad = dot_nt(low, outw_buf[...]).astype(jnp.bfloat16)
            grad_mix[at] = dot_nn(grad, spread).astype(jnp.bfloat16)
            tick(tick_at + b)
            return c

        lax.fori_loop(0, blocks, norm_two, 0)
        tick_at = tick_at + blocks
        state_load = load(state.at[layer], wide, 0)
        normed_load = load(normed.at[layer], act_buf, 3)
        state_load.start()
        normed_load.start()
        qkv_load.wait()
        lse_load.wait()
        scale = head_dim ** (-0.5)

        @pl.when(it == 0)
        def _():
            part_load.wait()
            sum_begin(2)


        def attend(m, c):
            head = m // blocks
            b = lax.rem(m, blocks)
            at = row_block(b)
            lanes = pl.ds(pl.multiple_of(head * 128, 128), 128)
            query = qkv_buf[0, head, at]
            key = qkv_buf[1, head]
            value = qkv_buf[2, head]
            grad = grad_mix[at, lanes]
            scores = dot_nt(query, key) * scale
            probs = jnp.exp(scores - lse_buf[head, at, 0:1])
            column = lax.broadcasted_iota(jnp.int32, probs.shape, 1)
            probs = jnp.where(column < tokens, probs, 0.0)
            grad_weights = dot_nt(grad, value)
            center = jnp.sum(probs * grad_weights, axis=-1, keepdims=True)
            raw = (probs * (grad_weights - center) * scale).astype(jnp.bfloat16)
            grad_query = dot_nn(raw, key)
            small[0:1, lanes] += fold(grad_query)
            cat[at, lanes] = grad_query.astype(jnp.bfloat16)
            add_k = dot_tn(raw, query)
            add_v = dot_tn(probs.astype(jnp.bfloat16), grad)

            @pl.when(b == 0)
            def _():
                acc_k[...] = add_k
                acc_v[...] = add_v

            @pl.when(b > 0)
            def _():
                acc_k[...] += add_k
                acc_v[...] += add_v

            @pl.when(b == blocks - 1)
            def _():
                at_k = pl.ds(pl.multiple_of((heads + head) * 128, 128), 128)
                at_v = pl.ds(pl.multiple_of((2 * heads + head) * 128, 128), 128)
                cat[:, at_k] = acc_k[...].astype(jnp.bfloat16)
                cat[:, at_v] = acc_v[...].astype(jnp.bfloat16)
                small[0:1, pl.ds(pl.multiple_of((heads + head) * 128, 128), 128)] += fold(acc_v[...])

            @pl.when(it == 0)
            def _():
                sum_step(2, 2 * m)
                sum_step(2, 2 * m + 1)

            tick(tick_at + m)
            return c

        lax.fori_loop(0, heads * blocks, attend, 0)
        tick_at = tick_at + heads * blocks
        qkvw_load.wait()

        def project(b, c):
            at = row_block(b)
            out = None
            for i in range(3):
                lanes = pl.ds(i * heads * 128, heads * 128)
                narrow = dot_nt(cat[at, lanes], spread).astype(jnp.bfloat16)
                tight[i, at] = narrow
                term = dot_nn(narrow, qkvw_buf[i])
                out = term if out is None else out + term
            part[at] = out

            @pl.when(it == 0)
            def _():
                hid_low[at] = total[at].astype(jnp.bfloat16)

            tick(tick_at + b)
            return c

        lax.fori_loop(0, blocks, project, 0)
        tick_at = tick_at + blocks
        sum_begin(1)
        encoded_store = load(hid_low, encoded, 1)
        pl.when(it == 0)(encoded_store.start)
        normed_load.wait()
        mix_load.wait()

        def attention_weights(j, c):
            sum_step(1, j)

            @pl.when((j >= 1) & (j < 5))
            def _():
                stage_copy(lax.rem(j - 1, 2), base_row, local_width).wait()

            slot = lax.rem(j, 2)

            @pl.when(j < 3)
            def _():
                stage_buf[slot] = dot_tn(tight[j], act_buf[...])

            @pl.when(j == 3)
            def _():
                stage_buf[slot] = dot_tn(mix_buf[...], flow_low[...])

            @pl.when(j < 4)
            def _():
                stage_copy(slot, base_row + off_qkv + j * local_width, local_width).start()

            tick(tick_at + j)
            return c

        lax.fori_loop(0, sum_steps, attention_weights, 0)
        tick_at = tick_at + sum_steps
        state_load.wait()

        def norm_one(b, c):
            at = row_block(b)
            step_grad, gain_grad, shift_grad = norm_back(total[at], wide[at], gain_buf[layer, 0:1])
            small[4:5] += gain_grad
            small[6:7] += shift_grad
            flow[at] = flow[at] + step_grad
            tick(tick_at + b)
            return c

        lax.fori_loop(0, blocks, norm_one, 0)
        tail = pltpu.make_async_copy(
            small, grads.at[pl.ds(pl.multiple_of(base_row + off_small, 8), small.shape[0])], load_sem.at[10]
        )
        tail.start()
        tail.wait()
        pl.when(it == 0)(encoded_store.wait)
        return carry

    lax.fori_loop(0, layers, layer_body, 0)

    def lower(b, c):
        flow_low[row_block(b)] = flow[row_block(b)].astype(jnp.bfloat16)
        return c

    lax.fori_loop(0, blocks, lower, 0)
    image_store = load(flow_low, image_grad, 0)
    image_store.start()

    tail = layers * layer_ticks - FIRST
    weaves, at_step = [], tail
    for k in range(2):
        last_row = (layers - 1) * layer_rows + (k + 1) * units_rows
        ready = -(-last_row // (PARTS * unit)) * ROUND + TICK_SPAN
        at_step = max(at_step, ready)
        weaves.append(at_step)
        at_step += tiles + 1

    def each_size(tile, body):
        pl.when(tile < tiles - 1)(lambda: body(128))
        pl.when(tile == tiles - 1)(lambda: body(last_rows))

    def weave_in(k, tile, layer, rows_here):
        row = pl.multiple_of((layers - 1 - layer) * layer_rows + k * units_rows + tile * 128, 8)
        slot = lax.rem(tile, 2)
        return pltpu.make_async_copy(
            totals.at[pl.ds(row, rows_here)],
            stage_buf.at[slot, pl.ds(layer * 128, rows_here)],
            weave_sem.at[slot, layer],
        )

    def weave_out(target, tile, rows_here):
        slot = lax.rem(tile, 2)
        return pltpu.make_async_copy(
            woven.at[slot, pl.ds(0, rows_here)], target.at[pl.ds(tile * 128, rows_here)], turn_sem.at[slot]
        )

    def weave(k, target, tile):
        def begin(rows_here):
            for layer in range(layers):
                weave_in(k, tile, layer, rows_here).start()

        def arrive(rows_here):
            for layer in range(layers):
                weave_in(k, tile - 1, layer, rows_here).wait()

        each_size(tile, begin)

        @pl.when(tile >= 1)
        def _():
            each_size(tile - 1, arrive)
            slot = lax.rem(tile - 1, 2)

            @pl.when(tile >= 3)
            def _():
                weave_out(target, tile - 3, 128).wait()

            for layer in range(layers):
                woven[slot, :, layer, :] = stage_buf[slot, pl.ds(layer * 128, 128)]
            each_size(tile - 1, lambda rows_here: weave_out(target, tile - 1, rows_here).start())

        @pl.when(tile == tiles)
        def _():
            weave_out(target, tiles - 2, 128).wait()
            weave_out(target, tiles - 1, last_rows).wait()

    def rest(step, c):
        tick(step)
        if dp_sum:
            for k, target in enumerate((down_grad, up_grad)):
                tile = step - weaves[k]

                @pl.when((tile >= 0) & (tile <= tiles))
                def _():
                    weave(k, target, tile)

        return c

    lax.fori_loop(tail, max(steps + TICK_SPAN, at_step), rest, 0)
    image_store.wait()


def backward(
    tokens, head_dim, hidden_units, unit, collective_id, dp_sum,
    cotangent, hidden, active, normed_two, normed, middle, state, qkv, logsum, mixed,
    down, up, qkv_w, out_w, gain, last_part,
):
    layers, rows, width = middle.shape
    heads = qkv.shape[2]
    units_rows = -(-hidden_units // 8) * 8
    send_rows = -(-tokens // (2 * PIECE)) * 2 * PIECE
    pieces = send_rows // (2 * PIECE)
    layer_rows = 2 * units_rows + 4 * heads * head_dim + TAIL_ROWS
    steps = layers * layer_rows // (PARTS * unit) * ROUND
    assert steps * PARTS * unit == layers * layer_rows * ROUND
    buffers, sems = tick_scratch(unit, width)
    f32, low = jnp.float32, jnp.bfloat16
    half = (send_rows // 2, width)
    full = (rows, width)
    any_spec = pl.BlockSpec(memory_space=pl.ANY)
    grads = jax.ShapeDtypeStruct((layers * layer_rows, width), f32)
    return pl.pallas_call(
        functools.partial(
            backward_kernel, dp_sum, tokens, layers, heads, units_rows, head_dim, send_rows, unit, steps
        ),
        out_shape=(
            grads,
            grads,
            jax.ShapeDtypeStruct(full, low),
            jax.ShapeDtypeStruct(full, low),
            jax.ShapeDtypeStruct((units_rows, layers, width), f32),
            jax.ShapeDtypeStruct((units_rows, layers, width), f32),
        ),
        in_specs=[any_spec] * 16,
        out_specs=(any_spec,) * 6,
        scratch_shapes=[
            pltpu.VMEM(cotangent.shape, low),
            pltpu.VMEM(full, f32),
            pltpu.VMEM(full, low),
            pltpu.VMEM(full, low),
            pltpu.VMEM(qkv.shape[1:], low),
            pltpu.VMEM(logsum.shape[1:], f32),
            pltpu.VMEM(mixed.shape[1:], low),
            pltpu.VMEM(down.shape[1:], low),
            pltpu.VMEM(up.shape[1:], low),
            pltpu.VMEM(qkv_w.shape[1:], low),
            pltpu.VMEM(out_w.shape[1:], low),
            pltpu.VMEM(gain.shape, f32),
            pltpu.VMEM(full, f32),
            pltpu.VMEM(full, low),
            pltpu.VMEM(full, low),
            pltpu.VMEM(full, f32),
            pltpu.VMEM(full, f32),
            pltpu.VMEM(half, f32),
            pltpu.VMEM(half, f32),
            pltpu.VMEM((3,) + half, f32),
            pltpu.VMEM((rows, heads * 128), low),
            pltpu.VMEM((rows, 3 * heads * 128), low),
            pltpu.VMEM((3, rows, heads * head_dim), low),
            pltpu.VMEM((rows, 128), f32),
            pltpu.VMEM((rows, 128), f32),
            pltpu.VMEM((2, heads * head_dim, width), f32),
            pltpu.VMEM((TAIL_ROWS, width), f32),
            pltpu.VMEM((2, 128, layers, width), f32),
        ]
        + [pltpu.SemaphoreType.DMA((12,)), pltpu.SemaphoreType.DMA((2,)), pltpu.SemaphoreType.DMA((2,)), pltpu.SemaphoreType.DMA((2, layers))]
        + [pltpu.SemaphoreType.DMA((3, pieces))] * 6
        + buffers
        + sems,
        compiler_params=pltpu.CompilerParams(
            collective_id=collective_id, has_side_effects=True, vmem_limit_bytes=63 << 20
        ),
    )(
        cotangent, hidden, active, normed_two, normed, middle, state, qkv, logsum, mixed,
        down, up, qkv_w, out_w, gain, last_part,
    )


def lift_rows(source, target, tokens, size):
    blocks = target.shape[0] // size

    def one(b, c):
        at = pl.ds(pl.multiple_of(b * size, 16), size)
        target[at] = source[at].astype(jnp.float32)
        return c

    lax.fori_loop(0, blocks - 1, one, 0)
    begin = (blocks - 1) * size
    target[pl.ds(begin, size)] = jnp.zeros((size, target.shape[1]), jnp.float32)
    last = pl.ds(begin, tokens - begin)
    target[last] = source[last].astype(jnp.float32)


def lower_rows(source, target, wide, tokens):
    full = tokens // BLOCK

    def one(b, c):
        at = pl.ds(pl.multiple_of(b * BLOCK, 16), BLOCK)
        target[at] = source[at]
        return c

    lax.fori_loop(0, full, one, 0)
    tail = pl.ds(full * BLOCK, target.shape[0] - full * BLOCK)
    wide[tail] = jnp.zeros((target.shape[0] - full * BLOCK, target.shape[1]), jnp.float32)
    some = pl.ds(full * BLOCK, tokens - full * BLOCK)
    wide[some] = source[some].astype(jnp.float32)
    target[tail] = wide[tail].astype(jnp.bfloat16)


def spread_matrix(heads, head_dim):
    shape = (heads * head_dim, heads * 128)
    source = lax.broadcasted_iota(jnp.int32, shape, 0)
    lane = lax.broadcasted_iota(jnp.int32, shape, 1)
    hit = (lane // 128 * head_dim + lane % 128 == source) & (lane % 128 < head_dim)
    return jnp.where(hit, 1.0, 0.0).astype(jnp.bfloat16)


def norm_unit(state):
    centred = state - jnp.mean(state, axis=-1, keepdims=True)
    return centred * lax.rsqrt(jnp.mean(centred * centred, axis=-1, keepdims=True) + EPSILON)


def gelu(v):
    return 0.5 * v * (1.0 + jnp.tanh(0.7978845608028654 * (v + 0.044715 * (v * v * v))))


def block_sum(pieces, dp, tensor, part, core_in, y_in, total, sems):
    core = tensor % 2
    core_peer = (dp, tensor + 1 - 2 * core)
    y_peer = (dp, lax.rem(tensor + 2, 4))
    core_sem, y_sem, back_sem = sems
    per_block = WIDE_BLOCK // (2 * PIECE)

    def mine(i):
        return pl.ds(pl.multiple_of((2 * i + core) * PIECE, 8), PIECE)

    def other(i):
        return pl.ds(pl.multiple_of((2 * i + 1 - core) * PIECE, 8), PIECE)

    def here(i):
        return pl.ds(pl.multiple_of(i * PIECE, 8), PIECE)

    def remote(src, dst, sem, i, peer):
        return pltpu.make_async_remote_copy(
            src_ref=src, dst_ref=dst, send_sem=sem.at[0, i], recv_sem=sem.at[1, i],
            device_id=peer, device_id_type=MESH,
        )

    def to_core(i):
        return remote(part.at[other(i)], core_in.at[here(i)], core_sem, i, core_peer)

    def to_y(i):
        return remote(core_in.at[here(i)], y_in.at[here(i)], y_sem, i, y_peer)

    def to_back(i):
        return remote(total.at[mine(i)], total.at[mine(i)], back_sem, i, core_peer)

    def from_back(i):
        return remote(total.at[other(i)], total.at[other(i)], back_sem, i, core_peer)

    def each(b, body):
        def go(k, c):
            i = b * per_block + k

            @pl.when(i < pieces)
            def _():
                body(i)

            return c

        lax.fori_loop(0, per_block, go, 0)

    def send(b):
        each(b, lambda i: to_core(i).start())

    def meet(b):
        def body(i):
            to_core(i).wait_recv()
            core_in[here(i)] = core_in[here(i)] + part[mine(i)]
            to_y(i).start()

        each(b, body)

    def close(b):
        def body(i):
            to_y(i).wait_recv()
            total[mine(i)] = core_in[here(i)] + y_in[here(i)]
            to_back(i).start()

        each(b, body)

    def finish(b):
        def body(i):
            to_core(i).wait_send()
            to_y(i).wait_send()
            to_back(i).wait_send()
            from_back(i).wait_recv()

        each(b, body)

    return send, meet, close, finish


def pair_sum(pieces, dp, tensor, part, core_in, total, sems):
    core = tensor % 2
    core_peer = (dp, tensor + 1 - 2 * core)
    core_sem, back_sem = sems
    per_block = WIDE_BLOCK // (2 * PIECE)

    def mine(i):
        return pl.ds(pl.multiple_of((2 * i + core) * PIECE, 8), PIECE)

    def other(i):
        return pl.ds(pl.multiple_of((2 * i + 1 - core) * PIECE, 8), PIECE)

    def here(i):
        return pl.ds(pl.multiple_of(i * PIECE, 8), PIECE)

    def remote(src, dst, sem, i):
        return pltpu.make_async_remote_copy(
            src_ref=src, dst_ref=dst, send_sem=sem.at[0, i], recv_sem=sem.at[1, i],
            device_id=core_peer, device_id_type=MESH,
        )

    def to_core(i):
        return remote(part.at[other(i)], core_in.at[here(i)], core_sem, i)

    def to_back(i):
        return remote(total.at[mine(i)], total.at[mine(i)], back_sem, i)

    def from_back(i):
        return remote(total.at[other(i)], total.at[other(i)], back_sem, i)

    def each(b, body):
        def go(k, c):
            i = b * per_block + k

            @pl.when(i < pieces)
            def _():
                body(i)

            return c

        lax.fori_loop(0, per_block, go, 0)

    def send(b):
        each(b, lambda i: to_core(i).start())

    def meet(b):
        def body(i):
            to_core(i).wait_recv()
            total[mine(i)] = core_in[here(i)] + part[mine(i)]
            to_back(i).start()

        each(b, body)

    def finish(b):
        def body(i):
            to_core(i).wait_send()
            to_back(i).wait_send()
            from_back(i).wait_recv()

        each(b, body)

    return send, meet, finish


def forward_kernel(
    dp_size, tokens, layers, heads, head_dim, send_rows,
    images, qkv_w, qv_b, out_w, out_b, up, up_b, down, down_b, gain, shift,
    hidden, active, normed_two, normed, middle, state, qkv, logsum, mixed, down_rows, up_rows, last_part,
    image_buf, upb_raw, flow, normed_buf, qkv_buf, lse_buf, mix_buf, tight_buf, two_buf, hidden_buf, active_buf,
    qkvw_buf, outw_buf, up_buf, down_buf, qvb_buf, outb_buf, upb_buf, downb_buf, gain_buf, shift_buf,
    part_a, core_in_a, total_a, part_b, core_in_b, y_in_b, total_b,
    quarter_buf, y_rows, both_w, both_mix, packed, y_packed,
    pair_buf, edge_buf, load_sem, weight_sem, store_sem, block_sem, split_sem, split_out_sem,
    quarter_sem, rows_sem, packed_sem, *sum_sems
):
    rows, width = flow.shape
    local_width = heads * head_dim
    blocks = rows // WIDE_BLOCK
    pieces = send_rows // (2 * PIECE)
    dp = lax.axis_index("dp")
    tensor = lax.axis_index("tensor")
    core = tensor % 2
    barrier = pltpu.get_barrier_semaphore()
    y_peer = (dp, lax.rem(tensor + 2, 4))
    upper = tensor // 2
    spot = dp % 4
    spot_one = spot + 1 - 2 * (dp % 2)
    spot_two = lax.rem(spot + 2, 4)
    peer_one = (dp + 1 - 2 * (dp % 2), tensor)
    peer_two = (dp + 2 - 4 * (spot // 2), tensor)
    for peer in [(dp, tensor + 1 - 2 * core), y_peer, peer_one, peer_two]:
        pl.semaphore_signal(barrier, inc=1, device_id=peer, device_id_type=MESH)
    quarter = quarter_buf.shape[1]
    group = packed.shape[1]

    def remote(src, dst, sem, peer):
        return pltpu.make_async_remote_copy(
            src_ref=src, dst_ref=dst, send_sem=sem[0], recv_sem=sem[1], device_id=peer, device_id_type=MESH
        )

    def quarter_rows(at):
        return pl.ds(pl.multiple_of(at * quarter, 8), quarter)

    def quarter_out(layer):
        return remote(
            quarter_buf.at[layer], y_rows.at[layer, quarter_rows(spot)],
            (quarter_sem.at[0, layer], quarter_sem.at[1, layer]), y_peer,
        )

    def rows_copy(layer, k, at, peer):
        here = y_rows.at[layer, quarter_rows(at)]
        return remote(here, here, (rows_sem.at[0, layer, k], rows_sem.at[1, layer, k]), peer)

    def rows_out(layer, k):
        at, peer = ((spot, peer_one), (spot, peer_two), (spot_one, peer_two))[k]
        return rows_copy(layer, k, at, peer)

    def rows_back(layer, k):
        at, peer = ((spot_one, peer_one), (spot_two, peer_two), (3 - spot, peer_two))[k]
        return rows_copy(layer, k, at, peer)

    def share_own(layer):
        quarter_out(layer).wait_recv()
        rows_out(layer, 0).start()
        rows_out(layer, 1).start()

    def share_other(layer):
        rows_back(layer, 0).wait_recv()
        rows_out(layer, 2).start()

    def packed_out(layer, b):
        return remote(
            packed.at[b], y_packed.at[layer, b], (packed_sem.at[0, layer, b], packed_sem.at[1, layer, b]), y_peer
        )

    def weights(layer):
        return (pltpu.make_async_copy(qkv_w.at[layer], qkvw_buf, weight_sem.at[0]),)

    tiles = up_buf.shape[0] // 128
    units = up.shape[0]
    last_units = units - (tiles - 1) * 128

    def split_in(k, tile, size):
        slot = lax.rem(k * tiles + tile, SPLIT_SLOTS)
        source = (up, down)[k]
        return pltpu.make_async_copy(
            source.at[pl.ds(tile * 128, size)], pair_buf.at[slot, pl.ds(0, size)], split_sem.at[0, slot]
        )

    def split_size(tile, body):
        pl.when(tile < tiles - 1)(lambda: body(128))
        pl.when(tile == tiles - 1)(lambda: body(last_units))

    def split_begin():
        for tile in range(SPLIT_SLOTS - 1):
            split_in(0, tile, 128).start()

    def split_out(k, layer):
        source, target = ((up_buf, up_rows), (down_buf, down_rows))[k]
        return pltpu.make_async_copy(source, target.at[layer], split_out_sem.at[k])

    def split(layer):
        for k, target in enumerate((up_buf, down_buf)):

            def one(tile, c):
                slot = lax.rem(k * tiles + tile, SPLIT_SLOTS)
                ahead = tile + SPLIT_SLOTS - 1
                pl.when(ahead < tiles)(lambda: split_size(ahead, lambda size: split_in(k, ahead, size).start()))
                if k == 0:
                    pl.when(ahead >= tiles)(lambda: split_in(1, ahead - tiles, 128).start())
                split_size(tile, lambda size: split_in(k, tile, size).wait())
                at = pl.ds(pl.multiple_of(tile * 128, 128), 128)

                @pl.when(tile < tiles - 1)
                def _():
                    target[at] = pair_buf[slot, :, layer, :]

                @pl.when(tile == tiles - 1)
                def _():
                    edge_buf[...] = jnp.zeros_like(edge_buf)
                    edge_buf[pl.ds(0, last_units)] = pair_buf[slot, pl.ds(0, last_units), layer, :].astype(jnp.float32)
                    target[at] = edge_buf[...].astype(jnp.bfloat16)

                return c

            lax.fori_loop(0, tiles, one, 0)
            split_out(k, layer).start()


    singles = [
        pltpu.make_async_copy(source, target, load_sem.at[i])
        for i, (source, target) in enumerate(
            (
                (out_w, outw_buf), (images, image_buf), (gain, gain_buf), (shift, shift_buf), (qv_b, qvb_buf),
                (out_b, outb_buf), (up_b, upb_raw), (down_b, downb_buf),
            )
        )
    ]
    for copy in singles:
        copy.start()
    current = weights(0)
    current[0].start()
    split_begin()
    spread = spread_matrix(heads, head_dim)
    total_a[pl.ds(send_rows, rows - send_rows)] = jnp.zeros((rows - send_rows, width), jnp.float32)
    total_b[pl.ds(send_rows, rows - send_rows)] = jnp.zeros((rows - send_rows, width), jnp.float32)
    singles[0].wait()
    for k in range(4):

        @pl.when(spot == k)
        def _():
            lead_rows = k * quarter % 16
            for layer in range(layers):
                some = outw_buf[layer, pl.ds(k * quarter - lead_rows, quarter + 8)].astype(jnp.float32)
                quarter_buf[layer] = some[lead_rows : lead_rows + quarter]

    pl.semaphore_wait(barrier, 4)
    quarter_out(0).start()
    for copy in singles[1:]:
        copy.wait()

    def row_block(b):
        return pl.ds(pl.multiple_of(b * WIDE_BLOCK, 16), WIDE_BLOCK)

    scale = head_dim ** (-0.5)
    stores = {}

    def block_store(layer, b, kind):
        at = row_block(b)
        source, target = (
            (flow, middle.at[layer, at]),
            (two_buf, normed_two.at[layer, at]),
            (hidden_buf, hidden.at[layer, at]),
            (active_buf, active.at[layer, at]),
            (part_b, last_part.at[at]),
        )[kind]
        return pltpu.make_async_copy(source.at[at], target, block_sem.at[kind, b])

    def keep(name, source, target, index):
        copy = pltpu.make_async_copy(source, target, store_sem.at[index])
        copy.start()
        stores[name] = copy

    def settle(*names):
        for name in names:
            if name in stores:
                stores.pop(name).wait()

    def project(layer, b, value):
        at = row_block(b)
        flow[at] = value
        low = (norm_unit(value) * gain_buf[layer, 0:1] + shift_buf[layer, 0:1]).astype(jnp.bfloat16)
        normed_buf[at] = low
        for i in range(3):
            out = dot_nt(low, qkvw_buf[i])
            if i != 1:
                out = out + qvb_buf[layer, i // 2 : i // 2 + 1]
            wide = dot_nn(out.astype(jnp.bfloat16), spread).astype(jnp.bfloat16)
            for head in range(heads):
                qkv_buf[i, head, at] = wide[:, head * 128 : (head + 1) * 128]

    def first(b, c):
        project(0, b, flow[row_block(b)])
        return c

    lift_rows(image_buf, flow, tokens, WIDE_BLOCK)
    upb_buf[...] = jnp.zeros_like(upb_buf)
    upb_buf[:, pl.ds(0, upb_raw.shape[1])] = upb_raw[...]
    current[0].wait()
    lax.fori_loop(0, blocks, first, 0)

    for layer in range(layers):
        keep("state", flow, state.at[layer], 0)
        keep("normed", normed_buf, normed.at[layer], 1)
        keep("qkv", qkv_buf, qkv.at[layer], 2)
        settle("logsum", "mixed")
        send_a, meet_a, finish_a = pair_sum(
            pieces, dp, tensor, part_a, core_in_a, total_a, [s.at[layer] for s in sum_sems[:2]]
        )
        send_b, meet_b, close_b, finish_b = block_sum(
            pieces, dp, tensor, part_b, core_in_b, y_in_b, total_b, [s.at[layer] for s in sum_sems[2:]]
        )
        is_last = layer == layers - 1
        if not is_last:
            following = weights(layer + 1)
            following[0].start()

        both_w[upper] = outw_buf[layer]

        def attend(b, c):
            if layer == 0:
                pl.when(b == 1)(lambda: share_own(0))
            at = row_block(b)

            def one_head(head):
                scores = dot_nt(qkv_buf[0, head, at], qkv_buf[1, head]) * scale
                column = lax.broadcasted_iota(jnp.int32, scores.shape, 1)
                scores = jnp.where(column < tokens, scores, -jnp.inf)
                peak = jnp.max(scores, axis=-1, keepdims=True)
                expo = jnp.exp(scores - peak)
                denominator = jnp.sum(expo, axis=-1, keepdims=True)
                probs = (expo / denominator).astype(jnp.bfloat16)
                value = dot_nn(probs, qkv_buf[2, head]).astype(jnp.bfloat16)
                return value, jnp.broadcast_to(peak + jnp.log(denominator), (WIDE_BLOCK, 128))

            def two_heads(pair, c):
                both = [one_head(2 * pair + i) for i in range(2)]
                for i, (value, logs) in enumerate(both):
                    head = 2 * pair + i
                    mix_buf[:, pl.ds(pl.multiple_of(head * 128, 128), 128)] = value
                    lse_buf[head, at] = logs
                return c

            lax.fori_loop(0, heads // 2, two_heads, 0)
            tight = dot_nt(mix_buf[...], spread).astype(jnp.bfloat16)
            tight_buf[at] = tight
            loose = tight.astype(jnp.float32)
            for g in range(heads):
                packed[b, :, g * local_width : (g + 1) * local_width] = loose[g * group : (g + 1) * group]
            packed_out(layer, b).start()
            return c

        lax.fori_loop(0, blocks, attend, 0)
        if layer == 0:
            share_other(0)
        if not is_last:
            quarter_out(layer + 1).start()
        keep("logsum", lse_buf, logsum.at[layer], 3)
        keep("mixed", tight_buf, mixed.at[layer], 4)
        settle("state")
        if layer == 0:
            split(0)
        for k in (1, 2):
            rows_back(layer, k).wait_recv()
        both_w[1 - upper] = y_rows[layer].astype(jnp.bfloat16)

        def output(b):
            packed_out(layer, b).wait_recv()
            both_mix[upper] = tight_buf[row_block(b)]
            for g in range(heads):
                both_mix[1 - upper, pl.ds(g * group, group)] = y_packed[
                    layer, b, :, g * local_width : (g + 1) * local_width
                ].astype(jnp.bfloat16)
            part_a[row_block(b)] = dot_nn(both_mix[0], both_w[0]) + dot_nn(both_mix[1], both_w[1])
            send_a(b)

        def mlp(b):
            at = row_block(b)
            finish_a(b)
            value = flow[at] + total_a[at] + outb_buf[layer : layer + 1]
            flow[at] = value
            block_store(layer, b, 0).start()
            low = (norm_unit(value) * gain_buf[layer, 1:2] + shift_buf[layer, 1:2]).astype(jnp.bfloat16)
            two_buf[at] = low
            hid = dot_nt(low, up_buf[...]) + upb_buf[layer : layer + 1]
            hidden_buf[at] = hid
            act = gelu(hid).astype(jnp.bfloat16)
            active_buf[at] = act
            for kind in range(1, 4):
                block_store(layer, b, kind).start()
            partial = dot_nn(act, down_buf[...])
            if is_last:
                lead = jnp.where(tensor == 0, 1.0, 0.0)
                partial = partial + lead * (value + downb_buf[layer : layer + 1])
            part_b[at] = partial
            if is_last:
                block_store(layer, b, 4).start()
            else:
                send_b(b)

        def output_and_mlp(b, c):
            pl.when(b > 0)(lambda: meet_a(b - 1))
            pl.when(b < blocks)(lambda: output(b))
            if not is_last:
                pl.when(b > 1)(lambda: meet_b(b - 2))
            pl.when(b > 0)(lambda: mlp(b - 1))
            return c

        lax.fori_loop(0, blocks + 1, output_and_mlp, 0)
        if not is_last:
            meet_b(blocks - 1)
        quarter_out(layer).wait_send()
        for k in range(3):
            rows_out(layer, k).wait_send()
        for b in range(blocks):
            packed_out(layer, b).wait_send()
        if not is_last:
            share_own(layer + 1)

        def stored(*kinds):
            def one(b, c):
                for kind in kinds:
                    block_store(layer, b, kind).wait()
                return c

            lax.fori_loop(0, blocks, one, 0)

        if is_last:
            stored(0, 1, 2, 3, 4)
        else:
            for k in range(2):
                split_out(k, layer).wait()
            split_begin()
            split(layer + 1)
            following[0].wait()
            settle("normed", "qkv")

            def next_project(b, c):
                at = row_block(b)
                close_b(b)
                finish_b(b)
                block_store(layer, b, 0).wait()
                project(layer + 1, b, flow[at] + total_b[at] + downb_buf[layer : layer + 1])
                return c

            lax.fori_loop(0, blocks, next_project, 0)
            share_other(layer + 1)
            stored(1, 2, 3)
            current = following
    for k in range(2):
        split_out(k, layers - 1).wait()
    settle(*list(stores))


def forward(
    dp_size, tokens, head_dim, collective_id,
    images, qkv_w, qv_b, out_w, out_b, up, up_b, down, down_b, gain, shift,
):
    layers = qkv_w.shape[0]
    width = images.shape[1]
    rows = -(-tokens // WIDE_BLOCK) * WIDE_BLOCK
    heads = qkv_w.shape[2] // head_dim
    units = -(-up.shape[0] // 128) * 128
    send_rows = -(-tokens // (2 * PIECE)) * 2 * PIECE
    pieces = send_rows // (2 * PIECE)
    f32, low = jnp.float32, jnp.bfloat16
    full = (rows, width)
    half = (send_rows // 2, width)
    any_spec = pl.BlockSpec(memory_space=pl.ANY)

    def out(shape, dtype):
        return jax.ShapeDtypeStruct(shape, dtype)

    lanes = heads * 128
    blocks = rows // WIDE_BLOCK
    local_width = heads * head_dim
    return pl.pallas_call(
        functools.partial(forward_kernel, dp_size, tokens, layers, heads, head_dim, send_rows),
        out_shape=(
            out((layers, rows, units), f32),
            out((layers, rows, units), low),
            out((layers,) + full, low),
            out((layers,) + full, low),
            out((layers,) + full, f32),
            out((layers,) + full, f32),
            out((layers, 3, heads, rows, 128), low),
            out((layers, heads, rows, 128), f32),
            out((layers, rows, heads * head_dim), low),
            out((layers, units, width), low),
            out((layers, units, width), low),
            out(full, f32),
        ),
        in_specs=[any_spec] * 11,
        out_specs=(any_spec,) * 12,
        scratch_shapes=[
            pltpu.VMEM(images.shape, low),
            pltpu.VMEM(up_b.shape, f32),
            pltpu.VMEM(full, f32),
            pltpu.VMEM(full, low),
            pltpu.VMEM((3, heads, rows, 128), low),
            pltpu.VMEM((heads, rows, 128), f32),
            pltpu.VMEM((WIDE_BLOCK, lanes), low),
            pltpu.VMEM((rows, heads * head_dim), low),
            pltpu.VMEM(full, low),
            pltpu.VMEM((rows, units), f32),
            pltpu.VMEM((rows, units), low),
            pltpu.VMEM(qkv_w.shape[1:], low),
            pltpu.VMEM(out_w.shape, low),
            pltpu.VMEM((units, width), low),
            pltpu.VMEM((units, width), low),
            pltpu.VMEM(qv_b.shape, f32),
            pltpu.VMEM(out_b.shape, f32),
            pltpu.VMEM((layers, units), f32),
            pltpu.VMEM(down_b.shape, f32),
            pltpu.VMEM(gain.shape, f32),
            pltpu.VMEM(shift.shape, f32),
        ]
        + [pltpu.VMEM(s, f32) for s in (full, half, full, full, half, half, full)]
        + [
            pltpu.VMEM((layers, local_width // 4, width), f32),
            pltpu.VMEM((layers, local_width, width), f32),
            pltpu.VMEM((2, local_width, width), low),
            pltpu.VMEM((2, WIDE_BLOCK, local_width), low),
            pltpu.VMEM((blocks, WIDE_BLOCK // heads, heads * local_width), f32),
            pltpu.VMEM((layers, blocks, WIDE_BLOCK // heads, heads * local_width), f32),
            pltpu.VMEM((SPLIT_SLOTS, 128, layers, width), low),
            pltpu.VMEM((128, width), f32),
            pltpu.SemaphoreType.DMA((8,)),
            pltpu.SemaphoreType.DMA((1,)),
            pltpu.SemaphoreType.DMA((9,)),
            pltpu.SemaphoreType.DMA((5, rows // WIDE_BLOCK)),
            pltpu.SemaphoreType.DMA((1, SPLIT_SLOTS)),
            pltpu.SemaphoreType.DMA((2,)),
            pltpu.SemaphoreType.DMA((2, layers)),
            pltpu.SemaphoreType.DMA((2, layers, 3)),
            pltpu.SemaphoreType.DMA((2, layers, blocks)),
        ]
        + [pltpu.SemaphoreType.DMA((layers, 2, pieces))] * 5,
        compiler_params=pltpu.CompilerParams(
            collective_id=collective_id, has_side_effects=True, vmem_limit_bytes=63 << 20
        ),
    )(images, qkv_w, qv_b, out_w, out_b, up, up_b, down, down_b, gain, shift)


def finish_kernel(
    layers, heads, head_dim, hidden_units, layer_rows, off_qkv,
    totals, down_rows, up_rows, image_rows, encoded_rows,
    encoded, image_grad, qkv_grad, qv_grad, out_grad, out_b, up_grad, up_b, down_grad, down_b, gain, shift,
    down_buf, up_wide, rows_buf, long_a, long_b, short_a, short_b, small, qv_buf, up_buf, plain, pair, sem,
):
    width = totals.shape[1]
    local_width = heads * head_dim
    count = [0]

    def move(source, target):
        copy = pltpu.make_async_copy(source, target, sem.at[count[0]])
        count[0] += 1
        copy.start()
        return copy

    small_rows = small.shape[1]
    off_small = off_qkv + 4 * local_width
    firsts = [(layers - 1 - l) * layer_rows for l in range(layers)]
    fetch = [move(totals.at[pl.ds(firsts[l] + off_small, small_rows)], small.at[l]) for l in range(layers)]
    fetch_a = move(encoded_rows, long_a)
    fetch_b = move(image_rows, long_b)
    through = []
    for source, buffer, target in ((down_rows, down_buf, down_grad), (up_rows, up_wide, up_grad)):
        for at in range(0, hidden_units, 128):
            here = pl.ds(at, min(128, hidden_units - at))
            through.append((move(source.at[here], buffer.at[here]), buffer.at[here], target.at[here]))
    for l in range(layers):
        begin = firsts[l] + off_qkv
        for i in range(4):
            rows = pl.ds(begin + i * local_width, local_width)
            target = qkv_grad.at[l, i] if i < 3 else out_grad.at[l]
            through.append((move(totals.at[rows], rows_buf.at[l, i]), rows_buf.at[l, i], target))
    moves = []
    for arrived, buffer, target in through:
        arrived.wait()
        moves.append(move(buffer, target))
    for copy in fetch:
        copy.wait()
    for l in range(layers):
        for i in range(2):
            for h in range(heads):
                lane = (i * heads + h) * 128
                qv_buf[l, i : i + 1, h * head_dim : (h + 1) * head_dim] = small[l, 0:1, lane : lane + head_dim]
        plain[0, l : l + 1] = small[l, 1:2]
        up_buf[l : l + 1] = small[l, 2:3, :hidden_units]
        plain[1, l : l + 1] = small[l, 3:4]
        pair[0, l] = small[l, 4:6]
        pair[1, l] = small[l, 6:8]
    moves += [
        move(qv_buf, qv_grad), move(plain.at[0], out_b), move(up_buf, up_b), move(plain.at[1], down_b),
        move(pair.at[0], gain), move(pair.at[1], shift),
    ]
    tokens = short_a.shape[0]
    fetch_a.wait()
    short_a[...] = long_a[:tokens]
    moves.append(move(short_a, encoded))
    fetch_b.wait()
    short_b[...] = long_b[:tokens]
    moves.append(move(short_b, image_grad))
    for copy in moves:
        copy.wait()


def finish(tokens, heads, head_dim, hidden_units, totals, down_rows, up_rows, image_rows, encoded_rows):
    layers = down_rows.shape[1]
    width = totals.shape[1]
    rows = image_rows.shape[0]
    layer_rows = totals.shape[0] // layers
    off_qkv = 2 * down_rows.shape[0]
    local_width = heads * head_dim
    f32, low = jnp.float32, jnp.bfloat16
    any_spec = pl.BlockSpec(memory_space=pl.ANY)

    def out(shape, dtype=f32):
        return jax.ShapeDtypeStruct(shape, dtype)

    copies = 4 * -(-hidden_units // 128) + 9 * layers + 10
    return pl.pallas_call(
        functools.partial(finish_kernel, layers, heads, head_dim, hidden_units, layer_rows, off_qkv),
        out_shape=(
            out((tokens, width), low),
            out((tokens, width), low),
            out((layers, 3, local_width, width)),
            out((layers, 2, local_width)),
            out((layers, local_width, width)),
            out((layers, width)),
            out((hidden_units, layers, width)),
            out((layers, hidden_units)),
            out((hidden_units, layers, width)),
            out((layers, width)),
            out((layers, 2, width)),
            out((layers, 2, width)),
        ),
        in_specs=[any_spec] * 5,
        out_specs=(any_spec,) * 12,
        scratch_shapes=[
            pltpu.VMEM((hidden_units, layers, width), f32),
            pltpu.VMEM((hidden_units, layers, width), f32),
            pltpu.VMEM((layers, 4, local_width, width), f32),
            pltpu.VMEM((rows, width), low),
            pltpu.VMEM((rows, width), low),
            pltpu.VMEM((tokens, width), low),
            pltpu.VMEM((tokens, width), low),
            pltpu.VMEM((layers, TAIL_ROWS, width), f32),
            pltpu.VMEM((layers, 2, local_width), f32),
            pltpu.VMEM((layers, hidden_units), f32),
            pltpu.VMEM((2, layers, width), f32),
            pltpu.VMEM((2, layers, 2, width), f32),
            pltpu.SemaphoreType.DMA((copies,)),
        ],
        compiler_params=pltpu.CompilerParams(has_side_effects=True, vmem_limit_bytes=56 << 20),
    )(totals, down_rows, up_rows, image_rows, encoded_rows)


def local(
    dp_size,
    images,
    qkv_weight,
    qv_bias,
    out_weight,
    out_bias,
    up_weight,
    up_bias,
    down_weight,
    down_bias,
    norm_gain,
    norm_shift,
    cotangent,
):
    tokens, width = images.shape[1:]
    layers = qkv_weight.shape[0]
    local_width = qkv_weight.shape[3]
    heads = local_width // HEAD
    hidden_units = up_weight.shape[2]
    qkv_rows = jnp.swapaxes(qkv_weight, 2, 3)
    up = jnp.transpose(up_weight, (2, 0, 1))
    down = jnp.swapaxes(down_weight, 0, 1)
    *kept, last_part = forward(
        dp_size, tokens, HEAD, 0,
        images[0], qkv_rows, qv_bias, out_weight, out_bias, up, up_bias, down, down_bias,
        norm_gain, norm_shift,
    )
    flat, summed, image_grad, encoded, down_rows, up_rows = backward(
        tokens, HEAD, hidden_units, UNIT, 1, dp_size == 8,
        cotangent[0], *kept, qkv_rows, out_weight, norm_gain, last_part,
    )
    if dp_size != 8:
        summed = lax.psum(flat, "dp")
        per_layer = summed.reshape(layers, summed.shape[0] // layers, width)[::-1]
        stop = down_rows.shape[0]
        down_rows = jnp.swapaxes(per_layer[:, :stop], 0, 1)
        up_rows = jnp.swapaxes(per_layer[:, stop : 2 * stop], 0, 1)
    encoded, image_grad, qkv_grad, qv_grad, out_grad, out_b, up_grad, up_b, down_grad, down_b, gain, shift = finish(
        tokens, heads, HEAD, hidden_units, summed, down_rows, up_rows, image_grad, encoded
    )
    return (
        encoded[None],
        image_grad[None],
        jnp.swapaxes(qkv_grad, 2, 3),
        qv_grad,
        out_grad,
        out_b,
        jnp.transpose(up_grad, (1, 2, 0)),
        up_b,
        jnp.swapaxes(down_grad, 0, 1),
        down_b,
        gain,
        shift,
    )


def solution(mesh):
    in_specs = (
        P("dp", None, None),
        P(None, None, None, "tensor"),
        P(None, None, "tensor"),
        P(None, "tensor", None),
        P(),
        P(None, None, "tensor"),
        P(None, "tensor"),
        P(None, "tensor", None),
        P(),
        P(),
        P(),
        P("dp", None, None),
    )
    out_specs = (
        P("dp", None, None),
        P("dp", None, None),
        P(None, None, None, "tensor"),
        P(None, None, "tensor"),
        P(None, "tensor", None),
        P(),
        P(None, None, "tensor"),
        P(None, "tensor"),
        P(None, "tensor", None),
        P(),
        P(),
        P(),
    )
    return jax.shard_map(
        functools.partial(local, mesh.shape["dp"]), mesh=mesh, in_specs=in_specs, out_specs=out_specs, check_vma=False)
```

```python
import functools

import jax
import jax.numpy as jnp
from jax import lax
from jax.experimental import pallas as pl
from jax.experimental.pallas import tpu as pltpu
from jax.sharding import PartitionSpec as P

MESH = pl.DeviceIdType.MESH
SLOTS = 24
FEW = 8
HOP = 3
ROUND = 3
PARTS = 10
TICK_SPAN = 7 * HOP + 2
TICK_BUFFERS = 17


def grad_sum_ticks(dp_sum, unit, steps, grads, totals, buffers, sems):
    (
        x_in, inner_in, mid_in, own_a, total_a,
        whole_in, half_in, side_in, own_b, total_b,
        far_in, cross_in, near_in, end_in, own_f, own_n, total_e,
    ) = buffers
    (
        x_sem, inner_sem, mid_sem, out_pair_sem, out_x_sem,
        whole_sem, half_sem, side_sem, back_mid_sem, back_pair_sem, relay_sem,
        far_sem, cross_sem, near_sem, end_sem, back_one_sem, back_two_sem, back_three_sem,
        load_a_sem, store_a_sem, load_b_sem, store_b_sem, load_f_sem, load_n_sem, store_e_sem,
    ) = sems
    dp = lax.axis_index("dp")
    tensor = lax.axis_index("tensor")
    z = dp // 2
    x = dp % 2
    is_mid = (z == 1) | (z == 2)
    is_end = jnp.logical_not(is_mid)
    x_peer = (dp + 1 - 2 * x, tensor)
    pair_peer = (dp + 2 - 4 * (z % 2), tensor)
    mid_z = jnp.where(is_mid, 3 - z, z)
    mid_peer = (mid_z * 2 + x, tensor)
    side = jnp.where(z == 2, 1, 0)
    near = jnp.where(z >= 2, 1, 0)

    def greet(others):
        barrier = pltpu.get_barrier_semaphore()
        for peer in others + ((x_peer, pair_peer) if dp_sum else ()):
            pl.semaphore_signal(barrier, inc=1, device_id=peer, device_id_type=MESH)
        if dp_sum:

            @pl.when(is_mid)
            def _():
                pl.semaphore_signal(barrier, inc=1, device_id=mid_peer, device_id_type=MESH)

    def met(others):
        barrier = pltpu.get_barrier_semaphore()
        if dp_sum:
            pl.when(is_mid)(lambda: pl.semaphore_wait(barrier, 3 + len(others)))
            pl.when(is_end)(lambda: pl.semaphore_wait(barrier, 2 + len(others)))
        else:
            pl.semaphore_wait(barrier, len(others))

    def rows(chunk, part, count=1):
        return pl.ds(pl.multiple_of((chunk * PARTS + part) * unit, 8), count * unit)

    def row_a(c, part):
        return rows(c // ROUND, 2 * lax.rem(c, ROUND) + part)

    def row_m(c, part, count=1):
        return rows(c, 6 + part, count)

    def row_e(c, part):
        return rows(c, 8 + part)

    def remote(src, dst, sem, slot, peer):
        return pltpu.make_async_remote_copy(
            src_ref=src, dst_ref=dst, send_sem=sem.at[0, slot], recv_sem=sem.at[1, slot],
            device_id=peer, device_id_type=MESH,
        )

    def local_copy(src, dst, sem, slot):
        return pltpu.make_async_copy(src, dst, sem.at[slot])

    def a_x(c, s):
        return remote(grads.at[row_a(c, 1 - x)], x_in.at[s], x_sem, s, x_peer)

    def a_load(c, s):
        return local_copy(grads.at[row_a(c, x)], own_a.at[s], load_a_sem, s)

    def a_inner(c, s):
        return remote(own_a.at[s], inner_in.at[s], inner_sem, s, pair_peer)

    def a_mid(c, s):
        return remote(own_a.at[s], mid_in.at[s], mid_sem, s, mid_peer)

    def a_out_pair(c, s):
        return remote(total_a.at[s], totals.at[row_a(c, x)], out_pair_sem, s, pair_peer)

    def a_out_x(c, s):
        return remote(total_a.at[s], totals.at[row_a(c, x)], out_x_sem, s, x_peer)

    def a_store(c, s):
        return local_copy(total_a.at[s], totals.at[row_a(c, x)], store_a_sem, s)

    def a_relay(c, s):
        return remote(totals.at[row_a(c, x)], totals.at[row_a(c, x)], out_x_sem, s, x_peer)

    def a_back(c, s):
        return remote(totals.at[row_a(c, x)], totals.at[row_a(c, 1 - x)], out_x_sem, s, x_peer)

    def m_whole(c, s):
        return remote(grads.at[row_m(c, 0, 2)], whole_in.at[s], whole_sem, s, pair_peer)

    def m_load(c, s):
        return local_copy(grads.at[row_m(c, 0, 2)], own_b.at[s], load_b_sem, s)

    def m_half(c, s):
        return remote(own_b.at[s, pl.ds((1 - side) * unit, unit)], half_in.at[s], half_sem, s, mid_peer)

    def m_side(c, s):
        return remote(own_b.at[s, pl.ds(side * unit, unit)], side_in.at[s], side_sem, s, x_peer)

    def m_store(c, s):
        return local_copy(total_b.at[s], totals.at[row_m(c, side)], store_b_sem, s)

    def m_back_mid(c, s):
        return remote(total_b.at[s], totals.at[row_m(c, side)], back_mid_sem, s, mid_peer)

    def m_back_pair(c, s):
        return remote(total_b.at[s], totals.at[row_m(c, side)], back_pair_sem, s, pair_peer)

    def m_relay(c, s):
        return remote(totals.at[row_m(c, 1 - side)], totals.at[row_m(c, 1 - side)], relay_sem, s, pair_peer)

    def e_far(c, s):
        return remote(grads.at[row_e(c, 1 - near)], far_in.at[s], far_sem, s, pair_peer)

    def e_load_far(c, s):
        return local_copy(grads.at[row_e(c, 1 - near)], own_f.at[s], load_f_sem, s)

    def e_load_near(c, s):
        return local_copy(grads.at[row_e(c, near)], own_n.at[s], load_n_sem, s)

    def e_cross(c, s):
        return remote(own_f.at[s], cross_in.at[s], cross_sem, s, mid_peer)

    def e_near(c, s):
        return remote(own_n.at[s], near_in.at[s], near_sem, s, pair_peer)

    def e_end(c, s):
        return remote(own_n.at[s], end_in.at[s], end_sem, s, x_peer)

    def e_store(c, s):
        return local_copy(total_e.at[s], totals.at[row_e(c, near)], store_e_sem, s)

    def e_back_one(c, s):
        return remote(total_e.at[s], totals.at[row_e(c, near)], back_one_sem, s, pair_peer)

    def e_back_two(c, s):
        return remote(totals.at[row_e(c, near)], totals.at[row_e(c, near)], back_two_sem, s, mid_peer)

    def e_back_three(c, s):
        return remote(totals.at[row_e(c, 1 - near)], totals.at[row_e(c, 1 - near)], back_three_sem, s, pair_peer)

    def a_start(c, s):
        a_x(c, s).start()
        a_load(c, s).start()

    def a_one(c, s):
        a_load(c, s).wait()
        a_x(c, s).wait_recv()
        own_a[s] = own_a[s] + x_in[s]
        pl.when(is_end)(lambda: a_inner(c, s).start())

    def a_two(c, s):
        a_inner(c, s).wait_recv()
        own_a[s] = own_a[s] + inner_in[s]
        a_mid(c, s).start()

    def a_three(c, s):
        a_mid(c, s).wait_recv()
        total_a[s] = own_a[s] + mid_in[s]
        a_out_pair(c, s).start()
        a_out_x(c, s).start()
        a_store(c, s).start()

    def a_four(c, s):
        a_out_pair(c, s).wait_recv()
        a_relay(c, s).start()

    def a_five(c, s):
        a_back(c, s).wait_recv()

    def a_done(c, s):
        a_x(c, s).wait_send()
        a_out_x(c, s).wait_send()
        pl.when(is_end)(lambda: a_inner(c, s).wait_send())

        @pl.when(is_mid)
        def _():
            a_mid(c, s).wait_send()
            a_out_pair(c, s).wait_send()
            a_store(c, s).wait()

    def m_start(c, s):
        pl.when(is_end)(lambda: m_whole(c, s).start())
        pl.when(is_mid)(lambda: m_load(c, s).start())

    def m_one(c, s):
        m_load(c, s).wait()
        m_whole(c, s).wait_recv()
        own_b[s] = own_b[s] + whole_in[s]
        m_half(c, s).start()

    def m_two(c, s):
        m_half(c, s).wait_recv()
        mine = pl.ds(pl.multiple_of(side * unit, 8), unit)
        own_b[s, mine] = own_b[s, mine] + half_in[s]
        m_side(c, s).start()

    def m_three(c, s):
        m_side(c, s).wait_recv()
        mine = pl.ds(pl.multiple_of(side * unit, 8), unit)
        total_b[s] = own_b[s, mine] + side_in[s]
        m_back_mid(c, s).start()
        m_back_pair(c, s).start()
        m_store(c, s).start()

    def m_four(c, s):
        m_back_mid(c, s).wait_recv()
        m_relay(c, s).start()

    def m_five(c, s):
        m_back_pair(c, s).wait_recv()
        m_relay(c, s).wait_recv()

    def m_done(c, s):
        pl.when(is_end)(lambda: m_whole(c, s).wait_send())

        @pl.when(is_mid)
        def _():
            m_half(c, s).wait_send()
            m_side(c, s).wait_send()
            m_back_mid(c, s).wait_send()
            m_back_pair(c, s).wait_send()
            m_store(c, s).wait()
            m_relay(c, s).wait_send()

    def e_start(c, s):
        e_load_near(c, s).start()
        pl.when(is_end)(lambda: e_far(c, s).start())
        pl.when(is_mid)(lambda: e_load_far(c, s).start())

    def e_one(c, s):
        e_load_far(c, s).wait()
        e_far(c, s).wait_recv()
        own_f[s] = own_f[s] + far_in[s]
        e_cross(c, s).start()

    def e_two(c, s):
        e_load_near(c, s).wait()
        e_cross(c, s).wait_recv()
        own_n[s] = own_n[s] + cross_in[s]
        e_near(c, s).start()

    def e_three(c, s):
        e_load_near(c, s).wait()
        e_near(c, s).wait_recv()
        own_n[s] = own_n[s] + near_in[s]
        e_end(c, s).start()

    def e_four(c, s):
        e_end(c, s).wait_recv()
        total_e[s] = own_n[s] + end_in[s]
        e_back_one(c, s).start()
        e_store(c, s).start()

    def e_five(c, s):
        e_back_one(c, s).wait_recv()
        e_back_two(c, s).start()

    def e_six(c, s):
        e_back_two(c, s).wait_recv()
        e_back_three(c, s).start()

    def e_seven(c, s):
        e_back_three(c, s).wait_recv()

    def e_done(c, s):
        @pl.when(is_end)
        def _():
            e_far(c, s).wait_send()
            e_end(c, s).wait_send()
            e_back_one(c, s).wait_send()
            e_store(c, s).wait()

        @pl.when(is_mid)
        def _():
            e_cross(c, s).wait_send()
            e_near(c, s).wait_send()
            e_back_two(c, s).wait_send()
            e_back_three(c, s).wait_send()

    def stage(step, offset, phase, guard, body):
        at = step - offset
        ok = (at >= 0) & (at < steps)
        if guard is not None:
            ok = ok & guard
        if phase is None:
            chunk, slots = at, SLOTS
        else:
            ok = ok & (lax.rem(at, ROUND) == phase)
            chunk, slots = at // ROUND, FEW

        @pl.when(ok)
        def _():
            body(chunk, lax.rem(chunk, slots))

    def tick(step):
        if not dp_sum:
            return
        stage(step, 0, None, None, a_start)
        stage(step, 0, 0, None, m_start)
        stage(step, 0, 1, None, e_start)
        stage(step, 6 * HOP, 1, is_mid, e_six)
        stage(step, 5 * HOP, 1, is_mid, e_five)
        stage(step, 4 * HOP, 1, is_end, e_four)
        stage(step, 4 * HOP, 0, is_mid, m_four)
        stage(step, 3 * HOP, None, is_mid, a_three)
        stage(step, 3 * HOP, 0, is_mid, m_three)
        stage(step, 4 * HOP, None, is_end, a_four)
        stage(step, 3 * HOP, 1, is_end, e_three)
        stage(step, 2 * HOP, None, is_mid, a_two)
        stage(step, 2 * HOP, 0, is_mid, m_two)
        stage(step, 2 * HOP, 1, is_mid, e_two)
        stage(step, HOP, None, None, a_one)
        stage(step, HOP, 0, is_mid, m_one)
        stage(step, HOP, 1, is_mid, e_one)
        stage(step, 5 * HOP, None, None, a_five)
        stage(step, 5 * HOP, 0, is_end, m_five)
        stage(step, 7 * HOP, 1, is_end, e_seven)
        stage(step, 5 * HOP + 1, None, None, a_done)
        stage(step, 5 * HOP + 1, 0, None, m_done)
        stage(step, 7 * HOP + 1, 1, None, e_done)

    return tick, greet, met


def tick_scratch(unit, width):
    many, few, double = (SLOTS, unit, width), (FEW, unit, width), (FEW, 2 * unit, width)
    shapes = [many] * 5 + [double, few, few, double, few] + [few] * 7
    buffers = [pltpu.VMEM(shape, jnp.float32) for shape in shapes]
    sems = [pltpu.SemaphoreType.DMA((2, SLOTS))] * 5 + [pltpu.SemaphoreType.DMA((2, FEW))] * 13
    sems += [pltpu.SemaphoreType.DMA((SLOTS,))] * 2 + [pltpu.SemaphoreType.DMA((FEW,))] * 5
    return buffers, sems


HEAD = 72
EPSILON = 1e-06
UNIT = 8
TAIL_ROWS = 8


FIRST = 1
PIECE = 16
LAG = 4
LEAD = 3
BLOCK = 128
WIDE_BLOCK = 192
SPLIT_SLOTS = 4


def dot_nn(left, right):
    return lax.dot_general(left, right, (((1,), (0,)), ((), ())), preferred_element_type=jnp.float32)


def dot_nt(left, right):
    return lax.dot_general(left, right, (((1,), (1,)), ((), ())), preferred_element_type=jnp.float32)


def dot_tn(left, right):
    return lax.dot_general(left, right, (((0,), (0,)), ((), ())), preferred_element_type=jnp.float32)


def fold(array):
    return jnp.sum(array, axis=0, keepdims=True)


def gelu_slope(v):
    root = 0.7978845608028654
    inner = jnp.tanh(root * (v + 0.044715 * (v * v * v)))
    return 0.5 * (1.0 + inner) + 0.5 * v * (1.0 - inner * inner) * (root * (1.0 + 0.134145 * (v * v)))


def norm_back(grad_normed, state, gain):
    centred = state - jnp.mean(state, axis=-1, keepdims=True)
    inverse = lax.rsqrt(jnp.mean(centred * centred, axis=-1, keepdims=True) + EPSILON)
    unit = centred * inverse
    grad_unit = grad_normed * gain
    inner = (
        grad_unit
        - jnp.mean(grad_unit, axis=-1, keepdims=True)
        - unit * jnp.mean(grad_unit * unit, axis=-1, keepdims=True)
    )
    return inverse * inner, fold(grad_normed * unit), fold(grad_normed)


def backward_kernel(
    dp_sum, tokens, layers, heads, units_rows, head_dim, send_rows, unit, steps,
    cotangent, hidden, active, normed_two, normed, middle, state, qkv, logsum, mixed,
    down, up, qkv_w, out_w, gain, last_part,
    grads, totals, image_grad, encoded, down_grad, up_grad,
    raw_buf, wide, act_buf, two_buf, qkv_buf, lse_buf, mix_buf, down_buf, up_buf, qkvw_buf, outw_buf, gain_buf,
    flow, flow_low, hid_low, part, total, core_in, acc, y_in, grad_mix, cat, tight, acc_k, acc_v, stage_buf, small,
    woven, load_sem, stage_sem, turn_sem, weave_sem, core_send, core_recv, y_send, y_recv, back_send, back_recv,
    *tick_refs
):
    width = grads.shape[1]
    rows = part.shape[0]
    blocks = rows // BLOCK
    half = send_rows // 2
    pieces = half // PIECE
    tick, greet, met = grad_sum_ticks(
        dp_sum, unit, steps, grads, totals, tick_refs[:TICK_BUFFERS], tick_refs[TICK_BUFFERS:]
    )
    dp = lax.axis_index("dp")
    tensor = lax.axis_index("tensor")
    core = tensor % 2
    core_peer = (dp, tensor + 1 - 2 * core)
    y_peer = (dp, lax.rem(tensor + 2, 4))
    greet((core_peer, y_peer))
    layer_rows = grads.shape[0] // layers
    off_up = units_rows
    local_width = heads * head_dim
    off_qkv = 2 * units_rows
    off_out = off_qkv + 3 * local_width
    off_small = off_out + local_width
    spread = spread_matrix(heads, head_dim)

    def mine(i):
        return pl.ds(pl.multiple_of(core * half + i * PIECE, 8), PIECE)

    def other(i):
        return pl.ds(pl.multiple_of((1 - core) * half + i * PIECE, 8), PIECE)

    def here(i):
        return pl.ds(pl.multiple_of(i * PIECE, 8), PIECE)

    def remote(src, dst, send, recv, peer):
        return pltpu.make_async_remote_copy(
            src_ref=src, dst_ref=dst, send_sem=send, recv_sem=recv, device_id=peer, device_id_type=MESH
        )

    def to_core(p, i):
        return remote(
            part.at[other(i)], core_in.at[here(i)], core_send.at[p, i], core_recv.at[p, i], core_peer
        )

    def to_y(p, i):
        return remote(acc.at[here(i)], y_in.at[p, here(i)], y_send.at[p, i], y_recv.at[p, i], y_peer)

    def to_back(p, i):
        return remote(total.at[mine(i)], total.at[mine(i)], back_send.at[p, i], back_recv.at[p, i], core_peer)

    def from_back(p, i):
        return remote(
            total.at[other(i)], total.at[other(i)], back_send.at[p, i], back_recv.at[p, i], core_peer
        )

    def sum_begin(p):
        def go(i, c):
            to_core(p, i).start()
            return c

        lax.fori_loop(0, LEAD, go, 0)

    def sum_step(p, j):
        pl.when(j + LEAD < pieces)(lambda: to_core(p, j + LEAD).start())

        @pl.when(j < pieces)
        def _():
            to_core(p, j).wait_recv()
            acc[here(j)] = part[mine(j)] + core_in[here(j)]
            to_y(p, j).start()

        late = j - LAG

        @pl.when((late >= 0) & (late < pieces))
        def _():
            to_y(p, late).wait_recv()
            total[mine(late)] = acc[here(late)] + y_in[p, here(late)]
            to_back(p, late).start()

        last = j - LAG - 2

        @pl.when((last >= 0) & (last < pieces))
        def _():
            to_core(p, last).wait_send()
            to_y(p, last).wait_send()
            to_back(p, last).wait_send()
            from_back(p, last).wait_recv()

    sum_steps = pieces + LAG + 2

    def load(source, target, sem):
        return pltpu.make_async_copy(source, target, load_sem.at[sem])

    def stage_copy(slot, row, size):
        return pltpu.make_async_copy(
            stage_buf.at[slot, pl.ds(0, size)], grads.at[pl.ds(pl.multiple_of(row, 8), size)], stage_sem.at[slot]
        )

    tiles = width // 128
    last_rows = units_rows - (tiles - 1) * 128
    layer_ticks = tiles + 1 + 4 * blocks + 2 * sum_steps + heads * blocks

    def row_block(b):
        return pl.ds(pl.multiple_of(b * BLOCK, 16), BLOCK)

    total[pl.ds(send_rows, rows - send_rows)] = jnp.zeros((rows - send_rows, width), jnp.float32)
    start = load(cotangent, raw_buf, 11)
    start.start()
    load(active.at[layers - 1], act_buf, 3).start()
    gain_load = load(gain, gain_buf, 10)
    gain_load.start()
    start.wait()
    lower_rows(raw_buf, flow_low, wide, tokens)
    met((core_peer, y_peer))

    def layer_body(it, carry):
        layer = layers - 1 - it
        base_tick = it * layer_ticks - FIRST
        base_row = it * layer_rows
        hidden_load = load(hidden.at[layer], wide, 0)
        down_load = load(down.at[layer], down_buf, 1)
        up_load = load(up.at[layer], up_buf, 2)
        active_load = load(active.at[layer], act_buf, 3)
        two_load = load(normed_two.at[layer], two_buf, 4)
        outw_load = load(out_w.at[layer], outw_buf, 5)
        qkv_load = load(qkv.at[layer], qkv_buf, 6)
        lse_load = load(logsum.at[layer], lse_buf, 7)
        mix_load = load(mixed.at[layer], mix_buf, 8)
        qkvw_load = load(qkv_w.at[layer], qkvw_buf, 9)
        pl.when(it > 0)(active_load.start)
        small[...] = jnp.zeros_like(small)

        def lower(b, c):
            at = row_block(b)
            flow_low[at] = flow[at].astype(jnp.bfloat16)
            return c

        @pl.when(it > 0)
        def _():
            lax.fori_loop(0, blocks, lower, 0)

        active_load.wait()
        for copy in (hidden_load, down_load, up_load, two_load, outw_load, qkv_load, lse_load, mix_load, qkvw_load):
            copy.start()

        def tile_copy(tile, row):
            slot = lax.rem(tile, 2)
            pl.when(tile < tiles - 1)(lambda: stage_copy(slot, row, 128).start())
            pl.when(tile == tiles - 1)(lambda: stage_copy(slot, row, last_rows).start())

        def tile_done(tile):
            slot = lax.rem(tile, 2)
            pl.when((tile >= 0) & (tile < tiles - 1))(lambda: stage_copy(slot, base_row, 128).wait())
            pl.when(tile == tiles - 1)(lambda: stage_copy(slot, base_row, last_rows).wait())

        def down_weights(j, c):
            tile_done(j - 1)
            tick(base_tick + j)

            @pl.when(j < tiles)
            def _():
                lanes = pl.ds(pl.multiple_of(j * 128, 128), 128)
                stage_buf[lax.rem(j, 2), pl.ds(0, 128)] = dot_tn(act_buf[:, lanes], flow_low[...])
                tile_copy(j, base_row + j * 128)

            return c

        lax.fori_loop(0, tiles + 1, down_weights, 0)
        tick_at = base_tick + tiles + 1

        @pl.when(it == 0)
        def _():
            gain_load.wait()
            lift_rows(raw_buf, flow, tokens, BLOCK)

        hidden_load.wait()
        down_load.wait()
        up_load.wait()

        def mlp(b, c):
            at = row_block(b)
            small[3:4] += fold(flow[at])
            grad_hidden = dot_nt(flow_low[at], down_buf[...]) * gelu_slope(wide[at])
            small[2:3] += fold(grad_hidden)
            hid = grad_hidden.astype(jnp.bfloat16)
            hid_low[at] = hid
            part[at] = dot_nn(hid, up_buf[...])
            tick(tick_at + b)
            return c

        lax.fori_loop(0, blocks, mlp, 0)
        sum_begin(0)
        middle_load = load(middle.at[layer], wide, 0)
        middle_load.start()
        two_load.wait()
        tick_at = tick_at + blocks

        def up_weights(j, c):
            sum_step(0, j)
            tile_done(j - 1)

            @pl.when(j < tiles)
            def _():
                lanes = pl.ds(pl.multiple_of(j * 128, 128), 128)
                stage_buf[lax.rem(j, 2), pl.ds(0, 128)] = dot_tn(hid_low[:, lanes], two_buf[...])
                tile_copy(j, base_row + off_up + j * 128)

            tick(tick_at + j)
            return c

        lax.fori_loop(0, sum_steps, up_weights, 0)
        tick_at = tick_at + sum_steps
        part_load = load(last_part, part, 1)
        pl.when(it == 0)(part_load.start)
        middle_load.wait()
        outw_load.wait()

        def norm_two(b, c):
            at = row_block(b)
            step_grad, gain_grad, shift_grad = norm_back(total[at], wide[at], gain_buf[layer, 1:2])
            small[5:6] += gain_grad
            small[7:8] += shift_grad
            grad = flow[at] + step_grad
            flow[at] = grad
            small[1:2] += fold(grad)
            low = grad.astype(jnp.bfloat16)
            flow_low[at] = low
            grad = dot_nt(low, outw_buf[...]).astype(jnp.bfloat16)
            grad_mix[at] = dot_nn(grad, spread).astype(jnp.bfloat16)
            tick(tick_at + b)
            return c

        lax.fori_loop(0, blocks, norm_two, 0)
        tick_at = tick_at + blocks
        state_load = load(state.at[layer], wide, 0)
        normed_load = load(normed.at[layer], act_buf, 3)
        state_load.start()
        normed_load.start()
        qkv_load.wait()
        lse_load.wait()
        scale = head_dim ** (-0.5)

        @pl.when(it == 0)
        def _():
            part_load.wait()
            sum_begin(2)


        def attend(m, c):
            head = m // blocks
            b = lax.rem(m, blocks)
            at = row_block(b)
            lanes = pl.ds(pl.multiple_of(head * 128, 128), 128)
            query = qkv_buf[0, head, at]
            key = qkv_buf[1, head]
            value = qkv_buf[2, head]
            grad = grad_mix[at, lanes]
            scores = dot_nt(query, key) * scale
            probs = jnp.exp(scores - lse_buf[head, at, 0:1])
            column = lax.broadcasted_iota(jnp.int32, probs.shape, 1)
            probs = jnp.where(column < tokens, probs, 0.0)
            grad_weights = dot_nt(grad, value)
            center = jnp.sum(probs * grad_weights, axis=-1, keepdims=True)
            raw = (probs * (grad_weights - center) * scale).astype(jnp.bfloat16)
            grad_query = dot_nn(raw, key)
            small[0:1, lanes] += fold(grad_query)
            cat[at, lanes] = grad_query.astype(jnp.bfloat16)
            add_k = dot_tn(raw, query)
            add_v = dot_tn(probs.astype(jnp.bfloat16), grad)

            @pl.when(b == 0)
            def _():
                acc_k[...] = add_k
                acc_v[...] = add_v

            @pl.when(b > 0)
            def _():
                acc_k[...] += add_k
                acc_v[...] += add_v

            @pl.when(b == blocks - 1)
            def _():
                at_k = pl.ds(pl.multiple_of((heads + head) * 128, 128), 128)
                at_v = pl.ds(pl.multiple_of((2 * heads + head) * 128, 128), 128)
                cat[:, at_k] = acc_k[...].astype(jnp.bfloat16)
                cat[:, at_v] = acc_v[...].astype(jnp.bfloat16)
                small[0:1, pl.ds(pl.multiple_of((heads + head) * 128, 128), 128)] += fold(acc_v[...])

            @pl.when(it == 0)
            def _():
                sum_step(2, 2 * m)
                sum_step(2, 2 * m + 1)

            tick(tick_at + m)
            return c

        lax.fori_loop(0, heads * blocks, attend, 0)
        tick_at = tick_at + heads * blocks
        qkvw_load.wait()

        def project(b, c):
            at = row_block(b)
            out = None
            for i in range(3):
                lanes = pl.ds(i * heads * 128, heads * 128)
                narrow = dot_nt(cat[at, lanes], spread).astype(jnp.bfloat16)
                tight[i, at] = narrow
                term = dot_nn(narrow, qkvw_buf[i])
                out = term if out is None else out + term
            part[at] = out

            @pl.when(it == 0)
            def _():
                hid_low[at] = total[at].astype(jnp.bfloat16)

            tick(tick_at + b)
            return c

        lax.fori_loop(0, blocks, project, 0)
        tick_at = tick_at + blocks
        sum_begin(1)
        encoded_store = load(hid_low, encoded, 1)
        pl.when(it == 0)(encoded_store.start)
        normed_load.wait()
        mix_load.wait()

        def attention_weights(j, c):
            sum_step(1, j)

            @pl.when((j >= 1) & (j < 5))
            def _():
                stage_copy(lax.rem(j - 1, 2), base_row, local_width).wait()

            slot = lax.rem(j, 2)

            @pl.when(j < 3)
            def _():
                stage_buf[slot] = dot_tn(tight[j], act_buf[...])

            @pl.when(j == 3)
            def _():
                stage_buf[slot] = dot_tn(mix_buf[...], flow_low[...])

            @pl.when(j < 4)
            def _():
                stage_copy(slot, base_row + off_qkv + j * local_width, local_width).start()

            tick(tick_at + j)
            return c

        lax.fori_loop(0, sum_steps, attention_weights, 0)
        tick_at = tick_at + sum_steps
        state_load.wait()

        def norm_one(b, c):
            at = row_block(b)
            step_grad, gain_grad, shift_grad = norm_back(total[at], wide[at], gain_buf[layer, 0:1])
            small[4:5] += gain_grad
            small[6:7] += shift_grad
            flow[at] = flow[at] + step_grad
            tick(tick_at + b)
            return c

        lax.fori_loop(0, blocks, norm_one, 0)
        tail = pltpu.make_async_copy(
            small, grads.at[pl.ds(pl.multiple_of(base_row + off_small, 8), small.shape[0])], load_sem.at[10]
        )
        tail.start()
        tail.wait()
        pl.when(it == 0)(encoded_store.wait)
        return carry

    lax.fori_loop(0, layers, layer_body, 0)

    def lower(b, c):
        flow_low[row_block(b)] = flow[row_block(b)].astype(jnp.bfloat16)
        return c

    lax.fori_loop(0, blocks, lower, 0)
    image_store = load(flow_low, image_grad, 0)
    image_store.start()

    tail = layers * layer_ticks - FIRST
    weaves, at_step = [], tail
    for k in range(2):
        last_row = (layers - 1) * layer_rows + (k + 1) * units_rows
        ready = -(-last_row // (PARTS * unit)) * ROUND + TICK_SPAN
        at_step = max(at_step, ready)
        weaves.append(at_step)
        at_step += tiles + 1

    def each_size(tile, body):
        pl.when(tile < tiles - 1)(lambda: body(128))
        pl.when(tile == tiles - 1)(lambda: body(last_rows))

    def weave_in(k, tile, layer, rows_here):
        row = pl.multiple_of((layers - 1 - layer) * layer_rows + k * units_rows + tile * 128, 8)
        slot = lax.rem(tile, 2)
        return pltpu.make_async_copy(
            totals.at[pl.ds(row, rows_here)],
            stage_buf.at[slot, pl.ds(layer * 128, rows_here)],
            weave_sem.at[slot, layer],
        )

    def weave_out(target, tile, rows_here):
        slot = lax.rem(tile, 2)
        return pltpu.make_async_copy(
            woven.at[slot, pl.ds(0, rows_here)], target.at[pl.ds(tile * 128, rows_here)], turn_sem.at[slot]
        )

    def weave(k, target, tile):
        def begin(rows_here):
            for layer in range(layers):
                weave_in(k, tile, layer, rows_here).start()

        def arrive(rows_here):
            for layer in range(layers):
                weave_in(k, tile - 1, layer, rows_here).wait()

        each_size(tile, begin)

        @pl.when(tile >= 1)
        def _():
            each_size(tile - 1, arrive)
            slot = lax.rem(tile - 1, 2)

            @pl.when(tile >= 3)
            def _():
                weave_out(target, tile - 3, 128).wait()

            for layer in range(layers):
                woven[slot, :, layer, :] = stage_buf[slot, pl.ds(layer * 128, 128)]
            each_size(tile - 1, lambda rows_here: weave_out(target, tile - 1, rows_here).start())

        @pl.when(tile == tiles)
        def _():
            weave_out(target, tiles - 2, 128).wait()
            weave_out(target, tiles - 1, last_rows).wait()

    def rest(step, c):
        tick(step)
        if dp_sum:
            for k, target in enumerate((down_grad, up_grad)):
                tile = step - weaves[k]

                @pl.when((tile >= 0) & (tile <= tiles))
                def _():
                    weave(k, target, tile)

        return c

    lax.fori_loop(tail, max(steps + TICK_SPAN, at_step), rest, 0)
    image_store.wait()


def backward(
    tokens, head_dim, hidden_units, unit, collective_id, dp_sum,
    cotangent, hidden, active, normed_two, normed, middle, state, qkv, logsum, mixed,
    down, up, qkv_w, out_w, gain, last_part,
):
    layers, rows, width = middle.shape
    heads = qkv.shape[2]
    units_rows = -(-hidden_units // 8) * 8
    send_rows = -(-tokens // (2 * PIECE)) * 2 * PIECE
    pieces = send_rows // (2 * PIECE)
    layer_rows = 2 * units_rows + 4 * heads * head_dim + TAIL_ROWS
    steps = layers * layer_rows // (PARTS * unit) * ROUND
    assert steps * PARTS * unit == layers * layer_rows * ROUND
    buffers, sems = tick_scratch(unit, width)
    f32, low = jnp.float32, jnp.bfloat16
    half = (send_rows // 2, width)
    full = (rows, width)
    any_spec = pl.BlockSpec(memory_space=pl.ANY)
    grads = jax.ShapeDtypeStruct((layers * layer_rows, width), f32)
    return pl.pallas_call(
        functools.partial(
            backward_kernel, dp_sum, tokens, layers, heads, units_rows, head_dim, send_rows, unit, steps
        ),
        out_shape=(
            grads,
            grads,
            jax.ShapeDtypeStruct(full, low),
            jax.ShapeDtypeStruct(full, low),
            jax.ShapeDtypeStruct((units_rows, layers, width), f32),
            jax.ShapeDtypeStruct((units_rows, layers, width), f32),
        ),
        in_specs=[any_spec] * 16,
        out_specs=(any_spec,) * 6,
        scratch_shapes=[
            pltpu.VMEM(cotangent.shape, low),
            pltpu.VMEM(full, f32),
            pltpu.VMEM(full, low),
            pltpu.VMEM(full, low),
            pltpu.VMEM(qkv.shape[1:], low),
            pltpu.VMEM(logsum.shape[1:], f32),
            pltpu.VMEM(mixed.shape[1:], low),
            pltpu.VMEM(down.shape[1:], low),
            pltpu.VMEM(up.shape[1:], low),
            pltpu.VMEM(qkv_w.shape[1:], low),
            pltpu.VMEM(out_w.shape[1:], low),
            pltpu.VMEM(gain.shape, f32),
            pltpu.VMEM(full, f32),
            pltpu.VMEM(full, low),
            pltpu.VMEM(full, low),
            pltpu.VMEM(full, f32),
            pltpu.VMEM(full, f32),
            pltpu.VMEM(half, f32),
            pltpu.VMEM(half, f32),
            pltpu.VMEM((3,) + half, f32),
            pltpu.VMEM((rows, heads * 128), low),
            pltpu.VMEM((rows, 3 * heads * 128), low),
            pltpu.VMEM((3, rows, heads * head_dim), low),
            pltpu.VMEM((rows, 128), f32),
            pltpu.VMEM((rows, 128), f32),
            pltpu.VMEM((2, heads * head_dim, width), f32),
            pltpu.VMEM((TAIL_ROWS, width), f32),
            pltpu.VMEM((2, 128, layers, width), f32),
        ]
        + [pltpu.SemaphoreType.DMA((12,)), pltpu.SemaphoreType.DMA((2,)), pltpu.SemaphoreType.DMA((2,)), pltpu.SemaphoreType.DMA((2, layers))]
        + [pltpu.SemaphoreType.DMA((3, pieces))] * 6
        + buffers
        + sems,
        compiler_params=pltpu.CompilerParams(
            collective_id=collective_id, has_side_effects=True, vmem_limit_bytes=63 << 20
        ),
    )(
        cotangent, hidden, active, normed_two, normed, middle, state, qkv, logsum, mixed,
        down, up, qkv_w, out_w, gain, last_part,
    )


def lift_rows(source, target, tokens, size):
    blocks = target.shape[0] // size

    def one(b, c):
        at = pl.ds(pl.multiple_of(b * size, 16), size)
        target[at] = source[at].astype(jnp.float32)
        return c

    lax.fori_loop(0, blocks - 1, one, 0)
    begin = (blocks - 1) * size
    target[pl.ds(begin, size)] = jnp.zeros((size, target.shape[1]), jnp.float32)
    last = pl.ds(begin, tokens - begin)
    target[last] = source[last].astype(jnp.float32)


def lower_rows(source, target, wide, tokens):
    full = tokens // BLOCK

    def one(b, c):
        at = pl.ds(pl.multiple_of(b * BLOCK, 16), BLOCK)
        target[at] = source[at]
        return c

    lax.fori_loop(0, full, one, 0)
    tail = pl.ds(full * BLOCK, target.shape[0] - full * BLOCK)
    wide[tail] = jnp.zeros((target.shape[0] - full * BLOCK, target.shape[1]), jnp.float32)
    some = pl.ds(full * BLOCK, tokens - full * BLOCK)
    wide[some] = source[some].astype(jnp.float32)
    target[tail] = wide[tail].astype(jnp.bfloat16)


def spread_matrix(heads, head_dim):
    shape = (heads * head_dim, heads * 128)
    source = lax.broadcasted_iota(jnp.int32, shape, 0)
    lane = lax.broadcasted_iota(jnp.int32, shape, 1)
    hit = (lane // 128 * head_dim + lane % 128 == source) & (lane % 128 < head_dim)
    return jnp.where(hit, 1.0, 0.0).astype(jnp.bfloat16)


def norm_unit(state):
    centred = state - jnp.mean(state, axis=-1, keepdims=True)
    return centred * lax.rsqrt(jnp.mean(centred * centred, axis=-1, keepdims=True) + EPSILON)


def gelu(v):
    return 0.5 * v * (1.0 + jnp.tanh(0.7978845608028654 * (v + 0.044715 * (v * v * v))))


def block_sum(pieces, dp, tensor, part, core_in, y_in, total, sems):
    core = tensor % 2
    core_peer = (dp, tensor + 1 - 2 * core)
    y_peer = (dp, lax.rem(tensor + 2, 4))
    core_sem, y_sem, back_sem = sems
    per_block = WIDE_BLOCK // (2 * PIECE)

    def mine(i):
        return pl.ds(pl.multiple_of((2 * i + core) * PIECE, 8), PIECE)

    def other(i):
        return pl.ds(pl.multiple_of((2 * i + 1 - core) * PIECE, 8), PIECE)

    def here(i):
        return pl.ds(pl.multiple_of(i * PIECE, 8), PIECE)

    def remote(src, dst, sem, i, peer):
        return pltpu.make_async_remote_copy(
            src_ref=src, dst_ref=dst, send_sem=sem.at[0, i], recv_sem=sem.at[1, i],
            device_id=peer, device_id_type=MESH,
        )

    def to_core(i):
        return remote(part.at[other(i)], core_in.at[here(i)], core_sem, i, core_peer)

    def to_y(i):
        return remote(core_in.at[here(i)], y_in.at[here(i)], y_sem, i, y_peer)

    def to_back(i):
        return remote(total.at[mine(i)], total.at[mine(i)], back_sem, i, core_peer)

    def from_back(i):
        return remote(total.at[other(i)], total.at[other(i)], back_sem, i, core_peer)

    def each(b, body):
        def go(k, c):
            i = b * per_block + k

            @pl.when(i < pieces)
            def _():
                body(i)

            return c

        lax.fori_loop(0, per_block, go, 0)

    def send(b):
        each(b, lambda i: to_core(i).start())

    def meet(b):
        def body(i):
            to_core(i).wait_recv()
            core_in[here(i)] = core_in[here(i)] + part[mine(i)]
            to_y(i).start()

        each(b, body)

    def close(b):
        def body(i):
            to_y(i).wait_recv()
            total[mine(i)] = core_in[here(i)] + y_in[here(i)]
            to_back(i).start()

        each(b, body)

    def finish(b):
        def body(i):
            to_core(i).wait_send()
            to_y(i).wait_send()
            to_back(i).wait_send()
            from_back(i).wait_recv()

        each(b, body)

    return send, meet, close, finish


def pair_sum(pieces, dp, tensor, part, core_in, total, sems):
    core = tensor % 2
    core_peer = (dp, tensor + 1 - 2 * core)
    core_sem, back_sem = sems
    per_block = WIDE_BLOCK // (2 * PIECE)

    def mine(i):
        return pl.ds(pl.multiple_of((2 * i + core) * PIECE, 8), PIECE)

    def other(i):
        return pl.ds(pl.multiple_of((2 * i + 1 - core) * PIECE, 8), PIECE)

    def here(i):
        return pl.ds(pl.multiple_of(i * PIECE, 8), PIECE)

    def remote(src, dst, sem, i):
        return pltpu.make_async_remote_copy(
            src_ref=src, dst_ref=dst, send_sem=sem.at[0, i], recv_sem=sem.at[1, i],
            device_id=core_peer, device_id_type=MESH,
        )

    def to_core(i):
        return remote(part.at[other(i)], core_in.at[here(i)], core_sem, i)

    def to_back(i):
        return remote(total.at[mine(i)], total.at[mine(i)], back_sem, i)

    def from_back(i):
        return remote(total.at[other(i)], total.at[other(i)], back_sem, i)

    def each(b, body):
        def go(k, c):
            i = b * per_block + k

            @pl.when(i < pieces)
            def _():
                body(i)

            return c

        lax.fori_loop(0, per_block, go, 0)

    def send(b):
        each(b, lambda i: to_core(i).start())

    def meet(b):
        def body(i):
            to_core(i).wait_recv()
            total[mine(i)] = core_in[here(i)] + part[mine(i)]
            to_back(i).start()

        each(b, body)

    def finish(b):
        def body(i):
            to_core(i).wait_send()
            to_back(i).wait_send()
            from_back(i).wait_recv()

        each(b, body)

    return send, meet, finish


def forward_kernel(
    dp_size, tokens, layers, heads, head_dim, send_rows,
    images, qkv_w, qv_b, out_w, out_b, up, up_b, down, down_b, gain, shift,
    hidden, active, normed_two, normed, middle, state, qkv, logsum, mixed, down_rows, up_rows, last_part,
    image_buf, upb_raw, flow, normed_buf, qkv_buf, lse_buf, mix_buf, tight_buf, two_buf, hidden_buf, active_buf,
    qkvw_buf, outw_buf, up_buf, down_buf, qvb_buf, outb_buf, upb_buf, downb_buf, gain_buf, shift_buf,
    part_a, core_in_a, total_a, part_b, core_in_b, y_in_b, total_b,
    quarter_buf, y_rows, both_w, both_mix, packed, y_packed,
    pair_buf, edge_buf, load_sem, weight_sem, store_sem, block_sem, split_sem, split_out_sem,
    quarter_sem, rows_sem, packed_sem, *sum_sems
):
    rows, width = flow.shape
    local_width = heads * head_dim
    blocks = rows // WIDE_BLOCK
    pieces = send_rows // (2 * PIECE)
    dp = lax.axis_index("dp")
    tensor = lax.axis_index("tensor")
    core = tensor % 2
    barrier = pltpu.get_barrier_semaphore()
    y_peer = (dp, lax.rem(tensor + 2, 4))
    upper = tensor // 2
    spot = dp % 4
    spot_one = spot + 1 - 2 * (dp % 2)
    spot_two = lax.rem(spot + 2, 4)
    peer_one = (dp + 1 - 2 * (dp % 2), tensor)
    peer_two = (dp + 2 - 4 * (spot // 2), tensor)
    for peer in [(dp, tensor + 1 - 2 * core), y_peer, peer_one, peer_two]:
        pl.semaphore_signal(barrier, inc=1, device_id=peer, device_id_type=MESH)
    quarter = quarter_buf.shape[1]
    group = packed.shape[1]

    def remote(src, dst, sem, peer):
        return pltpu.make_async_remote_copy(
            src_ref=src, dst_ref=dst, send_sem=sem[0], recv_sem=sem[1], device_id=peer, device_id_type=MESH
        )

    def quarter_rows(at):
        return pl.ds(pl.multiple_of(at * quarter, 8), quarter)

    def quarter_out(layer):
        return remote(
            quarter_buf.at[layer], y_rows.at[layer, quarter_rows(spot)],
            (quarter_sem.at[0, layer], quarter_sem.at[1, layer]), y_peer,
        )

    def rows_copy(layer, k, at, peer):
        here = y_rows.at[layer, quarter_rows(at)]
        return remote(here, here, (rows_sem.at[0, layer, k], rows_sem.at[1, layer, k]), peer)

    def rows_out(layer, k):
        at, peer = ((spot, peer_one), (spot, peer_two), (spot_one, peer_two))[k]
        return rows_copy(layer, k, at, peer)

    def rows_back(layer, k):
        at, peer = ((spot_one, peer_one), (spot_two, peer_two), (3 - spot, peer_two))[k]
        return rows_copy(layer, k, at, peer)

    def share_own(layer):
        quarter_out(layer).wait_recv()
        rows_out(layer, 0).start()
        rows_out(layer, 1).start()

    def share_other(layer):
        rows_back(layer, 0).wait_recv()
        rows_out(layer, 2).start()

    def packed_out(layer, b):
        return remote(
            packed.at[b], y_packed.at[layer, b], (packed_sem.at[0, layer, b], packed_sem.at[1, layer, b]), y_peer
        )

    def weights(layer):
        return (pltpu.make_async_copy(qkv_w.at[layer], qkvw_buf, weight_sem.at[0]),)

    tiles = up_buf.shape[0] // 128
    units = up.shape[0]
    last_units = units - (tiles - 1) * 128

    def split_in(k, tile, size):
        slot = lax.rem(k * tiles + tile, SPLIT_SLOTS)
        source = (up, down)[k]
        return pltpu.make_async_copy(
            source.at[pl.ds(tile * 128, size)], pair_buf.at[slot, pl.ds(0, size)], split_sem.at[0, slot]
        )

    def split_size(tile, body):
        pl.when(tile < tiles - 1)(lambda: body(128))
        pl.when(tile == tiles - 1)(lambda: body(last_units))

    def split_begin():
        for tile in range(SPLIT_SLOTS - 1):
            split_in(0, tile, 128).start()

    def split_out(k, layer):
        source, target = ((up_buf, up_rows), (down_buf, down_rows))[k]
        return pltpu.make_async_copy(source, target.at[layer], split_out_sem.at[k])

    def split(layer):
        for k, target in enumerate((up_buf, down_buf)):

            def one(tile, c):
                slot = lax.rem(k * tiles + tile, SPLIT_SLOTS)
                ahead = tile + SPLIT_SLOTS - 1
                pl.when(ahead < tiles)(lambda: split_size(ahead, lambda size: split_in(k, ahead, size).start()))
                if k == 0:
                    pl.when(ahead >= tiles)(lambda: split_in(1, ahead - tiles, 128).start())
                split_size(tile, lambda size: split_in(k, tile, size).wait())
                at = pl.ds(pl.multiple_of(tile * 128, 128), 128)

                @pl.when(tile < tiles - 1)
                def _():
                    target[at] = pair_buf[slot, :, layer, :]

                @pl.when(tile == tiles - 1)
                def _():
                    edge_buf[...] = jnp.zeros_like(edge_buf)
                    edge_buf[pl.ds(0, last_units)] = pair_buf[slot, pl.ds(0, last_units), layer, :].astype(jnp.float32)
                    target[at] = edge_buf[...].astype(jnp.bfloat16)

                return c

            lax.fori_loop(0, tiles, one, 0)
            split_out(k, layer).start()


    singles = [
        pltpu.make_async_copy(source, target, load_sem.at[i])
        for i, (source, target) in enumerate(
            (
                (out_w, outw_buf), (images, image_buf), (gain, gain_buf), (shift, shift_buf), (qv_b, qvb_buf),
                (out_b, outb_buf), (up_b, upb_raw), (down_b, downb_buf),
            )
        )
    ]
    for copy in singles:
        copy.start()
    current = weights(0)
    current[0].start()
    split_begin()
    spread = spread_matrix(heads, head_dim)
    total_a[pl.ds(send_rows, rows - send_rows)] = jnp.zeros((rows - send_rows, width), jnp.float32)
    total_b[pl.ds(send_rows, rows - send_rows)] = jnp.zeros((rows - send_rows, width), jnp.float32)
    singles[0].wait()
    for k in range(4):

        @pl.when(spot == k)
        def _():
            lead_rows = k * quarter % 16
            for layer in range(layers):
                some = outw_buf[layer, pl.ds(k * quarter - lead_rows, quarter + 8)].astype(jnp.float32)
                quarter_buf[layer] = some[lead_rows : lead_rows + quarter]

    pl.semaphore_wait(barrier, 4)
    quarter_out(0).start()
    for copy in singles[1:]:
        copy.wait()

    def row_block(b):
        return pl.ds(pl.multiple_of(b * WIDE_BLOCK, 16), WIDE_BLOCK)

    scale = head_dim ** (-0.5)
    stores = {}

    def block_store(layer, b, kind):
        at = row_block(b)
        source, target = (
            (flow, middle.at[layer, at]),
            (two_buf, normed_two.at[layer, at]),
            (hidden_buf, hidden.at[layer, at]),
            (active_buf, active.at[layer, at]),
            (part_b, last_part.at[at]),
        )[kind]
        return pltpu.make_async_copy(source.at[at], target, block_sem.at[kind, b])

    def keep(name, source, target, index):
        copy = pltpu.make_async_copy(source, target, store_sem.at[index])
        copy.start()
        stores[name] = copy

    def settle(*names):
        for name in names:
            if name in stores:
                stores.pop(name).wait()

    def project(layer, b, value):
        at = row_block(b)
        flow[at] = value
        low = (norm_unit(value) * gain_buf[layer, 0:1] + shift_buf[layer, 0:1]).astype(jnp.bfloat16)
        normed_buf[at] = low
        for i in range(3):
            out = dot_nt(low, qkvw_buf[i])
            if i != 1:
                out = out + qvb_buf[layer, i // 2 : i // 2 + 1]
            wide = dot_nn(out.astype(jnp.bfloat16), spread).astype(jnp.bfloat16)
            for head in range(heads):
                qkv_buf[i, head, at] = wide[:, head * 128 : (head + 1) * 128]

    def first(b, c):
        project(0, b, flow[row_block(b)])
        return c

    lift_rows(image_buf, flow, tokens, WIDE_BLOCK)
    upb_buf[...] = jnp.zeros_like(upb_buf)
    upb_buf[:, pl.ds(0, upb_raw.shape[1])] = upb_raw[...]
    current[0].wait()
    lax.fori_loop(0, blocks, first, 0)

    for layer in range(layers):
        keep("state", flow, state.at[layer], 0)
        keep("normed", normed_buf, normed.at[layer], 1)
        keep("qkv", qkv_buf, qkv.at[layer], 2)
        settle("logsum", "mixed")
        send_a, meet_a, finish_a = pair_sum(
            pieces, dp, tensor, part_a, core_in_a, total_a, [s.at[layer] for s in sum_sems[:2]]
        )
        send_b, meet_b, close_b, finish_b = block_sum(
            pieces, dp, tensor, part_b, core_in_b, y_in_b, total_b, [s.at[layer] for s in sum_sems[2:]]
        )
        is_last = layer == layers - 1
        if not is_last:
            following = weights(layer + 1)
            following[0].start()

        both_w[upper] = outw_buf[layer]

        def attend(b, c):
            if layer == 0:
                pl.when(b == 1)(lambda: share_own(0))
            at = row_block(b)

            def one_head(head):
                scores = dot_nt(qkv_buf[0, head, at], qkv_buf[1, head]) * scale
                whole = tokens // 128 * 128
                edge = scores[:, whole:]
                column = lax.broadcasted_iota(jnp.int32, edge.shape, 1) + whole
                edge = jnp.where(column < tokens, edge, -jnp.inf)
                scores = jnp.concatenate([scores[:, :whole], edge], axis=1)
                peak = jnp.max(scores, axis=-1, keepdims=True)
                expo = jnp.exp(scores - peak)
                denominator = jnp.sum(expo, axis=-1, keepdims=True)
                probs = (expo * (1.0 / denominator)).astype(jnp.bfloat16)
                value = dot_nn(probs, qkv_buf[2, head]).astype(jnp.bfloat16)
                return value, jnp.broadcast_to(peak + jnp.log(denominator), (WIDE_BLOCK, 128))

            def two_heads(pair, c):
                both = [one_head(2 * pair + i) for i in range(2)]
                for i, (value, logs) in enumerate(both):
                    head = 2 * pair + i
                    mix_buf[:, pl.ds(pl.multiple_of(head * 128, 128), 128)] = value
                    lse_buf[head, at] = logs
                return c

            lax.fori_loop(0, heads // 2, two_heads, 0)
            tight = dot_nt(mix_buf[...], spread).astype(jnp.bfloat16)
            tight_buf[at] = tight
            loose = tight.astype(jnp.float32)
            for g in range(heads):
                packed[b, :, g * local_width : (g + 1) * local_width] = loose[g * group : (g + 1) * group]
            packed_out(layer, b).start()
            return c

        lax.fori_loop(0, blocks, attend, 0)
        if layer == 0:
            share_other(0)
        if not is_last:
            quarter_out(layer + 1).start()
        keep("logsum", lse_buf, logsum.at[layer], 3)
        keep("mixed", tight_buf, mixed.at[layer], 4)
        settle("state")
        if layer == 0:
            split(0)
        for k in (1, 2):
            rows_back(layer, k).wait_recv()
        both_w[1 - upper] = y_rows[layer].astype(jnp.bfloat16)

        def output(b):
            packed_out(layer, b).wait_recv()
            both_mix[upper] = tight_buf[row_block(b)]
            for g in range(heads):
                both_mix[1 - upper, pl.ds(g * group, group)] = y_packed[
                    layer, b, :, g * local_width : (g + 1) * local_width
                ].astype(jnp.bfloat16)
            part_a[row_block(b)] = dot_nn(both_mix[0], both_w[0]) + dot_nn(both_mix[1], both_w[1])
            send_a(b)

        def mlp(b):
            at = row_block(b)
            finish_a(b)
            value = flow[at] + total_a[at] + outb_buf[layer : layer + 1]
            flow[at] = value
            block_store(layer, b, 0).start()
            low = (norm_unit(value) * gain_buf[layer, 1:2] + shift_buf[layer, 1:2]).astype(jnp.bfloat16)
            two_buf[at] = low
            hid = dot_nt(low, up_buf[...]) + upb_buf[layer : layer + 1]
            hidden_buf[at] = hid
            act = gelu(hid).astype(jnp.bfloat16)
            active_buf[at] = act
            for kind in range(1, 4):
                block_store(layer, b, kind).start()
            partial = dot_nn(act, down_buf[...])
            if is_last:
                lead = jnp.where(tensor == 0, 1.0, 0.0)
                partial = partial + lead * (value + downb_buf[layer : layer + 1])
            part_b[at] = partial
            if is_last:
                block_store(layer, b, 4).start()
            else:
                send_b(b)

        def output_and_mlp(b, c):
            pl.when(b > 0)(lambda: meet_a(b - 1))
            pl.when(b < blocks)(lambda: output(b))
            if not is_last:
                pl.when(b > 1)(lambda: meet_b(b - 2))
            pl.when(b > 0)(lambda: mlp(b - 1))
            return c

        lax.fori_loop(0, blocks + 1, output_and_mlp, 0)
        if not is_last:
            meet_b(blocks - 1)
        quarter_out(layer).wait_send()
        for k in range(3):
            rows_out(layer, k).wait_send()
        for b in range(blocks):
            packed_out(layer, b).wait_send()
        if not is_last:
            share_own(layer + 1)

        def stored(*kinds):
            def one(b, c):
                for kind in kinds:
                    block_store(layer, b, kind).wait()
                return c

            lax.fori_loop(0, blocks, one, 0)

        if is_last:
            stored(0, 1, 2, 3, 4)
        else:
            for k in range(2):
                split_out(k, layer).wait()
            split_begin()
            split(layer + 1)
            following[0].wait()
            settle("normed", "qkv")

            def next_project(b, c):
                at = row_block(b)
                close_b(b)
                finish_b(b)
                block_store(layer, b, 0).wait()
                project(layer + 1, b, flow[at] + total_b[at] + downb_buf[layer : layer + 1])
                return c

            lax.fori_loop(0, blocks, next_project, 0)
            share_other(layer + 1)
            stored(1, 2, 3)
            current = following
    for k in range(2):
        split_out(k, layers - 1).wait()
    settle(*list(stores))


def forward(
    dp_size, tokens, head_dim, collective_id,
    images, qkv_w, qv_b, out_w, out_b, up, up_b, down, down_b, gain, shift,
):
    layers = qkv_w.shape[0]
    width = images.shape[1]
    rows = -(-tokens // WIDE_BLOCK) * WIDE_BLOCK
    heads = qkv_w.shape[2] // head_dim
    units = -(-up.shape[0] // 128) * 128
    send_rows = -(-tokens // (2 * PIECE)) * 2 * PIECE
    pieces = send_rows // (2 * PIECE)
    f32, low = jnp.float32, jnp.bfloat16
    full = (rows, width)
    half = (send_rows // 2, width)
    any_spec = pl.BlockSpec(memory_space=pl.ANY)

    def out(shape, dtype):
        return jax.ShapeDtypeStruct(shape, dtype)

    lanes = heads * 128
    blocks = rows // WIDE_BLOCK
    local_width = heads * head_dim
    return pl.pallas_call(
        functools.partial(forward_kernel, dp_size, tokens, layers, heads, head_dim, send_rows),
        out_shape=(
            out((layers, rows, units), f32),
            out((layers, rows, units), low),
            out((layers,) + full, low),
            out((layers,) + full, low),
            out((layers,) + full, f32),
            out((layers,) + full, f32),
            out((layers, 3, heads, rows, 128), low),
            out((layers, heads, rows, 128), f32),
            out((layers, rows, heads * head_dim), low),
            out((layers, units, width), low),
            out((layers, units, width), low),
            out(full, f32),
        ),
        in_specs=[any_spec] * 11,
        out_specs=(any_spec,) * 12,
        scratch_shapes=[
            pltpu.VMEM(images.shape, low),
            pltpu.VMEM(up_b.shape, f32),
            pltpu.VMEM(full, f32),
            pltpu.VMEM(full, low),
            pltpu.VMEM((3, heads, rows, 128), low),
            pltpu.VMEM((heads, rows, 128), f32),
            pltpu.VMEM((WIDE_BLOCK, lanes), low),
            pltpu.VMEM((rows, heads * head_dim), low),
            pltpu.VMEM(full, low),
            pltpu.VMEM((rows, units), f32),
            pltpu.VMEM((rows, units), low),
            pltpu.VMEM(qkv_w.shape[1:], low),
            pltpu.VMEM(out_w.shape, low),
            pltpu.VMEM((units, width), low),
            pltpu.VMEM((units, width), low),
            pltpu.VMEM(qv_b.shape, f32),
            pltpu.VMEM(out_b.shape, f32),
            pltpu.VMEM((layers, units), f32),
            pltpu.VMEM(down_b.shape, f32),
            pltpu.VMEM(gain.shape, f32),
            pltpu.VMEM(shift.shape, f32),
        ]
        + [pltpu.VMEM(s, f32) for s in (full, half, full, full, half, half, full)]
        + [
            pltpu.VMEM((layers, local_width // 4, width), f32),
            pltpu.VMEM((layers, local_width, width), f32),
            pltpu.VMEM((2, local_width, width), low),
            pltpu.VMEM((2, WIDE_BLOCK, local_width), low),
            pltpu.VMEM((blocks, WIDE_BLOCK // heads, heads * local_width), f32),
            pltpu.VMEM((layers, blocks, WIDE_BLOCK // heads, heads * local_width), f32),
            pltpu.VMEM((SPLIT_SLOTS, 128, layers, width), low),
            pltpu.VMEM((128, width), f32),
            pltpu.SemaphoreType.DMA((8,)),
            pltpu.SemaphoreType.DMA((1,)),
            pltpu.SemaphoreType.DMA((9,)),
            pltpu.SemaphoreType.DMA((5, rows // WIDE_BLOCK)),
            pltpu.SemaphoreType.DMA((1, SPLIT_SLOTS)),
            pltpu.SemaphoreType.DMA((2,)),
            pltpu.SemaphoreType.DMA((2, layers)),
            pltpu.SemaphoreType.DMA((2, layers, 3)),
            pltpu.SemaphoreType.DMA((2, layers, blocks)),
        ]
        + [pltpu.SemaphoreType.DMA((layers, 2, pieces))] * 5,
        compiler_params=pltpu.CompilerParams(
            collective_id=collective_id, has_side_effects=True, vmem_limit_bytes=63 << 20
        ),
    )(images, qkv_w, qv_b, out_w, out_b, up, up_b, down, down_b, gain, shift)


def finish_kernel(
    layers, heads, head_dim, hidden_units, layer_rows, off_qkv,
    totals, down_rows, up_rows, image_rows, encoded_rows,
    encoded, image_grad, qkv_grad, qv_grad, out_grad, out_b, up_grad, up_b, down_grad, down_b, gain, shift,
    down_buf, up_wide, rows_buf, long_a, long_b, short_a, short_b, small, qv_buf, up_buf, plain, pair, sem,
):
    width = totals.shape[1]
    local_width = heads * head_dim
    count = [0]

    def move(source, target):
        copy = pltpu.make_async_copy(source, target, sem.at[count[0]])
        count[0] += 1
        copy.start()
        return copy

    small_rows = small.shape[1]
    off_small = off_qkv + 4 * local_width
    firsts = [(layers - 1 - l) * layer_rows for l in range(layers)]
    fetch = [move(totals.at[pl.ds(firsts[l] + off_small, small_rows)], small.at[l]) for l in range(layers)]
    fetch_a = move(encoded_rows, long_a)
    fetch_b = move(image_rows, long_b)
    through = []
    for source, buffer, target in ((down_rows, down_buf, down_grad), (up_rows, up_wide, up_grad)):
        for at in range(0, hidden_units, 128):
            here = pl.ds(at, min(128, hidden_units - at))
            through.append((move(source.at[here], buffer.at[here]), buffer.at[here], target.at[here]))
    for l in range(layers):
        begin = firsts[l] + off_qkv
        for i in range(4):
            rows = pl.ds(begin + i * local_width, local_width)
            target = qkv_grad.at[l, i] if i < 3 else out_grad.at[l]
            through.append((move(totals.at[rows], rows_buf.at[l, i]), rows_buf.at[l, i], target))
    moves = []
    for arrived, buffer, target in through:
        arrived.wait()
        moves.append(move(buffer, target))
    for copy in fetch:
        copy.wait()
    for l in range(layers):
        for i in range(2):
            for h in range(heads):
                lane = (i * heads + h) * 128
                qv_buf[l, i : i + 1, h * head_dim : (h + 1) * head_dim] = small[l, 0:1, lane : lane + head_dim]
        plain[0, l : l + 1] = small[l, 1:2]
        up_buf[l : l + 1] = small[l, 2:3, :hidden_units]
        plain[1, l : l + 1] = small[l, 3:4]
        pair[0, l] = small[l, 4:6]
        pair[1, l] = small[l, 6:8]
    moves += [
        move(qv_buf, qv_grad), move(plain.at[0], out_b), move(up_buf, up_b), move(plain.at[1], down_b),
        move(pair.at[0], gain), move(pair.at[1], shift),
    ]
    tokens = short_a.shape[0]
    fetch_a.wait()
    short_a[...] = long_a[:tokens]
    moves.append(move(short_a, encoded))
    fetch_b.wait()
    short_b[...] = long_b[:tokens]
    moves.append(move(short_b, image_grad))
    for copy in moves:
        copy.wait()


def finish(tokens, heads, head_dim, hidden_units, totals, down_rows, up_rows, image_rows, encoded_rows):
    layers = down_rows.shape[1]
    width = totals.shape[1]
    rows = image_rows.shape[0]
    layer_rows = totals.shape[0] // layers
    off_qkv = 2 * down_rows.shape[0]
    local_width = heads * head_dim
    f32, low = jnp.float32, jnp.bfloat16
    any_spec = pl.BlockSpec(memory_space=pl.ANY)

    def out(shape, dtype=f32):
        return jax.ShapeDtypeStruct(shape, dtype)

    copies = 4 * -(-hidden_units // 128) + 9 * layers + 10
    return pl.pallas_call(
        functools.partial(finish_kernel, layers, heads, head_dim, hidden_units, layer_rows, off_qkv),
        out_shape=(
            out((tokens, width), low),
            out((tokens, width), low),
            out((layers, 3, local_width, width)),
            out((layers, 2, local_width)),
            out((layers, local_width, width)),
            out((layers, width)),
            out((hidden_units, layers, width)),
            out((layers, hidden_units)),
            out((hidden_units, layers, width)),
            out((layers, width)),
            out((layers, 2, width)),
            out((layers, 2, width)),
        ),
        in_specs=[any_spec] * 5,
        out_specs=(any_spec,) * 12,
        scratch_shapes=[
            pltpu.VMEM((hidden_units, layers, width), f32),
            pltpu.VMEM((hidden_units, layers, width), f32),
            pltpu.VMEM((layers, 4, local_width, width), f32),
            pltpu.VMEM((rows, width), low),
            pltpu.VMEM((rows, width), low),
            pltpu.VMEM((tokens, width), low),
            pltpu.VMEM((tokens, width), low),
            pltpu.VMEM((layers, TAIL_ROWS, width), f32),
            pltpu.VMEM((layers, 2, local_width), f32),
            pltpu.VMEM((layers, hidden_units), f32),
            pltpu.VMEM((2, layers, width), f32),
            pltpu.VMEM((2, layers, 2, width), f32),
            pltpu.SemaphoreType.DMA((copies,)),
        ],
        compiler_params=pltpu.CompilerParams(has_side_effects=True, vmem_limit_bytes=56 << 20),
    )(totals, down_rows, up_rows, image_rows, encoded_rows)


def local(
    dp_size,
    images,
    qkv_weight,
    qv_bias,
    out_weight,
    out_bias,
    up_weight,
    up_bias,
    down_weight,
    down_bias,
    norm_gain,
    norm_shift,
    cotangent,
):
    tokens, width = images.shape[1:]
    layers = qkv_weight.shape[0]
    local_width = qkv_weight.shape[3]
    heads = local_width // HEAD
    hidden_units = up_weight.shape[2]
    qkv_rows = jnp.swapaxes(qkv_weight, 2, 3)
    up = jnp.transpose(up_weight, (2, 0, 1))
    down = jnp.swapaxes(down_weight, 0, 1)
    *kept, last_part = forward(
        dp_size, tokens, HEAD, 0,
        images[0], qkv_rows, qv_bias, out_weight, out_bias, up, up_bias, down, down_bias,
        norm_gain, norm_shift,
    )
    flat, summed, image_grad, encoded, down_rows, up_rows = backward(
        tokens, HEAD, hidden_units, UNIT, 1, dp_size == 8,
        cotangent[0], *kept, qkv_rows, out_weight, norm_gain, last_part,
    )
    if dp_size != 8:
        summed = lax.psum(flat, "dp")
        per_layer = summed.reshape(layers, summed.shape[0] // layers, width)[::-1]
        stop = down_rows.shape[0]
        down_rows = jnp.swapaxes(per_layer[:, :stop], 0, 1)
        up_rows = jnp.swapaxes(per_layer[:, stop : 2 * stop], 0, 1)
    encoded, image_grad, qkv_grad, qv_grad, out_grad, out_b, up_grad, up_b, down_grad, down_b, gain, shift = finish(
        tokens, heads, HEAD, hidden_units, summed, down_rows, up_rows, image_grad, encoded
    )
    return (
        encoded[None],
        image_grad[None],
        jnp.swapaxes(qkv_grad, 2, 3),
        qv_grad,
        out_grad,
        out_b,
        jnp.transpose(up_grad, (1, 2, 0)),
        up_b,
        jnp.swapaxes(down_grad, 0, 1),
        down_b,
        gain,
        shift,
    )


def solution(mesh):
    in_specs = (
        P("dp", None, None),
        P(None, None, None, "tensor"),
        P(None, None, "tensor"),
        P(None, "tensor", None),
        P(),
        P(None, None, "tensor"),
        P(None, "tensor"),
        P(None, "tensor", None),
        P(),
        P(),
        P(),
        P("dp", None, None),
    )
    out_specs = (
        P("dp", None, None),
        P("dp", None, None),
        P(None, None, None, "tensor"),
        P(None, None, "tensor"),
        P(None, "tensor", None),
        P(),
        P(None, None, "tensor"),
        P(None, "tensor"),
        P(None, "tensor", None),
        P(),
        P(),
        P(),
    )
    return jax.shard_map(
        functools.partial(local, mesh.shape["dp"]), mesh=mesh, in_specs=in_specs, out_specs=out_specs, check_vma=False)
```
